32 devices in a mesh: dp: 8 (over z, y), vocab: 4 (over x, core).
Axes of the slice: x: 2, y: 2, z: 4, core: 2. Of those that a mesh axis runs over, the one named last changes fastest.
Arguments:
- tokens: int32 [2, 8, 1024], P(None, 'dp', 'vocab'), may hold values from 0 to 32127
- targets: int32 [2, 8, 1024], P(None, 'dp', 'vocab'), may hold values from 0 to 32127
- loss_mask: int32 [2, 8, 1024], P(None, 'dp', 'vocab'), may hold values from 0 to 1
- seg_lengths: int32 [2, 8, 3], P(None, 'dp'), may hold values from 101 to 822, as said below
- task_ids: int32 [2, 8, 3], P(None, 'dp'), may hold values from 0 to 7
- embedding: bfloat16 [32128, 768], P('vocab'), may hold values from -24 to 24
- attend_in: bfloat16 [3, 768, 2304], P(None, 'dp'), may hold values from -0.21875 to 0.21875
- attend_out: bfloat16 [3, 768, 768], P(None, 'dp'), may hold values from -4 to 4
- expand_weights: bfloat16 [2, 768, 3072], P(None, 'dp'), may hold values from -0.21875 to 0.21875
- reduce_weights: bfloat16 [2, 3072, 768], P(None, 'dp'), may hold values from -0.109375 to 0.109375
- norm_gains: float32 [7, 768], replicated, may hold values from 0.25 to 1.75
- prompt: float32 [8, 100, 768], P(None, None, 'vocab'), may hold values from -6 to 6
- first_moment: float32 [8, 100, 768], P(None, None, 'vocab'), may hold values from -4.4703484e-08 to 4.4703484e-08
- row_moment: float32 [8, 100], replicated, may hold values from 6.5104165e-19 to 2.6041666e-18
- column_moment: float32 [8, 768], P(None, 'vocab'), may hold values from 6.5104165e-19 to 2.6041666e-18
Outputs:
- loss_mean: float32 [], replicated
- grad_norm: float32 [], replicated
- prompt_grad: float32 [8, 100, 768], P(None, None, 'vocab')
- new_moment: float32 [8, 100, 768], P(None, None, 'vocab')
- row_second: float32 [8, 100], replicated
- column_second: float32 [8, 768], P(None, 'vocab')
- new_prompt: float32 [8, 100, 768], P(None, None, 'vocab')
The draws below stay inside these ranges and needn't reach their ends.
Inputs may be any that keep to these rules, and one draw needn't show every extreme that they name: `seg_lengths`: each row holds 3 segments whose lengths sum to 1024; the first and the last are shorter than 256.
All inputs are finite; a program needn't handle non-finite values.
Results may differ from the reference program's by a relative error of at most 0.0058.
Values may be sent and summed in bfloat16 or wider, within the bound.
A program may use at most 384 MiB of HBM per device.

```python
import math
import jax
import jax.numpy as jnp
import numpy as np
from jax import lax

D = 768
FF = 3072
DH = 64
V = 32128
L = 1024
P_SIZE = 100
TASKS = 8
SEGS = 3
MICRO = 2
STEP = 5
ROWS = 8
SPAN = 256


def draw_loss_mask(key, part):
    key = jax.random.fold_in(key, 5)
    positions = jnp.arange(L, dtype=jnp.int32)
    row_index = jnp.arange(ROWS, dtype=jnp.int32)
    position_rate = 300 + 700 * positions // L
    row_rate = 350 + 650 * row_index // ROWS
    threshold = row_rate[:, None] * position_rate[None, :] // 1000
    random_codes = jax.random.randint(key, (MICRO, ROWS, L), 0, 1000)
    return (random_codes < threshold[None]).astype(jnp.int32)


def draw_seg_lengths(key, part):
    key = jax.random.fold_in(key, 7)
    outer_lengths = jax.random.randint(key, (MICRO, ROWS, 2), P_SIZE + 1, SPAN)
    outer_lengths = outer_lengths.at[0, 0].set(P_SIZE + 1)
    middle = L - outer_lengths[..., 0] - outer_lengths[..., 1]
    return jnp.stack([outer_lengths[..., 0], middle, outer_lengths[..., 1]], -1).astype(jnp.int32)


def draw_norm_gains(key, part):
    key = jax.random.fold_in(key, 9)
    fraction = jnp.arange(D, dtype=jnp.float32) / D
    row_scale = 0.5 + fraction
    jitter = jax.random.uniform(key, (7, D), jnp.float32, 0.85, 1.15)
    return (row_scale[None, :] * jitter).astype(jnp.float32)


def draw_embedding(key, part):
    key = jax.random.fold_in(key, 13)
    fraction = jnp.arange(V, dtype=jnp.float32) / V
    entries = jnp.clip(jax.random.normal(key, (V, D), jnp.float32), -7.5, 7.5)
    row_scale = 1.0 + 2.0 * fraction
    return (entries * row_scale[:, None]).astype(jnp.bfloat16)


def place_ends(drawn, stream_key, least, largest):
    dims = drawn.shape
    index_at = [jax.random.randint(jax.random.fold_in(stream_key, axis), (), 0, dims[axis]) for axis in range(len(dims))]
    drawn = drawn.at[tuple(index_at)].set(least)
    longest = dims.index(max(dims))
    index_at[longest] = (index_at[longest] + 1) % dims[longest]
    return drawn.at[tuple(index_at)].set(largest)


def level_of(key, extent, pieces, smallest, high):
    level = 1.0
    for axis_at, blocks in pieces:
        steps = jax.random.uniform(jax.random.fold_in(jax.random.fold_in(key, 6), axis_at), (blocks,), jnp.float32, smallest / len(pieces), high / len(pieces))
        level = level * jnp.repeat(jnp.exp(steps), extent[axis_at] // blocks).reshape((-1,) + (1,) * (len(extent) - 1 - axis_at))
    return level


def rank_table(count, lean):
    loads = [(1 << 20) // math.isqrt(standing ** lean) + 1 for standing in range(1, count + 1)]
    scale = 1 + sum(loads) // (1 << 30)
    return np.cumsum(np.array([max(1, weight // scale) for weight in loads]))


def ranked(key, shape, count, lean):
    grid = rank_table(count, lean)
    pick = jax.random.randint(jax.random.fold_in(key, 1), shape, 0, int(grid[count - 1]))
    grade = jnp.searchsorted(jnp.asarray(grid, jnp.int32), pick, side="right")
    return jax.random.permutation(jax.random.fold_in(key, 2), count)[grade].astype(jnp.int32)


def bell_draw(rng, extent, width, reach, pieces=(), kind=jnp.bfloat16):
    factor_of = level_of(rng, extent, pieces, -0.22, 0.18) if pieces else 1.0
    values = jax.random.normal(rng, extent, jnp.float32) * width * factor_of
    return jnp.minimum(jnp.maximum(values, -reach), reach).astype(kind)


def setup_inputs(seed: int = 0) -> dict:
    arg_keys = jax.random.split(jax.random.key(seed), 16)
    tokens = place_ends(ranked(arg_keys[0], (MICRO, ROWS, L), V, 2), jax.random.fold_in(arg_keys[0], 3), 0, V - 1).astype(jnp.int32)
    targets = place_ends(ranked(arg_keys[1], (MICRO, ROWS, L), V, 2), jax.random.fold_in(arg_keys[1], 3), 0, V - 1).astype(jnp.int32)
    loss_mask = draw_loss_mask(jax.random.fold_in(arg_keys[15], 71), 0)
    seg_lengths = draw_seg_lengths(jax.random.fold_in(arg_keys[15], 71), 0)
    task_ids = place_ends(jax.random.randint(arg_keys[4], (MICRO, ROWS, SEGS), 0, TASKS), jax.random.fold_in(arg_keys[4], 1), 0, TASKS - 1).astype(jnp.int32)
    embedding = draw_embedding(jax.random.fold_in(arg_keys[15], 71), 0)
    attend_in = bell_draw(arg_keys[6], (3, D, 3 * D), D ** -0.5, 0.21875, ((1, 8),))
    attend_out = bell_draw(arg_keys[7], (3, D, D), (3 * D // L) ** -0.5, 4.0, ((1, 8),))
    expand_weights = bell_draw(arg_keys[8], (2, D, FF), D ** -0.5, 0.21875, ((1, 8),))
    reduce_weights = bell_draw(arg_keys[9], (2, FF, D), FF ** -0.5, 0.109375, ((1, 8),))
    norm_gains = draw_norm_gains(jax.random.fold_in(arg_keys[15], 71), 0)
    prompt = bell_draw(arg_keys[11], (TASKS, P_SIZE, D), 1.0, 6.0, ((2, 4),), jnp.float32)
    first_moment = bell_draw(arg_keys[12], (TASKS, P_SIZE, D), (0.0000022 / (TASKS * P_SIZE * D) ** 0.5), 4.470348358154297e-08, ((2, 4),), jnp.float32)
    row_moment = jnp.clip(jnp.exp(jax.random.uniform(arg_keys[13], (TASKS, P_SIZE), jnp.float32, math.log(6.510416517953868e-19), math.log(2.6041666071815472e-18))), 6.510416517953868e-19, 2.6041666071815472e-18)
    column_moment = jnp.clip(jnp.exp(math.log(2.6041666071815472e-18) - 1.3862944 * jax.random.uniform(arg_keys[14], (TASKS, D), jnp.float32) ** level_of(arg_keys[14], (TASKS, D), ((1, 4),), -0.2, 0.2)), 6.510416517953868e-19, 2.6041666071815472e-18)
    return {"tokens": tokens, "targets": targets, "loss_mask": loss_mask, "seg_lengths": seg_lengths, "task_ids": task_ids, "embedding": embedding, "attend_in": attend_in, "attend_out": attend_out, "expand_weights": expand_weights, "reduce_weights": reduce_weights, "norm_gains": norm_gains, "prompt": prompt, "first_moment": first_moment, "row_moment": row_moment, "column_moment": column_moment}


NORM_EPS = 1e-06
CLIP_NORM = 2e-05
BETA_ONE = 0.9
BETA_TWO = 0.999
LEARN_RATE = 1.0
WEIGHT_DECAY = 1e-05
SQUARE_EPS = 1e-30
MASKED = -1e+30
PRECISE = lax.Precision.HIGHEST

@jax.custom_vjp
def low(v):
    return lax.optimization_barrier(v.astype(jnp.bfloat16)).astype(jnp.float32)

@jax.custom_vjp
def low_back(v):
    return v

def low_keep(v):
    return (low(v), None)

def low_pass(kept, grad):
    return (grad,)

def back_keep(v):
    return (v, None)

def back_low(kept, grad):
    return (low(grad),)
low.defvjp(low_keep, low_pass)
low_back.defvjp(back_keep, back_low)

def both_low(values):
    return low_back(low(values))

def matmul(left, right):
    return jnp.dot(left, right, precision=PRECISE)

def normed(values, gain):
    return values * lax.rsqrt(lax.optimization_barrier(jnp.mean(values * values, -1, keepdims=True)) + NORM_EPS) * gain

def layout(lengths, task_list):
    positions = jnp.arange(L, dtype=jnp.int32)
    seg_ends = jnp.cumsum(lengths).astype(jnp.int32)
    seg_starts = seg_ends - lengths
    segment = lax.optimization_barrier(jnp.sum((positions[:, None] >= seg_ends[None, :]).astype(jnp.int32), -1))
    member = segment[:, None] == jnp.arange(SEGS, dtype=jnp.int32)[None, :]
    in_segment = positions - lax.optimization_barrier(jnp.sum(jnp.where(member, seg_starts[None, :], 0), -1))
    task_of = lax.optimization_barrier(jnp.sum(jnp.where(member, task_list[None, :], 0), -1))
    return (segment.astype(jnp.int32), in_segment.astype(jnp.int32), task_of.astype(jnp.int32))

def per_task(task_of, amounts):
    hits = task_of[:, None] == jnp.arange(TASKS, dtype=jnp.int32)[None, :]
    return lax.optimization_barrier(jnp.sum(jnp.where(hits, amounts[:, None], 0.0), 0))

def attend(query_source, key_source, weight_in, weight_out, allowed):
    queries = both_low(matmul(query_source, weight_in[:, :D])).reshape(L, -1, DH)
    key_value = low(matmul(key_source, weight_in[:, D:]))
    key_rows = key_value[:, :D].reshape(L, -1, DH)
    value_rows = key_value[:, D:].reshape(L, -1, DH)
    score_rows = low_back(jnp.einsum('qhd,khd->hqk', queries, key_rows, precision=PRECISE) * DH ** (-0.5))
    score_rows = jnp.where(allowed[None], score_rows, MASKED)
    weights = low(jnp.exp(score_rows - jax.nn.logsumexp(score_rows, -1, keepdims=True)))
    mixed = both_low(jnp.einsum('hqk,khd->qhd', weights, value_rows, precision=PRECISE).reshape(L, D))
    return low_back(matmul(mixed, weight_out))

def feed(source, weight_one, weight_two):
    hidden_pre = low_back(matmul(source, weight_one))
    return low_back(matmul(low(jax.nn.gelu(hidden_pre, approximate=True)), weight_two))

def reference(tokens, targets, loss_mask, seg_lengths, task_ids, embedding, attend_in, attend_out, expand_weights, reduce_weights, norm_gains, prompt, first_moment, row_moment, column_moment):
    vocab_table = embedding.astype(jnp.float32)
    attend_in = attend_in.astype(jnp.float32)
    attend_out = attend_out.astype(jnp.float32)
    expand_weights = expand_weights.astype(jnp.float32)
    reduce_weights = reduce_weights.astype(jnp.float32)

    def one_row(prompt_low, row_tokens, row_targets, row_mask, row_lengths, row_tasks):
        segment, in_segment, task_of = layout(row_lengths, row_tasks)
        is_prompt = in_segment < P_SIZE
        slot_rows = prompt_low[task_of, jnp.minimum(in_segment, P_SIZE - 1)]
        enc_input = jnp.where(is_prompt[:, None], slot_rows, vocab_table[row_tokens])
        shifted = jnp.where(in_segment >= 1, jnp.roll(row_targets, 1), 0)
        dec_input = vocab_table[shifted]
        positions = jnp.arange(L, dtype=jnp.int32)
        allowed = segment[:, None] == segment[None, :]
        causal = allowed & (positions[:, None] >= positions[None, :])
        normed_in = low(normed(enc_input, norm_gains[0]))
        enc_mid = enc_input + attend(normed_in, normed_in, attend_in[0], attend_out[0], allowed)
        enc_last = enc_mid + feed(low(normed(enc_mid, norm_gains[1])), expand_weights[0], reduce_weights[0])
        encoded = low(normed(enc_last, norm_gains[2]))
        normed_dec = low(normed(dec_input, norm_gains[3]))
        dec_first = dec_input + attend(normed_dec, normed_dec, attend_in[1], attend_out[1], causal)
        dec_second = dec_first + attend(low(normed(dec_first, norm_gains[4])), encoded, attend_in[2], attend_out[2], allowed)
        dec_last = dec_second + feed(low(normed(dec_second, norm_gains[5])), expand_weights[1], reduce_weights[1])
        hidden = low(normed(dec_last, norm_gains[6]) * D ** (-0.5))
        logits = low_back(jnp.dot(hidden, vocab_table.T, precision=PRECISE))
        picked = jnp.take_along_axis(logits, row_targets[:, None], -1)[:, 0]
        token_loss = jax.nn.logsumexp(logits, -1) - picked
        counted = (row_mask * (in_segment >= P_SIZE)).astype(jnp.float32)
        return per_task(task_of, counted * token_loss)
    row_step = jax.checkpoint(one_row)
    batch = (tokens.reshape(MICRO * ROWS, L), targets.reshape(MICRO * ROWS, L), loss_mask.reshape(MICRO * ROWS, L), seg_lengths.reshape(MICRO * ROWS, SEGS), task_ids.reshape(MICRO * ROWS, SEGS))

    def summed(prompt_value):
        prompt_low = low(prompt_value)

        def accumulate(carry, row_data):
            return (carry + row_step(prompt_low, row_data[0], row_data[1], row_data[2], row_data[3], row_data[4]), None)
        result, _ = lax.scan(accumulate, jnp.zeros((TASKS,), jnp.float32), batch)
        return result
    task_loss, pullback = jax.vjp(summed, prompt)
    gradient = pullback(jnp.ones((TASKS,), jnp.float32))[0]

    def row_counts(row_mask, row_lengths, row_tasks):
        layout_rows = layout(row_lengths, row_tasks)
        counted = (row_mask * (layout_rows[1] >= P_SIZE)).astype(jnp.float32)
        return per_task(layout_rows[2], counted)
    counts = lax.optimization_barrier(jnp.sum(jax.vmap(row_counts)(batch[2], batch[3], batch[4]), 0))
    task_scale = 1.0 / (TASKS * jnp.maximum(counts, 1.0))
    loss_mean = jnp.sum(task_loss * task_scale)
    full_grad = gradient * task_scale[:, None, None]
    grad_norm = jnp.sqrt(jnp.sum(full_grad * full_grad))
    prompt_grad = full_grad * (CLIP_NORM / jnp.maximum(grad_norm, CLIP_NORM))
    squares = prompt_grad * prompt_grad
    row_second = BETA_TWO * row_moment + (1.0 - BETA_TWO) * (lax.optimization_barrier(jnp.mean(squares, -1)) + SQUARE_EPS)
    column_second = BETA_TWO * column_moment + (1.0 - BETA_TWO) * (lax.optimization_barrier(jnp.mean(squares, 1)) + SQUARE_EPS)
    new_moment = BETA_ONE * first_moment + (1.0 - BETA_ONE) * prompt_grad
    estimate = row_second[:, :, None] * column_second[:, None, :] / lax.optimization_barrier(jnp.mean(row_second, -1))[:, None, None]
    update = new_moment / (1.0 - BETA_ONE ** STEP) / jnp.sqrt(estimate / (1.0 - BETA_TWO ** STEP))
    new_prompt = prompt - LEARN_RATE * (update + WEIGHT_DECAY * prompt)
    return (loss_mean, grad_norm, prompt_grad, new_moment, row_second, column_second, new_prompt)
```

```python
import functools

import jax
import jax.numpy as jnp
from jax import lax
from jax.experimental import pallas as pl
from jax.experimental.pallas import tpu as pltpu
from jax.sharding import PartitionSpec as P

DH = 64
P_SIZE = 100
TASKS = 8
STEP = 5
HALO = 16
LANES = 128
VOCAB_BLOCK = 1024
VMEM_LIMIT = 60 * 1024 * 1024

NORM_EPS = 1e-06
CLIP_NORM = 2e-05
BETA_ONE = 0.9
BETA_TWO = 0.999
LEARN_RATE = 1.0
WEIGHT_DECAY = 1e-05
SQUARE_EPS = 1e-30
MASKED = -1e30

F32 = jnp.float32
BF16 = jnp.bfloat16


def dot(left, right):
    return jnp.dot(left, right, preferred_element_type=F32)


def dot_rows(left, right):
    return lax.dot_general(left, right, (((1,), (1,)), ((), ())), preferred_element_type=F32)


def dot_columns(left, right):
    return lax.dot_general(left, right, (((0,), (0,)), ((), ())), preferred_element_type=F32)


def normed(values, gain):
    inverse = lax.rsqrt(jnp.mean(values * values, -1, keepdims=True) + NORM_EPS)
    return (values * inverse * gain, inverse)


def normed_back(values, gain, inverse, gradient):
    unit_rows = values * inverse
    scaled = gradient * gain
    return inverse * (scaled - unit_rows * jnp.mean(scaled * unit_rows, -1, keepdims=True))


def smooth(values):
    return jax.nn.gelu(values, approximate=True)


def layout(lengths, task_list, positions):
    seg_ends = jnp.cumsum(lengths)
    seg_starts = seg_ends - lengths
    segment = jnp.sum((positions[:, None] >= seg_ends[None, :]).astype(jnp.int32), -1)
    member = segment[:, None] == jnp.arange(lengths.shape[0], dtype=jnp.int32)[None, :]
    in_segment = positions - jnp.sum(jnp.where(member, seg_starts[None, :], 0), -1)
    task_of = jnp.sum(jnp.where(member, task_list[None, :], 0), -1)
    return (segment, in_segment, task_of)


def per_task(task_of, amounts):
    hits = task_of[:, None] == jnp.arange(TASKS, dtype=jnp.int32)
    return jnp.sum(jnp.where(hits, amounts[:, None], 0.0), 0)


def attend_kernel(parts, own, causal, *refs):
    q_ref, k_refs, v_refs = refs[0], refs[1 : 1 + parts], refs[1 + parts : 1 + 2 * parts]
    q_info, k_info, out_ref, bias_ref = refs[1 + 2 * parts :]

    @pl.when(pl.program_id(0) == 0)
    def _():
        keep = q_info[:, 0:1] == k_info[0:1, :]
        if causal:
            keep = keep & (q_info[:, 1:2] >= k_info[1:2, :])
        bias_ref[...] = jnp.where(keep, 0.0, MASKED)

    low_half = lax.broadcasted_iota(jnp.int32, (own, LANES), 1) < DH
    queries = q_ref[...].astype(F32) * DH ** (-0.5)
    mixed = []
    for head in range(LANES // DH):
        query = jnp.where(low_half == (head == 0), queries, 0.0).astype(BF16)
        scores = [
            dot_rows(query, k_refs[k][...]) + bias_ref[:, k * own : (k + 1) * own]
            for k in range(parts)
        ]
        maxima = functools.reduce(jnp.maximum, [jnp.max(s, -1, keepdims=True) for s in scores])
        powers = [jnp.exp(s - maxima) for s in scores]
        total = sum(jnp.sum(p, -1, keepdims=True) for p in powers)
        value = sum(dot(p.astype(BF16), v_refs[k][...]) for k, p in enumerate(powers))
        mixed.append(value / total)
    out_ref[...] = jnp.where(low_half, mixed[0], mixed[1]).astype(BF16)


def attend(queries, pairs, q_info, k_info, causal):
    own, width = queries.shape
    parts, length = len(pairs), k_info.shape[1]
    steps = width // LANES
    key_spec = pl.BlockSpec((own, LANES), lambda i: (0, i))
    value_spec = pl.BlockSpec((own, LANES), lambda i: (0, steps + i))
    return pl.pallas_call(
        functools.partial(attend_kernel, parts, own, causal),
        grid=(steps,),
        out_shape=jax.ShapeDtypeStruct((own, width), BF16),
        in_specs=[key_spec]
        + [key_spec] * parts
        + [value_spec] * parts
        + [
            pl.BlockSpec(q_info.shape, lambda i: (0, 0)),
            pl.BlockSpec(k_info.shape, lambda i: (0, 0)),
        ],
        out_specs=key_spec,
        scratch_shapes=[pltpu.VMEM((own, length), F32)],
        compiler_params=pltpu.CompilerParams(vmem_limit_bytes=VMEM_LIMIT),
        cost_estimate=pl.CostEstimate(
            flops=16 * own * length * width, bytes_accessed=6 * own * width, transcendentals=0
        ),
    )(queries, *pairs, *pairs, q_info, k_info)


def attend_back_kernel(parts, own, block, want_queries, *refs):
    q_ref, k_refs, v_refs = refs[0], refs[1 : 1 + parts], refs[1 + parts : 1 + 2 * parts]
    grad_ref, q_info, k_info = refs[1 + 2 * parts : 4 + 2 * parts]
    rest = refs[4 + 2 * parts :]
    dk_refs, dv_refs = rest[:parts], rest[parts : 2 * parts]
    dq_ref = rest[2 * parts] if want_queries else None
    bias_ref = rest[-1]

    @pl.when(pl.program_id(0) == 0)
    def _():
        bias_ref[...] = jnp.where(k_info[:, 0:1] == q_info[0:1, :], 0.0, MASKED)

    low_half = lax.broadcasted_iota(jnp.int32, (block, LANES), 1) < DH

    def rows(at, first):
        here = pl.ds(pl.multiple_of(at * block, block), block)
        queries = q_ref[here, :].astype(F32) * DH ** (-0.5)
        gradient = grad_ref[here, :].astype(F32)
        dk = [None] * parts
        dv = [None] * parts
        dq = []
        for head in range(LANES // DH):
            mask = low_half == (head == 0)
            query = jnp.where(mask, queries, 0.0).astype(BF16)
            grad = jnp.where(mask, gradient, 0.0).astype(BF16)
            scores = [
                dot_rows(k_refs[k][...], query) + bias_ref[k * own : (k + 1) * own, here]
                for k in range(parts)
            ]
            maxima = functools.reduce(jnp.maximum, [jnp.max(s, 0, keepdims=True) for s in scores])
            powers = [jnp.exp(s - maxima) for s in scores]
            inverse = 1.0 / sum(jnp.sum(p, 0, keepdims=True) for p in powers)
            weights = [p * inverse for p in powers]
            weight_grads = [dot_rows(v_refs[k][...], grad) for k in range(parts)]
            delta = sum(
                jnp.sum(w * dw, 0, keepdims=True) for w, dw in zip(weights, weight_grads)
            )
            score_grads = [
                (w * (dw - delta)).astype(BF16) for w, dw in zip(weights, weight_grads)
            ]
            for k in range(parts):
                key_term = dot(score_grads[k], query)
                value_term = dot(weights[k].astype(BF16), grad)
                dk[k] = key_term if head == 0 else dk[k] + key_term
                dv[k] = value_term if head == 0 else dv[k] + value_term
            if want_queries:
                dq.append(sum(dot_columns(score_grads[k], k_refs[k][...]) for k in range(parts)))
        for k in range(parts):
            dk_refs[k][...] = dk[k] if first else dk_refs[k][...] + dk[k]
            dv_refs[k][...] = dv[k] if first else dv_refs[k][...] + dv[k]
        if want_queries:
            dq_ref[here, :] = (jnp.where(low_half, dq[0], dq[1]) * DH ** (-0.5)).astype(BF16)

    rows(0, True)
    if own > block:
        lax.fori_loop(1, own // block, lambda at, _: (rows(at, False), 0)[1], 0)


def attend_back(queries, pairs, gradient, q_info, k_info, want_queries):
    own, width = queries.shape
    parts, length = len(pairs), k_info.shape[0]
    steps = width // LANES
    key_spec = pl.BlockSpec((own, LANES), lambda i: (0, i))
    value_spec = pl.BlockSpec((own, LANES), lambda i: (0, steps + i))
    shapes = [jax.ShapeDtypeStruct((own, width), F32)] * (2 * parts)
    if want_queries:
        shapes.append(jax.ShapeDtypeStruct((own, width), BF16))
    return pl.pallas_call(
        functools.partial(attend_back_kernel, parts, own, min(256, own), want_queries),
        grid=(steps,),
        out_shape=shapes,
        in_specs=[key_spec]
        + [key_spec] * parts
        + [value_spec] * parts
        + [
            key_spec,
            pl.BlockSpec(q_info.shape, lambda i: (0, 0)),
            pl.BlockSpec(k_info.shape, lambda i: (0, 0)),
        ],
        out_specs=[key_spec] * len(shapes),
        scratch_shapes=[pltpu.VMEM((length, own), F32)],
        compiler_params=pltpu.CompilerParams(vmem_limit_bytes=VMEM_LIMIT),
        cost_estimate=pl.CostEstimate(
            flops=40 * own * length * width, bytes_accessed=20 * own * width, transcendentals=0
        ),
    )(queries, *pairs, *pairs, gradient, q_info, k_info)


def vocab_kernel(tile, valid, h_ref, target_ref, table_hbm, grad_ref, stat_ref, table, sem):
    padded = table.shape[0]

    @pl.when(pl.program_id(0) == 0)
    def _():
        copy = pltpu.make_async_copy(table_hbm, table.at[pl.ds(0, valid), :], sem)
        copy.start()
        if padded > valid:
            table[valid:, :] = jnp.zeros((padded - valid, table.shape[1]), BF16)
        copy.wait()

    rows = h_ref.shape[0]
    hidden = h_ref[...]
    column = lax.broadcasted_iota(jnp.int32, (rows, tile), 1)
    target = target_ref[...]

    def block(at, carry, last):
        maxima, total = carry
        part = table[pl.ds(pl.multiple_of(at * tile, tile), tile), :]
        logits = dot_rows(hidden, part)
        if last and padded > valid:
            logits = jnp.where(column < valid - (padded - tile), logits, MASKED)
        highest = jnp.maximum(maxima, jnp.max(logits, -1, keepdims=True))
        powers = jnp.exp(logits - highest)
        scale = jnp.exp(maxima - highest)
        total = total * scale + jnp.sum(powers, -1, keepdims=True)
        powers = jnp.where(column == target - at * tile, 0.0, powers).astype(BF16)
        grad_ref[...] = grad_ref[...] * scale + dot(powers, part)
        return (highest, total)

    grad_ref[...] = jnp.zeros_like(grad_ref)
    blocks = padded // tile
    carry = (jnp.full((rows, 1), MASKED, F32), jnp.zeros((rows, 1), F32))
    carry = lax.fori_loop(0, blocks - 1, lambda at, c: block(at, c, False), carry)
    maxima, total = block(blocks - 1, carry, True)
    lane = lax.broadcasted_iota(jnp.int32, stat_ref.shape, 1)
    stat_ref[...] = jnp.where(lane == 0, maxima, total)


def vocab_pass(hidden, target_local, embedding, rows):
    count, width = hidden.shape
    valid = embedding.shape[0]
    tile = VOCAB_BLOCK
    padded = (valid + tile - 1) // tile * tile
    return pl.pallas_call(
        functools.partial(vocab_kernel, tile, valid),
        grid=(count // rows,),
        out_shape=[
            jax.ShapeDtypeStruct((count, width), F32),
            jax.ShapeDtypeStruct((count, LANES), F32),
        ],
        in_specs=[
            pl.BlockSpec((rows, width), lambda i: (i, 0)),
            pl.BlockSpec((rows, 1), lambda i: (i, 0)),
            pl.BlockSpec(memory_space=pl.ANY),
        ],
        out_specs=[
            pl.BlockSpec((rows, width), lambda i: (i, 0)),
            pl.BlockSpec((rows, LANES), lambda i: (i, 0)),
        ],
        scratch_shapes=[pltpu.VMEM((padded, width), BF16), pltpu.SemaphoreType.DMA],
        compiler_params=pltpu.CompilerParams(vmem_limit_bytes=VMEM_LIMIT),
        cost_estimate=pl.CostEstimate(
            flops=4 * count * padded * width, bytes_accessed=2 * valid * width, transcendentals=0
        ),
    )(hidden, target_local, embedding)


def gather_kernel(rows_z, rows_y, *refs):
    in_ref, out_ref, expand_ref, reduce_ref = refs[:4]
    in_full, out_full, expand_full, reduce_full = refs[4:7], refs[7:10], refs[10:12], refs[12:14]
    send_sem, recv_sem, local_sem = refs[14:]
    at, v = lax.axis_index("dp"), lax.axis_index("vocab")
    z, y, x, core = at // rows_y, lax.rem(at, rows_y), v // 2, lax.rem(v, 2)
    top = rows_z - 1
    above = {"dp": jnp.minimum(z + 1, top) * rows_y + y, "vocab": v}
    below = {"dp": jnp.maximum(z - 1, 0) * rows_y + y, "vocab": v}
    beside = {"dp": z * rows_y + (1 - y), "vocab": v}
    other_x = (1 - x) * 2 + core
    across = {"dp": at, "vocab": other_x}
    twin = {"dp": at, "vocab": x * 2 + (1 - core)}

    barrier = pltpu.get_barrier_semaphore()

    def greet(peer):
        pl.semaphore_signal(barrier, inc=1, device_id=peer, device_id_type=pl.DeviceIdType.MESH)

    pl.when(z < top)(lambda: greet(above))
    pl.when(z > 0)(lambda: greet(below))
    greet(beside)
    greet(across)
    greet(twin)
    inner = jnp.logical_and(z > 0, z < top)
    pl.when(inner)(lambda: pl.semaphore_wait(barrier, 5))
    pl.when(jnp.logical_not(inner))(lambda: pl.semaphore_wait(barrier, 4))

    names, tallies = {}, [0, 0]

    def remote(name, source, target, peer):
        if name not in names:
            names[name] = tallies[0]
            tallies[0] += 1
        return pltpu.make_async_remote_copy(
            src_ref=source,
            dst_ref=target,
            send_sem=send_sem.at[names[name]],
            recv_sem=recv_sem.at[names[name]],
            device_id=peer,
            device_id_type=pl.DeviceIdType.MESH,
        )

    def local(source, target):
        copy = pltpu.make_async_copy(source, target, local_sem.at[tallies[1]])
        tallies[1] += 1
        copy.start()
        return copy

    def columns(ref, full, index, blocks):
        wide = ref.shape[2] // blocks
        here = lambda b: pl.ds(pl.multiple_of(b * wide, wide), wide)
        return (
            lambda b: ref.at[index, :, here(b)],
            lambda zs, ys, b: full.at[zs, ys, :, here(b)],
            lambda ys, b: full.at[:, ys, :, here(b)],
            blocks == 4,
        )

    def row_blocks(ref, full, index):
        count = ref.shape[1] // 4
        return (
            lambda b: ref.at[index, pl.ds(pl.multiple_of(b * count, count), count), :],
            lambda zs, ys, b: full.at[zs, ys, b],
            lambda ys, b: full.at[:, ys, b],
            True,
        )

    def attention(j):
        return [columns(in_ref, in_full[j], j, 2), columns(out_ref, out_full[j], j, 2)]

    def feed(j):
        return [columns(expand_ref, expand_full[j], j, 4), row_blocks(reduce_ref, reduce_full[j], j)]

    waves = [feed(0) + attention(0), feed(1) + attention(1) + attention(2)]
    units = [u for wave in waves for u in wave]
    starts = [0, len(waves[0]), len(units)]
    blocks = [v if u[3] else core for u in units]
    sides = (("up", -1), ("down", 1))

    def there(side, k):
        return z - k >= 0 if side == "up" else z + k <= top

    def further(side):
        return z < top if side == "up" else z > 0

    def begin(i):
        source, target, _, quarter = units[i]
        b = blocks[i]
        piece = target(z, y, b)
        pl.when(z < top)(lambda: remote((i, "up", 1), source(b), piece, above).start())
        pl.when(z > 0)(lambda: remote((i, "down", 1), source(b), piece, below).start())
        remote((i, "y", 0), source(b), piece, beside).start()
        copies = [local(source(b), piece)]
        if quarter:
            copies.append(local(source(other_x), target(z, y, other_x)))
        return copies

    def step(i, k):
        _, target, _, quarter = units[i]
        for side, sign in sides:

            @pl.when(there(side, k))
            def _():
                piece = target(z + sign * k, y, blocks[i])
                remote((i, side, k), piece, piece, above).wait_recv()
                if k < top:

                    @pl.when(further(side))
                    def _():
                        peer = above if side == "up" else below
                        remote((i, side, k + 1), piece, piece, peer).start()

                remote((i, side, k, "y"), piece, piece, beside).start()
                if quarter:
                    remote((i, side, k, "x"), piece, piece, across).start()

    def came(i, k):
        _, target, _, quarter = units[i]
        if k == 0:
            piece = target(z, 1 - y, blocks[i])
            remote((i, "y", 0), piece, piece, beside).wait_recv()
            if quarter:
                remote((i, "yx", 0), piece, piece, across).start()
            return
        for side, sign in sides:

            @pl.when(there(side, k))
            def _():
                piece = target(z + sign * k, 1 - y, blocks[i])
                remote((i, side, k, "y"), piece, piece, beside).wait_recv()
                if quarter:
                    remote((i, side, k, "yx"), piece, piece, across).start()

    def to_twin(i, column, b, tag):
        block = units[i][2](column, b)
        remote((i, "core", tag), block, block, twin).start()

    def spread(i):
        for copy in locals_[i]:
            copy.wait()
        to_twin(i, y, blocks[i], 0)

    def spread_beside(i):
        to_twin(i, 1 - y, blocks[i], 1)

    def x_came(i, tag):
        _, target, _, _ = units[i]
        if tag == "yx":
            piece = target(z, 1 - y, other_x)
            remote((i, "yx", 0), piece, piece, across).wait_recv()
        for k in range(1, rows_z):
            for side, sign in sides:

                @pl.when(there(side, k))
                def _():
                    piece = target(z + sign * k, y if tag == "x" else 1 - y, other_x)
                    remote((i, side, k, tag), piece, piece, across).wait_recv()

        to_twin(i, y if tag == "x" else 1 - y, other_x, 2 if tag == "x" else 3)

    first, second = range(starts[0], starts[1]), range(starts[1], starts[2])
    locals_ = {}

    def each(action, wave, *rest):
        for i in wave:
            action(i, *rest)

    for i in first:
        locals_[i] = begin(i)
    locals_[second[0]] = begin(second[0])
    each(step, first, 1)
    for i in second[1:]:
        locals_[i] = begin(i)
    each(came, first, 0)
    each(step, first, 2)
    each(came, first, 1)
    each(step, second, 1)
    each(step, first, 3)
    each(spread, first)
    each(came, first, 2)
    each(step, second, 2)
    each(came, second, 0)
    for i in first:
        came(i, 3)
        spread_beside(i)
    each(came, second, 1)
    each(step, second, 3)
    each(spread, second)
    for i in first:
        if units[i][3]:
            x_came(i, "x")
    each(came, second, 2)
    for i in first:
        if units[i][3]:
            x_came(i, "yx")
    for i in second:
        came(i, 3)
        spread_beside(i)
    for i in second:
        if units[i][3]:
            x_came(i, "x")
            x_came(i, "yx")

    for i, (source, target, whole, quarter) in enumerate(units):
        b = blocks[i]
        for tag in range(4 if quarter else 2):
            block = whole(y, b)
            remote((i, "core", tag), block, block, twin).wait()
        piece = target(z, y, b)
        remote((i, "y", 0), piece, piece, beside).wait_send()
        if quarter:
            remote((i, "yx", 0), piece, piece, across).wait_send()
        for k in range(1, rows_z):
            for side, sign in sides:
                sent = there(side, k - 1) if k > 1 else True
                pl.when(jnp.logical_and(sent, further(side)))(
                    lambda: remote((i, side, k), piece, piece, above).wait_send()
                )

                @pl.when(there(side, k))
                def _():
                    remote((i, side, k, "y"), piece, piece, beside).wait_send()
                    if quarter:
                        remote((i, side, k, "x"), piece, piece, across).wait_send()
                        remote((i, side, k, "yx"), piece, piece, across).wait_send()


def gather_weights(attend_in, attend_out, expand_weights, reduce_weights):
    shards, rows_y = 8, 2
    rows_z = shards // rows_y
    rows = attend_in.shape[1]
    width = rows * shards
    tall = reduce_weights.shape[1]

    def full(*tail):
        return jax.ShapeDtypeStruct((rows_z, rows_y, *tail), BF16)

    shapes = (
        [full(rows, attend_in.shape[2])] * 3
        + [full(rows, attend_out.shape[2])] * 3
        + [full(rows, expand_weights.shape[2])] * 2
        + [full(4, tall // 4, width)] * 2
    )
    copies = 10 * (1 + 4 * (rows_z - 1) + 2) + 4 * (1 + 4 * (rows_z - 1) + 2)
    outs = pl.pallas_call(
        functools.partial(gather_kernel, rows_z, rows_y),
        out_shape=shapes,
        in_specs=[pl.BlockSpec(memory_space=pl.ANY)] * 4,
        out_specs=[pl.BlockSpec(memory_space=pl.ANY)] * 10,
        scratch_shapes=[
            pltpu.SemaphoreType.DMA((copies,)),
            pltpu.SemaphoreType.DMA((copies,)),
            pltpu.SemaphoreType.DMA((14,)),
        ],
        compiler_params=pltpu.CompilerParams(collective_id=0, has_side_effects=True),
        cost_estimate=pl.CostEstimate(flops=0, bytes_accessed=400_000_000, transcendentals=0),
    )(attend_in, attend_out, expand_weights, reduce_weights)
    return [o.reshape(-1, o.shape[-1]) for o in outs]


def whole_weights(attend_in, attend_out, expand_weights, reduce_weights):
    tensors = (attend_in, attend_out, expand_weights, reduce_weights)
    if lax.axis_size("dp") == 8 and lax.axis_size("vocab") == 4:
        flat = gather_weights(*tensors)
        return flat[:3], flat[3:6], flat[6:8], flat[8:]
    return tuple(lax.all_gather(tensor, "dp", axis=1, tiled=True) for tensor in tensors)


def on_device(
    tokens,
    targets,
    loss_mask,
    seg_lengths,
    task_ids,
    embedding,
    attend_in,
    attend_out,
    expand_weights,
    reduce_weights,
    norm_gains,
    prompt,
    first_moment,
    row_moment,
    column_moment,
):
    shards = lax.axis_size("vocab")
    micros, span = tokens.shape[0], tokens.shape[-1]
    length = span * shards
    group = shards // micros
    own = length // group
    me = lax.axis_index("vocab")
    micro, place = me // group, me % group
    shard_rows, width = embedding.shape
    share = prompt.shape[-1]

    def around(array, shift):
        pairs = [
            (m * group + r, m * group + (r + shift) % group)
            for m in range(micros)
            for r in range(group)
        ]
        return lax.ppermute(array, "vocab", pairs)

    ids = lax.all_gather(jnp.stack([tokens[:, 0], targets[:, 0], loss_mask[:, 0]]), "vocab")
    ids = jnp.transpose(ids, (1, 2, 0, 3)).reshape(3, micros, length)
    enc_ids = ids[0].reshape(shards, own)
    before = jnp.pad(ids[1], ((0, 0), (1, 0)))[:, :length].reshape(shards, own)[:, :1]
    dec_ids = jnp.concatenate(
        [jnp.zeros((shards, HALO - 1), jnp.int32), before, ids[1].reshape(shards, own)], 1
    )
    first_row = me * shard_rows

    def lookup(wanted):
        local = wanted.reshape(-1) - first_row
        inside = (local >= 0) & (local < shard_rows)
        picked = jnp.take(embedding, jnp.clip(local, 0, shard_rows - 1), axis=0)
        return jnp.where(inside[:, None], picked, 0)

    enc_rows = lax.psum_scatter(lookup(enc_ids), "vocab", scatter_dimension=0, tiled=True)
    dec_rows = lax.psum_scatter(lookup(dec_ids), "vocab", scatter_dimension=0, tiled=True)

    prompt_all = lax.all_gather(prompt.astype(BF16), "vocab", axis=2, tiled=True)
    prompt_flat = prompt_all.reshape(-1, width)
    attend_in, attend_out, expand_weights, reduce_weights = whole_weights(
        attend_in, attend_out, expand_weights, reduce_weights
    )

    lengths = lax.dynamic_index_in_dim(seg_lengths[:, 0], micro, 0, False)
    tasks = lax.dynamic_index_in_dim(task_ids[:, 0], micro, 0, False)
    steps = jnp.arange(own, dtype=jnp.int32)
    positions = place * own + steps
    segment, in_segment, task_of = layout(lengths, tasks, positions)
    key_positions = jnp.concatenate(
        [((place - k + group) % group) * own + steps for k in range(group)]
    )
    key_segment = layout(lengths, tasks, key_positions)[0]
    rows_info = jnp.stack([segment, positions], 1)
    keys_info = jnp.stack([key_segment, key_positions], 0)
    own_mask = lax.dynamic_slice(ids[2], (micro, place * own), (1, own))[0]
    counted = (own_mask * (in_segment >= P_SIZE)).astype(F32)

    def key_parts(source, weight):
        pair = dot(source, weight).astype(BF16)
        return [pair] + [around(pair, k) for k in range(1, group)]

    def project(source, weight):
        return dot(source, weight).astype(BF16)

    is_prompt = in_segment < P_SIZE
    slot = task_of * P_SIZE + jnp.minimum(in_segment, P_SIZE - 1)
    enc_input = jnp.where(
        is_prompt[:, None], jnp.take(prompt_flat, slot, axis=0), enc_rows
    ).astype(F32)
    target_rows = dec_rows[HALO:].astype(F32)
    dec_input = jnp.where(
        (in_segment >= 1)[:, None], dec_rows[HALO - 1 : HALO - 1 + own], dec_rows[:1]
    ).astype(F32)

    normed_in, inverse_in = normed(enc_input, norm_gains[0])
    normed_low = normed_in.astype(BF16)
    enc_pairs = key_parts(normed_low, attend_in[0][:, width:])
    enc_queries = project(normed_low, attend_in[0][:, :width])
    normed_dec = normed(dec_input, norm_gains[3])[0].astype(BF16)
    dec_pairs = key_parts(normed_dec, attend_in[1][:, width:])
    dec_queries = project(normed_dec, attend_in[1][:, :width])
    mixed = attend(enc_queries, enc_pairs, rows_info, keys_info, False)
    enc_mid = enc_input + dot(mixed, attend_out[0])
    normed_mid, inverse_mid = normed(enc_mid, norm_gains[1])
    enc_pre = dot(normed_mid.astype(BF16), expand_weights[0])
    enc_last = enc_mid + dot(smooth(enc_pre).astype(BF16), reduce_weights[0])
    encoded, inverse_last = normed(enc_last, norm_gains[2])
    cross_pairs = key_parts(encoded.astype(BF16), attend_in[2][:, width:])

    mixed = attend(dec_queries, dec_pairs, rows_info, keys_info, True)
    dec_first = dec_input + dot(mixed, attend_out[1])
    cross_queries = project(normed(dec_first, norm_gains[4])[0].astype(BF16), attend_in[2][:, :width])
    mixed = attend(cross_queries, cross_pairs, rows_info, keys_info, False)
    dec_second = dec_first + dot(mixed, attend_out[2])
    normed_second, inverse_second = normed(dec_second, norm_gains[5])
    dec_pre = dot(normed_second.astype(BF16), expand_weights[1])
    dec_last = dec_second + dot(smooth(dec_pre).astype(BF16), reduce_weights[1])
    output_norm, inverse_out = normed(dec_last, norm_gains[6])
    hidden = (output_norm * width ** (-0.5)).astype(BF16)

    all_hidden = lax.all_gather(hidden, "vocab", axis=0, tiled=True)
    target_local = ids[1].reshape(-1, 1) - first_row
    part, stats = vocab_pass(all_hidden, target_local, embedding, own)
    gathered = lax.all_gather(stats[:, :2].T, "vocab")
    maxima = jnp.max(gathered[:, 0], 0)
    log_total = maxima + jnp.log(
        jnp.sum(gathered[:, 1] * jnp.exp(gathered[:, 0] - maxima), 0)
    )
    scaled = part * jnp.exp(stats[:, 0] - log_total)[:, None]
    summed = lax.psum_scatter(scaled, "vocab", scatter_dimension=0, tiled=True)
    own_total = lax.dynamic_slice(log_total, (me * own,), (own,))
    target_logit = jnp.sum(hidden.astype(F32) * target_rows, -1)
    token_loss = own_total - target_logit
    target_coefficient = (jnp.exp(target_logit - own_total) - 1.0).astype(BF16).astype(F32)
    hidden_grad = counted[:, None] * (summed + target_coefficient[:, None] * target_rows)

    def feed_back(hidden_pre, weight_one, weight_two, gradient):
        active_grad = dot_rows(gradient.astype(BF16), weight_two)
        pre_grad = jax.vjp(smooth, hidden_pre)[1](active_grad)[0].astype(BF16)
        return dot_rows(pre_grad, weight_one)

    def keys_back(parts, weight):
        dk, dv = parts[:group], parts[group : 2 * group]
        pairs = [jnp.concatenate([dk[k], dv[k]], 1) for k in range(group)]
        total = pairs[0]
        for k in range(1, group):
            total = total + around(pairs[k], group - k)
        high = total.astype(BF16)
        rest = (total - high.astype(F32)).astype(BF16)
        return dot_rows(high, weight) + dot_rows(rest, weight)

    dec_grad = normed_back(
        dec_last, norm_gains[6], inverse_out, hidden_grad * width ** (-0.5)
    )
    dec_grad = dec_grad + normed_back(
        dec_second,
        norm_gains[5],
        inverse_second,
        feed_back(dec_pre, expand_weights[1], reduce_weights[1], dec_grad),
    )
    mixed_grad = dot_rows(dec_grad.astype(BF16), attend_out[2]).astype(BF16)
    back = attend_back(cross_queries, cross_pairs, mixed_grad, rows_info.T, keys_info.T, False)
    enc_grad = normed_back(
        enc_last, norm_gains[2], inverse_last, keys_back(back, attend_in[2][:, width:])
    )
    enc_grad = enc_grad + normed_back(
        enc_mid,
        norm_gains[1],
        inverse_mid,
        feed_back(enc_pre, expand_weights[0], reduce_weights[0], enc_grad),
    )
    mixed_grad = dot_rows(enc_grad.astype(BF16), attend_out[0]).astype(BF16)
    back = attend_back(enc_queries, enc_pairs, mixed_grad, rows_info.T, keys_info.T, True)
    source_grad = keys_back(back, attend_in[0][:, width:]) + dot_rows(
        back[-1], attend_in[0][:, :width]
    )
    enc_grad = enc_grad + normed_back(enc_input, norm_gains[0], inverse_in, source_grad)

    entries = TASKS * P_SIZE
    chosen = (
        (slot[:, None] == jnp.arange(entries, dtype=jnp.int32)) & is_prompt[:, None]
    ).astype(BF16)
    high = enc_grad.astype(BF16)
    rest = (enc_grad - high.astype(F32)).astype(BF16)
    gradient = dot_columns(chosen, high) + dot_columns(chosen, rest)
    tallies = jnp.stack([per_task(task_of, counted * token_loss), per_task(task_of, counted)])
    extra = jnp.zeros((8, share), F32).at[:2, :TASKS].set(tallies)
    gradient = jnp.concatenate([gradient, jnp.tile(extra, (1, shards))], 0)
    gradient = jnp.transpose(gradient.reshape(entries + 8, shards, share), (1, 0, 2))
    gradient = lax.psum_scatter(gradient, "vocab", scatter_dimension=0, tiled=True)[0]
    gradient = lax.psum(gradient, "dp")

    task_loss, counts = gradient[entries, :TASKS], gradient[entries + 1, :TASKS]
    task_scale = 1.0 / (TASKS * jnp.maximum(counts, 1.0))
    loss_mean = jnp.sum(task_loss * task_scale)
    full_grad = gradient[:entries].reshape(TASKS, P_SIZE, share) * task_scale[:, None, None]
    row_squares = jnp.sum(lax.all_gather(jnp.sum(full_grad * full_grad, -1), "vocab"), 0)
    grad_norm = jnp.sqrt(jnp.sum(row_squares))
    clip = CLIP_NORM / jnp.maximum(grad_norm, CLIP_NORM)
    prompt_grad = full_grad * clip
    row_second = BETA_TWO * row_moment + (1.0 - BETA_TWO) * (
        row_squares * clip * clip / width + SQUARE_EPS
    )
    column_second = BETA_TWO * column_moment + (1.0 - BETA_TWO) * (
        jnp.mean(prompt_grad * prompt_grad, 1) + SQUARE_EPS
    )
    new_moment = BETA_ONE * first_moment + (1.0 - BETA_ONE) * prompt_grad
    estimate = (
        row_second[:, :, None] * column_second[:, None, :] / jnp.mean(row_second, -1)[:, None, None]
    )
    update = new_moment / (1.0 - BETA_ONE**STEP) / jnp.sqrt(estimate / (1.0 - BETA_TWO**STEP))
    new_prompt = prompt - LEARN_RATE * (update + WEIGHT_DECAY * prompt)
    return (loss_mean, grad_norm, prompt_grad, new_moment, row_second, column_second, new_prompt)


def solution(mesh):
    placed = (
        P(None, "dp", "vocab"),
        P(None, "dp", "vocab"),
        P(None, "dp", "vocab"),
        P(None, "dp", None),
        P(None, "dp", None),
        P("vocab", None),
        P(None, "dp", None),
        P(None, "dp", None),
        P(None, "dp", None),
        P(None, "dp", None),
        P(),
        P(None, None, "vocab"),
        P(None, None, "vocab"),
        P(),
        P(None, "vocab"),
    )
    return jax.shard_map(
        on_device,
        mesh=mesh,
        in_specs=placed,
        out_specs=(
            P(),
            P(),
            P(None, None, "vocab"),
            P(None, None, "vocab"),
            P(),
            P(None, "vocab"),
            P(None, None, "vocab"),
        ),
        check_vma=False,
    )
```

```python
import functools

import jax
import jax.numpy as jnp
from jax import lax
from jax.experimental import pallas as pl
from jax.experimental.pallas import tpu as pltpu
from jax.sharding import PartitionSpec as P

DH = 64
P_SIZE = 100
TASKS = 8
STEP = 5
HALO = 16
LANES = 128
VOCAB_BLOCK = 1024
VMEM_LIMIT = 60 * 1024 * 1024

NORM_EPS = 1e-06
CLIP_NORM = 2e-05
BETA_ONE = 0.9
BETA_TWO = 0.999
LEARN_RATE = 1.0
WEIGHT_DECAY = 1e-05
SQUARE_EPS = 1e-30
MASKED = -1e30

F32 = jnp.float32
BF16 = jnp.bfloat16


def dot(left, right):
    return jnp.dot(left, right, preferred_element_type=F32)


def dot_rows(left, right):
    return lax.dot_general(left, right, (((1,), (1,)), ((), ())), preferred_element_type=F32)


def dot_columns(left, right):
    return lax.dot_general(left, right, (((0,), (0,)), ((), ())), preferred_element_type=F32)


def normed(values, gain):
    inverse = lax.rsqrt(jnp.mean(values * values, -1, keepdims=True) + NORM_EPS)
    return (values * inverse * gain, inverse)


def normed_back(values, gain, inverse, gradient):
    unit_rows = values * inverse
    scaled = gradient * gain
    return inverse * (scaled - unit_rows * jnp.mean(scaled * unit_rows, -1, keepdims=True))


def smooth(values):
    return jax.nn.gelu(values, approximate=True)


def layout(lengths, task_list, positions):
    seg_ends = jnp.cumsum(lengths)
    seg_starts = seg_ends - lengths
    segment = jnp.sum((positions[:, None] >= seg_ends[None, :]).astype(jnp.int32), -1)
    member = segment[:, None] == jnp.arange(lengths.shape[0], dtype=jnp.int32)[None, :]
    in_segment = positions - jnp.sum(jnp.where(member, seg_starts[None, :], 0), -1)
    task_of = jnp.sum(jnp.where(member, task_list[None, :], 0), -1)
    return (segment, in_segment, task_of)


def per_task(task_of, amounts):
    hits = task_of[:, None] == jnp.arange(TASKS, dtype=jnp.int32)
    return jnp.sum(jnp.where(hits, amounts[:, None], 0.0), 0)


def attend_kernel(parts, own, causal, *refs):
    q_ref, k_refs, v_refs = refs[0], refs[1 : 1 + parts], refs[1 + parts : 1 + 2 * parts]
    q_info, k_info, out_ref, bias_ref = refs[1 + 2 * parts :]

    @pl.when(pl.program_id(0) == 0)
    def _():
        keep = q_info[:, 0:1] == k_info[0:1, :]
        if causal:
            keep = keep & (q_info[:, 1:2] >= k_info[1:2, :])
        bias_ref[...] = jnp.where(keep, 0.0, MASKED)

    low_half = lax.broadcasted_iota(jnp.int32, (own, LANES), 1) < DH
    queries = q_ref[...].astype(F32) * DH ** (-0.5)
    mixed = []
    for head in range(LANES // DH):
        query = jnp.where(low_half == (head == 0), queries, 0.0).astype(BF16)
        scores = [
            dot_rows(query, k_refs[k][...]) + bias_ref[:, k * own : (k + 1) * own]
            for k in range(parts)
        ]
        maxima = functools.reduce(jnp.maximum, [jnp.max(s, -1, keepdims=True) for s in scores])
        powers = [jnp.exp(s - maxima) for s in scores]
        total = sum(jnp.sum(p, -1, keepdims=True) for p in powers)
        value = sum(dot(p.astype(BF16), v_refs[k][...]) for k, p in enumerate(powers))
        mixed.append(value / total)
    out_ref[...] = jnp.where(low_half, mixed[0], mixed[1]).astype(BF16)


def attend(queries, pairs, q_info, k_info, causal):
    own, width = queries.shape
    parts, length = len(pairs), k_info.shape[1]
    steps = width // LANES
    key_spec = pl.BlockSpec((own, LANES), lambda i: (0, i))
    value_spec = pl.BlockSpec((own, LANES), lambda i: (0, steps + i))
    return pl.pallas_call(
        functools.partial(attend_kernel, parts, own, causal),
        grid=(steps,),
        out_shape=jax.ShapeDtypeStruct((own, width), BF16),
        in_specs=[key_spec]
        + [key_spec] * parts
        + [value_spec] * parts
        + [
            pl.BlockSpec(q_info.shape, lambda i: (0, 0)),
            pl.BlockSpec(k_info.shape, lambda i: (0, 0)),
        ],
        out_specs=key_spec,
        scratch_shapes=[pltpu.VMEM((own, length), F32)],
        compiler_params=pltpu.CompilerParams(vmem_limit_bytes=VMEM_LIMIT),
        cost_estimate=pl.CostEstimate(
            flops=16 * own * length * width, bytes_accessed=6 * own * width, transcendentals=0
        ),
    )(queries, *pairs, *pairs, q_info, k_info)


def attend_back_kernel(parts, own, block, want_queries, *refs):
    q_ref, k_refs, v_refs = refs[0], refs[1 : 1 + parts], refs[1 + parts : 1 + 2 * parts]
    grad_ref, q_info, k_info = refs[1 + 2 * parts : 4 + 2 * parts]
    rest = refs[4 + 2 * parts :]
    dk_refs, dv_refs = rest[:parts], rest[parts : 2 * parts]
    dq_ref = rest[2 * parts] if want_queries else None
    bias_ref = rest[-1]

    @pl.when(pl.program_id(0) == 0)
    def _():
        bias_ref[...] = jnp.where(k_info[:, 0:1] == q_info[0:1, :], 0.0, MASKED)

    low_half = lax.broadcasted_iota(jnp.int32, (block, LANES), 1) < DH

    def rows(at, first):
        here = pl.ds(pl.multiple_of(at * block, block), block)
        queries = q_ref[here, :].astype(F32) * DH ** (-0.5)
        gradient = grad_ref[here, :].astype(F32)
        dk = [None] * parts
        dv = [None] * parts
        dq = []
        for head in range(LANES // DH):
            mask = low_half == (head == 0)
            query = jnp.where(mask, queries, 0.0).astype(BF16)
            grad = jnp.where(mask, gradient, 0.0).astype(BF16)
            scores = [
                dot_rows(k_refs[k][...], query) + bias_ref[k * own : (k + 1) * own, here]
                for k in range(parts)
            ]
            maxima = functools.reduce(jnp.maximum, [jnp.max(s, 0, keepdims=True) for s in scores])
            powers = [jnp.exp(s - maxima) for s in scores]
            inverse = 1.0 / sum(jnp.sum(p, 0, keepdims=True) for p in powers)
            weights = [p * inverse for p in powers]
            weight_grads = [dot_rows(v_refs[k][...], grad) for k in range(parts)]
            delta = sum(
                jnp.sum(w * dw, 0, keepdims=True) for w, dw in zip(weights, weight_grads)
            )
            score_grads = [
                (w * (dw - delta)).astype(BF16) for w, dw in zip(weights, weight_grads)
            ]
            for k in range(parts):
                key_term = dot(score_grads[k], query)
                value_term = dot(weights[k].astype(BF16), grad)
                dk[k] = key_term if head == 0 else dk[k] + key_term
                dv[k] = value_term if head == 0 else dv[k] + value_term
            if want_queries:
                dq.append(sum(dot_columns(score_grads[k], k_refs[k][...]) for k in range(parts)))
        for k in range(parts):
            dk_refs[k][...] = dk[k] if first else dk_refs[k][...] + dk[k]
            dv_refs[k][...] = dv[k] if first else dv_refs[k][...] + dv[k]
        if want_queries:
            dq_ref[here, :] = (jnp.where(low_half, dq[0], dq[1]) * DH ** (-0.5)).astype(BF16)

    rows(0, True)
    if own > block:
        lax.fori_loop(1, own // block, lambda at, _: (rows(at, False), 0)[1], 0)


def attend_back(queries, pairs, gradient, q_info, k_info, want_queries):
    own, width = queries.shape
    parts, length = len(pairs), k_info.shape[0]
    steps = width // LANES
    key_spec = pl.BlockSpec((own, LANES), lambda i: (0, i))
    value_spec = pl.BlockSpec((own, LANES), lambda i: (0, steps + i))
    shapes = [jax.ShapeDtypeStruct((own, width), F32)] * (2 * parts)
    if want_queries:
        shapes.append(jax.ShapeDtypeStruct((own, width), BF16))
    return pl.pallas_call(
        functools.partial(attend_back_kernel, parts, own, min(256, own), want_queries),
        grid=(steps,),
        out_shape=shapes,
        in_specs=[key_spec]
        + [key_spec] * parts
        + [value_spec] * parts
        + [
            key_spec,
            pl.BlockSpec(q_info.shape, lambda i: (0, 0)),
            pl.BlockSpec(k_info.shape, lambda i: (0, 0)),
        ],
        out_specs=[key_spec] * len(shapes),
        scratch_shapes=[pltpu.VMEM((length, own), F32)],
        compiler_params=pltpu.CompilerParams(vmem_limit_bytes=VMEM_LIMIT),
        cost_estimate=pl.CostEstimate(
            flops=40 * own * length * width, bytes_accessed=20 * own * width, transcendentals=0
        ),
    )(queries, *pairs, *pairs, gradient, q_info, k_info)


def vocab_kernel(tile, valid, h_ref, target_ref, table_hbm, grad_ref, stat_ref, table, sem):
    padded = table.shape[0]

    @pl.when(pl.program_id(0) == 0)
    def _():
        copy = pltpu.make_async_copy(table_hbm, table.at[pl.ds(0, valid), :], sem)
        copy.start()
        if padded > valid:
            table[valid:, :] = jnp.zeros((padded - valid, table.shape[1]), BF16)
        copy.wait()

    rows = h_ref.shape[0]
    hidden = h_ref[...]
    column = lax.broadcasted_iota(jnp.int32, (rows, tile), 1)
    target = target_ref[...]

    def block(at, carry, last):
        maxima, total = carry
        part = table[pl.ds(pl.multiple_of(at * tile, tile), tile), :]
        logits = dot_rows(hidden, part)
        if last and padded > valid:
            logits = jnp.where(column < valid - (padded - tile), logits, MASKED)
        highest = jnp.maximum(maxima, jnp.max(logits, -1, keepdims=True))
        powers = jnp.exp(logits - highest)
        scale = jnp.exp(maxima - highest)
        total = total * scale + jnp.sum(powers, -1, keepdims=True)
        powers = jnp.where(column == target - at * tile, 0.0, powers).astype(BF16)
        grad_ref[...] = grad_ref[...] * scale + dot(powers, part)
        return (highest, total)

    grad_ref[...] = jnp.zeros_like(grad_ref)
    blocks = padded // tile
    carry = (jnp.full((rows, 1), MASKED, F32), jnp.zeros((rows, 1), F32))
    carry = lax.fori_loop(0, blocks - 1, lambda at, c: block(at, c, False), carry)
    maxima, total = block(blocks - 1, carry, True)
    lane = lax.broadcasted_iota(jnp.int32, stat_ref.shape, 1)
    stat_ref[...] = jnp.where(lane == 0, maxima, total)


def vocab_pass(hidden, target_local, embedding, rows):
    count, width = hidden.shape
    valid = embedding.shape[0]
    tile = VOCAB_BLOCK
    padded = (valid + tile - 1) // tile * tile
    return pl.pallas_call(
        functools.partial(vocab_kernel, tile, valid),
        grid=(count // rows,),
        out_shape=[
            jax.ShapeDtypeStruct((count, width), F32),
            jax.ShapeDtypeStruct((count, LANES), F32),
        ],
        in_specs=[
            pl.BlockSpec((rows, width), lambda i: (i, 0)),
            pl.BlockSpec((rows, 1), lambda i: (i, 0)),
            pl.BlockSpec(memory_space=pl.ANY),
        ],
        out_specs=[
            pl.BlockSpec((rows, width), lambda i: (i, 0)),
            pl.BlockSpec((rows, LANES), lambda i: (i, 0)),
        ],
        scratch_shapes=[pltpu.VMEM((padded, width), BF16), pltpu.SemaphoreType.DMA],
        compiler_params=pltpu.CompilerParams(vmem_limit_bytes=VMEM_LIMIT),
        cost_estimate=pl.CostEstimate(
            flops=4 * count * padded * width, bytes_accessed=2 * valid * width, transcendentals=0
        ),
    )(hidden, target_local, embedding)


def gather_kernel(rows_z, rows_y, *refs):
    in_ref, out_ref, expand_ref, reduce_ref = refs[:4]
    in_full, out_full, expand_full, reduce_full = refs[4:7], refs[7:10], refs[10:12], refs[12:14]
    send_sem, recv_sem, local_sem = refs[14:]
    at, v = lax.axis_index("dp"), lax.axis_index("vocab")
    z, y, x, core = at // rows_y, lax.rem(at, rows_y), v // 2, lax.rem(v, 2)
    top = rows_z - 1
    above = {"dp": jnp.minimum(z + 1, top) * rows_y + y, "vocab": v}
    below = {"dp": jnp.maximum(z - 1, 0) * rows_y + y, "vocab": v}
    beside = {"dp": z * rows_y + (1 - y), "vocab": v}
    other_x = (1 - x) * 2 + core
    across = {"dp": at, "vocab": other_x}
    twin = {"dp": at, "vocab": x * 2 + (1 - core)}

    barrier = pltpu.get_barrier_semaphore()

    def greet(peer):
        pl.semaphore_signal(barrier, inc=1, device_id=peer, device_id_type=pl.DeviceIdType.MESH)

    pl.when(z < top)(lambda: greet(above))
    pl.when(z > 0)(lambda: greet(below))
    greet(beside)
    greet(across)
    greet(twin)
    inner = jnp.logical_and(z > 0, z < top)
    pl.when(inner)(lambda: pl.semaphore_wait(barrier, 5))
    pl.when(jnp.logical_not(inner))(lambda: pl.semaphore_wait(barrier, 4))

    names, tallies = {}, [0, 0]

    def remote(name, source, target, peer):
        if name not in names:
            names[name] = tallies[0]
            tallies[0] += 1
        return pltpu.make_async_remote_copy(
            src_ref=source,
            dst_ref=target,
            send_sem=send_sem.at[names[name]],
            recv_sem=recv_sem.at[names[name]],
            device_id=peer,
            device_id_type=pl.DeviceIdType.MESH,
        )

    def local(source, target):
        copy = pltpu.make_async_copy(source, target, local_sem.at[tallies[1]])
        tallies[1] += 1
        copy.start()
        return copy

    def columns(ref, full, index, blocks):
        wide = ref.shape[2] // blocks
        here = lambda b: pl.ds(pl.multiple_of(b * wide, wide), wide)
        return (
            lambda b: ref.at[index, :, here(b)],
            lambda zs, ys, b: full.at[zs, ys, :, here(b)],
            lambda ys, b: full.at[:, ys, :, here(b)],
            blocks == 4,
        )

    def row_blocks(ref, full, index):
        count = ref.shape[1] // 4
        return (
            lambda b: ref.at[index, pl.ds(pl.multiple_of(b * count, count), count), :],
            lambda zs, ys, b: full.at[zs, ys, b],
            lambda ys, b: full.at[:, ys, b],
            True,
        )

    def attention(j):
        return [columns(in_ref, in_full[j], j, 2), columns(out_ref, out_full[j], j, 2)]

    def feed(j):
        return [columns(expand_ref, expand_full[j], j, 4), row_blocks(reduce_ref, reduce_full[j], j)]

    waves = [feed(0) + attention(0), feed(1) + attention(1) + attention(2)]
    units = [u for wave in waves for u in wave]
    starts = [0, len(waves[0]), len(units)]
    blocks = [v if u[3] else core for u in units]
    sides = (("up", -1), ("down", 1))

    def there(side, k):
        return z - k >= 0 if side == "up" else z + k <= top

    def further(side):
        return z < top if side == "up" else z > 0

    def begin(i):
        source, target, _, quarter = units[i]
        b = blocks[i]
        piece = target(z, y, b)
        pl.when(z < top)(lambda: remote((i, "up", 1), source(b), piece, above).start())
        pl.when(z > 0)(lambda: remote((i, "down", 1), source(b), piece, below).start())
        remote((i, "y", 0), source(b), piece, beside).start()
        copies = [local(source(b), piece)]
        if quarter:
            copies.append(local(source(other_x), target(z, y, other_x)))
        return copies

    def step(i, k):
        _, target, _, quarter = units[i]
        for side, sign in sides:

            @pl.when(there(side, k))
            def _():
                piece = target(z + sign * k, y, blocks[i])
                remote((i, side, k), piece, piece, above).wait_recv()
                if k < top:

                    @pl.when(further(side))
                    def _():
                        peer = above if side == "up" else below
                        remote((i, side, k + 1), piece, piece, peer).start()

                remote((i, side, k, "y"), piece, piece, beside).start()
                if quarter:
                    remote((i, side, k, "x"), piece, piece, across).start()

    def came(i, k):
        _, target, _, quarter = units[i]
        if k == 0:
            piece = target(z, 1 - y, blocks[i])
            remote((i, "y", 0), piece, piece, beside).wait_recv()
            if quarter:
                remote((i, "yx", 0), piece, piece, across).start()
            return
        for side, sign in sides:

            @pl.when(there(side, k))
            def _():
                piece = target(z + sign * k, 1 - y, blocks[i])
                remote((i, side, k, "y"), piece, piece, beside).wait_recv()
                if quarter:
                    remote((i, side, k, "yx"), piece, piece, across).start()

    def to_twin(i, column, b, tag):
        block = units[i][2](column, b)
        remote((i, "core", tag), block, block, twin).start()

    def spread(i):
        for copy in locals_[i]:
            copy.wait()
        to_twin(i, y, blocks[i], 0)

    def spread_beside(i):
        to_twin(i, 1 - y, blocks[i], 1)

    def x_came(i, tag):
        _, target, _, _ = units[i]
        if tag == "yx":
            piece = target(z, 1 - y, other_x)
            remote((i, "yx", 0), piece, piece, across).wait_recv()
        for k in range(1, rows_z):
            for side, sign in sides:

                @pl.when(there(side, k))
                def _():
                    piece = target(z + sign * k, y if tag == "x" else 1 - y, other_x)
                    remote((i, side, k, tag), piece, piece, across).wait_recv()

        to_twin(i, y if tag == "x" else 1 - y, other_x, 2 if tag == "x" else 3)

    first, second = range(starts[0], starts[1]), range(starts[1], starts[2])
    locals_ = {}

    def each(action, wave, *rest):
        for i in wave:
            action(i, *rest)

    for i in first:
        locals_[i] = begin(i)
    locals_[second[0]] = begin(second[0])
    each(step, first, 1)
    for i in second[1:]:
        locals_[i] = begin(i)
    each(came, first, 0)
    each(step, first, 2)
    each(came, first, 1)
    each(step, second, 1)
    each(step, first, 3)
    each(spread, first)
    each(came, first, 2)
    each(step, second, 2)
    each(came, second, 0)
    for i in first:
        came(i, 3)
        spread_beside(i)
    each(came, second, 1)
    each(step, second, 3)
    each(spread, second)
    for i in first:
        if units[i][3]:
            x_came(i, "x")
    each(came, second, 2)
    for i in first:
        if units[i][3]:
            x_came(i, "yx")
    for i in second:
        came(i, 3)
        spread_beside(i)
    for i in second:
        if units[i][3]:
            x_came(i, "x")
            x_came(i, "yx")

    for i, (source, target, whole, quarter) in enumerate(units):
        b = blocks[i]
        for tag in range(4 if quarter else 2):
            block = whole(y, b)
            remote((i, "core", tag), block, block, twin).wait()
        piece = target(z, y, b)
        remote((i, "y", 0), piece, piece, beside).wait_send()
        if quarter:
            remote((i, "yx", 0), piece, piece, across).wait_send()
        for k in range(1, rows_z):
            for side, sign in sides:
                sent = there(side, k - 1) if k > 1 else True
                pl.when(jnp.logical_and(sent, further(side)))(
                    lambda: remote((i, side, k), piece, piece, above).wait_send()
                )

                @pl.when(there(side, k))
                def _():
                    remote((i, side, k, "y"), piece, piece, beside).wait_send()
                    if quarter:
                        remote((i, side, k, "x"), piece, piece, across).wait_send()
                        remote((i, side, k, "yx"), piece, piece, across).wait_send()


def gather_weights(attend_in, attend_out, expand_weights, reduce_weights):
    shards, rows_y = 8, 2
    rows_z = shards // rows_y
    rows = attend_in.shape[1]
    width = rows * shards
    tall = reduce_weights.shape[1]

    def full(*tail):
        return jax.ShapeDtypeStruct((rows_z, rows_y, *tail), BF16)

    shapes = (
        [full(rows, attend_in.shape[2])] * 3
        + [full(rows, attend_out.shape[2])] * 3
        + [full(rows, expand_weights.shape[2])] * 2
        + [full(4, tall // 4, width)] * 2
    )
    copies = 10 * (1 + 4 * (rows_z - 1) + 2) + 4 * (1 + 4 * (rows_z - 1) + 2)
    outs = pl.pallas_call(
        functools.partial(gather_kernel, rows_z, rows_y),
        out_shape=shapes,
        in_specs=[pl.BlockSpec(memory_space=pl.ANY)] * 4,
        out_specs=[pl.BlockSpec(memory_space=pl.ANY)] * 10,
        scratch_shapes=[
            pltpu.SemaphoreType.DMA((copies,)),
            pltpu.SemaphoreType.DMA((copies,)),
            pltpu.SemaphoreType.DMA((14,)),
        ],
        compiler_params=pltpu.CompilerParams(collective_id=0, has_side_effects=True),
        cost_estimate=pl.CostEstimate(flops=0, bytes_accessed=400_000_000, transcendentals=0),
    )(attend_in, attend_out, expand_weights, reduce_weights)
    return [o.reshape(-1, o.shape[-1]) for o in outs]


def whole_weights(attend_in, attend_out, expand_weights, reduce_weights):
    tensors = (attend_in, attend_out, expand_weights, reduce_weights)
    if lax.axis_size("dp") == 8 and lax.axis_size("vocab") == 4:
        flat = gather_weights(*tensors)
        return flat[:3], flat[3:6], flat[6:8], flat[8:]
    return tuple(lax.all_gather(tensor, "dp", axis=1, tiled=True) for tensor in tensors)


def vocab_exchange_kernel(tile, valid, h_ref, target_ref, table_hbm, grad_ref, stat_ref, *scratch):
    table, held, logits_a, logits_b, powers_a, powers_b, scale_a, scale_b = scratch[:8]
    maxima_ref, total_ref, parcel, arrived, send_sem, recv_sem, table_sem = scratch[8:]
    rows, width = h_ref.shape
    padded = table.shape[0]
    tiles = padded // tile
    v = lax.axis_index("vocab")
    x, core = v // 2, lax.rem(v, 2)
    twin, across, diagonal = x * 2 + 1 - core, (1 - x) * 2 + core, (1 - x) * 2 + 1 - core

    barrier = pltpu.get_barrier_semaphore()
    for peer in (twin, across, diagonal):
        pl.semaphore_signal(
            barrier, inc=1, device_id={"vocab": peer}, device_id_type=pl.DeviceIdType.MESH
        )
    pl.semaphore_wait(barrier, 3)

    def remote(source, target, index, peer):
        return pltpu.make_async_remote_copy(
            src_ref=source,
            dst_ref=target,
            send_sem=send_sem.at[index],
            recv_sem=recv_sem.at[index],
            device_id={"vocab": peer},
            device_id_type=pl.DeviceIdType.MESH,
        )

    to_twin = remote(h_ref, held.at[0], 0, twin)
    to_across = remote(h_ref, held.at[1], 1, across)
    passed_on = remote(held.at[1], held.at[2], 2, twin)
    results = [
        remote(parcel.at[k], arrived.at[k], 3 + k, peer)
        for k, peer in enumerate((twin, across, diagonal))
    ]
    to_twin.start()
    to_across.start()
    held[3] = h_ref[...]

    sizes = [min(tile, valid - k * tile) for k in range(tiles)]
    loads = [
        pltpu.make_async_copy(
            table_hbm.at[pl.ds(k * tile, size), :],
            table.at[pl.ds(k * tile, size), :],
            table_sem.at[k],
        )
        for k, size in enumerate(sizes)
    ]
    for load in loads:
        load.start()
    if padded > valid:
        table[valid:, :] = jnp.zeros((padded - valid, width), BF16)
    to_twin.wait_recv()
    for load in loads:
        load.wait()

    logits_of, powers_of, scale_of = (logits_a, logits_b), (powers_a, powers_b), (scale_a, scale_b)
    column = lax.broadcasted_iota(jnp.int32, (rows, tile), 1)
    lane = lax.broadcasted_iota(jnp.int32, (rows, LANES), 1)

    def turn(k, _):
        @pl.when(k == 1)
        def _():
            to_across.wait_recv()
            passed_on.start()

        @pl.when(k == 2)
        def _():
            passed_on.wait_recv()

        owner = jnp.where(k == 0, twin, jnp.where(k == 1, across, jnp.where(k == 2, diagonal, v)))

        def part(at):
            return table[at * tile : (at + 1) * tile, :]

        def scores(at):
            logits_of[at % 2][...] = dot_rows(held[k], part(at))

        def soften(at):
            logits = logits_of[at % 2][...]
            if at == tiles - 1 and padded > valid:
                logits = jnp.where(column < valid - at * tile, logits, MASKED)
            highest = jnp.maximum(maxima_ref[...], jnp.max(logits, -1, keepdims=True))
            powers = jnp.exp(logits - highest)
            scale = jnp.exp(maxima_ref[...] - highest)
            maxima_ref[...] = highest
            total_ref[...] = total_ref[...] * scale + jnp.sum(powers, -1, keepdims=True)
            scale_of[at % 2][...] = scale
            powers_of[at % 2][...] = jnp.where(
                column == target_ref[owner] - at * tile, 0.0, powers
            ).astype(BF16)

        def gather(at):
            term = dot(powers_of[at % 2][...], part(at))
            grad_ref[...] = grad_ref[...] * scale_of[at % 2][...] + term

        maxima_ref[...] = jnp.full((rows, 1), MASKED, F32)
        total_ref[...] = jnp.zeros((rows, 1), F32)
        grad_ref[...] = jnp.zeros_like(grad_ref)
        for at in range(tiles + 2):
            if at < tiles:
                scores(at)
            if 0 <= at - 1 < tiles:
                soften(at - 1)
            if at >= 2:
                gather(at - 2)

        @pl.when(k < 3)
        def _():
            parcel[k, :, :width] = grad_ref[...].astype(BF16)
            tail = jnp.zeros((rows, LANES), F32)
            for first, value in ((0, maxima_ref[...]), (3, total_ref[...])):
                for step in range(3):
                    piece = value.astype(BF16).astype(F32)
                    tail = jnp.where(lane == first + step, piece, tail)
                    value = value - piece
            parcel[k, :, width:] = tail.astype(BF16)

        for index, result in enumerate(results):
            pl.when(k == index)(result.start)
        return 0

    lax.fori_loop(0, 4, turn, 0)
    for result in results:
        result.wait_recv()
    tails = [arrived[k, :, width:].astype(F32) for k in range(3)]
    highs = [t[:, 0:1] + t[:, 1:2] + t[:, 2:3] for t in tails] + [maxima_ref[...]]
    totals = [t[:, 3:4] + t[:, 4:5] + t[:, 5:6] for t in tails] + [total_ref[...]]
    highest = functools.reduce(jnp.maximum, highs)
    log_total = highest + jnp.log(sum(t * jnp.exp(m - highest) for m, t in zip(highs, totals)))
    summed = grad_ref[...] * jnp.exp(highs[3] - log_total)
    for k in range(3):
        summed = summed + arrived[k, :, :width].astype(F32) * jnp.exp(highs[k] - log_total)
    grad_ref[...] = summed
    stat_ref[...] = jnp.where(lane == 0, log_total, 0.0)
    for copy in [to_twin, to_across, passed_on, *results]:
        copy.wait_send()


def vocab_exchange(hidden, target_local, embedding):
    rows, width = hidden.shape
    valid = embedding.shape[0]
    tile = 2 * VOCAB_BLOCK
    padded = (valid + tile - 1) // tile * tile
    vmem = pl.BlockSpec(memory_space=pltpu.VMEM)
    return pl.pallas_call(
        functools.partial(vocab_exchange_kernel, tile, valid),
        out_shape=[
            jax.ShapeDtypeStruct((rows, width), F32),
            jax.ShapeDtypeStruct((rows, LANES), F32),
        ],
        in_specs=[vmem, vmem, pl.BlockSpec(memory_space=pl.ANY)],
        out_specs=[vmem, vmem],
        scratch_shapes=[
            pltpu.VMEM((padded, width), BF16),
            pltpu.VMEM((4, rows, width), BF16),
            pltpu.VMEM((rows, tile), F32),
            pltpu.VMEM((rows, tile), F32),
            pltpu.VMEM((rows, tile), BF16),
            pltpu.VMEM((rows, tile), BF16),
            pltpu.VMEM((rows, 1), F32),
            pltpu.VMEM((rows, 1), F32),
            pltpu.VMEM((rows, 1), F32),
            pltpu.VMEM((rows, 1), F32),
            pltpu.VMEM((3, rows, width + LANES), BF16),
            pltpu.VMEM((3, rows, width + LANES), BF16),
            pltpu.SemaphoreType.DMA((6,)),
            pltpu.SemaphoreType.DMA((6,)),
            pltpu.SemaphoreType.DMA((padded // tile,)),
        ],
        compiler_params=pltpu.CompilerParams(
            collective_id=1, has_side_effects=True, vmem_limit_bytes=VMEM_LIMIT
        ),
        cost_estimate=pl.CostEstimate(
            flops=16 * rows * padded * width, bytes_accessed=2 * valid * width, transcendentals=0
        ),
    )(hidden, target_local.reshape(4, rows, 1), embedding)


def reduce_kernel(rows_dp, task_ref, table_ref, stat_ref, out_ref, stats_out, squares_out, *scratch):
    cast, crossed, swap, swapped, own, outgoing, pieces, result, results = scratch[:9]
    stats, squares, send_sem, recv_sem = scratch[9:]
    features = own.shape[1]
    at, v = lax.axis_index("dp"), lax.axis_index("vocab")
    x, core = v // 2, lax.rem(v, 2)
    twin, across = x * 2 + 1 - core, (1 - x) * 2 + core
    dp_peers = [lax.rem(at + k, rows_dp) for k in range(1, rows_dp)]
    vocab_peers = [lax.rem(v + k, 4) for k in range(1, 4)]

    barrier = pltpu.get_barrier_semaphore()
    for peer in [{"vocab": p} for p in vocab_peers] + [{"dp": p} for p in dp_peers]:
        pl.semaphore_signal(barrier, inc=1, device_id=peer, device_id_type=pl.DeviceIdType.MESH)
    pl.semaphore_wait(barrier, rows_dp + 2)

    def remote(source, target, send, recv, peer):
        return pltpu.make_async_remote_copy(
            src_ref=source,
            dst_ref=target,
            send_sem=send_sem.at[send],
            recv_sem=recv_sem.at[recv],
            device_id=peer,
            device_id_type=pl.DeviceIdType.MESH,
        )

    half = 2 * features
    there = pl.ds(pl.multiple_of((1 - x) * half, half), half)
    here = pl.ds(pl.multiple_of(x * half, half), half)
    stats[0] = stat_ref[...]
    cast[...] = table_ref[there, :].astype(BF16)
    over_x = remote(cast, crossed, 0, 0, {"vocab": across})
    stat_x = remote(stats.at[0], stats.at[1], 1, 1, {"vocab": across})
    over_x.start()
    stat_x.start()
    over_x.wait_recv()
    stat_x.wait_recv()

    stats[2] = stats[0] + stats[1]
    stat_core = remote(stats.at[2], stats.at[3], 2, 2, {"vocab": twin})
    stat_core.start()
    tasks = [[task_ref[m, s] for s in range(task_ref.shape[1])] for m in range(2)]
    other = jnp.where(x == 0, 1, 0)

    def by_task(part, t):
        start = pl.multiple_of(part * features, features)
        mine = table_ref[pl.ds(pl.multiple_of(x * half + part * features, features), features), :]
        theirs = crossed[pl.ds(start, features), :].astype(F32)
        total = jnp.zeros((features, LANES), F32)
        for s in range(task_ref.shape[1]):
            lanes = slice(s * LANES, (s + 1) * LANES)
            mine_task = jnp.where(x == 0, tasks[0][s], tasks[1][s])
            their_task = jnp.where(x == 0, tasks[1][s], tasks[0][s])
            total = total + jnp.where(mine_task == t, mine[:, lanes], 0.0)
            total = total + jnp.where(their_task == t, theirs[:, lanes], 0.0)
        return total

    for t in range(TASKS):
        swap[t] = by_task(1 - core, t).astype(BF16)
    over_core = remote(swap, swapped, 3, 3, {"vocab": twin})
    over_core.start()
    for t in range(TASKS):
        own[t] = by_task(core, t)
    over_core.wait_recv()
    stat_core.wait_recv()
    stats[4 + at] = stats[2] + stats[3]
    for t in range(TASKS):
        own[t] = own[t] + swapped[t].astype(F32)
        outgoing[t] = own[t].astype(BF16)

    base = 4
    spread, tallies = [], []
    for k, peer in enumerate(dp_peers):
        spread.append(
            remote(outgoing.at[peer], pieces.at[at], base + k, base + at, {"dp": peer})
        )
        tallies.append(
            remote(
                stats.at[4 + at],
                stats.at[4 + at],
                base + rows_dp + k,
                base + rows_dp + at,
                {"dp": peer},
            )
        )
    for copy in spread + tallies:
        copy.start()
    total = own[at]
    for peer in dp_peers:
        remote(outgoing.at[peer], pieces.at[peer], base, base + peer, {"dp": peer}).wait_recv()
        total = total + pieces[peer].astype(F32)
    result[...] = total.astype(BF16)
    results[at] = result[...]
    returns = []
    for k, peer in enumerate(dp_peers):
        returns.append(
            remote(
                result,
                results.at[at],
                base + 2 * rows_dp + k,
                base + 2 * rows_dp + at,
                {"dp": peer},
            )
        )
    for copy in returns:
        copy.start()
    for peer in dp_peers:
        remote(
            stats.at[4 + peer], stats.at[4 + peer], base, base + rows_dp + peer, {"dp": peer}
        ).wait_recv()
    tally = functools.reduce(jnp.add, [stats[4 + k] for k in range(rows_dp)])
    stats_out[...] = tally
    for peer in dp_peers:
        remote(result, results.at[peer], base, base + 2 * rows_dp + peer, {"dp": peer}).wait_recv()
    for t in range(TASKS):
        scale = 1.0 / (TASKS * jnp.maximum(tally[1:2, t : t + 1], 1.0))
        scaled = results[t].astype(F32) * scale
        out_ref[t] = scaled
        squares[v, t : t + 1, :] = jnp.sum(scaled * scaled, 0, keepdims=True)
    last = base + 3 * rows_dp
    shares = [
        remote(squares.at[v], squares.at[v], last + k, last + v, {"vocab": peer})
        for k, peer in enumerate(vocab_peers)
    ]
    for copy in shares:
        copy.start()
    for peer in vocab_peers:
        remote(squares.at[peer], squares.at[peer], last, last + peer, {"vocab": peer}).wait_recv()
    squares_out[...] = squares[0] + squares[1] + squares[2] + squares[3]
    for copy in [over_x, stat_x, stat_core, over_core, *spread, *tallies, *returns, *shares]:
        copy.wait_send()


def reduce_over_devices(task_list, table, stats):
    rows_dp = lax.axis_size("dp")
    features = table.shape[0] // 4
    vmem = pl.BlockSpec(memory_space=pltpu.VMEM)
    copies = 4 + 3 * rows_dp + 4
    return pl.pallas_call(
        functools.partial(reduce_kernel, rows_dp),
        out_shape=[
            jax.ShapeDtypeStruct((TASKS, features, LANES), F32),
            jax.ShapeDtypeStruct((8, LANES), F32),
            jax.ShapeDtypeStruct((8, LANES), F32),
        ],
        in_specs=[pl.BlockSpec(memory_space=pltpu.SMEM), vmem, vmem],
        out_specs=[vmem] * 3,
        scratch_shapes=[
            pltpu.VMEM((2 * features, table.shape[1]), BF16),
            pltpu.VMEM((2 * features, table.shape[1]), BF16),
            pltpu.VMEM((TASKS, features, LANES), BF16),
            pltpu.VMEM((TASKS, features, LANES), BF16),
            pltpu.VMEM((TASKS, features, LANES), F32),
            pltpu.VMEM((TASKS, features, LANES), BF16),
            pltpu.VMEM((rows_dp, features, LANES), BF16),
            pltpu.VMEM((features, LANES), BF16),
            pltpu.VMEM((rows_dp, features, LANES), BF16),
            pltpu.VMEM((4 + rows_dp, 8, LANES), F32),
            pltpu.VMEM((4, 8, LANES), F32),
            pltpu.SemaphoreType.DMA((copies,)),
            pltpu.SemaphoreType.DMA((copies,)),
        ],
        compiler_params=pltpu.CompilerParams(
            collective_id=2, has_side_effects=True, vmem_limit_bytes=VMEM_LIMIT
        ),
    )(task_list, table, stats)


def on_device(
    tokens,
    targets,
    loss_mask,
    seg_lengths,
    task_ids,
    embedding,
    attend_in,
    attend_out,
    expand_weights,
    reduce_weights,
    norm_gains,
    prompt,
    first_moment,
    row_moment,
    column_moment,
):
    shards = lax.axis_size("vocab")
    micros, span = tokens.shape[0], tokens.shape[-1]
    length = span * shards
    group = shards // micros
    own = length // group
    me = lax.axis_index("vocab")
    micro, place = me // group, me % group
    shard_rows, width = embedding.shape
    share = prompt.shape[-1]

    def around(array, shift):
        pairs = [
            (m * group + r, m * group + (r + shift) % group)
            for m in range(micros)
            for r in range(group)
        ]
        return lax.ppermute(array, "vocab", pairs)

    ids = lax.all_gather(jnp.stack([tokens[:, 0], targets[:, 0], loss_mask[:, 0]]), "vocab")
    ids = jnp.transpose(ids, (1, 2, 0, 3)).reshape(3, micros, length)
    enc_ids = ids[0].reshape(shards, own)
    before = jnp.pad(ids[1], ((0, 0), (1, 0)))[:, :length].reshape(shards, own)[:, :1]
    dec_ids = jnp.concatenate(
        [jnp.zeros((shards, HALO - 1), jnp.int32), before, ids[1].reshape(shards, own)], 1
    )
    first_row = me * shard_rows

    def lookup(wanted):
        local = wanted.reshape(-1) - first_row
        inside = (local >= 0) & (local < shard_rows)
        picked = jnp.take(embedding, jnp.clip(local, 0, shard_rows - 1), axis=0)
        return jnp.where(inside[:, None], picked, 0)

    enc_rows = lax.psum_scatter(lookup(enc_ids), "vocab", scatter_dimension=0, tiled=True)
    dec_rows = lax.psum_scatter(lookup(dec_ids), "vocab", scatter_dimension=0, tiled=True)

    prompt_all = lax.all_gather(prompt.astype(BF16), "vocab", axis=2, tiled=True)
    prompt_flat = prompt_all.reshape(-1, width)
    attend_in, attend_out, expand_weights, reduce_weights = whole_weights(
        attend_in, attend_out, expand_weights, reduce_weights
    )

    lengths = lax.dynamic_index_in_dim(seg_lengths[:, 0], micro, 0, False)
    tasks = lax.dynamic_index_in_dim(task_ids[:, 0], micro, 0, False)
    steps = jnp.arange(own, dtype=jnp.int32)
    positions = place * own + steps
    segment, in_segment, task_of = layout(lengths, tasks, positions)
    key_positions = jnp.concatenate(
        [((place - k + group) % group) * own + steps for k in range(group)]
    )
    key_segment = layout(lengths, tasks, key_positions)[0]
    rows_info = jnp.stack([segment, positions], 1)
    keys_info = jnp.stack([key_segment, key_positions], 0)
    own_mask = lax.dynamic_slice(ids[2], (micro, place * own), (1, own))[0]
    counted = (own_mask * (in_segment >= P_SIZE)).astype(F32)

    def key_parts(source, weight):
        pair = dot(source, weight).astype(BF16)
        return [pair] + [around(pair, k) for k in range(1, group)]

    def project(source, weight):
        return dot(source, weight).astype(BF16)

    is_prompt = in_segment < P_SIZE
    slot = task_of * P_SIZE + jnp.minimum(in_segment, P_SIZE - 1)
    enc_input = jnp.where(
        is_prompt[:, None], jnp.take(prompt_flat, slot, axis=0), enc_rows
    ).astype(F32)
    target_rows = dec_rows[HALO:].astype(F32)
    dec_input = jnp.where(
        (in_segment >= 1)[:, None], dec_rows[HALO - 1 : HALO - 1 + own], dec_rows[:1]
    ).astype(F32)

    normed_in, inverse_in = normed(enc_input, norm_gains[0])
    normed_low = normed_in.astype(BF16)
    enc_pairs = key_parts(normed_low, attend_in[0][:, width:])
    enc_queries = project(normed_low, attend_in[0][:, :width])
    normed_dec = normed(dec_input, norm_gains[3])[0].astype(BF16)
    dec_pairs = key_parts(normed_dec, attend_in[1][:, width:])
    dec_queries = project(normed_dec, attend_in[1][:, :width])
    mixed = attend(enc_queries, enc_pairs, rows_info, keys_info, False)
    enc_mid = enc_input + dot(mixed, attend_out[0])
    normed_mid, inverse_mid = normed(enc_mid, norm_gains[1])
    enc_pre = dot(normed_mid.astype(BF16), expand_weights[0])
    enc_last = enc_mid + dot(smooth(enc_pre).astype(BF16), reduce_weights[0])
    encoded, inverse_last = normed(enc_last, norm_gains[2])
    cross_pairs = key_parts(encoded.astype(BF16), attend_in[2][:, width:])

    mixed = attend(dec_queries, dec_pairs, rows_info, keys_info, True)
    dec_first = dec_input + dot(mixed, attend_out[1])
    cross_queries = project(normed(dec_first, norm_gains[4])[0].astype(BF16), attend_in[2][:, :width])
    mixed = attend(cross_queries, cross_pairs, rows_info, keys_info, False)
    dec_second = dec_first + dot(mixed, attend_out[2])
    normed_second, inverse_second = normed(dec_second, norm_gains[5])
    dec_pre = dot(normed_second.astype(BF16), expand_weights[1])
    dec_last = dec_second + dot(smooth(dec_pre).astype(BF16), reduce_weights[1])
    output_norm, inverse_out = normed(dec_last, norm_gains[6])
    hidden = (output_norm * width ** (-0.5)).astype(BF16)

    target_local = ids[1].reshape(-1, 1) - first_row
    if shards == 4:
        summed, stats = vocab_exchange(hidden, target_local, embedding)
        own_total = stats[:, 0]
    else:
        all_hidden = lax.all_gather(hidden, "vocab", axis=0, tiled=True)
        part, stats = vocab_pass(all_hidden, target_local, embedding, own)
        gathered = lax.all_gather(stats[:, :2].T, "vocab")
        maxima = jnp.max(gathered[:, 0], 0)
        log_total = maxima + jnp.log(
            jnp.sum(gathered[:, 1] * jnp.exp(gathered[:, 0] - maxima), 0)
        )
        scaled = part * jnp.exp(stats[:, 0] - log_total)[:, None]
        summed = lax.psum_scatter(scaled, "vocab", scatter_dimension=0, tiled=True)
        own_total = lax.dynamic_slice(log_total, (me * own,), (own,))
    target_logit = jnp.sum(hidden.astype(F32) * target_rows, -1)
    token_loss = own_total - target_logit
    target_coefficient = (jnp.exp(target_logit - own_total) - 1.0).astype(BF16).astype(F32)
    hidden_grad = counted[:, None] * (summed + target_coefficient[:, None] * target_rows)

    def feed_back(hidden_pre, weight_one, weight_two, gradient):
        active_grad = dot_rows(gradient.astype(BF16), weight_two)
        pre_grad = jax.vjp(smooth, hidden_pre)[1](active_grad)[0].astype(BF16)
        return dot_rows(pre_grad, weight_one)

    def keys_back(parts, weight):
        dk, dv = parts[:group], parts[group : 2 * group]
        pairs = [jnp.concatenate([dk[k], dv[k]], 1) for k in range(group)]
        total = pairs[0]
        for k in range(1, group):
            total = total + around(pairs[k], group - k)
        high = total.astype(BF16)
        rest = (total - high.astype(F32)).astype(BF16)
        return dot_rows(high, weight) + dot_rows(rest, weight)

    dec_grad = normed_back(
        dec_last, norm_gains[6], inverse_out, hidden_grad * width ** (-0.5)
    )
    dec_grad = dec_grad + normed_back(
        dec_second,
        norm_gains[5],
        inverse_second,
        feed_back(dec_pre, expand_weights[1], reduce_weights[1], dec_grad),
    )
    mixed_grad = dot_rows(dec_grad.astype(BF16), attend_out[2]).astype(BF16)
    back = attend_back(cross_queries, cross_pairs, mixed_grad, rows_info.T, keys_info.T, False)
    enc_grad = normed_back(
        enc_last, norm_gains[2], inverse_last, keys_back(back, attend_in[2][:, width:])
    )
    enc_grad = enc_grad + normed_back(
        enc_mid,
        norm_gains[1],
        inverse_mid,
        feed_back(enc_pre, expand_weights[0], reduce_weights[0], enc_grad),
    )
    mixed_grad = dot_rows(enc_grad.astype(BF16), attend_out[0]).astype(BF16)
    back = attend_back(enc_queries, enc_pairs, mixed_grad, rows_info.T, keys_info.T, True)
    source_grad = keys_back(back, attend_in[0][:, width:]) + dot_rows(
        back[-1], attend_in[0][:, :width]
    )
    enc_grad = enc_grad + normed_back(enc_input, norm_gains[0], inverse_in, source_grad)

    segments = lengths.shape[0]
    place_of = segment * LANES + in_segment
    chosen = (
        (place_of[:, None] == jnp.arange(segments * LANES, dtype=jnp.int32)) & is_prompt[:, None]
    ).astype(BF16)
    high = enc_grad.astype(BF16)
    rest = (enc_grad - high.astype(F32)).astype(BF16)
    table = dot_columns(high, chosen) + dot_columns(rest, chosen)
    tallies = jnp.stack([per_task(task_of, counted * token_loss), per_task(task_of, counted)])
    stats = jnp.zeros((8, LANES), F32).at[:2, :TASKS].set(tallies)
    if shards == 4 and lax.axis_size("dp") == TASKS:
        gradient, stats, squares = reduce_over_devices(task_ids[:, 0], table, stats)
        full_grad = jnp.swapaxes(gradient[:, :, :P_SIZE], 1, 2)
        row_squares = squares[:, :P_SIZE]
        task_scale = 1.0 / (TASKS * jnp.maximum(stats[1, :TASKS], 1.0))
    else:
        hits = (tasks[:, None] == jnp.arange(TASKS, dtype=jnp.int32)).astype(F32)
        by_task = jnp.einsum(
            "fsp,st->tpf",
            table.reshape(width, segments, LANES)[:, :, :P_SIZE],
            hits,
            precision=lax.Precision.HIGHEST,
        )
        stats = lax.psum(stats, ("dp", "vocab"))
        gradient = lax.psum_scatter(by_task, "vocab", scatter_dimension=2, tiled=True)
        task_scale = 1.0 / (TASKS * jnp.maximum(stats[1, :TASKS], 1.0))
        full_grad = lax.psum(gradient, "dp") * task_scale[:, None, None]
        row_squares = jnp.sum(lax.all_gather(jnp.sum(full_grad * full_grad, -1), "vocab"), 0)
    loss_mean = jnp.sum(stats[0, :TASKS] * task_scale)
    grad_norm = jnp.sqrt(jnp.sum(row_squares))
    clip = CLIP_NORM / jnp.maximum(grad_norm, CLIP_NORM)
    prompt_grad = full_grad * clip
    row_second = BETA_TWO * row_moment + (1.0 - BETA_TWO) * (
        row_squares * clip * clip / width + SQUARE_EPS
    )
    column_second = BETA_TWO * column_moment + (1.0 - BETA_TWO) * (
        jnp.mean(prompt_grad * prompt_grad, 1) + SQUARE_EPS
    )
    new_moment = BETA_ONE * first_moment + (1.0 - BETA_ONE) * prompt_grad
    estimate = (
        row_second[:, :, None] * column_second[:, None, :] / jnp.mean(row_second, -1)[:, None, None]
    )
    update = new_moment / (1.0 - BETA_ONE**STEP) / jnp.sqrt(estimate / (1.0 - BETA_TWO**STEP))
    new_prompt = prompt - LEARN_RATE * (update + WEIGHT_DECAY * prompt)
    return (loss_mean, grad_norm, prompt_grad, new_moment, row_second, column_second, new_prompt)


def solution(mesh):
    placed = (
        P(None, "dp", "vocab"),
        P(None, "dp", "vocab"),
        P(None, "dp", "vocab"),
        P(None, "dp", None),
        P(None, "dp", None),
        P("vocab", None),
        P(None, "dp", None),
        P(None, "dp", None),
        P(None, "dp", None),
        P(None, "dp", None),
        P(),
        P(None, None, "vocab"),
        P(None, None, "vocab"),
        P(),
        P(None, "vocab"),
    )
    return jax.shard_map(
        on_device,
        mesh=mesh,
        in_specs=placed,
        out_specs=(
            P(),
            P(),
            P(None, None, "vocab"),
            P(None, None, "vocab"),
            P(),
            P(None, "vocab"),
            P(None, None, "vocab"),
        ),
        check_vma=False,
    )
```

```python
import functools

import jax
import jax.numpy as jnp
from jax import lax
from jax.experimental import pallas as pl
from jax.experimental.pallas import tpu as pltpu
from jax.sharding import PartitionSpec as P

DH = 64
P_SIZE = 100
TASKS = 8
STEP = 5
HALO = 16
LANES = 128
SEGS = 3
VOCAB_BLOCK = 1024
MIB = 1024 * 1024

NORM_EPS = 1e-06
CLIP_NORM = 2e-05
BETA_ONE = 0.9
BETA_TWO = 0.999
LEARN_RATE = 1.0
WEIGHT_DECAY = 1e-05
SQUARE_EPS = 1e-30
MASKED = -1e30

F32 = jnp.float32
BF16 = jnp.bfloat16


def dot(left, right):
    return jnp.dot(left, right, preferred_element_type=F32)


def dot_rows(left, right):
    return lax.dot_general(left, right, (((1,), (1,)), ((), ())), preferred_element_type=F32)


def dot_columns(left, right):
    return lax.dot_general(left, right, (((0,), (0,)), ((), ())), preferred_element_type=F32)


def normed(values, gain):
    inverse = lax.rsqrt(jnp.mean(values * values, -1, keepdims=True) + NORM_EPS)
    return (values * inverse * gain, inverse)


def normed_back(values, gain, inverse, gradient):
    unit_rows = values * inverse
    scaled = gradient * gain
    return inverse * (scaled - unit_rows * jnp.mean(scaled * unit_rows, -1, keepdims=True))


def smooth(values):
    return jax.nn.gelu(values, approximate=True)


def layout(lengths, task_list, positions):
    seg_ends = jnp.cumsum(lengths)
    seg_starts = seg_ends - lengths
    segment = jnp.sum((positions[:, None] >= seg_ends[None, :]).astype(jnp.int32), -1)
    member = segment[:, None] == jnp.arange(lengths.shape[0], dtype=jnp.int32)[None, :]
    in_segment = positions - jnp.sum(jnp.where(member, seg_starts[None, :], 0), -1)
    task_of = jnp.sum(jnp.where(member, task_list[None, :], 0), -1)
    return (segment, in_segment, task_of)


def per_task(task_of, amounts):
    hits = task_of[:, None] == jnp.arange(TASKS, dtype=jnp.int32)
    return jnp.sum(jnp.where(hits, amounts[:, None], 0.0), 0)


def pair_lanes(pair, first=0):
    return pl.ds(pl.multiple_of(first + pair * LANES, LANES), LANES)


def head_mask(shape, head, axis=1):
    return (lax.broadcasted_iota(jnp.int32, shape, axis) < DH) == (head == 0)


def segment_columns(segment, is_key, shape):
    column = lax.rem(lax.broadcasted_iota(jnp.int32, shape, 1), DH)
    if is_key:
        return jnp.where((column < SEGS) & (column != segment), MASKED, 0.0).astype(BF16)
    return jnp.where(column == segment, 1.0, 0.0).astype(BF16)


def head_part(values, rest, head):
    return jnp.where(head_mask(values.shape, head), values, rest)


def over_heads(pairs, scores, soften, mix):
    scores(0, 0)
    scores(0, 1)
    soften(0, 0)

    def step(pair, _):
        scores(pair + 1, 0)
        soften(pair, 1)
        mix(pair, 0)
        scores(pair + 1, 1)
        soften(pair + 1, 0)
        mix(pair, 1)
        return 0

    lax.fori_loop(0, pairs - 1, step, 0)
    soften(pairs - 1, 1)
    mix(pairs - 1, 0)
    mix(pairs - 1, 1)


def attend_kernel(parts, causal, *refs):
    q_ref, pair_refs = refs[0], refs[1 : 1 + parts]
    residual_ref, weight_ref, q_info, k_info, k_rows, out_ref, mixed_ref, log_ref = refs[
        1 + parts : 9 + parts
    ]
    bias_ref, q_mark, k_mark, low_ref, scores_a, scores_b, powers_a, powers_b = refs[9 + parts :]
    width = q_ref.shape[1]
    own = pair_refs[0].shape[0]
    scores_of, powers_of = (scores_a, scores_b), (powers_a, powers_b)
    rows = [slice(k * own, (k + 1) * own) for k in range(parts)]
    q_mark[...] = segment_columns(q_info[:, 0:1], False, q_mark.shape)
    k_mark[...] = segment_columns(k_info[:, 0:1], True, k_mark.shape)
    if causal:
        bias_ref[...] = jnp.where(q_info[:, 1:2] >= k_rows[...], 0.0, MASKED)
    log_ref[...] = jnp.zeros_like(log_ref)
    lane = lax.broadcasted_iota(jnp.int32, log_ref.shape, 1)

    def scores(pair, head):
        query = q_ref[:, pair_lanes(pair)] * jnp.asarray(DH ** (-0.5), BF16)
        query = head_part(query, q_mark[...], head)
        for k in range(parts):
            keys = head_part(pair_refs[k][:, pair_lanes(pair)], k_mark[rows[k], :], head)
            values = dot_rows(query, keys)
            if causal:
                values = values + bias_ref[:, rows[k]]
            scores_of[head][:, rows[k]] = values

    def soften(pair, head):
        values = scores_of[head][...]
        highest = jnp.max(values, -1, keepdims=True)
        powers_of[head][...] = jnp.exp(values - highest).astype(BF16)
        log_ref[...] += jnp.where(lane == 2 * pair + head, highest, 0.0)

    def mix(pair, head):
        value = None
        for k in range(parts):
            values = pair_refs[k][:, pair_lanes(pair, width)]
            values = head_part(values, jnp.ones_like(values), head)
            term = dot(powers_of[head][:, rows[k]], values)
            value = term if value is None else value + term
        total = value[:, LANES - 1 :] if head == 0 else value[:, :1]
        value = value / total
        log_ref[...] += jnp.where(lane == 2 * pair + head, jnp.log(total), 0.0)
        lanes = pair_lanes(pair)
        if head:
            value = jnp.where(head_mask(value.shape, 0), mixed_ref[:, lanes], value)
        mixed_ref[:, lanes] = value
        if head:
            low_ref[:, lanes] = value.astype(BF16)

    over_heads(width // LANES, scores, soften, mix)
    out_ref[...] = residual_ref[...] + dot(low_ref[...], weight_ref[...])


def attend(queries, pairs, residual, weight, q_info, k_info, causal):
    own, width = queries.shape
    parts, length = len(pairs), k_info.shape[0]
    vmem = pl.BlockSpec(memory_space=pltpu.VMEM)
    return pl.pallas_call(
        functools.partial(attend_kernel, parts, causal),
        out_shape=[
            jax.ShapeDtypeStruct((own, width), F32),
            jax.ShapeDtypeStruct((own, width), F32),
            jax.ShapeDtypeStruct((own, LANES), F32),
        ],
        in_specs=[vmem] * (parts + 6),
        out_specs=[vmem] * 3,
        scratch_shapes=[
            pltpu.VMEM((own, length), F32),
            pltpu.VMEM((own, LANES), BF16),
            pltpu.VMEM((length, LANES), BF16),
            pltpu.VMEM((own, width), BF16),
            pltpu.VMEM((own, length), F32),
            pltpu.VMEM((own, length), F32),
            pltpu.VMEM((own, length), BF16),
            pltpu.VMEM((own, length), BF16),
        ],
        compiler_params=pltpu.CompilerParams(vmem_limit_bytes=26 * MIB),
        cost_estimate=pl.CostEstimate(
            flops=10 * own * length * width, bytes_accessed=6 * own * width, transcendentals=0
        ),
    )(queries, *pairs, residual, weight, q_info, k_info, k_info[:, 1:].T)


def attend_back_kernel(parts, want_queries, *refs):
    q_ref, pair_refs = refs[0], refs[1 : 1 + parts]
    grad_ref, weight_ref, mixed_ref, log_ref, q_info, k_info = refs[1 + parts : 7 + parts]
    rest = refs[7 + parts :]
    out_refs = rest[:parts]
    dq_ref = rest[parts] if want_queries else None
    q_mark, k_mark, low_ref, delta_ref, *rest = rest[parts + want_queries :]
    scores_of, grads_of, weights_of, steps_of = rest[0:2], rest[2:4], rest[4:6], rest[6:8]
    width = q_ref.shape[1]
    own = pair_refs[0].shape[0]
    rows = [slice(k * own, (k + 1) * own) for k in range(parts)]
    scale = jnp.asarray(DH ** (-0.5), BF16)
    q_mark[...] = segment_columns(q_info[:, 0:1], False, q_mark.shape)
    k_mark[...] = segment_columns(k_info[:, 0:1], True, k_mark.shape)
    low_ref[...] = dot_rows(grad_ref[...].astype(BF16), weight_ref[...]).astype(BF16)
    product = low_ref[...].astype(F32) * mixed_ref[...]
    high = product.astype(BF16)
    shape = (2 * 8, width)
    belongs = lax.broadcasted_iota(jnp.int32, shape, 1) // DH == lax.broadcasted_iota(
        jnp.int32, shape, 0
    )
    belongs = jnp.where(belongs, 1.0, 0.0).astype(BF16)
    delta_ref[...] = dot_rows(belongs, high) + dot_rows(
        belongs, (product - high.astype(F32)).astype(BF16)
    )

    def scores(pair, head):
        query = head_part(q_ref[:, pair_lanes(pair)] * scale, q_mark[...], head)
        grad = low_ref[:, pair_lanes(pair)]
        grad = head_part(grad, jnp.zeros_like(grad), head)
        for k in range(parts):
            keys = head_part(pair_refs[k][:, pair_lanes(pair)], k_mark[rows[k], :], head)
            scores_of[head][rows[k], :] = dot_rows(keys, query)
            grads_of[head][rows[k], :] = dot_rows(pair_refs[k][:, pair_lanes(pair, width)], grad)

    def soften(pair, head):
        at = pl.ds(2 * pair + head, 1)
        weights = jnp.exp(scores_of[head][...] - log_ref[at, :])
        weights_of[head][...] = weights.astype(BF16)
        steps_of[head][...] = (weights * (grads_of[head][...] - delta_ref[at, :])).astype(BF16)

    def mix(pair, head):
        keys, values = pair_lanes(pair), pair_lanes(pair, width)
        query, grad = q_ref[:, keys] * scale, low_ref[:, keys]
        query = head_part(query, jnp.zeros_like(query), head)
        grad = head_part(grad, jnp.zeros_like(grad), head)
        dq = None
        for k in range(parts):
            step = steps_of[head][rows[k], :]
            dk = dot(step, query)
            dv = dot(weights_of[head][rows[k], :], grad)
            out_refs[k][:, keys] = dk if head == 0 else out_refs[k][:, keys] + dk
            out_refs[k][:, values] = dv if head == 0 else out_refs[k][:, values] + dv
            if want_queries:
                term = dot_columns(pair_refs[k][:, keys], step)
                dq = term if dq is None else dq + term
        if want_queries:
            here = pl.ds(pl.multiple_of(pair * LANES, LANES), LANES)
            dq = (dq * DH ** (-0.5)).astype(BF16)
            if head:
                dq = jnp.where(head_mask(dq.shape, 0, 0), dq_ref[here, :], dq)
            dq_ref[here, :] = dq

    over_heads(width // LANES, scores, soften, mix)


def attend_back(queries, pairs, gradient, weight, mixed, logs, q_info, k_info, want_queries):
    own, width = queries.shape
    parts, length = len(pairs), k_info.shape[0]
    shapes = [jax.ShapeDtypeStruct(pair.shape, F32) for pair in pairs]
    if want_queries:
        shapes.append(jax.ShapeDtypeStruct((width, own), BF16))
    return pl.pallas_call(
        functools.partial(attend_back_kernel, parts, want_queries),
        out_shape=shapes,
        in_specs=[pl.BlockSpec(memory_space=pltpu.VMEM)] * (parts + 7),
        out_specs=[pl.BlockSpec(memory_space=pltpu.VMEM)] * len(shapes),
        scratch_shapes=[
            pltpu.VMEM((own, LANES), BF16),
            pltpu.VMEM((length, LANES), BF16),
            pltpu.VMEM((own, width), BF16),
            pltpu.VMEM((16, own), F32),
        ]
        + [pltpu.VMEM((length, own), F32)] * 4
        + [pltpu.VMEM((length, own), BF16)] * 4,
        compiler_params=pltpu.CompilerParams(vmem_limit_bytes=34 * MIB),
        cost_estimate=pl.CostEstimate(
            flops=20 * own * length * width, bytes_accessed=20 * own * width, transcendentals=0
        ),
    )(queries, *pairs, gradient, weight, mixed, logs.T[:16], q_info, k_info)


def feed(rows, gain, weights_one, weights_two):
    values, inverse = normed(rows, gain)
    source = values.astype(BF16)
    before = [dot(source, one) for one in weights_one]
    for pre, two in zip(before, weights_two):
        rows = rows + dot(smooth(pre).astype(BF16), two)
    return rows, (before, inverse)


def feed_back(gradient, rows, gain, kept, weights_one, weights_two):
    before, inverse = kept
    low = gradient.astype(BF16)
    total = 0.0
    for pre, one, two in zip(before, weights_one, weights_two):
        active_grad = dot_rows(low, two)
        step = jax.vjp(smooth, pre)[1](active_grad)[0].astype(BF16)
        total = total + dot_rows(step, one)
    return gradient + normed_back(rows, gain, inverse, total)


def vocab_kernel(tile, valid, h_ref, target_ref, table_hbm, grad_ref, stat_ref, table, sem):
    padded = table.shape[0]

    @pl.when(pl.program_id(0) == 0)
    def _():
        copy = pltpu.make_async_copy(table_hbm, table.at[pl.ds(0, valid), :], sem)
        copy.start()
        if padded > valid:
            table[valid:, :] = jnp.zeros((padded - valid, table.shape[1]), BF16)
        copy.wait()

    rows = h_ref.shape[0]
    hidden = h_ref[...]
    column = lax.broadcasted_iota(jnp.int32, (rows, tile), 1)
    target = target_ref[...]

    def block(at, carry, last):
        maxima, total = carry
        part = table[pl.ds(pl.multiple_of(at * tile, tile), tile), :]
        logits = dot_rows(hidden, part)
        if last and padded > valid:
            logits = jnp.where(column < valid - (padded - tile), logits, MASKED)
        highest = jnp.maximum(maxima, jnp.max(logits, -1, keepdims=True))
        powers = jnp.exp(logits - highest)
        scale = jnp.exp(maxima - highest)
        total = total * scale + jnp.sum(powers, -1, keepdims=True)
        powers = jnp.where(column == target - at * tile, 0.0, powers).astype(BF16)
        grad_ref[...] = grad_ref[...] * scale + dot(powers, part)
        return (highest, total)

    grad_ref[...] = jnp.zeros_like(grad_ref)
    blocks = padded // tile
    carry = (jnp.full((rows, 1), MASKED, F32), jnp.zeros((rows, 1), F32))
    carry = lax.fori_loop(0, blocks - 1, lambda at, c: block(at, c, False), carry)
    maxima, total = block(blocks - 1, carry, True)
    lane = lax.broadcasted_iota(jnp.int32, stat_ref.shape, 1)
    stat_ref[...] = jnp.where(lane == 0, maxima, total)


def vocab_pass(hidden, target_local, embedding, rows):
    count, width = hidden.shape
    valid = embedding.shape[0]
    tile = VOCAB_BLOCK
    padded = (valid + tile - 1) // tile * tile
    return pl.pallas_call(
        functools.partial(vocab_kernel, tile, valid),
        grid=(count // rows,),
        out_shape=[
            jax.ShapeDtypeStruct((count, width), F32),
            jax.ShapeDtypeStruct((count, LANES), F32),
        ],
        in_specs=[
            pl.BlockSpec((rows, width), lambda i: (i, 0)),
            pl.BlockSpec((rows, 1), lambda i: (i, 0)),
            pl.BlockSpec(memory_space=pl.ANY),
        ],
        out_specs=[
            pl.BlockSpec((rows, width), lambda i: (i, 0)),
            pl.BlockSpec((rows, LANES), lambda i: (i, 0)),
        ],
        scratch_shapes=[pltpu.VMEM((padded, width), BF16), pltpu.SemaphoreType.DMA],
        compiler_params=pltpu.CompilerParams(vmem_limit_bytes=56 * MIB),
        cost_estimate=pl.CostEstimate(
            flops=4 * count * padded * width, bytes_accessed=2 * valid * width, transcendentals=0
        ),
    )(hidden, target_local, embedding)


def gather_kernel(rows_z, rows_y, *refs):
    in_ref, out_ref, expand_ref, reduce_ref = refs[:4]
    in_full, out_full, expand_full, reduce_full = refs[4:7], refs[7:10], refs[10:12], refs[12:14]
    send_sem, recv_sem, local_sem = refs[14:]
    at, v = lax.axis_index("dp"), lax.axis_index("vocab")
    z, y, x, core = at // rows_y, lax.rem(at, rows_y), v // 2, lax.rem(v, 2)
    top = rows_z - 1
    above = {"dp": jnp.minimum(z + 1, top) * rows_y + y, "vocab": v}
    below = {"dp": jnp.maximum(z - 1, 0) * rows_y + y, "vocab": v}
    beside = {"dp": z * rows_y + (1 - y), "vocab": v}
    other_x = (1 - x) * 2 + core
    across = {"dp": at, "vocab": other_x}
    twin = {"dp": at, "vocab": x * 2 + (1 - core)}

    barrier = pltpu.get_barrier_semaphore()

    def greet(peer):
        pl.semaphore_signal(barrier, inc=1, device_id=peer, device_id_type=pl.DeviceIdType.MESH)

    pl.when(z < top)(lambda: greet(above))
    pl.when(z > 0)(lambda: greet(below))
    greet(beside)
    greet(across)
    greet(twin)
    inner = jnp.logical_and(z > 0, z < top)
    pl.when(inner)(lambda: pl.semaphore_wait(barrier, 5))
    pl.when(jnp.logical_not(inner))(lambda: pl.semaphore_wait(barrier, 4))

    names, tallies = {}, [0, 0]

    def remote(name, source, target, peer):
        if name not in names:
            names[name] = tallies[0]
            tallies[0] += 1
        return pltpu.make_async_remote_copy(
            src_ref=source,
            dst_ref=target,
            send_sem=send_sem.at[names[name]],
            recv_sem=recv_sem.at[names[name]],
            device_id=peer,
            device_id_type=pl.DeviceIdType.MESH,
        )

    def local(source, target):
        copy = pltpu.make_async_copy(source, target, local_sem.at[tallies[1]])
        tallies[1] += 1
        copy.start()
        return copy

    def columns(ref, full, index, blocks):
        wide = ref.shape[2] // blocks
        here = lambda b: pl.ds(pl.multiple_of(b * wide, wide), wide)
        return (
            lambda b: ref.at[index, :, here(b)],
            lambda zs, ys, b: full.at[zs, ys, :, here(b)],
            lambda ys, b: full.at[:, ys, :, here(b)],
            blocks == 4,
        )

    def row_blocks(ref, full, index):
        count = ref.shape[1] // 4
        return (
            lambda b: ref.at[index, pl.ds(pl.multiple_of(b * count, count), count), :],
            lambda zs, ys, b: full.at[zs, ys, b],
            lambda ys, b: full.at[:, ys, b],
            True,
        )

    def attention(j):
        return [columns(in_ref, in_full[j], j, 2), columns(out_ref, out_full[j], j, 2)]

    def feed(j):
        return [columns(expand_ref, expand_full[j], j, 4), row_blocks(reduce_ref, reduce_full[j], j)]

    waves = [feed(0) + attention(0), feed(1) + attention(1) + attention(2)]
    units = [u for wave in waves for u in wave]
    starts = [0, len(waves[0]), len(units)]
    blocks = [v if u[3] else core for u in units]
    sides = (("up", -1), ("down", 1))

    def there(side, k):
        return z - k >= 0 if side == "up" else z + k <= top

    def further(side):
        return z < top if side == "up" else z > 0

    def begin(i):
        source, target, _, quarter = units[i]
        b = blocks[i]
        piece = target(z, y, b)
        pl.when(z < top)(lambda: remote((i, "up", 1), source(b), piece, above).start())
        pl.when(z > 0)(lambda: remote((i, "down", 1), source(b), piece, below).start())
        remote((i, "y", 0), source(b), piece, beside).start()
        copies = [local(source(b), piece)]
        if quarter:
            copies.append(local(source(other_x), target(z, y, other_x)))
        return copies

    def step(i, k):
        _, target, _, quarter = units[i]
        for side, sign in sides:

            @pl.when(there(side, k))
            def _():
                piece = target(z + sign * k, y, blocks[i])
                remote((i, side, k), piece, piece, above).wait_recv()
                if k < top:

                    @pl.when(further(side))
                    def _():
                        peer = above if side == "up" else below
                        remote((i, side, k + 1), piece, piece, peer).start()

                remote((i, side, k, "y"), piece, piece, beside).start()
                if quarter:
                    remote((i, side, k, "x"), piece, piece, across).start()

    def came(i, k):
        _, target, _, quarter = units[i]
        if k == 0:
            piece = target(z, 1 - y, blocks[i])
            remote((i, "y", 0), piece, piece, beside).wait_recv()
            if quarter:
                remote((i, "yx", 0), piece, piece, across).start()
            return
        for side, sign in sides:

            @pl.when(there(side, k))
            def _():
                piece = target(z + sign * k, 1 - y, blocks[i])
                remote((i, side, k, "y"), piece, piece, beside).wait_recv()
                if quarter:
                    remote((i, side, k, "yx"), piece, piece, across).start()

    def to_twin(i, column, b, tag):
        block = units[i][2](column, b)
        remote((i, "core", tag), block, block, twin).start()

    def spread(i):
        for copy in locals_[i]:
            copy.wait()
        to_twin(i, y, blocks[i], 0)

    def spread_beside(i):
        to_twin(i, 1 - y, blocks[i], 1)

    def x_came(i, tag):
        _, target, _, _ = units[i]
        if tag == "yx":
            piece = target(z, 1 - y, other_x)
            remote((i, "yx", 0), piece, piece, across).wait_recv()
        for k in range(1, rows_z):
            for side, sign in sides:

                @pl.when(there(side, k))
                def _():
                    piece = target(z + sign * k, y if tag == "x" else 1 - y, other_x)
                    remote((i, side, k, tag), piece, piece, across).wait_recv()

        to_twin(i, y if tag == "x" else 1 - y, other_x, 2 if tag == "x" else 3)

    first, second = range(starts[0], starts[1]), range(starts[1], starts[2])
    locals_ = {}

    def each(action, wave, *rest):
        for i in wave:
            action(i, *rest)

    for i in first:
        locals_[i] = begin(i)
    locals_[second[0]] = begin(second[0])
    each(step, first, 1)
    for i in second[1:]:
        locals_[i] = begin(i)
    each(came, first, 0)
    each(step, first, 2)
    each(came, first, 1)
    each(step, second, 1)
    each(step, first, 3)
    each(spread, first)
    each(came, first, 2)
    each(step, second, 2)
    each(came, second, 0)
    for i in first:
        came(i, 3)
        spread_beside(i)
    each(came, second, 1)
    each(step, second, 3)
    each(spread, second)
    for i in first:
        if units[i][3]:
            x_came(i, "x")
    each(came, second, 2)
    for i in first:
        if units[i][3]:
            x_came(i, "yx")
    for i in second:
        came(i, 3)
        spread_beside(i)
    for i in second:
        if units[i][3]:
            x_came(i, "x")
            x_came(i, "yx")

    for i, (source, target, whole, quarter) in enumerate(units):
        b = blocks[i]
        for tag in range(4 if quarter else 2):
            block = whole(y, b)
            remote((i, "core", tag), block, block, twin).wait()
        piece = target(z, y, b)
        remote((i, "y", 0), piece, piece, beside).wait_send()
        if quarter:
            remote((i, "yx", 0), piece, piece, across).wait_send()
        for k in range(1, rows_z):
            for side, sign in sides:
                sent = there(side, k - 1) if k > 1 else True
                pl.when(jnp.logical_and(sent, further(side)))(
                    lambda: remote((i, side, k), piece, piece, above).wait_send()
                )

                @pl.when(there(side, k))
                def _():
                    remote((i, side, k, "y"), piece, piece, beside).wait_send()
                    if quarter:
                        remote((i, side, k, "x"), piece, piece, across).wait_send()
                        remote((i, side, k, "yx"), piece, piece, across).wait_send()


def gather_weights(attend_in, attend_out, expand_weights, reduce_weights):
    shards, rows_y = 8, 2
    rows_z = shards // rows_y
    rows = attend_in.shape[1]
    width = rows * shards
    tall = reduce_weights.shape[1]

    def full(*tail):
        return jax.ShapeDtypeStruct((rows_z, rows_y, *tail), BF16)

    shapes = (
        [full(rows, attend_in.shape[2])] * 3
        + [full(rows, attend_out.shape[2])] * 3
        + [full(rows, expand_weights.shape[2])] * 2
        + [full(4, tall // 4, width)] * 2
    )
    copies = 10 * (1 + 4 * (rows_z - 1) + 2) + 4 * (1 + 4 * (rows_z - 1) + 2)
    outs = pl.pallas_call(
        functools.partial(gather_kernel, rows_z, rows_y),
        out_shape=shapes,
        in_specs=[pl.BlockSpec(memory_space=pl.ANY)] * 4,
        out_specs=[pl.BlockSpec(memory_space=pl.ANY)] * 10,
        scratch_shapes=[
            pltpu.SemaphoreType.DMA((copies,)),
            pltpu.SemaphoreType.DMA((copies,)),
            pltpu.SemaphoreType.DMA((14,)),
        ],
        compiler_params=pltpu.CompilerParams(
            collective_id=0, has_side_effects=True, vmem_limit_bytes=60 * MIB
        ),
        cost_estimate=pl.CostEstimate(flops=0, bytes_accessed=400_000_000, transcendentals=0),
    )(attend_in, attend_out, expand_weights, reduce_weights)
    return [o.reshape(-1, o.shape[-1]) for o in outs]


def whole_weights(attend_in, attend_out, expand_weights, reduce_weights):
    tensors = (attend_in, attend_out, expand_weights, reduce_weights)
    shards = lax.axis_size("dp")
    if shards != 8 or lax.axis_size("vocab") != 4:
        whole = [lax.all_gather(tensor, "dp", axis=1, tiled=True) for tensor in tensors]
        return (whole[0], whole[1], whole[2][:, None], whole[3][:, None])
    flat = gather_weights(*tensors)
    return flat[:3], flat[3:6], [[w] for w in flat[6:8]], [[w] for w in flat[8:]]


def vocab_exchange_kernel(tile, h_ref, target_ref, table_ref, grad_ref, stat_ref, *scratch):
    tail, held, logits_a, logits_b, powers_a, powers_b, scale_a, scale_b = scratch[:8]
    maxima_ref, total_ref, parcel, arrived, send_sem, recv_sem = scratch[8:]
    rows, width = h_ref.shape
    valid = table_ref.shape[0]
    tiles = (valid + tile - 1) // tile
    padded = tiles * tile
    v = lax.axis_index("vocab")
    x, core = v // 2, lax.rem(v, 2)
    twin, across, diagonal = x * 2 + 1 - core, (1 - x) * 2 + core, (1 - x) * 2 + 1 - core

    barrier = pltpu.get_barrier_semaphore()
    for peer in (twin, across, diagonal):
        pl.semaphore_signal(
            barrier, inc=1, device_id={"vocab": peer}, device_id_type=pl.DeviceIdType.MESH
        )
    pl.semaphore_wait(barrier, 3)

    def remote(source, target, index, peer):
        return pltpu.make_async_remote_copy(
            src_ref=source,
            dst_ref=target,
            send_sem=send_sem.at[index],
            recv_sem=recv_sem.at[index],
            device_id={"vocab": peer},
            device_id_type=pl.DeviceIdType.MESH,
        )

    to_twin = remote(h_ref, held.at[0], 0, twin)
    to_across = remote(h_ref, held.at[1], 1, across)
    passed_on = remote(held.at[1], held.at[2], 2, twin)
    results = [
        remote(parcel.at[k], arrived.at[k], 3 + k, peer)
        for k, peer in enumerate((twin, across, diagonal))
    ]
    to_twin.start()
    to_across.start()
    held[3] = h_ref[...]

    short = padded - valid
    if short:
        tail[: tile - short, :] = table_ref[padded - tile :, :]
        tail[tile - short :, :] = jnp.zeros((short, width), BF16)
    to_twin.wait_recv()

    logits_of, powers_of, scale_of = (logits_a, logits_b), (powers_a, powers_b), (scale_a, scale_b)
    column = lax.broadcasted_iota(jnp.int32, (rows, tile), 1)
    lane = lax.broadcasted_iota(jnp.int32, (rows, LANES), 1)

    def turn(k, _):
        @pl.when(k == 1)
        def _():
            to_across.wait_recv()
            passed_on.start()

        @pl.when(k == 2)
        def _():
            passed_on.wait_recv()

        owner = jnp.where(k == 0, twin, jnp.where(k == 1, across, jnp.where(k == 2, diagonal, v)))

        def part(at):
            if short and at == tiles - 1:
                return tail[...]
            return table_ref[at * tile : (at + 1) * tile, :]

        def scores(at):
            logits_of[at % 2][...] = dot_rows(held[k], part(at))

        def soften(at):
            logits = logits_of[at % 2][...]
            if at == tiles - 1 and padded > valid:
                logits = jnp.where(column < valid - at * tile, logits, MASKED)
            highest = jnp.maximum(maxima_ref[...], jnp.max(logits, -1, keepdims=True))
            powers = jnp.exp(logits - highest)
            scale = jnp.exp(maxima_ref[...] - highest)
            maxima_ref[...] = highest
            total_ref[...] = total_ref[...] * scale + jnp.sum(powers, -1, keepdims=True)
            scale_of[at % 2][...] = scale
            powers_of[at % 2][...] = jnp.where(
                column == target_ref[owner] - at * tile, 0.0, powers
            ).astype(BF16)

        def gather(at):
            term = dot(powers_of[at % 2][...], part(at))
            grad_ref[...] = grad_ref[...] * scale_of[at % 2][...] + term

        maxima_ref[...] = jnp.full((rows, 1), MASKED, F32)
        total_ref[...] = jnp.zeros((rows, 1), F32)
        grad_ref[...] = jnp.zeros_like(grad_ref)
        for at in range(tiles + 2):
            if at < tiles:
                scores(at)
            if 0 <= at - 1 < tiles:
                soften(at - 1)
            if at >= 2:
                gather(at - 2)

        @pl.when(k < 3)
        def _():
            parcel[k, :, :width] = grad_ref[...].astype(BF16)
            tail = jnp.zeros((rows, LANES), F32)
            for first, value in ((0, maxima_ref[...]), (3, total_ref[...])):
                for step in range(3):
                    piece = value.astype(BF16).astype(F32)
                    tail = jnp.where(lane == first + step, piece, tail)
                    value = value - piece
            parcel[k, :, width:] = tail.astype(BF16)

        for index, result in enumerate(results):
            pl.when(k == index)(result.start)
        return 0

    lax.fori_loop(0, 4, turn, 0)
    for result in results:
        result.wait_recv()
    tails = [arrived[k, :, width:].astype(F32) for k in range(3)]
    highs = [t[:, 0:1] + t[:, 1:2] + t[:, 2:3] for t in tails] + [maxima_ref[...]]
    totals = [t[:, 3:4] + t[:, 4:5] + t[:, 5:6] for t in tails] + [total_ref[...]]
    highest = functools.reduce(jnp.maximum, highs)
    log_total = highest + jnp.log(sum(t * jnp.exp(m - highest) for m, t in zip(highs, totals)))
    summed = grad_ref[...] * jnp.exp(highs[3] - log_total)
    for k in range(3):
        summed = summed + arrived[k, :, :width].astype(F32) * jnp.exp(highs[k] - log_total)
    grad_ref[...] = summed
    stat_ref[...] = jnp.where(lane == 0, log_total, 0.0)
    for copy in [to_twin, to_across, passed_on, *results]:
        copy.wait_send()


def vocab_exchange(hidden, target_local, embedding):
    rows, width = hidden.shape
    valid = embedding.shape[0]
    tile = 2 * VOCAB_BLOCK
    padded = (valid + tile - 1) // tile * tile
    vmem = pl.BlockSpec(memory_space=pltpu.VMEM)
    return pl.pallas_call(
        functools.partial(vocab_exchange_kernel, tile),
        out_shape=[
            jax.ShapeDtypeStruct((rows, width), F32),
            jax.ShapeDtypeStruct((rows, LANES), F32),
        ],
        in_specs=[vmem, vmem, vmem],
        out_specs=[vmem, vmem],
        scratch_shapes=[
            pltpu.VMEM((tile, width), BF16),
            pltpu.VMEM((4, rows, width), BF16),
            pltpu.VMEM((rows, tile), F32),
            pltpu.VMEM((rows, tile), F32),
            pltpu.VMEM((rows, tile), BF16),
            pltpu.VMEM((rows, tile), BF16),
            pltpu.VMEM((rows, 1), F32),
            pltpu.VMEM((rows, 1), F32),
            pltpu.VMEM((rows, 1), F32),
            pltpu.VMEM((rows, 1), F32),
            pltpu.VMEM((3, rows, width + LANES), BF16),
            pltpu.VMEM((3, rows, width + LANES), BF16),
            pltpu.SemaphoreType.DMA((6,)),
            pltpu.SemaphoreType.DMA((6,)),
        ],
        compiler_params=pltpu.CompilerParams(
            collective_id=1, has_side_effects=True, vmem_limit_bytes=52 * MIB
        ),
        cost_estimate=pl.CostEstimate(
            flops=16 * rows * padded * width, bytes_accessed=2 * valid * width, transcendentals=0
        ),
    )(hidden, target_local.reshape(4, rows, 1), embedding)


def reduce_kernel(rows_dp, task_ref, table_ref, stat_ref, out_ref, stats_out, squares_out, *scratch):
    cast, crossed, swap, swapped, own, outgoing, pieces, result, results = scratch[:9]
    stats, squares, send_sem, recv_sem = scratch[9:]
    features = own.shape[1]
    at, v = lax.axis_index("dp"), lax.axis_index("vocab")
    x, core = v // 2, lax.rem(v, 2)
    twin, across = x * 2 + 1 - core, (1 - x) * 2 + core
    dp_peers = [lax.rem(at + k, rows_dp) for k in range(1, rows_dp)]
    vocab_peers = [lax.rem(v + k, 4) for k in range(1, 4)]

    barrier = pltpu.get_barrier_semaphore()
    for peer in [{"vocab": p} for p in vocab_peers] + [{"dp": p} for p in dp_peers]:
        pl.semaphore_signal(barrier, inc=1, device_id=peer, device_id_type=pl.DeviceIdType.MESH)
    pl.semaphore_wait(barrier, rows_dp + 2)

    def remote(source, target, send, recv, peer):
        return pltpu.make_async_remote_copy(
            src_ref=source,
            dst_ref=target,
            send_sem=send_sem.at[send],
            recv_sem=recv_sem.at[recv],
            device_id=peer,
            device_id_type=pl.DeviceIdType.MESH,
        )

    half = 2 * features
    there = pl.ds(pl.multiple_of((1 - x) * half, half), half)
    here = pl.ds(pl.multiple_of(x * half, half), half)
    stats[0] = stat_ref[...]
    cast[...] = table_ref[there, :].astype(BF16)
    over_x = remote(cast, crossed, 0, 0, {"vocab": across})
    stat_x = remote(stats.at[0], stats.at[1], 1, 1, {"vocab": across})
    over_x.start()
    stat_x.start()
    over_x.wait_recv()
    stat_x.wait_recv()

    stats[2] = stats[0] + stats[1]
    stat_core = remote(stats.at[2], stats.at[3], 2, 2, {"vocab": twin})
    stat_core.start()
    tasks = [[task_ref[m, s] for s in range(task_ref.shape[1])] for m in range(2)]
    other = jnp.where(x == 0, 1, 0)

    def by_task(part, t):
        start = pl.multiple_of(part * features, features)
        mine = table_ref[pl.ds(pl.multiple_of(x * half + part * features, features), features), :]
        theirs = crossed[pl.ds(start, features), :].astype(F32)
        total = jnp.zeros((features, LANES), F32)
        for s in range(task_ref.shape[1]):
            lanes = slice(s * LANES, (s + 1) * LANES)
            mine_task = jnp.where(x == 0, tasks[0][s], tasks[1][s])
            their_task = jnp.where(x == 0, tasks[1][s], tasks[0][s])
            total = total + jnp.where(mine_task == t, mine[:, lanes], 0.0)
            total = total + jnp.where(their_task == t, theirs[:, lanes], 0.0)
        return total

    for t in range(TASKS):
        swap[t] = by_task(1 - core, t).astype(BF16)
    over_core = remote(swap, swapped, 3, 3, {"vocab": twin})
    over_core.start()
    for t in range(TASKS):
        own[t] = by_task(core, t)
    over_core.wait_recv()
    stat_core.wait_recv()
    stats[4 + at] = stats[2] + stats[3]
    for t in range(TASKS):
        own[t] = own[t] + swapped[t].astype(F32)
        outgoing[t] = own[t].astype(BF16)

    base = 4
    spread, tallies = [], []
    for k, peer in enumerate(dp_peers):
        spread.append(
            remote(outgoing.at[peer], pieces.at[at], base + k, base + at, {"dp": peer})
        )
        tallies.append(
            remote(
                stats.at[4 + at],
                stats.at[4 + at],
                base + rows_dp + k,
                base + rows_dp + at,
                {"dp": peer},
            )
        )
    for copy in spread + tallies:
        copy.start()
    total = own[at]
    for peer in dp_peers:
        remote(outgoing.at[peer], pieces.at[peer], base, base + peer, {"dp": peer}).wait_recv()
        total = total + pieces[peer].astype(F32)
    result[...] = total.astype(BF16)
    results[at] = result[...]
    returns = []
    for k, peer in enumerate(dp_peers):
        returns.append(
            remote(
                result,
                results.at[at],
                base + 2 * rows_dp + k,
                base + 2 * rows_dp + at,
                {"dp": peer},
            )
        )
    for copy in returns:
        copy.start()
    for peer in dp_peers:
        remote(
            stats.at[4 + peer], stats.at[4 + peer], base, base + rows_dp + peer, {"dp": peer}
        ).wait_recv()
    tally = functools.reduce(jnp.add, [stats[4 + k] for k in range(rows_dp)])
    stats_out[...] = tally
    for peer in dp_peers:
        remote(result, results.at[peer], base, base + 2 * rows_dp + peer, {"dp": peer}).wait_recv()
    for t in range(TASKS):
        scale = 1.0 / (TASKS * jnp.maximum(tally[1:2, t : t + 1], 1.0))
        scaled = results[t].astype(F32) * scale
        out_ref[t] = scaled
        squares[v, t : t + 1, :] = jnp.sum(scaled * scaled, 0, keepdims=True)
    last = base + 3 * rows_dp
    shares = [
        remote(squares.at[v], squares.at[v], last + k, last + v, {"vocab": peer})
        for k, peer in enumerate(vocab_peers)
    ]
    for copy in shares:
        copy.start()
    for peer in vocab_peers:
        remote(squares.at[peer], squares.at[peer], last, last + peer, {"vocab": peer}).wait_recv()
    squares_out[...] = squares[0] + squares[1] + squares[2] + squares[3]
    for copy in [over_x, stat_x, stat_core, over_core, *spread, *tallies, *returns, *shares]:
        copy.wait_send()


def reduce_over_devices(task_list, table, stats):
    rows_dp = lax.axis_size("dp")
    features = table.shape[0] // 4
    vmem = pl.BlockSpec(memory_space=pltpu.VMEM)
    copies = 4 + 3 * rows_dp + 4
    return pl.pallas_call(
        functools.partial(reduce_kernel, rows_dp),
        out_shape=[
            jax.ShapeDtypeStruct((TASKS, features, LANES), F32),
            jax.ShapeDtypeStruct((8, LANES), F32),
            jax.ShapeDtypeStruct((8, LANES), F32),
        ],
        in_specs=[pl.BlockSpec(memory_space=pltpu.SMEM), vmem, vmem],
        out_specs=[vmem] * 3,
        scratch_shapes=[
            pltpu.VMEM((2 * features, table.shape[1]), BF16),
            pltpu.VMEM((2 * features, table.shape[1]), BF16),
            pltpu.VMEM((TASKS, features, LANES), BF16),
            pltpu.VMEM((TASKS, features, LANES), BF16),
            pltpu.VMEM((TASKS, features, LANES), F32),
            pltpu.VMEM((TASKS, features, LANES), BF16),
            pltpu.VMEM((rows_dp, features, LANES), BF16),
            pltpu.VMEM((features, LANES), BF16),
            pltpu.VMEM((rows_dp, features, LANES), BF16),
            pltpu.VMEM((4 + rows_dp, 8, LANES), F32),
            pltpu.VMEM((4, 8, LANES), F32),
            pltpu.SemaphoreType.DMA((copies,)),
            pltpu.SemaphoreType.DMA((copies,)),
        ],
        compiler_params=pltpu.CompilerParams(
            collective_id=2, has_side_effects=True, vmem_limit_bytes=24 * MIB
        ),
    )(task_list, table, stats)


def on_device(
    tokens,
    targets,
    loss_mask,
    seg_lengths,
    task_ids,
    embedding,
    attend_in,
    attend_out,
    expand_weights,
    reduce_weights,
    norm_gains,
    prompt,
    first_moment,
    row_moment,
    column_moment,
):
    shards = lax.axis_size("vocab")
    micros, span = tokens.shape[0], tokens.shape[-1]
    length = span * shards
    group = shards // micros
    own = length // group
    me = lax.axis_index("vocab")
    micro, place = me // group, me % group
    shard_rows, width = embedding.shape
    share = prompt.shape[-1]

    def around(array, shift):
        pairs = [
            (m * group + r, m * group + (r + shift) % group)
            for m in range(micros)
            for r in range(group)
        ]
        return lax.ppermute(array, "vocab", pairs)

    ids = lax.all_gather(jnp.stack([tokens[:, 0], targets[:, 0], loss_mask[:, 0]]), "vocab")
    ids = jnp.transpose(ids, (1, 2, 0, 3)).reshape(3, micros, length)
    enc_ids = ids[0].reshape(shards, own)

    segments = seg_lengths.shape[-1]
    row_lengths = seg_lengths[:, 0]
    if group == 2 and segments == 3 and 2 * span + 2 * P_SIZE <= length - span:
        half = (length - segments * P_SIZE) // group
        heads = (half + LANES - 1) // LANES * LANES
        extra = (half + 2 * P_SIZE - own + HALO - 1) // HALO * HALO
        starts = [0, own - extra]
        near = [P_SIZE, half + 2 * P_SIZE]
        far = [2 * P_SIZE, half + 3 * P_SIZE]
        turns = [row_lengths[:, 0] - P_SIZE, length - row_lengths[:, 2] - near[1]]
    else:
        half = heads = own
        extra = 0
        starts = near = far = [p * own for p in range(group)]
        turns = [row_lengths[:, 0]] * group
    held = own + extra
    entries = jnp.arange(heads, dtype=jnp.int32)

    def of_rows(values, m, p):
        values = jnp.pad(values, (0, heads + far[p]))
        return jnp.where(
            entries < turns[p][m],
            values[near[p] : near[p] + heads],
            values[far[p] : far[p] + heads],
        )

    everyone = [(m, p) for m in range(micros) for p in range(group)]
    dec_ids = jnp.stack(
        [
            jnp.concatenate(
                [
                    jnp.zeros((HALO - 1,), jnp.int32),
                    jnp.pad(ids[1, m], (1, 0))[starts[p] : starts[p] + 1 + held],
                ]
            )
            for m, p in everyone
        ]
    )
    head_targets = jnp.stack([of_rows(ids[1, m], m, p) for m, p in everyone])
    first_row = me * shard_rows

    def lookup(wanted):
        local = wanted.reshape(-1) - first_row
        inside = (local >= 0) & (local < shard_rows)
        picked = jnp.take(embedding, jnp.clip(local, 0, shard_rows - 1), axis=0)
        return jnp.where(inside[:, None], picked, 0)

    enc_rows = lax.psum_scatter(lookup(enc_ids), "vocab", scatter_dimension=0, tiled=True)
    dec_rows = lax.psum_scatter(lookup(dec_ids), "vocab", scatter_dimension=0, tiled=True)

    prompt_all = lax.all_gather(prompt.astype(BF16), "vocab", axis=2, tiled=True)
    prompt_flat = prompt_all.reshape(-1, width)
    attend_in, attend_out, expand_weights, reduce_weights = whole_weights(
        attend_in, attend_out, expand_weights, reduce_weights
    )

    lengths = lax.dynamic_index_in_dim(seg_lengths[:, 0], micro, 0, False)
    tasks = lax.dynamic_index_in_dim(task_ids[:, 0], micro, 0, False)
    steps = jnp.arange(own, dtype=jnp.int32)
    positions = place * own + steps
    segment, in_segment, task_of = layout(lengths, tasks, positions)
    key_positions = jnp.concatenate(
        [((place - k + group) % group) * own + steps for k in range(group)]
    )
    key_segment = layout(lengths, tasks, key_positions)[0]
    rows_info = jnp.stack([segment, positions], 1)
    keys_info = jnp.stack([key_segment, key_positions], 1)
    turn = jnp.stack(turns)[place, micro]
    near_row = jnp.asarray(near, jnp.int32)[place]
    far_row = jnp.asarray(far, jnp.int32)[place]
    first_held = jnp.asarray(starts, jnp.int32)[place]
    head_positions = jnp.where(entries < turn, near_row, far_row) + entries
    head_positions = jnp.minimum(head_positions, length - 1)
    head_segment, head_in_segment, head_task = layout(lengths, tasks, head_positions)
    heads_info = jnp.stack([head_segment, head_positions], 1)
    head_mask_row = jnp.stack([of_rows(ids[2, m], m, p) for m, p in everyone])[me]
    counted = (head_mask_row * ((head_in_segment >= P_SIZE) & (entries < half))).astype(F32)

    def head_rows(values):
        values = jnp.pad(values, ((0, heads), (0, 0)))
        shape = (heads, values.shape[1])
        return jnp.where(
            (entries < turn)[:, None],
            lax.dynamic_slice(values, (near_row - first_held, 0), shape),
            lax.dynamic_slice(values, (far_row - first_held, 0), shape),
        )

    def key_parts(source, weight):
        pair = dot(source, weight).astype(BF16)
        return [pair] + [around(pair, k) for k in range(1, group)]

    def project(source, weight):
        return dot(source, weight).astype(BF16)

    is_prompt = in_segment < P_SIZE
    slot = task_of * P_SIZE + jnp.minimum(in_segment, P_SIZE - 1)
    enc_input = jnp.where(
        is_prompt[:, None], jnp.take(prompt_flat, slot, axis=0), enc_rows
    ).astype(F32)
    held_positions = first_held + jnp.arange(held, dtype=jnp.int32)
    begun = layout(lengths, tasks, held_positions)[1] >= 1
    dec_held = jnp.where(begun[:, None], dec_rows[HALO - 1 : HALO - 1 + held], dec_rows[:1])
    dec_keys = lax.dynamic_slice(dec_held, (place * own - first_held, 0), (own, width)).astype(F32)
    dec_input = head_rows(dec_held).astype(F32)
    target_rows = head_rows(dec_rows[HALO:]).astype(F32)

    normed_in, inverse_in = normed(enc_input, norm_gains[0])
    normed_low = normed_in.astype(BF16)
    enc_pairs = key_parts(normed_low, attend_in[0][:, width:])
    enc_queries = project(normed_low, attend_in[0][:, :width])
    normed_keys = normed(dec_keys, norm_gains[3])[0].astype(BF16)
    dec_pairs = key_parts(normed_keys, attend_in[1][:, width:])
    normed_dec = normed(dec_input, norm_gains[3])[0].astype(BF16)
    dec_queries = project(normed_dec, attend_in[1][:, :width])
    enc_mid, enc_mixed, enc_logs = attend(
        enc_queries, enc_pairs, enc_input, attend_out[0], rows_info, keys_info, False
    )
    enc_last, enc_kept = feed(enc_mid, norm_gains[1], expand_weights[0], reduce_weights[0])
    encoded, inverse_last = normed(enc_last, norm_gains[2])
    cross_pairs = key_parts(encoded.astype(BF16), attend_in[2][:, width:])

    dec_first = attend(
        dec_queries, dec_pairs, dec_input, attend_out[1], heads_info, keys_info, True
    )[0]
    cross_queries = project(normed(dec_first, norm_gains[4])[0].astype(BF16), attend_in[2][:, :width])
    dec_second, cross_mixed, cross_logs = attend(
        cross_queries, cross_pairs, dec_first, attend_out[2], heads_info, keys_info, False
    )
    dec_last, dec_kept = feed(dec_second, norm_gains[5], expand_weights[1], reduce_weights[1])
    output_norm, inverse_out = normed(dec_last, norm_gains[6])
    hidden = (output_norm * width ** (-0.5)).astype(BF16)

    target_local = head_targets.reshape(-1, 1) - first_row
    if shards == 4:
        summed, stats = vocab_exchange(hidden, target_local, embedding)
        own_total = stats[:, 0]
    else:
        all_hidden = lax.all_gather(hidden, "vocab", axis=0, tiled=True)
        part, stats = vocab_pass(all_hidden, target_local, embedding, heads)
        gathered = lax.all_gather(stats[:, :2].T, "vocab")
        maxima = jnp.max(gathered[:, 0], 0)
        log_total = maxima + jnp.log(
            jnp.sum(gathered[:, 1] * jnp.exp(gathered[:, 0] - maxima), 0)
        )
        scaled = part * jnp.exp(stats[:, 0] - log_total)[:, None]
        summed = lax.psum_scatter(scaled, "vocab", scatter_dimension=0, tiled=True)
        own_total = lax.dynamic_slice(log_total, (me * heads,), (heads,))
    target_logit = jnp.sum(hidden.astype(F32) * target_rows, -1)
    token_loss = own_total - target_logit
    target_coefficient = (jnp.exp(target_logit - own_total) - 1.0).astype(BF16).astype(F32)
    hidden_grad = counted[:, None] * (summed + target_coefficient[:, None] * target_rows)

    def keys_back(pairs, weight):
        total = pairs[0]
        for k in range(1, group):
            total = total + around(pairs[k], group - k)
        high = total.astype(BF16)
        rest = (total - high.astype(F32)).astype(BF16)
        return dot_rows(high, weight) + dot_rows(rest, weight)

    dec_grad = normed_back(
        dec_last, norm_gains[6], inverse_out, hidden_grad * width ** (-0.5)
    )
    dec_grad = feed_back(
        dec_grad, dec_second, norm_gains[5], dec_kept, expand_weights[1], reduce_weights[1]
    )
    back = attend_back(
        cross_queries,
        cross_pairs,
        dec_grad,
        attend_out[2],
        cross_mixed,
        cross_logs,
        heads_info,
        keys_info,
        False,
    )
    enc_grad = normed_back(
        enc_last, norm_gains[2], inverse_last, keys_back(back, attend_in[2][:, width:])
    )
    enc_grad = feed_back(
        enc_grad, enc_mid, norm_gains[1], enc_kept, expand_weights[0], reduce_weights[0]
    )
    *back, back_queries = attend_back(
        enc_queries,
        enc_pairs,
        enc_grad,
        attend_out[0],
        enc_mixed,
        enc_logs,
        rows_info,
        keys_info,
        True,
    )
    source_grad = keys_back(back, attend_in[0][:, width:]) + lax.dot_general(
        back_queries,
        attend_in[0][:, :width],
        (((0,), (1,)), ((), ())),
        preferred_element_type=F32,
    )
    enc_grad = enc_grad + normed_back(enc_input, norm_gains[0], inverse_in, source_grad)

    place_of = segment * LANES + in_segment
    chosen = (
        (place_of[:, None] == jnp.arange(segments * LANES, dtype=jnp.int32)) & is_prompt[:, None]
    ).astype(BF16)
    high = enc_grad.astype(BF16)
    rest = (enc_grad - high.astype(F32)).astype(BF16)
    table = dot_columns(high, chosen) + dot_columns(rest, chosen)
    tallies = jnp.stack([per_task(head_task, counted * token_loss), per_task(head_task, counted)])
    stats = jnp.zeros((8, LANES), F32).at[:2, :TASKS].set(tallies)
    if shards == 4 and lax.axis_size("dp") == TASKS:
        gradient, stats, squares = reduce_over_devices(task_ids[:, 0], table, stats)
        full_grad = jnp.swapaxes(gradient[:, :, :P_SIZE], 1, 2)
        row_squares = squares[:, :P_SIZE]
        task_scale = 1.0 / (TASKS * jnp.maximum(stats[1, :TASKS], 1.0))
    else:
        hits = (tasks[:, None] == jnp.arange(TASKS, dtype=jnp.int32)).astype(F32)
        by_task = jnp.einsum(
            "fsp,st->tpf",
            table.reshape(width, segments, LANES)[:, :, :P_SIZE],
            hits,
            precision=lax.Precision.HIGHEST,
        )
        stats = lax.psum(stats, ("dp", "vocab"))
        gradient = lax.psum_scatter(by_task, "vocab", scatter_dimension=2, tiled=True)
        task_scale = 1.0 / (TASKS * jnp.maximum(stats[1, :TASKS], 1.0))
        full_grad = lax.psum(gradient, "dp") * task_scale[:, None, None]
        row_squares = jnp.sum(lax.all_gather(jnp.sum(full_grad * full_grad, -1), "vocab"), 0)
    loss_mean = jnp.sum(stats[0, :TASKS] * task_scale)
    grad_norm = jnp.sqrt(jnp.sum(row_squares))
    clip = CLIP_NORM / jnp.maximum(grad_norm, CLIP_NORM)
    prompt_grad = full_grad * clip
    row_second = BETA_TWO * row_moment + (1.0 - BETA_TWO) * (
        row_squares * clip * clip / width + SQUARE_EPS
    )
    column_second = BETA_TWO * column_moment + (1.0 - BETA_TWO) * (
        jnp.mean(prompt_grad * prompt_grad, 1) + SQUARE_EPS
    )
    new_moment = BETA_ONE * first_moment + (1.0 - BETA_ONE) * prompt_grad
    estimate = (
        row_second[:, :, None] * column_second[:, None, :] / jnp.mean(row_second, -1)[:, None, None]
    )
    update = new_moment / (1.0 - BETA_ONE**STEP) / jnp.sqrt(estimate / (1.0 - BETA_TWO**STEP))
    new_prompt = prompt - LEARN_RATE * (update + WEIGHT_DECAY * prompt)
    return (loss_mean, grad_norm, prompt_grad, new_moment, row_second, column_second, new_prompt)


def solution(mesh):
    placed = (
        P(None, "dp", "vocab"),
        P(None, "dp", "vocab"),
        P(None, "dp", "vocab"),
        P(None, "dp", None),
        P(None, "dp", None),
        P("vocab", None),
        P(None, "dp", None),
        P(None, "dp", None),
        P(None, "dp", None),
        P(None, "dp", None),
        P(),
        P(None, None, "vocab"),
        P(None, None, "vocab"),
        P(),
        P(None, "vocab"),
    )
    return jax.shard_map(
        on_device,
        mesh=mesh,
        in_specs=placed,
        out_specs=(
            P(),
            P(),
            P(None, None, "vocab"),
            P(None, None, "vocab"),
            P(),
            P(None, "vocab"),
            P(None, None, "vocab"),
        ),
        check_vma=False,
    )
```

```python
import functools

import jax
import jax.numpy as jnp
from jax import lax
from jax.experimental import pallas as pl
from jax.experimental.pallas import tpu as pltpu
from jax.sharding import PartitionSpec as P

DH = 64
P_SIZE = 100
TASKS = 8
STEP = 5
HALO = 16
LANES = 128
SEGS = 3
VOCAB_BLOCK = 1024
MIB = 1024 * 1024

NORM_EPS = 1e-06
CLIP_NORM = 2e-05
BETA_ONE = 0.9
BETA_TWO = 0.999
LEARN_RATE = 1.0
WEIGHT_DECAY = 1e-05
SQUARE_EPS = 1e-30
MASKED = -1e30

F32 = jnp.float32
BF16 = jnp.bfloat16


def dot(left, right):
    return jnp.dot(left, right, preferred_element_type=F32)


def dot_rows(left, right):
    return lax.dot_general(left, right, (((1,), (1,)), ((), ())), preferred_element_type=F32)


def dot_columns(left, right):
    return lax.dot_general(left, right, (((0,), (0,)), ((), ())), preferred_element_type=F32)


def normed(values, gain):
    inverse = lax.rsqrt(jnp.mean(values * values, -1, keepdims=True) + NORM_EPS)
    return (values * inverse * gain, inverse)


def normed_back(values, gain, inverse, gradient):
    unit_rows = values * inverse
    scaled = gradient * gain
    return inverse * (scaled - unit_rows * jnp.mean(scaled * unit_rows, -1, keepdims=True))


def smooth(values):
    return jax.nn.gelu(values, approximate=True)


def layout(lengths, task_list, positions):
    seg_ends = jnp.cumsum(lengths)
    seg_starts = seg_ends - lengths
    segment = jnp.sum((positions[:, None] >= seg_ends[None, :]).astype(jnp.int32), -1)
    member = segment[:, None] == jnp.arange(lengths.shape[0], dtype=jnp.int32)[None, :]
    in_segment = positions - jnp.sum(jnp.where(member, seg_starts[None, :], 0), -1)
    task_of = jnp.sum(jnp.where(member, task_list[None, :], 0), -1)
    return (segment, in_segment, task_of)


def per_task(task_of, amounts):
    hits = task_of[:, None] == jnp.arange(TASKS, dtype=jnp.int32)
    return jnp.sum(jnp.where(hits, amounts[:, None], 0.0), 0)


def pair_lanes(pair, first=0):
    return pl.ds(pl.multiple_of(first + pair * LANES, LANES), LANES)


def head_mask(shape, head, axis=1):
    return (lax.broadcasted_iota(jnp.int32, shape, axis) < DH) == (head == 0)


def segment_columns(segment, is_key, shape):
    column = lax.rem(lax.broadcasted_iota(jnp.int32, shape, 1), DH)
    if is_key:
        return jnp.where((column < SEGS) & (column != segment), MASKED, 0.0).astype(BF16)
    return jnp.where(column == segment, 1.0, 0.0).astype(BF16)


def head_part(values, rest, head):
    return jnp.where(head_mask(values.shape, head), values, rest)


def over_heads(pairs, scores, soften, mix):
    scores(0, 0)
    scores(0, 1)
    soften(0, 0)

    def step(pair, _):
        scores(pair + 1, 0)
        soften(pair, 1)
        mix(pair, 0)
        scores(pair + 1, 1)
        soften(pair + 1, 0)
        mix(pair, 1)
        return 0

    lax.fori_loop(0, pairs - 1, step, 0)
    soften(pairs - 1, 1)
    mix(pairs - 1, 0)
    mix(pairs - 1, 1)


def attend_kernel(parts, causal, *refs):
    q_ref, pair_refs = refs[0], refs[1 : 1 + parts]
    residual_ref, weight_ref, q_info, k_info, k_rows, out_ref, mixed_ref, log_ref = refs[
        1 + parts : 9 + parts
    ]
    bias_ref, q_mark, k_mark, low_ref, scores_a, scores_b, powers_a, powers_b = refs[9 + parts :]
    width = q_ref.shape[1]
    own = pair_refs[0].shape[0]
    scores_of, powers_of = (scores_a, scores_b), (powers_a, powers_b)
    rows = [slice(k * own, (k + 1) * own) for k in range(parts)]
    q_mark[...] = segment_columns(q_info[:, 0:1], False, q_mark.shape)
    k_mark[...] = segment_columns(k_info[:, 0:1], True, k_mark.shape)
    if causal:
        bias_ref[...] = jnp.where(q_info[:, 1:2] >= k_rows[...], 0.0, MASKED)
    log_ref[...] = jnp.zeros_like(log_ref)
    lane = lax.broadcasted_iota(jnp.int32, log_ref.shape, 1)

    def scores(pair, head):
        query = q_ref[:, pair_lanes(pair)] * jnp.asarray(DH ** (-0.5), BF16)
        query = head_part(query, q_mark[...], head)
        for k in range(parts):
            keys = head_part(pair_refs[k][:, pair_lanes(pair)], k_mark[rows[k], :], head)
            values = dot_rows(query, keys)
            if causal:
                values = values + bias_ref[:, rows[k]]
            scores_of[head][:, rows[k]] = values

    def soften(pair, head):
        values = scores_of[head][...]
        highest = jnp.max(values, -1, keepdims=True)
        powers_of[head][...] = jnp.exp(values - highest).astype(BF16)
        log_ref[...] += jnp.where(lane == 2 * pair + head, highest, 0.0)

    def mix(pair, head):
        value = None
        for k in range(parts):
            values = pair_refs[k][:, pair_lanes(pair, width)]
            values = head_part(values, jnp.ones_like(values), head)
            term = dot(powers_of[head][:, rows[k]], values)
            value = term if value is None else value + term
        total = value[:, LANES - 1 :] if head == 0 else value[:, :1]
        value = value / total
        log_ref[...] += jnp.where(lane == 2 * pair + head, jnp.log(total), 0.0)
        lanes = pair_lanes(pair)
        if head:
            value = jnp.where(head_mask(value.shape, 0), mixed_ref[:, lanes], value)
        mixed_ref[:, lanes] = value
        if head:
            low_ref[:, lanes] = value.astype(BF16)

    over_heads(width // LANES, scores, soften, mix)
    out_ref[...] = residual_ref[...] + dot(low_ref[...], weight_ref[...])


def attend(queries, pairs, residual, weight, q_info, k_info, causal):
    own, width = queries.shape
    parts, length = len(pairs), k_info.shape[0]
    vmem = pl.BlockSpec(memory_space=pltpu.VMEM)
    return pl.pallas_call(
        functools.partial(attend_kernel, parts, causal),
        out_shape=[
            jax.ShapeDtypeStruct((own, width), F32),
            jax.ShapeDtypeStruct((own, width), F32),
            jax.ShapeDtypeStruct((own, LANES), F32),
        ],
        in_specs=[vmem] * (parts + 6),
        out_specs=[vmem] * 3,
        scratch_shapes=[
            pltpu.VMEM((own, length), F32),
            pltpu.VMEM((own, LANES), BF16),
            pltpu.VMEM((length, LANES), BF16),
            pltpu.VMEM((own, width), BF16),
            pltpu.VMEM((own, length), F32),
            pltpu.VMEM((own, length), F32),
            pltpu.VMEM((own, length), BF16),
            pltpu.VMEM((own, length), BF16),
        ],
        compiler_params=pltpu.CompilerParams(vmem_limit_bytes=26 * MIB),
        cost_estimate=pl.CostEstimate(
            flops=10 * own * length * width, bytes_accessed=6 * own * width, transcendentals=0
        ),
    )(queries, *pairs, residual, weight, q_info, k_info, k_info[:, 1:].T)


def attend_back_kernel(parts, want_queries, *refs):
    q_ref, pair_refs = refs[0], refs[1 : 1 + parts]
    grad_ref, weight_ref, mixed_ref, log_ref, q_info, k_info = refs[1 + parts : 7 + parts]
    rest = refs[7 + parts :]
    out_refs = rest[:parts]
    dq_ref = rest[parts] if want_queries else None
    q_mark, k_mark, low_ref, delta_ref, *rest = rest[parts + want_queries :]
    scores_of, grads_of, weights_of, steps_of = rest[0:2], rest[2:4], rest[4:6], rest[6:8]
    width = q_ref.shape[1]
    own = pair_refs[0].shape[0]
    rows = [slice(k * own, (k + 1) * own) for k in range(parts)]
    scale = jnp.asarray(DH ** (-0.5), BF16)
    q_mark[...] = segment_columns(q_info[:, 0:1], False, q_mark.shape)
    k_mark[...] = segment_columns(k_info[:, 0:1], True, k_mark.shape)
    low_ref[...] = dot_rows(grad_ref[...].astype(BF16), weight_ref[...]).astype(BF16)
    product = low_ref[...].astype(F32) * mixed_ref[...]
    high = product.astype(BF16)
    shape = (2 * 8, width)
    belongs = lax.broadcasted_iota(jnp.int32, shape, 1) // DH == lax.broadcasted_iota(
        jnp.int32, shape, 0
    )
    belongs = jnp.where(belongs, 1.0, 0.0).astype(BF16)
    delta_ref[...] = dot_rows(belongs, high) + dot_rows(
        belongs, (product - high.astype(F32)).astype(BF16)
    )

    def scores(pair, head):
        query = head_part(q_ref[:, pair_lanes(pair)] * scale, q_mark[...], head)
        grad = low_ref[:, pair_lanes(pair)]
        grad = head_part(grad, jnp.zeros_like(grad), head)
        for k in range(parts):
            keys = head_part(pair_refs[k][:, pair_lanes(pair)], k_mark[rows[k], :], head)
            scores_of[head][rows[k], :] = dot_rows(keys, query)
            grads_of[head][rows[k], :] = dot_rows(pair_refs[k][:, pair_lanes(pair, width)], grad)

    def soften(pair, head):
        at = pl.ds(2 * pair + head, 1)
        weights = jnp.exp(scores_of[head][...] - log_ref[at, :])
        weights_of[head][...] = weights.astype(BF16)
        steps_of[head][...] = (weights * (grads_of[head][...] - delta_ref[at, :])).astype(BF16)

    def mix(pair, head):
        keys, values = pair_lanes(pair), pair_lanes(pair, width)
        query, grad = q_ref[:, keys] * scale, low_ref[:, keys]
        query = head_part(query, jnp.zeros_like(query), head)
        grad = head_part(grad, jnp.zeros_like(grad), head)
        dq = None
        for k in range(parts):
            step = steps_of[head][rows[k], :]
            dk = dot(step, query)
            dv = dot(weights_of[head][rows[k], :], grad)
            out_refs[k][:, keys] = dk if head == 0 else out_refs[k][:, keys] + dk
            out_refs[k][:, values] = dv if head == 0 else out_refs[k][:, values] + dv
            if want_queries:
                term = dot_columns(pair_refs[k][:, keys], step)
                dq = term if dq is None else dq + term
        if want_queries:
            here = pl.ds(pl.multiple_of(pair * LANES, LANES), LANES)
            dq = (dq * DH ** (-0.5)).astype(BF16)
            if head:
                dq = jnp.where(head_mask(dq.shape, 0, 0), dq_ref[here, :], dq)
            dq_ref[here, :] = dq

    over_heads(width // LANES, scores, soften, mix)


def attend_back(queries, pairs, gradient, weight, mixed, logs, q_info, k_info, want_queries):
    own, width = queries.shape
    parts, length = len(pairs), k_info.shape[0]
    shapes = [jax.ShapeDtypeStruct(pair.shape, F32) for pair in pairs]
    if want_queries:
        shapes.append(jax.ShapeDtypeStruct((width, own), BF16))
    return pl.pallas_call(
        functools.partial(attend_back_kernel, parts, want_queries),
        out_shape=shapes,
        in_specs=[pl.BlockSpec(memory_space=pltpu.VMEM)] * (parts + 7),
        out_specs=[pl.BlockSpec(memory_space=pltpu.VMEM)] * len(shapes),
        scratch_shapes=[
            pltpu.VMEM((own, LANES), BF16),
            pltpu.VMEM((length, LANES), BF16),
            pltpu.VMEM((own, width), BF16),
            pltpu.VMEM((16, own), F32),
        ]
        + [pltpu.VMEM((length, own), F32)] * 4
        + [pltpu.VMEM((length, own), BF16)] * 4,
        compiler_params=pltpu.CompilerParams(vmem_limit_bytes=34 * MIB),
        cost_estimate=pl.CostEstimate(
            flops=20 * own * length * width, bytes_accessed=20 * own * width, transcendentals=0
        ),
    )(queries, *pairs, gradient, weight, mixed, logs.T[:16], q_info, k_info)


def feed(rows, gain, weights_one, weights_two):
    values, inverse = normed(rows, gain)
    source = values.astype(BF16)
    before = [dot(source, one) for one in weights_one]
    for pre, two in zip(before, weights_two):
        rows = rows + dot(smooth(pre).astype(BF16), two)
    return rows, (before, inverse)


def feed_back(gradient, rows, gain, kept, weights_one, weights_two):
    before, inverse = kept
    low = gradient.astype(BF16)
    total = 0.0
    for pre, one, two in zip(before, weights_one, weights_two):
        active_grad = dot_rows(low, two)
        step = jax.vjp(smooth, pre)[1](active_grad)[0].astype(BF16)
        total = total + dot_rows(step, one)
    return gradient + normed_back(rows, gain, inverse, total)


def vocab_kernel(tile, valid, h_ref, target_ref, table_hbm, grad_ref, stat_ref, table, sem):
    padded = table.shape[0]

    @pl.when(pl.program_id(0) == 0)
    def _():
        copy = pltpu.make_async_copy(table_hbm, table.at[pl.ds(0, valid), :], sem)
        copy.start()
        if padded > valid:
            table[valid:, :] = jnp.zeros((padded - valid, table.shape[1]), BF16)
        copy.wait()

    rows = h_ref.shape[0]
    hidden = h_ref[...]
    column = lax.broadcasted_iota(jnp.int32, (rows, tile), 1)
    target = target_ref[...]

    def block(at, carry, last):
        maxima, total = carry
        part = table[pl.ds(pl.multiple_of(at * tile, tile), tile), :]
        logits = dot_rows(hidden, part)
        if last and padded > valid:
            logits = jnp.where(column < valid - (padded - tile), logits, MASKED)
        highest = jnp.maximum(maxima, jnp.max(logits, -1, keepdims=True))
        powers = jnp.exp(logits - highest)
        scale = jnp.exp(maxima - highest)
        total = total * scale + jnp.sum(powers, -1, keepdims=True)
        powers = jnp.where(column == target - at * tile, 0.0, powers).astype(BF16)
        grad_ref[...] = grad_ref[...] * scale + dot(powers, part)
        return (highest, total)

    grad_ref[...] = jnp.zeros_like(grad_ref)
    blocks = padded // tile
    carry = (jnp.full((rows, 1), MASKED, F32), jnp.zeros((rows, 1), F32))
    carry = lax.fori_loop(0, blocks - 1, lambda at, c: block(at, c, False), carry)
    maxima, total = block(blocks - 1, carry, True)
    lane = lax.broadcasted_iota(jnp.int32, stat_ref.shape, 1)
    stat_ref[...] = jnp.where(lane == 0, maxima, total)


def vocab_pass(hidden, target_local, embedding, rows):
    count, width = hidden.shape
    valid = embedding.shape[0]
    tile = VOCAB_BLOCK
    padded = (valid + tile - 1) // tile * tile
    return pl.pallas_call(
        functools.partial(vocab_kernel, tile, valid),
        grid=(count // rows,),
        out_shape=[
            jax.ShapeDtypeStruct((count, width), F32),
            jax.ShapeDtypeStruct((count, LANES), F32),
        ],
        in_specs=[
            pl.BlockSpec((rows, width), lambda i: (i, 0)),
            pl.BlockSpec((rows, 1), lambda i: (i, 0)),
            pl.BlockSpec(memory_space=pl.ANY),
        ],
        out_specs=[
            pl.BlockSpec((rows, width), lambda i: (i, 0)),
            pl.BlockSpec((rows, LANES), lambda i: (i, 0)),
        ],
        scratch_shapes=[pltpu.VMEM((padded, width), BF16), pltpu.SemaphoreType.DMA],
        compiler_params=pltpu.CompilerParams(vmem_limit_bytes=56 * MIB),
        cost_estimate=pl.CostEstimate(
            flops=4 * count * padded * width, bytes_accessed=2 * valid * width, transcendentals=0
        ),
    )(hidden, target_local, embedding)


def gather_kernel(rows_z, rows_y, *refs):
    in_ref, out_ref, expand_ref, reduce_ref, wanted_ref, table_hbm = refs[:6]
    in_full, out_full, expand_full, reduce_full = refs[6:9], refs[9:12], refs[12:14], refs[14:16]
    found_ref, table_low, table, stage, far, near, sister, from_core, from_x, from_sister = refs[16:26]
    send_sem, recv_sem, local_sem, table_sem = refs[26:]
    at, v = lax.axis_index("dp"), lax.axis_index("vocab")
    z, y, x, core = at // rows_y, lax.rem(at, rows_y), v // 2, lax.rem(v, 2)
    top = rows_z - 1
    above = {"dp": jnp.minimum(z + 1, top) * rows_y + y, "vocab": v}
    below = {"dp": jnp.maximum(z - 1, 0) * rows_y + y, "vocab": v}
    beside = {"dp": z * rows_y + (1 - y), "vocab": v}
    other_x = (1 - x) * 2 + core
    across = {"dp": at, "vocab": other_x}
    twin = {"dp": at, "vocab": x * 2 + (1 - core)}

    barrier = pltpu.get_barrier_semaphore()

    def greet(peer):
        pl.semaphore_signal(barrier, inc=1, device_id=peer, device_id_type=pl.DeviceIdType.MESH)

    pl.when(z < top)(lambda: greet(above))
    pl.when(z > 0)(lambda: greet(below))
    greet(beside)
    greet(across)
    greet(twin)
    inner = jnp.logical_and(z > 0, z < top)
    pl.when(inner)(lambda: pl.semaphore_wait(barrier, 5))
    pl.when(jnp.logical_not(inner))(lambda: pl.semaphore_wait(barrier, 4))

    names, tallies = {}, [0, 0]

    def remote(name, source, target, peer):
        if name not in names:
            names[name] = tallies[0]
            tallies[0] += 1
        return pltpu.make_async_remote_copy(
            src_ref=source,
            dst_ref=target,
            send_sem=send_sem.at[names[name]],
            recv_sem=recv_sem.at[names[name]],
            device_id=peer,
            device_id_type=pl.DeviceIdType.MESH,
        )

    def local(source, target):
        copy = pltpu.make_async_copy(source, target, local_sem.at[tallies[1]])
        tallies[1] += 1
        copy.start()
        return copy

    def columns(ref, full, index, blocks):
        wide = ref.shape[2] // blocks
        here = lambda b: pl.ds(pl.multiple_of(b * wide, wide), wide)
        return (
            lambda b: ref.at[index, :, here(b)],
            lambda zs, ys, b: full.at[zs, ys, :, here(b)],
            lambda ys, b: full.at[:, ys, :, here(b)],
            blocks == 4,
        )

    def row_blocks(ref, full, index):
        count = ref.shape[1] // 4
        return (
            lambda b: ref.at[index, pl.ds(pl.multiple_of(b * count, count), count), :],
            lambda zs, ys, b: full.at[zs, ys, b],
            lambda ys, b: full.at[:, ys, b],
            True,
        )

    def attention(j):
        return [columns(in_ref, in_full[j], j, 2), columns(out_ref, out_full[j], j, 2)]

    def feed(j):
        return [columns(expand_ref, expand_full[j], j, 4), row_blocks(reduce_ref, reduce_full[j], j)]

    waves = [feed(0) + attention(0), feed(1) + attention(1) + attention(2)]
    units = [u for wave in waves for u in wave]
    starts = [0, len(waves[0]), len(units)]
    blocks = [v if u[3] else core for u in units]
    sides = (("up", -1), ("down", 1))

    def there(side, k):
        return z - k >= 0 if side == "up" else z + k <= top

    def further(side):
        return z < top if side == "up" else z > 0

    def begin(i):
        source, target, _, quarter = units[i]
        b = blocks[i]
        piece = target(z, y, b)
        pl.when(z < top)(lambda: remote((i, "up", 1), source(b), piece, above).start())
        pl.when(z > 0)(lambda: remote((i, "down", 1), source(b), piece, below).start())
        remote((i, "y", 0), source(b), piece, beside).start()
        copies = [local(source(b), piece)]
        if quarter:
            copies.append(local(source(other_x), target(z, y, other_x)))
        return copies

    def step(i, k):
        _, target, _, quarter = units[i]
        for side, sign in sides:

            @pl.when(there(side, k))
            def _():
                piece = target(z + sign * k, y, blocks[i])
                remote((i, side, k), piece, piece, above).wait_recv()
                if k < top:

                    @pl.when(further(side))
                    def _():
                        peer = above if side == "up" else below
                        remote((i, side, k + 1), piece, piece, peer).start()

                remote((i, side, k, "y"), piece, piece, beside).start()
                if quarter:
                    remote((i, side, k, "x"), piece, piece, across).start()

    def came(i, k):
        _, target, _, quarter = units[i]
        if k == 0:
            piece = target(z, 1 - y, blocks[i])
            remote((i, "y", 0), piece, piece, beside).wait_recv()
            if quarter:
                remote((i, "yx", 0), piece, piece, across).start()
            return
        for side, sign in sides:

            @pl.when(there(side, k))
            def _():
                piece = target(z + sign * k, 1 - y, blocks[i])
                remote((i, side, k, "y"), piece, piece, beside).wait_recv()
                if quarter:
                    remote((i, side, k, "yx"), piece, piece, across).start()

    def to_twin(i, column, b, tag):
        block = units[i][2](column, b)
        remote((i, "core", tag), block, block, twin).start()

    def spread(i):
        for copy in locals_[i]:
            copy.wait()
        to_twin(i, y, blocks[i], 0)

    def spread_beside(i):
        to_twin(i, 1 - y, blocks[i], 1)

    def x_came(i, tag):
        _, target, _, _ = units[i]
        if tag == "yx":
            piece = target(z, 1 - y, other_x)
            remote((i, "yx", 0), piece, piece, across).wait_recv()
        for k in range(1, rows_z):
            for side, sign in sides:

                @pl.when(there(side, k))
                def _():
                    piece = target(z + sign * k, y if tag == "x" else 1 - y, other_x)
                    remote((i, side, k, tag), piece, piece, across).wait_recv()

        to_twin(i, y if tag == "x" else 1 - y, other_x, 2 if tag == "x" else 3)

    valid, width = table_low.shape
    share = far.shape[0]
    table_copy = pltpu.make_async_copy(table_hbm, table_low, table_sem)
    table_copy.start()

    def widen(at, _):
        here = pl.ds(pl.multiple_of(at * 32, 32), 32)
        table[here, :] = table_low[here, :].astype(F32)
        return 0

    def prepare():
        table_copy.wait()
        table[valid:, :] = jnp.zeros((table.shape[0] - valid, width), F32)
        lax.fori_loop(0, valid // 32, widen, 0)

    def look_up(target, owner, part):
        count = stage.shape[0]

        def rows(at, _):
            for step in range(8):
                i = at * 8 + step
                row = wanted_ref[owner * share + part * count + i]
                stage[pl.ds(i, 1), :] = table[pl.ds(row, 1), :]
            return 0

        lax.fori_loop(0, count // 8, rows, 0)
        target[part * count : (part + 1) * count, :] = stage[...].astype(BF16)

    sums = {
        "far": remote("far", far, from_core, twin),
        "near": remote("near", near, from_x, across),
        "sister": remote("sister", sister, from_sister, twin),
    }

    def send_far():
        sums["far"].start()

    def send_near():
        sums["far"].wait_recv()
        near[...] = (near[...].astype(F32) + from_core[...].astype(F32)).astype(BF16)
        sums["near"].start()

    def send_sister():
        sums["sister"].start()

    def finish_rows():
        sums["sister"].wait_recv()
        sums["near"].wait_recv()
        total = found_ref[...].astype(F32) + from_sister[...].astype(F32)
        found_ref[...] = (total + from_x[...].astype(F32)).astype(BF16)

    jobs = [prepare]
    for target, owner, after in (
        (far, (1 - x) * 2 + 1 - core, send_far),
        (near, other_x, send_near),
        (sister, x * 2 + 1 - core, send_sister),
        (found_ref, v, None),
    ):
        for part in range(share // stage.shape[0]):
            jobs.append(functools.partial(look_up, target, owner, part))
        if after:
            jobs.append(after)
    jobs = jobs[::-1]

    def work(count):
        for _ in range(min(count, len(jobs))):
            jobs.pop()()

    first, second = range(starts[0], starts[1]), range(starts[1], starts[2])
    locals_ = {}

    def each(action, wave, *rest):
        for i in wave:
            action(i, *rest)

    for i in first:
        locals_[i] = begin(i)
    locals_[second[0]] = begin(second[0])
    work(2)
    each(step, first, 1)
    for i in second[1:]:
        locals_[i] = begin(i)
    work(3)
    each(came, first, 0)
    work(1)
    each(step, first, 2)
    work(2)
    each(came, first, 1)
    work(1)
    each(step, second, 1)
    work(2)
    each(step, first, 3)
    each(spread, first)
    work(2)
    each(came, first, 2)
    work(1)
    each(step, second, 2)
    work(1)
    each(came, second, 0)
    work(1)
    for i in first:
        came(i, 3)
        spread_beside(i)
    work(len(jobs))
    each(came, second, 1)
    each(step, second, 3)
    each(spread, second)
    for i in first:
        if units[i][3]:
            x_came(i, "x")
    each(came, second, 2)
    for i in first:
        if units[i][3]:
            x_came(i, "yx")
    for i in second:
        came(i, 3)
        spread_beside(i)
    for i in second:
        if units[i][3]:
            x_came(i, "x")
            x_came(i, "yx")
    finish_rows()
    for copy in sums.values():
        copy.wait_send()

    for i, (source, target, whole, quarter) in enumerate(units):
        b = blocks[i]
        for tag in range(4 if quarter else 2):
            block = whole(y, b)
            remote((i, "core", tag), block, block, twin).wait()
        piece = target(z, y, b)
        remote((i, "y", 0), piece, piece, beside).wait_send()
        if quarter:
            remote((i, "yx", 0), piece, piece, across).wait_send()
        for k in range(1, rows_z):
            for side, sign in sides:
                sent = there(side, k - 1) if k > 1 else True
                pl.when(jnp.logical_and(sent, further(side)))(
                    lambda: remote((i, side, k), piece, piece, above).wait_send()
                )

                @pl.when(there(side, k))
                def _():
                    remote((i, side, k, "y"), piece, piece, beside).wait_send()
                    if quarter:
                        remote((i, side, k, "x"), piece, piece, across).wait_send()
                        remote((i, side, k, "yx"), piece, piece, across).wait_send()


def gather_weights(attend_in, attend_out, expand_weights, reduce_weights, wanted, table):
    shards, rows_y = 8, 2
    rows_z = shards // rows_y
    rows = attend_in.shape[1]
    width = rows * shards
    tall = reduce_weights.shape[1]
    share = wanted.shape[0] // 4
    valid = table.shape[0]

    def full(*tail):
        return jax.ShapeDtypeStruct((rows_z, rows_y, *tail), BF16)

    shapes = (
        [full(rows, attend_in.shape[2])] * 3
        + [full(rows, attend_out.shape[2])] * 3
        + [full(rows, expand_weights.shape[2])] * 2
        + [full(4, tall // 4, width)] * 2
        + [jax.ShapeDtypeStruct((share, width), BF16)]
    )
    copies = 10 * (1 + 4 * (rows_z - 1) + 2) + 4 * (1 + 4 * (rows_z - 1) + 2) + 3
    anywhere = pl.BlockSpec(memory_space=pl.ANY)
    outs = pl.pallas_call(
        functools.partial(gather_kernel, rows_z, rows_y),
        out_shape=shapes,
        in_specs=[anywhere] * 4 + [pl.BlockSpec(memory_space=pltpu.SMEM), anywhere],
        out_specs=[anywhere] * 10 + [pl.BlockSpec(memory_space=pltpu.VMEM)],
        scratch_shapes=[
            pltpu.VMEM((valid, width), BF16),
            pltpu.VMEM((valid + 8, width), F32),
            pltpu.VMEM((share // 3, width), F32),
        ]
        + [pltpu.VMEM((share, width), BF16)] * 6
        + [
            pltpu.SemaphoreType.DMA((copies,)),
            pltpu.SemaphoreType.DMA((copies,)),
            pltpu.SemaphoreType.DMA((14,)),
            pltpu.SemaphoreType.DMA,
        ],
        compiler_params=pltpu.CompilerParams(
            collective_id=0, has_side_effects=True, vmem_limit_bytes=60 * MIB
        ),
        cost_estimate=pl.CostEstimate(flops=0, bytes_accessed=400_000_000, transcendentals=0),
    )(attend_in, attend_out, expand_weights, reduce_weights, wanted, table)
    return [o.reshape(-1, o.shape[-1]) for o in outs]


def vocab_exchange_kernel(tile, h_ref, target_ref, table_ref, grad_ref, stat_ref, *scratch):
    tail, held, logits_a, logits_b, powers_a, powers_b, scale_a, scale_b = scratch[:8]
    maxima_ref, total_ref, parcel, arrived, send_sem, recv_sem = scratch[8:]
    rows, width = h_ref.shape
    valid = table_ref.shape[0]
    tiles = (valid + tile - 1) // tile
    padded = tiles * tile
    v = lax.axis_index("vocab")
    x, core = v // 2, lax.rem(v, 2)
    twin, across, diagonal = x * 2 + 1 - core, (1 - x) * 2 + core, (1 - x) * 2 + 1 - core

    barrier = pltpu.get_barrier_semaphore()
    for peer in (twin, across, diagonal):
        pl.semaphore_signal(
            barrier, inc=1, device_id={"vocab": peer}, device_id_type=pl.DeviceIdType.MESH
        )
    pl.semaphore_wait(barrier, 3)

    def remote(source, target, index, peer):
        return pltpu.make_async_remote_copy(
            src_ref=source,
            dst_ref=target,
            send_sem=send_sem.at[index],
            recv_sem=recv_sem.at[index],
            device_id={"vocab": peer},
            device_id_type=pl.DeviceIdType.MESH,
        )

    to_twin = remote(h_ref, held.at[0], 0, twin)
    to_across = remote(h_ref, held.at[1], 1, across)
    passed_on = remote(held.at[1], held.at[2], 2, twin)
    results = [
        remote(parcel.at[k], arrived.at[k], 3 + k, peer)
        for k, peer in enumerate((twin, across, diagonal))
    ]
    to_twin.start()
    to_across.start()
    held[3] = h_ref[...]

    short = padded - valid
    if short:
        tail[: tile - short, :] = table_ref[padded - tile :, :]
        tail[tile - short :, :] = jnp.zeros((short, width), BF16)
    to_twin.wait_recv()

    logits_of, powers_of, scale_of = (logits_a, logits_b), (powers_a, powers_b), (scale_a, scale_b)
    column = lax.broadcasted_iota(jnp.int32, (rows, tile), 1)
    lane = lax.broadcasted_iota(jnp.int32, (rows, LANES), 1)

    def turn(k, _):
        @pl.when(k == 1)
        def _():
            to_across.wait_recv()
            passed_on.start()

        @pl.when(k == 2)
        def _():
            passed_on.wait_recv()

        owner = jnp.where(k == 0, twin, jnp.where(k == 1, across, jnp.where(k == 2, diagonal, v)))

        def part(at):
            if short and at == tiles - 1:
                return tail[...]
            return table_ref[at * tile : (at + 1) * tile, :]

        def scores(at):
            logits_of[at % 2][...] = dot_rows(held[k], part(at))

        def soften(at):
            logits = logits_of[at % 2][...]
            if at == tiles - 1 and padded > valid:
                logits = jnp.where(column < valid - at * tile, logits, MASKED)
            highest = jnp.maximum(maxima_ref[...], jnp.max(logits, -1, keepdims=True))
            powers = jnp.exp(logits - highest)
            scale = jnp.exp(maxima_ref[...] - highest)
            maxima_ref[...] = highest
            total_ref[...] = total_ref[...] * scale + jnp.sum(powers, -1, keepdims=True)
            scale_of[at % 2][...] = scale
            powers_of[at % 2][...] = jnp.where(
                column == target_ref[owner] - at * tile, 0.0, powers
            ).astype(BF16)

        def gather(at):
            term = dot(powers_of[at % 2][...], part(at))
            grad_ref[...] = grad_ref[...] * scale_of[at % 2][...] + term

        maxima_ref[...] = jnp.full((rows, 1), MASKED, F32)
        total_ref[...] = jnp.zeros((rows, 1), F32)
        grad_ref[...] = jnp.zeros_like(grad_ref)
        for at in range(tiles + 2):
            if at < tiles:
                scores(at)
            if 0 <= at - 1 < tiles:
                soften(at - 1)
            if at >= 2:
                gather(at - 2)

        @pl.when(k < 3)
        def _():
            parcel[k, :, :width] = grad_ref[...].astype(BF16)
            tail = jnp.zeros((rows, LANES), F32)
            for first, value in ((0, maxima_ref[...]), (3, total_ref[...])):
                for step in range(3):
                    piece = value.astype(BF16).astype(F32)
                    tail = jnp.where(lane == first + step, piece, tail)
                    value = value - piece
            parcel[k, :, width:] = tail.astype(BF16)

        for index, result in enumerate(results):
            pl.when(k == index)(result.start)
        return 0

    lax.fori_loop(0, 4, turn, 0)
    for result in results:
        result.wait_recv()
    tails = [arrived[k, :, width:].astype(F32) for k in range(3)]
    highs = [t[:, 0:1] + t[:, 1:2] + t[:, 2:3] for t in tails] + [maxima_ref[...]]
    totals = [t[:, 3:4] + t[:, 4:5] + t[:, 5:6] for t in tails] + [total_ref[...]]
    highest = functools.reduce(jnp.maximum, highs)
    log_total = highest + jnp.log(sum(t * jnp.exp(m - highest) for m, t in zip(highs, totals)))
    summed = grad_ref[...] * jnp.exp(highs[3] - log_total)
    for k in range(3):
        summed = summed + arrived[k, :, :width].astype(F32) * jnp.exp(highs[k] - log_total)
    grad_ref[...] = summed
    stat_ref[...] = jnp.where(lane == 0, log_total, 0.0)
    for copy in [to_twin, to_across, passed_on, *results]:
        copy.wait_send()


def vocab_exchange(hidden, target_local, embedding):
    rows, width = hidden.shape
    valid = embedding.shape[0]
    tile = 2 * VOCAB_BLOCK
    padded = (valid + tile - 1) // tile * tile
    vmem = pl.BlockSpec(memory_space=pltpu.VMEM)
    return pl.pallas_call(
        functools.partial(vocab_exchange_kernel, tile),
        out_shape=[
            jax.ShapeDtypeStruct((rows, width), F32),
            jax.ShapeDtypeStruct((rows, LANES), F32),
        ],
        in_specs=[vmem, vmem, vmem],
        out_specs=[vmem, vmem],
        scratch_shapes=[
            pltpu.VMEM((tile, width), BF16),
            pltpu.VMEM((4, rows, width), BF16),
            pltpu.VMEM((rows, tile), F32),
            pltpu.VMEM((rows, tile), F32),
            pltpu.VMEM((rows, tile), BF16),
            pltpu.VMEM((rows, tile), BF16),
            pltpu.VMEM((rows, 1), F32),
            pltpu.VMEM((rows, 1), F32),
            pltpu.VMEM((rows, 1), F32),
            pltpu.VMEM((rows, 1), F32),
            pltpu.VMEM((3, rows, width + LANES), BF16),
            pltpu.VMEM((3, rows, width + LANES), BF16),
            pltpu.SemaphoreType.DMA((6,)),
            pltpu.SemaphoreType.DMA((6,)),
        ],
        compiler_params=pltpu.CompilerParams(
            collective_id=1, has_side_effects=True, vmem_limit_bytes=52 * MIB
        ),
        cost_estimate=pl.CostEstimate(
            flops=16 * rows * padded * width, bytes_accessed=2 * valid * width, transcendentals=0
        ),
    )(hidden, target_local.reshape(4, rows, 1), embedding)


def reduce_kernel(rows_dp, task_ref, table_ref, stat_ref, out_ref, stats_out, squares_out, *scratch):
    cast, crossed, swap, swapped, own, outgoing, pieces, result, results = scratch[:9]
    stats, squares, send_sem, recv_sem = scratch[9:]
    features = own.shape[1]
    at, v = lax.axis_index("dp"), lax.axis_index("vocab")
    x, core = v // 2, lax.rem(v, 2)
    twin, across = x * 2 + 1 - core, (1 - x) * 2 + core
    dp_peers = [lax.rem(at + k, rows_dp) for k in range(1, rows_dp)]
    vocab_peers = [lax.rem(v + k, 4) for k in range(1, 4)]

    barrier = pltpu.get_barrier_semaphore()
    for peer in [{"vocab": p} for p in vocab_peers] + [{"dp": p} for p in dp_peers]:
        pl.semaphore_signal(barrier, inc=1, device_id=peer, device_id_type=pl.DeviceIdType.MESH)
    pl.semaphore_wait(barrier, rows_dp + 2)

    def remote(source, target, send, recv, peer):
        return pltpu.make_async_remote_copy(
            src_ref=source,
            dst_ref=target,
            send_sem=send_sem.at[send],
            recv_sem=recv_sem.at[recv],
            device_id=peer,
            device_id_type=pl.DeviceIdType.MESH,
        )

    half = 2 * features
    there = pl.ds(pl.multiple_of((1 - x) * half, half), half)
    here = pl.ds(pl.multiple_of(x * half, half), half)
    stats[0] = stat_ref[...]
    cast[...] = table_ref[there, :].astype(BF16)
    over_x = remote(cast, crossed, 0, 0, {"vocab": across})
    stat_x = remote(stats.at[0], stats.at[1], 1, 1, {"vocab": across})
    over_x.start()
    stat_x.start()
    over_x.wait_recv()
    stat_x.wait_recv()

    stats[2] = stats[0] + stats[1]
    stat_core = remote(stats.at[2], stats.at[3], 2, 2, {"vocab": twin})
    stat_core.start()
    tasks = [[task_ref[m, s] for s in range(task_ref.shape[1])] for m in range(2)]
    other = jnp.where(x == 0, 1, 0)

    def by_task(part, t):
        start = pl.multiple_of(part * features, features)
        mine = table_ref[pl.ds(pl.multiple_of(x * half + part * features, features), features), :]
        theirs = crossed[pl.ds(start, features), :].astype(F32)
        total = jnp.zeros((features, LANES), F32)
        for s in range(task_ref.shape[1]):
            lanes = slice(s * LANES, (s + 1) * LANES)
            mine_task = jnp.where(x == 0, tasks[0][s], tasks[1][s])
            their_task = jnp.where(x == 0, tasks[1][s], tasks[0][s])
            total = total + jnp.where(mine_task == t, mine[:, lanes], 0.0)
            total = total + jnp.where(their_task == t, theirs[:, lanes], 0.0)
        return total

    for t in range(TASKS):
        swap[t] = by_task(1 - core, t).astype(BF16)
    over_core = remote(swap, swapped, 3, 3, {"vocab": twin})
    over_core.start()
    for t in range(TASKS):
        own[t] = by_task(core, t)
    over_core.wait_recv()
    stat_core.wait_recv()
    stats[4 + at] = stats[2] + stats[3]
    for t in range(TASKS):
        own[t] = own[t] + swapped[t].astype(F32)
        outgoing[t] = own[t].astype(BF16)

    base = 4
    spread, tallies = [], []
    for k, peer in enumerate(dp_peers):
        spread.append(
            remote(outgoing.at[peer], pieces.at[at], base + k, base + at, {"dp": peer})
        )
        tallies.append(
            remote(
                stats.at[4 + at],
                stats.at[4 + at],
                base + rows_dp + k,
                base + rows_dp + at,
                {"dp": peer},
            )
        )
    for copy in spread + tallies:
        copy.start()
    total = own[at]
    for peer in dp_peers:
        remote(outgoing.at[peer], pieces.at[peer], base, base + peer, {"dp": peer}).wait_recv()
        total = total + pieces[peer].astype(F32)
    result[...] = total.astype(BF16)
    results[at] = result[...]
    returns = []
    for k, peer in enumerate(dp_peers):
        returns.append(
            remote(
                result,
                results.at[at],
                base + 2 * rows_dp + k,
                base + 2 * rows_dp + at,
                {"dp": peer},
            )
        )
    for copy in returns:
        copy.start()
    for peer in dp_peers:
        remote(
            stats.at[4 + peer], stats.at[4 + peer], base, base + rows_dp + peer, {"dp": peer}
        ).wait_recv()
    tally = functools.reduce(jnp.add, [stats[4 + k] for k in range(rows_dp)])
    stats_out[...] = tally
    for peer in dp_peers:
        remote(result, results.at[peer], base, base + 2 * rows_dp + peer, {"dp": peer}).wait_recv()
    for t in range(TASKS):
        scale = 1.0 / (TASKS * jnp.maximum(tally[1:2, t : t + 1], 1.0))
        scaled = results[t].astype(F32) * scale
        out_ref[t] = scaled
        squares[v, t : t + 1, :] = jnp.sum(scaled * scaled, 0, keepdims=True)
    last = base + 3 * rows_dp
    shares = [
        remote(squares.at[v], squares.at[v], last + k, last + v, {"vocab": peer})
        for k, peer in enumerate(vocab_peers)
    ]
    for copy in shares:
        copy.start()
    for peer in vocab_peers:
        remote(squares.at[peer], squares.at[peer], last, last + peer, {"vocab": peer}).wait_recv()
    squares_out[...] = squares[0] + squares[1] + squares[2] + squares[3]
    for copy in [over_x, stat_x, stat_core, over_core, *spread, *tallies, *returns, *shares]:
        copy.wait_send()


def reduce_over_devices(task_list, table, stats):
    rows_dp = lax.axis_size("dp")
    features = table.shape[0] // 4
    vmem = pl.BlockSpec(memory_space=pltpu.VMEM)
    copies = 4 + 3 * rows_dp + 4
    return pl.pallas_call(
        functools.partial(reduce_kernel, rows_dp),
        out_shape=[
            jax.ShapeDtypeStruct((TASKS, features, LANES), F32),
            jax.ShapeDtypeStruct((8, LANES), F32),
            jax.ShapeDtypeStruct((8, LANES), F32),
        ],
        in_specs=[pl.BlockSpec(memory_space=pltpu.SMEM), vmem, vmem],
        out_specs=[vmem] * 3,
        scratch_shapes=[
            pltpu.VMEM((2 * features, table.shape[1]), BF16),
            pltpu.VMEM((2 * features, table.shape[1]), BF16),
            pltpu.VMEM((TASKS, features, LANES), BF16),
            pltpu.VMEM((TASKS, features, LANES), BF16),
            pltpu.VMEM((TASKS, features, LANES), F32),
            pltpu.VMEM((TASKS, features, LANES), BF16),
            pltpu.VMEM((rows_dp, features, LANES), BF16),
            pltpu.VMEM((features, LANES), BF16),
            pltpu.VMEM((rows_dp, features, LANES), BF16),
            pltpu.VMEM((4 + rows_dp, 8, LANES), F32),
            pltpu.VMEM((4, 8, LANES), F32),
            pltpu.SemaphoreType.DMA((copies,)),
            pltpu.SemaphoreType.DMA((copies,)),
        ],
        compiler_params=pltpu.CompilerParams(
            collective_id=2, has_side_effects=True, vmem_limit_bytes=24 * MIB
        ),
    )(task_list, table, stats)


def on_device(
    tokens,
    targets,
    loss_mask,
    seg_lengths,
    task_ids,
    embedding,
    attend_in,
    attend_out,
    expand_weights,
    reduce_weights,
    norm_gains,
    prompt,
    first_moment,
    row_moment,
    column_moment,
):
    shards = lax.axis_size("vocab")
    micros, span = tokens.shape[0], tokens.shape[-1]
    length = span * shards
    group = shards // micros
    own = length // group
    me = lax.axis_index("vocab")
    micro, place = me // group, me % group
    shard_rows, width = embedding.shape
    share = prompt.shape[-1]

    def around(array, shift):
        pairs = [
            (m * group + r, m * group + (r + shift) % group)
            for m in range(micros)
            for r in range(group)
        ]
        return lax.ppermute(array, "vocab", pairs)

    ids = lax.all_gather(jnp.stack([tokens[:, 0], targets[:, 0], loss_mask[:, 0]]), "vocab")
    ids = jnp.transpose(ids, (1, 2, 0, 3)).reshape(3, micros, length)
    enc_ids = ids[0].reshape(shards, own)

    segments = seg_lengths.shape[-1]
    row_lengths = seg_lengths[:, 0]
    if group == 2 and segments == 3 and 2 * span + 2 * P_SIZE <= length - span:
        half = (length - segments * P_SIZE) // group
        heads = (half + LANES - 1) // LANES * LANES
        extra = (half + 2 * P_SIZE - own + HALO - 1) // HALO * HALO
        starts = [0, own - extra]
        near = [P_SIZE, half + 2 * P_SIZE]
        far = [2 * P_SIZE, half + 3 * P_SIZE]
        turns = [row_lengths[:, 0] - P_SIZE, length - row_lengths[:, 2] - near[1]]
    else:
        half = heads = own
        extra = 0
        starts = near = far = [p * own for p in range(group)]
        turns = [row_lengths[:, 0]] * group
    held = own + extra
    entries = jnp.arange(heads, dtype=jnp.int32)

    def of_rows(values, m, p):
        values = jnp.pad(values, (0, heads + far[p]))
        return jnp.where(
            entries < turns[p][m],
            values[near[p] : near[p] + heads],
            values[far[p] : far[p] + heads],
        )

    everyone = [(m, p) for m in range(micros) for p in range(group)]
    dec_ids = jnp.stack(
        [
            jnp.concatenate(
                [
                    jnp.zeros((HALO - 1,), jnp.int32),
                    jnp.pad(ids[1, m], (1, 0))[starts[p] : starts[p] + 1 + held],
                ]
            )
            for m, p in everyone
        ]
    )
    head_targets = jnp.stack([of_rows(ids[1, m], m, p) for m, p in everyone])
    first_row = me * shard_rows

    def here(wanted):
        local = wanted - first_row
        inside = (local >= 0) & (local < shard_rows)
        return local, inside

    prompt_all = lax.all_gather(prompt.astype(BF16), "vocab", axis=2, tiled=True)
    prompt_flat = prompt_all.reshape(-1, width)
    weights = (attend_in, attend_out, expand_weights, reduce_weights)
    if lax.axis_size("dp") == 8 and shards == 4 and shard_rows % 32 == 0:
        local, inside = here(jnp.concatenate([enc_ids, dec_ids], 1).reshape(-1))
        wanted = jnp.where(inside, local, shard_rows)
        *flat, found = gather_weights(*weights, wanted, embedding)
        attend_in, attend_out = flat[:3], flat[3:6]
        expand_weights, reduce_weights = [[w] for w in flat[6:8]], [[w] for w in flat[8:]]
        enc_rows, dec_rows = found[:own], found[own:]
    else:

        def lookup(wanted):
            local, inside = here(wanted.reshape(-1))
            picked = jnp.take(embedding, jnp.clip(local, 0, shard_rows - 1), axis=0)
            picked = jnp.where(inside[:, None], picked, 0)
            return lax.psum_scatter(picked, "vocab", scatter_dimension=0, tiled=True)

        enc_rows, dec_rows = lookup(enc_ids), lookup(dec_ids)
        whole = [lax.all_gather(tensor, "dp", axis=1, tiled=True) for tensor in weights]
        attend_in, attend_out = whole[:2]
        expand_weights, reduce_weights = whole[2][:, None], whole[3][:, None]

    lengths = lax.dynamic_index_in_dim(seg_lengths[:, 0], micro, 0, False)
    tasks = lax.dynamic_index_in_dim(task_ids[:, 0], micro, 0, False)
    steps = jnp.arange(own, dtype=jnp.int32)
    positions = place * own + steps
    segment, in_segment, task_of = layout(lengths, tasks, positions)
    key_positions = jnp.concatenate(
        [((place - k + group) % group) * own + steps for k in range(group)]
    )
    key_segment = layout(lengths, tasks, key_positions)[0]
    rows_info = jnp.stack([segment, positions], 1)
    keys_info = jnp.stack([key_segment, key_positions], 1)
    turn = jnp.stack(turns)[place, micro]
    near_row = jnp.asarray(near, jnp.int32)[place]
    far_row = jnp.asarray(far, jnp.int32)[place]
    first_held = jnp.asarray(starts, jnp.int32)[place]
    head_positions = jnp.where(entries < turn, near_row, far_row) + entries
    head_positions = jnp.minimum(head_positions, length - 1)
    head_segment, head_in_segment, head_task = layout(lengths, tasks, head_positions)
    heads_info = jnp.stack([head_segment, head_positions], 1)
    head_mask_row = jnp.stack([of_rows(ids[2, m], m, p) for m, p in everyone])[me]
    counted = (head_mask_row * ((head_in_segment >= P_SIZE) & (entries < half))).astype(F32)

    def head_rows(values):
        values = jnp.pad(values, ((0, heads), (0, 0)))
        shape = (heads, values.shape[1])
        return jnp.where(
            (entries < turn)[:, None],
            lax.dynamic_slice(values, (near_row - first_held, 0), shape),
            lax.dynamic_slice(values, (far_row - first_held, 0), shape),
        )

    def key_parts(source, weight):
        pair = dot(source, weight).astype(BF16)
        return [pair] + [around(pair, k) for k in range(1, group)]

    def project(source, weight):
        return dot(source, weight).astype(BF16)

    is_prompt = in_segment < P_SIZE
    slot = task_of * P_SIZE + jnp.minimum(in_segment, P_SIZE - 1)
    enc_input = jnp.where(
        is_prompt[:, None], jnp.take(prompt_flat, slot, axis=0), enc_rows
    ).astype(F32)
    held_positions = first_held + jnp.arange(held, dtype=jnp.int32)
    begun = layout(lengths, tasks, held_positions)[1] >= 1
    dec_held = jnp.where(begun[:, None], dec_rows[HALO - 1 : HALO - 1 + held], dec_rows[:1])
    dec_keys = lax.dynamic_slice(dec_held, (place * own - first_held, 0), (own, width)).astype(F32)
    dec_input = head_rows(dec_held).astype(F32)
    target_rows = head_rows(dec_rows[HALO:]).astype(F32)

    normed_in, inverse_in = normed(enc_input, norm_gains[0])
    normed_low = normed_in.astype(BF16)
    enc_pairs = key_parts(normed_low, attend_in[0][:, width:])
    enc_queries = project(normed_low, attend_in[0][:, :width])
    normed_keys = normed(dec_keys, norm_gains[3])[0].astype(BF16)
    dec_pairs = key_parts(normed_keys, attend_in[1][:, width:])
    normed_dec = normed(dec_input, norm_gains[3])[0].astype(BF16)
    dec_queries = project(normed_dec, attend_in[1][:, :width])
    enc_mid, enc_mixed, enc_logs = attend(
        enc_queries, enc_pairs, enc_input, attend_out[0], rows_info, keys_info, False
    )
    enc_last, enc_kept = feed(enc_mid, norm_gains[1], expand_weights[0], reduce_weights[0])
    encoded, inverse_last = normed(enc_last, norm_gains[2])
    cross_pairs = key_parts(encoded.astype(BF16), attend_in[2][:, width:])

    dec_first = attend(
        dec_queries, dec_pairs, dec_input, attend_out[1], heads_info, keys_info, True
    )[0]
    cross_queries = project(normed(dec_first, norm_gains[4])[0].astype(BF16), attend_in[2][:, :width])
    dec_second, cross_mixed, cross_logs = attend(
        cross_queries, cross_pairs, dec_first, attend_out[2], heads_info, keys_info, False
    )
    dec_last, dec_kept = feed(dec_second, norm_gains[5], expand_weights[1], reduce_weights[1])
    output_norm, inverse_out = normed(dec_last, norm_gains[6])
    hidden = (output_norm * width ** (-0.5)).astype(BF16)

    target_local = head_targets.reshape(-1, 1) - first_row
    if shards == 4:
        summed, stats = vocab_exchange(hidden, target_local, embedding)
        own_total = stats[:, 0]
    else:
        all_hidden = lax.all_gather(hidden, "vocab", axis=0, tiled=True)
        part, stats = vocab_pass(all_hidden, target_local, embedding, heads)
        gathered = lax.all_gather(stats[:, :2].T, "vocab")
        maxima = jnp.max(gathered[:, 0], 0)
        log_total = maxima + jnp.log(
            jnp.sum(gathered[:, 1] * jnp.exp(gathered[:, 0] - maxima), 0)
        )
        scaled = part * jnp.exp(stats[:, 0] - log_total)[:, None]
        summed = lax.psum_scatter(scaled, "vocab", scatter_dimension=0, tiled=True)
        own_total = lax.dynamic_slice(log_total, (me * heads,), (heads,))
    target_logit = jnp.sum(hidden.astype(F32) * target_rows, -1)
    token_loss = own_total - target_logit
    target_coefficient = (jnp.exp(target_logit - own_total) - 1.0).astype(BF16).astype(F32)
    hidden_grad = counted[:, None] * (summed + target_coefficient[:, None] * target_rows)

    def keys_back(pairs, weight):
        total = pairs[0]
        for k in range(1, group):
            total = total + around(pairs[k], group - k)
        high = total.astype(BF16)
        rest = (total - high.astype(F32)).astype(BF16)
        return dot_rows(high, weight) + dot_rows(rest, weight)

    dec_grad = normed_back(
        dec_last, norm_gains[6], inverse_out, hidden_grad * width ** (-0.5)
    )
    dec_grad = feed_back(
        dec_grad, dec_second, norm_gains[5], dec_kept, expand_weights[1], reduce_weights[1]
    )
    back = attend_back(
        cross_queries,
        cross_pairs,
        dec_grad,
        attend_out[2],
        cross_mixed,
        cross_logs,
        heads_info,
        keys_info,
        False,
    )
    enc_grad = normed_back(
        enc_last, norm_gains[2], inverse_last, keys_back(back, attend_in[2][:, width:])
    )
    enc_grad = feed_back(
        enc_grad, enc_mid, norm_gains[1], enc_kept, expand_weights[0], reduce_weights[0]
    )
    *back, back_queries = attend_back(
        enc_queries,
        enc_pairs,
        enc_grad,
        attend_out[0],
        enc_mixed,
        enc_logs,
        rows_info,
        keys_info,
        True,
    )
    source_grad = keys_back(back, attend_in[0][:, width:]) + lax.dot_general(
        back_queries,
        attend_in[0][:, :width],
        (((0,), (1,)), ((), ())),
        preferred_element_type=F32,
    )
    enc_grad = enc_grad + normed_back(enc_input, norm_gains[0], inverse_in, source_grad)

    place_of = segment * LANES + in_segment
    chosen = (
        (place_of[:, None] == jnp.arange(segments * LANES, dtype=jnp.int32)) & is_prompt[:, None]
    ).astype(BF16)
    high = enc_grad.astype(BF16)
    rest = (enc_grad - high.astype(F32)).astype(BF16)
    table = dot_columns(high, chosen) + dot_columns(rest, chosen)
    tallies = jnp.stack([per_task(head_task, counted * token_loss), per_task(head_task, counted)])
    stats = jnp.zeros((8, LANES), F32).at[:2, :TASKS].set(tallies)
    if shards == 4 and lax.axis_size("dp") == TASKS:
        gradient, stats, squares = reduce_over_devices(task_ids[:, 0], table, stats)
        full_grad = jnp.swapaxes(gradient[:, :, :P_SIZE], 1, 2)
        row_squares = squares[:, :P_SIZE]
        task_scale = 1.0 / (TASKS * jnp.maximum(stats[1, :TASKS], 1.0))
    else:
        hits = (tasks[:, None] == jnp.arange(TASKS, dtype=jnp.int32)).astype(F32)
        by_task = jnp.einsum(
            "fsp,st->tpf",
            table.reshape(width, segments, LANES)[:, :, :P_SIZE],
            hits,
            precision=lax.Precision.HIGHEST,
        )
        stats = lax.psum(stats, ("dp", "vocab"))
        gradient = lax.psum_scatter(by_task, "vocab", scatter_dimension=2, tiled=True)
        task_scale = 1.0 / (TASKS * jnp.maximum(stats[1, :TASKS], 1.0))
        full_grad = lax.psum(gradient, "dp") * task_scale[:, None, None]
        row_squares = jnp.sum(lax.all_gather(jnp.sum(full_grad * full_grad, -1), "vocab"), 0)
    loss_mean = jnp.sum(stats[0, :TASKS] * task_scale)
    grad_norm = jnp.sqrt(jnp.sum(row_squares))
    clip = CLIP_NORM / jnp.maximum(grad_norm, CLIP_NORM)
    prompt_grad = full_grad * clip
    row_second = BETA_TWO * row_moment + (1.0 - BETA_TWO) * (
        row_squares * clip * clip / width + SQUARE_EPS
    )
    column_second = BETA_TWO * column_moment + (1.0 - BETA_TWO) * (
        jnp.mean(prompt_grad * prompt_grad, 1) + SQUARE_EPS
    )
    new_moment = BETA_ONE * first_moment + (1.0 - BETA_ONE) * prompt_grad
    estimate = (
        row_second[:, :, None] * column_second[:, None, :] / jnp.mean(row_second, -1)[:, None, None]
    )
    update = new_moment / (1.0 - BETA_ONE**STEP) / jnp.sqrt(estimate / (1.0 - BETA_TWO**STEP))
    new_prompt = prompt - LEARN_RATE * (update + WEIGHT_DECAY * prompt)
    return (loss_mean, grad_norm, prompt_grad, new_moment, row_second, column_second, new_prompt)


def solution(mesh):
    placed = (
        P(None, "dp", "vocab"),
        P(None, "dp", "vocab"),
        P(None, "dp", "vocab"),
        P(None, "dp", None),
        P(None, "dp", None),
        P("vocab", None),
        P(None, "dp", None),
        P(None, "dp", None),
        P(None, "dp", None),
        P(None, "dp", None),
        P(),
        P(None, None, "vocab"),
        P(None, None, "vocab"),
        P(),
        P(None, "vocab"),
    )
    return jax.shard_map(
        on_device,
        mesh=mesh,
        in_specs=placed,
        out_specs=(
            P(),
            P(),
            P(None, None, "vocab"),
            P(None, None, "vocab"),
            P(),
            P(None, "vocab"),
            P(None, None, "vocab"),
        ),
        check_vma=False,
    )
```

```python
import collections
import functools

import jax
import jax.numpy as jnp
from jax import lax
from jax.experimental import pallas as pl
from jax.experimental.pallas import tpu as pltpu
from jax.sharding import PartitionSpec as P

DH = 64
P_SIZE = 100
TASKS = 8
STEP = 5
HALO = 16
LANES = 128
SEGS = 3
VOCAB_BLOCK = 1024
HIDDEN_PIECE = 512
MIB = 1024 * 1024

NORM_EPS = 1e-06
CLIP_NORM = 2e-05
BETA_ONE = 0.9
BETA_TWO = 0.999
LEARN_RATE = 1.0
WEIGHT_DECAY = 1e-05
SQUARE_EPS = 1e-30
MASKED = -1e30

F32 = jnp.float32
BF16 = jnp.bfloat16


def dot(left, right):
    return jnp.dot(left, right, preferred_element_type=F32)


def dot_rows(left, right):
    return lax.dot_general(left, right, (((1,), (1,)), ((), ())), preferred_element_type=F32)


def dot_columns(left, right):
    return lax.dot_general(left, right, (((0,), (0,)), ((), ())), preferred_element_type=F32)


def normed(values, gain):
    inverse = lax.rsqrt(jnp.mean(values * values, -1, keepdims=True) + NORM_EPS)
    return (values * inverse * gain, inverse)


def normed_back(values, gain, inverse, gradient):
    unit_rows = values * inverse
    scaled = gradient * gain
    return inverse * (scaled - unit_rows * jnp.mean(scaled * unit_rows, -1, keepdims=True))


def smooth(values):
    return jax.nn.gelu(values, approximate=True)


def layout(lengths, task_list, positions):
    seg_ends = jnp.cumsum(lengths)
    seg_starts = seg_ends - lengths
    segment = jnp.sum((positions[:, None] >= seg_ends[None, :]).astype(jnp.int32), -1)
    member = segment[:, None] == jnp.arange(lengths.shape[0], dtype=jnp.int32)[None, :]
    in_segment = positions - jnp.sum(jnp.where(member, seg_starts[None, :], 0), -1)
    task_of = jnp.sum(jnp.where(member, task_list[None, :], 0), -1)
    return (segment, in_segment, task_of)


def per_task(task_of, amounts):
    hits = task_of[:, None] == jnp.arange(TASKS, dtype=jnp.int32)
    return jnp.sum(jnp.where(hits, amounts[:, None], 0.0), 0)


def pair_lanes(pair, first=0):
    return pl.ds(pl.multiple_of(first + pair * LANES, LANES), LANES)


def head_mask(shape, head, axis=1):
    return (lax.broadcasted_iota(jnp.int32, shape, axis) < DH) == (head == 0)


Plan = collections.namedtuple(
    "Plan", ["length", "group", "own", "held", "heads", "half", "starts", "near", "far"]
)


def chosen(index, values):
    result = values[0]
    for k, value in enumerate(values[1:], 1):
        result = jnp.where(index == k, value, result)
    return result


def turn_of(plan, lengths_ref, m, place):
    last = plan.length - lengths_ref[m, SEGS - 1] - plan.near[-1]
    return jnp.where(place == 0, lengths_ref[m, 0] - P_SIZE, last)


def row_scalars(plan, lengths_ref, decoder):
    v = lax.axis_index("vocab")
    m, place = v // plan.group, lax.rem(v, plan.group)
    first = lengths_ref[m, 0]
    ends = [first, first + lengths_ref[m, 1]]
    if decoder:
        rows = [
            turn_of(plan, lengths_ref, m, place),
            chosen(place, plan.near),
            chosen(place, plan.far),
        ]
    else:
        rows = [0, place * plan.own, place * plan.own]
    starts = [lax.rem(place - k + plan.group, plan.group) * plan.own for k in range(plan.group)]
    return [*ends, *rows, *starts]


def row_positions(info, shape, axis):
    row = lax.broadcasted_iota(jnp.int32, shape, axis)
    return row + jnp.where(row < info[SEGS - 1], info[SEGS], info[SEGS + 1])


def key_positions(info, parts, own, shape, axis):
    row = lax.broadcasted_iota(jnp.int32, shape, axis)
    position = row + info[SEGS + 2]
    for k in range(1, parts):
        position = jnp.where(row < k * own, position, row - k * own + info[SEGS + 2 + k])
    return position


def segment_columns(info, position, is_key):
    segment = sum(jnp.where(position >= info[j], 1, 0) for j in range(SEGS - 1))
    column = lax.rem(lax.broadcasted_iota(jnp.int32, position.shape, 1), DH)
    if is_key:
        return jnp.where((column < SEGS) & (column != segment), MASKED, 0.0).astype(BF16)
    return jnp.where(column == segment, 1.0, 0.0).astype(BF16)


def head_part(values, rest, head):
    return jnp.where(head_mask(values.shape, head), values, rest)


def over_heads(pairs, scores, soften, mix):
    scores(0, 0)
    scores(0, 1)
    soften(0, 0)

    def step(pair, _):
        scores(pair + 1, 0)
        soften(pair, 1)
        mix(pair, 0)
        scores(pair + 1, 1)
        soften(pair + 1, 0)
        mix(pair, 1)
        return 0

    lax.fori_loop(0, pairs - 1, step, 0)
    soften(pairs - 1, 1)
    mix(pairs - 1, 0)
    mix(pairs - 1, 1)


def attend_kernel(plan, parts, decoder, causal, *refs):
    q_ref, pair_refs = refs[0], refs[1 : 1 + parts]
    residual_ref, weight_ref, lengths_ref, out_ref, mixed_ref, log_ref = refs[1 + parts : 7 + parts]
    info = row_scalars(plan, lengths_ref, decoder)
    bias_ref, q_mark, k_mark, low_ref, scores_a, scores_b, powers_a, powers_b = refs[7 + parts :]
    width = q_ref.shape[1]
    own = pair_refs[0].shape[0]
    scores_of, powers_of = (scores_a, scores_b), (powers_a, powers_b)
    rows = [slice(k * own, (k + 1) * own) for k in range(parts)]
    q_mark[...] = segment_columns(info, row_positions(info, q_mark.shape, 0), False)
    k_mark[...] = segment_columns(info, key_positions(info, parts, own, k_mark.shape, 0), True)
    if causal:
        shape = bias_ref.shape
        later = row_positions(info, shape, 0) >= key_positions(info, parts, own, shape, 1)
        bias_ref[...] = jnp.where(later, 0.0, MASKED)
    log_ref[...] = jnp.zeros_like(log_ref)
    lane = lax.broadcasted_iota(jnp.int32, log_ref.shape, 1)

    def scores(pair, head):
        query = q_ref[:, pair_lanes(pair)] * jnp.asarray(DH ** (-0.5), BF16)
        query = head_part(query, q_mark[...], head)
        for k in range(parts):
            keys = head_part(pair_refs[k][:, pair_lanes(pair)], k_mark[rows[k], :], head)
            values = dot_rows(query, keys)
            if causal:
                values = values + bias_ref[:, rows[k]]
            scores_of[head][:, rows[k]] = values

    def soften(pair, head):
        values = scores_of[head][...]
        highest = jnp.max(values, -1, keepdims=True)
        powers_of[head][...] = jnp.exp(values - highest).astype(BF16)
        log_ref[...] += jnp.where(lane == 2 * pair + head, highest, 0.0)

    def mix(pair, head):
        value = None
        for k in range(parts):
            values = pair_refs[k][:, pair_lanes(pair, width)]
            values = head_part(values, jnp.ones_like(values), head)
            term = dot(powers_of[head][:, rows[k]], values)
            value = term if value is None else value + term
        total = value[:, LANES - 1 :] if head == 0 else value[:, :1]
        value = value / total
        log_ref[...] += jnp.where(lane == 2 * pair + head, jnp.log(total), 0.0)
        lanes = pair_lanes(pair)
        if head:
            value = jnp.where(head_mask(value.shape, 0), mixed_ref[:, lanes], value)
        mixed_ref[:, lanes] = value
        if head:
            low_ref[:, lanes] = value.astype(BF16)

    over_heads(width // LANES, scores, soften, mix)
    out_ref[...] = residual_ref[...] + dot(low_ref[...], weight_ref[...])


def attend(plan, queries, pairs, residual, weight, row_lengths, decoder, causal):
    own, width = queries.shape
    parts, length = len(pairs), sum(pair.shape[0] for pair in pairs)
    vmem = pl.BlockSpec(memory_space=pltpu.VMEM)
    return pl.pallas_call(
        functools.partial(attend_kernel, plan, parts, decoder, causal),
        out_shape=[
            jax.ShapeDtypeStruct((own, width), F32),
            jax.ShapeDtypeStruct((own, width), F32),
            jax.ShapeDtypeStruct((own, LANES), F32),
        ],
        in_specs=[vmem] * (parts + 3) + [pl.BlockSpec(memory_space=pltpu.SMEM)],
        out_specs=[vmem] * 3,
        scratch_shapes=[
            pltpu.VMEM((own, length) if causal else (8, LANES), F32),
            pltpu.VMEM((own, LANES), BF16),
            pltpu.VMEM((length, LANES), BF16),
            pltpu.VMEM((own, width), BF16),
            pltpu.VMEM((own, length), F32),
            pltpu.VMEM((own, length), F32),
            pltpu.VMEM((own, length), BF16),
            pltpu.VMEM((own, length), BF16),
        ],
        compiler_params=pltpu.CompilerParams(vmem_limit_bytes=24 * MIB),
        cost_estimate=pl.CostEstimate(
            flops=44 * own * length * width, bytes_accessed=6 * own * width, transcendentals=0
        ),
    )(queries, *pairs, residual, weight, row_lengths)


def attend_back_kernel(plan, parts, decoder, want_queries, exchange, *refs):
    q_ref, pair_refs = refs[0], refs[1 : 1 + parts]
    grad_ref, weight_ref, mixed_ref, log_ref, lengths_ref = refs[1 + parts : 6 + parts]
    info = row_scalars(plan, lengths_ref, decoder)
    rest = refs[6 + parts :]
    if exchange:
        in_hbm, rows_hbm, gain_ref, result_ref = rest[:4]
        part_refs, arrived, send_sem, recv_sem = rest[4:6], rest[6], rest[7], rest[8]
        dq_ref, in_ref, rows_ref, late_sems = rest[9:13]
        rest = rest[13:]
        late = [
            pltpu.make_async_copy(in_hbm, in_ref, late_sems.at[0]),
            pltpu.make_async_copy(rows_hbm, rows_ref, late_sems.at[1]),
        ]
        for copy in late:
            copy.start()
        v = lax.axis_index("vocab")
        twin = {"vocab": v // 2 * 2 + 1 - lax.rem(v, 2)}
        barrier = pltpu.get_barrier_semaphore()
        pl.semaphore_signal(barrier, inc=1, device_id=twin, device_id_type=pl.DeviceIdType.MESH)
        pl.semaphore_wait(barrier, 1)
    else:
        part_refs = rest[:parts]
        dq_ref = rest[parts] if want_queries else None
        rest = rest[parts + want_queries :]
    q_mark, k_mark, low_ref, delta_ref, *rest = rest
    scores_of, grads_of, weights_of, steps_of = rest[0:2], rest[2:4], rest[4:6], rest[6:8]
    width = q_ref.shape[1]
    own = pair_refs[0].shape[0]
    pairs = width // LANES
    rows = [slice(k * own, (k + 1) * own) for k in range(parts)]
    scale = jnp.asarray(DH ** (-0.5), BF16)
    q_mark[...] = segment_columns(info, row_positions(info, q_mark.shape, 0), False)
    k_mark[...] = segment_columns(info, key_positions(info, parts, own, k_mark.shape, 0), True)
    low_ref[...] = dot_rows(grad_ref[...].astype(BF16), weight_ref[...]).astype(BF16)
    product = low_ref[...].astype(F32) * mixed_ref[...]
    high = product.astype(BF16)
    shape = (2 * 8, width)
    belongs = lax.broadcasted_iota(jnp.int32, shape, 1) // DH == lax.broadcasted_iota(
        jnp.int32, shape, 0
    )
    belongs = jnp.where(belongs, 1.0, 0.0).astype(BF16)
    delta_ref[...] = dot_rows(belongs, high) + dot_rows(
        belongs, (product - high.astype(F32)).astype(BF16)
    )

    def scores(pair, head):
        query = head_part(q_ref[:, pair_lanes(pair)] * scale, q_mark[...], head)
        grad = low_ref[:, pair_lanes(pair)]
        grad = head_part(grad, jnp.zeros_like(grad), head)
        for k in range(parts):
            keys = head_part(pair_refs[k][:, pair_lanes(pair)], k_mark[rows[k], :], head)
            scores_of[head][rows[k], :] = dot_rows(keys, query)
            grads_of[head][rows[k], :] = dot_rows(pair_refs[k][:, pair_lanes(pair, width)], grad)

    def soften(pair, head):
        at = pl.ds(2 * pair + head, 1)
        weights = jnp.exp(scores_of[head][...] - log_ref[at, :])
        weights_of[head][...] = weights.astype(BF16)
        steps_of[head][...] = (weights * (grads_of[head][...] - delta_ref[at, :])).astype(BF16)

    def away(pair, which):
        lanes = pair_lanes(pair, which * width)
        return pltpu.make_async_remote_copy(
            src_ref=part_refs[1].at[:, lanes],
            dst_ref=arrived.at[:, lanes],
            send_sem=send_sem.at[pair, which],
            recv_sem=recv_sem.at[pair, which],
            device_id=twin,
            device_id_type=pl.DeviceIdType.MESH,
        )

    def mix(pair, head):
        keys, values = pair_lanes(pair), pair_lanes(pair, width)
        query, grad = q_ref[:, keys] * scale, low_ref[:, keys]
        query = head_part(query, jnp.zeros_like(query), head)
        grad = head_part(grad, jnp.zeros_like(grad), head)
        dq = None
        for k in reversed(range(parts)):
            step = steps_of[head][rows[k], :]
            dk = dot(step, query)
            dv = dot(weights_of[head][rows[k], :], grad)
            part_refs[k][:, keys] = dk if head == 0 else part_refs[k][:, keys] + dk
            part_refs[k][:, values] = dv if head == 0 else part_refs[k][:, values] + dv
            if want_queries:
                term = dot_columns(pair_refs[k][:, keys], step)
                dq = term if dq is None else dq + term
        if want_queries:
            here = pl.ds(pl.multiple_of(pair * LANES, LANES), LANES)
            dq = dq * DH ** (-0.5)
            if head:
                dq = jnp.where(head_mask(dq.shape, 0, 0), dq_ref[here, :].astype(F32), dq)
            dq_ref[here, :] = dq.astype(dq_ref.dtype)
        if exchange and head:
            away(pair, 0).start()
            away(pair, 1).start()

    over_heads(pairs, scores, soften, mix)
    if not exchange:
        return
    total = None
    for copy in late:
        copy.wait()
    if want_queries:
        total = dot_rows(jnp.transpose(dq_ref[...]).astype(BF16), in_ref[:, :width])
    for pair in range(pairs):
        away(pair, 0).wait_recv()
        away(pair, 1).wait_recv()
    both = part_refs[0][...] + arrived[...]
    high = both.astype(BF16)
    low = (both - high.astype(F32)).astype(BF16)
    back = dot_rows(high, in_ref[:, width:]) + dot_rows(low, in_ref[:, width:])
    total = back if total is None else total + back
    values, gain = rows_ref[...], gain_ref[...]
    inverse = lax.rsqrt(jnp.mean(values * values, -1, keepdims=True) + NORM_EPS)
    total = normed_back(values, gain, inverse, total)
    result_ref[...] = grad_ref[...] + total if want_queries else total
    for pair in range(pairs):
        away(pair, 0).wait_send()
        away(pair, 1).wait_send()


def attend_back(
    plan, queries, pairs, gradient, weight, mixed, logs, row_lengths, decoder, want_queries, through
):
    heads, width = queries.shape
    own = pairs[0].shape[0]
    parts, length = len(pairs), sum(pair.shape[0] for pair in pairs)
    vmem = pl.BlockSpec(memory_space=pltpu.VMEM)
    operands = [queries, *pairs, gradient, weight, mixed, logs.T[:16], row_lengths]
    in_specs = [vmem] * (parts + 5) + [pl.BlockSpec(memory_space=pltpu.SMEM)]
    scratch = [
        pltpu.VMEM((heads, LANES), BF16),
        pltpu.VMEM((length, LANES), BF16),
        pltpu.VMEM((heads, width), BF16),
        pltpu.VMEM((16, heads), F32),
    ]
    scratch += [pltpu.VMEM((length, heads), F32)] * 4 + [pltpu.VMEM((length, heads), BF16)] * 4
    if through:
        attend_in, rows, gain, collective_id = through
        operands += [attend_in, rows, gain[None]]
        in_specs += [pl.BlockSpec(memory_space=pl.ANY)] * 2 + [vmem]
        shapes = jax.ShapeDtypeStruct(rows.shape, F32)
        out_specs = vmem
        each = pltpu.SemaphoreType.DMA((width // LANES, 2))
        scratch = (
            [pltpu.VMEM((own, 2 * width), F32)] * 3
            + [each, each, pltpu.VMEM((width, heads) if want_queries else (8, LANES), F32)]
            + [pltpu.VMEM(attend_in.shape, BF16), pltpu.VMEM(rows.shape, F32)]
            + [pltpu.SemaphoreType.DMA((2,))]
            + scratch
        )
        params = pltpu.CompilerParams(
            collective_id=collective_id, has_side_effects=True, vmem_limit_bytes=46 * MIB
        )
    else:
        shapes = [jax.ShapeDtypeStruct(pair.shape, F32) for pair in pairs]
        if want_queries:
            shapes.append(jax.ShapeDtypeStruct((width, heads), BF16))
        out_specs = [vmem] * len(shapes)
        params = pltpu.CompilerParams(vmem_limit_bytes=34 * MIB)
    return pl.pallas_call(
        functools.partial(
            attend_back_kernel, plan, parts, decoder, want_queries, through is not None
        ),
        out_shape=shapes,
        in_specs=in_specs,
        out_specs=out_specs,
        scratch_shapes=scratch,
        compiler_params=params,
        cost_estimate=pl.CostEstimate(
            flops=80 * heads * length * width, bytes_accessed=20 * own * width, transcendentals=0
        ),
    )(*operands)


def feed_kernel(rows_ref, gain_ref, one_ref, two_ref, out_ref, before_ref, source, *scratch):
    held_of, active_of = scratch[0:2], scratch[2:4]
    count = one_ref.shape[1] // HIDDEN_PIECE
    rows = rows_ref[...]
    source[...] = normed(rows, gain_ref[...])[0].astype(BF16)
    out_ref[...] = rows
    for n in range(count + 2):
        if n < count:
            here = slice(n * HIDDEN_PIECE, (n + 1) * HIDDEN_PIECE)
            before = dot(source[...], one_ref[:, here])
            held_of[n % 2][...] = before
            before_ref[:, here] = before
        if 0 < n <= count:
            active_of[(n - 1) % 2][...] = smooth(held_of[(n - 1) % 2][...]).astype(BF16)
        if n >= 2:
            there = slice((n - 2) * HIDDEN_PIECE, (n - 1) * HIDDEN_PIECE)
            out_ref[...] += dot(active_of[n % 2][...], two_ref[there, :])


def feed(rows, gain, one, two):
    own, width = rows.shape
    hidden = one.shape[1]
    vmem = pl.BlockSpec(memory_space=pltpu.VMEM)
    return pl.pallas_call(
        feed_kernel,
        out_shape=[
            jax.ShapeDtypeStruct((own, width), F32),
            jax.ShapeDtypeStruct((own, hidden), F32),
        ],
        in_specs=[vmem] * 4,
        out_specs=[vmem] * 2,
        scratch_shapes=[pltpu.VMEM((own, width), BF16)]
        + [pltpu.VMEM((own, HIDDEN_PIECE), F32)] * 2
        + [pltpu.VMEM((own, HIDDEN_PIECE), BF16)] * 2,
        compiler_params=pltpu.CompilerParams(vmem_limit_bytes=28 * MIB),
        cost_estimate=pl.CostEstimate(
            flops=4 * own * width * hidden, bytes_accessed=4 * width * hidden, transcendentals=0
        ),
    )(rows, gain[None], one, two)


def smooth_slope(u):
    rate = (2.0 / jnp.pi) ** 0.5
    bend = jnp.tanh(rate * (u + 0.044715 * (u * u * u)))
    inner = rate * (1.0 + 3.0 * 0.044715 * (u * u))
    return 0.5 * (1.0 + bend) + 0.5 * u * (1.0 - bend * bend) * inner


def feed_back_kernel(grad_ref, rows_ref, gain_ref, before_ref, one_ref, two_ref, out_ref, low, *scratch):
    active_of, step_of = scratch[0:2], scratch[2:4]
    count = one_ref.shape[1] // HIDDEN_PIECE
    low[...] = grad_ref[...].astype(BF16)
    out_ref[...] = jnp.zeros_like(out_ref)
    for n in range(count + 2):
        if n < count:
            here = slice(n * HIDDEN_PIECE, (n + 1) * HIDDEN_PIECE)
            active_of[n % 2][...] = dot_rows(low[...], two_ref[here, :])
        if 0 < n <= count:
            here = slice((n - 1) * HIDDEN_PIECE, n * HIDDEN_PIECE)
            step_of[(n - 1) % 2][...] = (
                active_of[(n - 1) % 2][...] * smooth_slope(before_ref[:, here])
            ).astype(BF16)
        if n >= 2:
            here = slice((n - 2) * HIDDEN_PIECE, (n - 1) * HIDDEN_PIECE)
            out_ref[...] += dot_rows(step_of[n % 2][...], one_ref[:, here])
    rows = rows_ref[...]
    inverse = lax.rsqrt(jnp.mean(rows * rows, -1, keepdims=True) + NORM_EPS)
    out_ref[...] = grad_ref[...] + normed_back(rows, gain_ref[...], inverse, out_ref[...])


def feed_back(gradient, rows, gain, before, one, two):
    own, width = rows.shape
    hidden = one.shape[1]
    vmem = pl.BlockSpec(memory_space=pltpu.VMEM)
    return pl.pallas_call(
        feed_back_kernel,
        out_shape=jax.ShapeDtypeStruct((own, width), F32),
        in_specs=[vmem] * 6,
        out_specs=vmem,
        scratch_shapes=[pltpu.VMEM((own, width), BF16)]
        + [pltpu.VMEM((own, HIDDEN_PIECE), F32)] * 2
        + [pltpu.VMEM((own, HIDDEN_PIECE), BF16)] * 2,
        compiler_params=pltpu.CompilerParams(vmem_limit_bytes=30 * MIB),
        cost_estimate=pl.CostEstimate(
            flops=4 * own * width * hidden, bytes_accessed=4 * width * hidden, transcendentals=0
        ),
    )(gradient, rows, gain[None], before, one, two)


def prompted(plan, rows_ref, prompt_ref, lengths_ref, tasks_ref):
    info = row_scalars(plan, lengths_ref, False)
    m = lax.axis_index("vocab") // plan.group
    shape = (plan.own, LANES)
    position = row_positions(info, shape, 0)
    lane = lax.broadcasted_iota(jnp.int32, shape, 1)
    begin = jnp.where(position >= info[1], info[1], jnp.where(position >= info[0], info[0], 0))
    place = position - begin
    total = None
    for j, start in enumerate([0, info[0], info[1]]):
        hit = (begin == start) & (place == lane) & (place < P_SIZE)
        term = dot_rows(jnp.where(hit, 1.0, 0.0).astype(BF16), prompt_ref[tasks_ref[m, j]])
        total = term if total is None else total + term
    return jnp.where(place[:, 0:1] < P_SIZE, total, rows_ref[...].astype(F32))


def project_kernel(plan, *refs):
    rows_ref, prompt_ref, keys_ref, heads_ref, gain_ref, lengths_ref, tasks_ref = refs[:7]
    first_hbm, second_hbm, out_ref, enc_q, enc_own, enc_other, dec_q, dec_own, dec_other = refs[7:16]
    first, second, sems, send_sem, recv_sem = refs[16:]
    width = rows_ref.shape[1]
    v = lax.axis_index("vocab")
    twin = {"vocab": v // 2 * 2 + 1 - lax.rem(v, 2)}
    barrier = pltpu.get_barrier_semaphore()
    pl.semaphore_signal(barrier, inc=1, device_id=twin, device_id_type=pl.DeviceIdType.MESH)
    pl.semaphore_wait(barrier, 1)
    loads = [
        pltpu.make_async_copy(first_hbm, first, sems.at[0]),
        pltpu.make_async_copy(second_hbm, second, sems.at[1]),
    ]
    for load in loads:
        load.start()

    def share(source, target, index):
        return pltpu.make_async_remote_copy(
            src_ref=source,
            dst_ref=target,
            send_sem=send_sem.at[index],
            recv_sem=recv_sem.at[index],
            device_id=twin,
            device_id_type=pl.DeviceIdType.MESH,
        )

    shares = [share(enc_own, enc_other, 0), share(dec_own, dec_other, 1)]
    rows = prompted(plan, rows_ref, prompt_ref, lengths_ref, tasks_ref)
    out_ref[...] = rows
    low = normed(rows, gain_ref[...])[0].astype(BF16)
    loads[0].wait()
    enc_own[...] = dot(low, first[:, width:]).astype(BF16)
    shares[0].start()
    enc_q[...] = dot(low, first[:, :width]).astype(BF16)
    loads[1].wait()
    dec_own[...] = dot(keys_ref[...], second[:, width:]).astype(BF16)
    shares[1].start()
    dec_q[...] = dot(heads_ref[...], second[:, :width]).astype(BF16)
    for copy in shares:
        copy.wait()


def project(plan, rows, prompts, keys, heads, gain, row_lengths, row_tasks, first, second):
    width = rows.shape[1]
    vmem, smem = pl.BlockSpec(memory_space=pltpu.VMEM), pl.BlockSpec(memory_space=pltpu.SMEM)
    anywhere = pl.BlockSpec(memory_space=pl.ANY)
    pair = jax.ShapeDtypeStruct((plan.own, 2 * width), BF16)
    outs = pl.pallas_call(
        functools.partial(project_kernel, plan),
        out_shape=[
            jax.ShapeDtypeStruct(rows.shape, F32),
            jax.ShapeDtypeStruct(rows.shape, BF16),
            pair,
            pair,
            jax.ShapeDtypeStruct(heads.shape, BF16),
            pair,
            pair,
        ],
        in_specs=[vmem] * 5 + [smem] * 2 + [anywhere] * 2,
        out_specs=[vmem] * 7,
        scratch_shapes=[pltpu.VMEM(first.shape, BF16)] * 2 + [pltpu.SemaphoreType.DMA((2,))] * 3,
        compiler_params=pltpu.CompilerParams(
            collective_id=5, has_side_effects=True, vmem_limit_bytes=40 * MIB
        ),
        cost_estimate=pl.CostEstimate(
            flops=10 * rows.size * width, bytes_accessed=4 * first.size, transcendentals=0
        ),
    )(rows, prompts, keys, heads, gain[None], row_lengths, row_tasks, first, second)
    return outs[0], outs[1], outs[2:4], outs[4], outs[5:7]


def vocab_kernel(tile, valid, h_ref, target_ref, table_hbm, grad_ref, stat_ref, table, sem):
    padded = table.shape[0]

    @pl.when(pl.program_id(0) == 0)
    def _():
        copy = pltpu.make_async_copy(table_hbm, table.at[pl.ds(0, valid), :], sem)
        copy.start()
        if padded > valid:
            table[valid:, :] = jnp.zeros((padded - valid, table.shape[1]), BF16)
        copy.wait()

    rows = h_ref.shape[0]
    hidden = h_ref[...]
    column = lax.broadcasted_iota(jnp.int32, (rows, tile), 1)
    target = target_ref[...]

    def block(at, carry, last):
        maxima, total = carry
        part = table[pl.ds(pl.multiple_of(at * tile, tile), tile), :]
        logits = dot_rows(hidden, part)
        if last and padded > valid:
            logits = jnp.where(column < valid - (padded - tile), logits, MASKED)
        highest = jnp.maximum(maxima, jnp.max(logits, -1, keepdims=True))
        powers = jnp.exp(logits - highest)
        scale = jnp.exp(maxima - highest)
        total = total * scale + jnp.sum(powers, -1, keepdims=True)
        powers = jnp.where(column == target - at * tile, 0.0, powers).astype(BF16)
        grad_ref[...] = grad_ref[...] * scale + dot(powers, part)
        return (highest, total)

    grad_ref[...] = jnp.zeros_like(grad_ref)
    blocks = padded // tile
    carry = (jnp.full((rows, 1), MASKED, F32), jnp.zeros((rows, 1), F32))
    carry = lax.fori_loop(0, blocks - 1, lambda at, c: block(at, c, False), carry)
    maxima, total = block(blocks - 1, carry, True)
    lane = lax.broadcasted_iota(jnp.int32, stat_ref.shape, 1)
    stat_ref[...] = jnp.where(lane == 0, maxima, total)


def vocab_pass(hidden, target_local, embedding, rows):
    count, width = hidden.shape
    valid = embedding.shape[0]
    tile = VOCAB_BLOCK
    padded = (valid + tile - 1) // tile * tile
    return pl.pallas_call(
        functools.partial(vocab_kernel, tile, valid),
        grid=(count // rows,),
        out_shape=[
            jax.ShapeDtypeStruct((count, width), F32),
            jax.ShapeDtypeStruct((count, LANES), F32),
        ],
        in_specs=[
            pl.BlockSpec((rows, width), lambda i: (i, 0)),
            pl.BlockSpec((rows, 1), lambda i: (i, 0)),
            pl.BlockSpec(memory_space=pl.ANY),
        ],
        out_specs=[
            pl.BlockSpec((rows, width), lambda i: (i, 0)),
            pl.BlockSpec((rows, LANES), lambda i: (i, 0)),
        ],
        scratch_shapes=[pltpu.VMEM((padded, width), BF16), pltpu.SemaphoreType.DMA],
        compiler_params=pltpu.CompilerParams(vmem_limit_bytes=56 * MIB),
        cost_estimate=pl.CostEstimate(
            flops=4 * count * padded * width, bytes_accessed=2 * valid * width, transcendentals=0
        ),
    )(hidden, target_local, embedding)


def gather_kernel(plan, rows_z, rows_y, *refs):
    in_ref, out_ref, expand_ref, reduce_ref, wanted_ref, table_hbm, lengths_ref, gain_ref = refs[:8]
    in_full, out_full, expand_full, reduce_full = refs[8:11], refs[11:14], refs[14:16], refs[16:18]
    enc_rows, dec_keys, dec_rows, dec_heads, target_rows = refs[18:23]
    found_ref, table_low, table, stage, far, near, sister, from_core, from_x, from_sister = refs[23:33]
    send_sem, recv_sem, local_sem, table_sem = refs[33:]
    at, v = lax.axis_index("dp"), lax.axis_index("vocab")
    z, y, x, core = at // rows_y, lax.rem(at, rows_y), v // 2, lax.rem(v, 2)
    top = rows_z - 1
    above = {"dp": jnp.minimum(z + 1, top) * rows_y + y, "vocab": v}
    below = {"dp": jnp.maximum(z - 1, 0) * rows_y + y, "vocab": v}
    beside = {"dp": z * rows_y + (1 - y), "vocab": v}
    other_x = (1 - x) * 2 + core
    across = {"dp": at, "vocab": other_x}
    twin = {"dp": at, "vocab": x * 2 + (1 - core)}

    barrier = pltpu.get_barrier_semaphore()

    def greet(peer):
        pl.semaphore_signal(barrier, inc=1, device_id=peer, device_id_type=pl.DeviceIdType.MESH)

    pl.when(z < top)(lambda: greet(above))
    pl.when(z > 0)(lambda: greet(below))
    greet(beside)
    greet(across)
    greet(twin)
    inner = jnp.logical_and(z > 0, z < top)
    pl.when(inner)(lambda: pl.semaphore_wait(barrier, 5))
    pl.when(jnp.logical_not(inner))(lambda: pl.semaphore_wait(barrier, 4))

    names, tallies = {}, [0, 0]

    def remote(name, source, target, peer):
        if name not in names:
            names[name] = tallies[0]
            tallies[0] += 1
        return pltpu.make_async_remote_copy(
            src_ref=source,
            dst_ref=target,
            send_sem=send_sem.at[names[name]],
            recv_sem=recv_sem.at[names[name]],
            device_id=peer,
            device_id_type=pl.DeviceIdType.MESH,
        )

    def local(source, target):
        copy = pltpu.make_async_copy(source, target, local_sem.at[tallies[1]])
        tallies[1] += 1
        copy.start()
        return copy

    def columns(ref, full, index, blocks):
        wide = ref.shape[2] // blocks
        here = lambda b: pl.ds(pl.multiple_of(b * wide, wide), wide)
        return (
            lambda b: ref.at[index, :, here(b)],
            lambda zs, ys, b: full.at[zs, ys, :, here(b)],
            lambda ys, b: full.at[:, ys, :, here(b)],
            blocks == 4,
        )

    def row_blocks(ref, full, index):
        count = ref.shape[1] // 4
        return (
            lambda b: ref.at[index, pl.ds(pl.multiple_of(b * count, count), count), :],
            lambda zs, ys, b: full.at[zs, ys, b],
            lambda ys, b: full.at[:, ys, b],
            True,
        )

    def attention(j):
        return [columns(in_ref, in_full[j], j, 2), columns(out_ref, out_full[j], j, 2)]

    def feed(j):
        return [columns(expand_ref, expand_full[j], j, 4), row_blocks(reduce_ref, reduce_full[j], j)]

    waves = [feed(0) + attention(0), feed(1) + attention(1) + attention(2)]
    units = [u for wave in waves for u in wave]
    starts = [0, len(waves[0]), len(units)]
    blocks = [v if u[3] else core for u in units]
    sides = (("up", -1), ("down", 1))

    def there(side, k):
        return z - k >= 0 if side == "up" else z + k <= top

    def further(side):
        return z < top if side == "up" else z > 0

    def begin(i):
        source, target, _, quarter = units[i]
        b = blocks[i]
        piece = target(z, y, b)
        pl.when(z < top)(lambda: remote((i, "up", 1), source(b), piece, above).start())
        pl.when(z > 0)(lambda: remote((i, "down", 1), source(b), piece, below).start())
        remote((i, "y", 0), source(b), piece, beside).start()
        copies = [local(source(b), piece)]
        if quarter:
            copies.append(local(source(other_x), target(z, y, other_x)))
        return copies

    def step(i, k):
        _, target, _, quarter = units[i]
        for side, sign in sides:

            @pl.when(there(side, k))
            def _():
                piece = target(z + sign * k, y, blocks[i])
                remote((i, side, k), piece, piece, above).wait_recv()
                if k < top:

                    @pl.when(further(side))
                    def _():
                        peer = above if side == "up" else below
                        remote((i, side, k + 1), piece, piece, peer).start()

                remote((i, side, k, "y"), piece, piece, beside).start()
                if quarter:
                    remote((i, side, k, "x"), piece, piece, across).start()

    def came(i, k):
        _, target, _, quarter = units[i]
        if k == 0:
            piece = target(z, 1 - y, blocks[i])
            remote((i, "y", 0), piece, piece, beside).wait_recv()
            if quarter:
                remote((i, "yx", 0), piece, piece, across).start()
            return
        for side, sign in sides:

            @pl.when(there(side, k))
            def _():
                piece = target(z + sign * k, 1 - y, blocks[i])
                remote((i, side, k, "y"), piece, piece, beside).wait_recv()
                if quarter:
                    remote((i, side, k, "yx"), piece, piece, across).start()

    def to_twin(i, column, b, tag):
        block = units[i][2](column, b)
        remote((i, "core", tag), block, block, twin).start()

    def spread(i):
        for copy in locals_[i]:
            copy.wait()
        to_twin(i, y, blocks[i], 0)

    def spread_beside(i):
        to_twin(i, 1 - y, blocks[i], 1)

    def x_came(i, tag):
        _, target, _, _ = units[i]
        if tag == "yx":
            piece = target(z, 1 - y, other_x)
            remote((i, "yx", 0), piece, piece, across).wait_recv()
        for k in range(1, rows_z):
            for side, sign in sides:

                @pl.when(there(side, k))
                def _():
                    piece = target(z + sign * k, y if tag == "x" else 1 - y, other_x)
                    remote((i, side, k, tag), piece, piece, across).wait_recv()

        to_twin(i, y if tag == "x" else 1 - y, other_x, 2 if tag == "x" else 3)

    valid, width = table_low.shape
    share = far.shape[0]
    table_copy = pltpu.make_async_copy(table_hbm, table_low, table_sem)
    table_copy.start()

    def widen(at, _):
        here = pl.ds(pl.multiple_of(at * 32, 32), 32)
        table[here, :] = table_low[here, :].astype(F32)
        return 0

    def prepare():
        table_copy.wait()
        table[valid:, :] = jnp.zeros((table.shape[0] - valid, width), F32)
        lax.fori_loop(0, valid // 32, widen, 0)

    def look_up(target, owner, part):
        count = stage.shape[0]

        def rows(at, _):
            for step in range(8):
                i = at * 8 + step
                row = wanted_ref[owner, part * count + i]
                stage[pl.ds(i, 1), :] = table[pl.ds(row, 1), :]
            return 0

        lax.fori_loop(0, count // 8, rows, 0)
        target[part * count : (part + 1) * count, :] = stage[...].astype(BF16)

    sums = {
        "far": remote("far", far, from_core, twin),
        "near": remote("near", near, from_x, across),
        "sister": remote("sister", sister, from_sister, twin),
    }

    def send_far():
        sums["far"].start()

    def send_near():
        sums["far"].wait_recv()
        near[...] = (near[...].astype(F32) + from_core[...].astype(F32)).astype(BF16)
        sums["near"].start()

    def send_sister():
        sums["sister"].start()

    def finish_rows():
        sums["sister"].wait_recv()
        sums["near"].wait_recv()
        total = found_ref[...].astype(F32) + from_sister[...].astype(F32)
        table[:share, :] = total + from_x[...].astype(F32)
        enc_rows[...] = table[: plan.own, :].astype(BF16)
        ends = [lengths_ref[x, 0], lengths_ref[x, 0] + lengths_ref[x, 1]]
        position = lax.broadcasted_iota(jnp.int32, (plan.held, 1), 0) + chosen(core, plan.starts)
        first_of = (position == 0) | (position == ends[0]) | (position == ends[1])
        base, held = plan.own + HALO, 2 * plan.own + plan.held
        table[held : held + plan.held, :] = jnp.where(
            first_of,
            table[plan.own : plan.own + 1, :],
            table[base - 1 : base - 1 + plan.held, :],
        )
        shift = held + core * (plan.own - plan.starts[1])
        keys = table[pl.ds(pl.multiple_of(shift, HALO), plan.own), :]
        gain = gain_ref[...]
        dec_keys[...] = normed(keys, gain)[0].astype(BF16)
        before_turn = lax.broadcasted_iota(jnp.int32, (plan.heads, 1), 0) < turn_of(
            plan, lengths_ref, x, core
        )

        def own_heads(first):
            def rows(offsets):
                first_place, second_place = [
                    table[first + o - s : first + o - s + plan.heads, :]
                    for o, s in zip(offsets, plan.starts)
                ]
                return jnp.where(core == 0, first_place, second_place)

            return jnp.where(before_turn, rows(plan.near), rows(plan.far))

        values = own_heads(held)
        dec_rows[...] = values.astype(BF16)
        dec_heads[...] = normed(values, gain)[0].astype(BF16)
        target_rows[...] = own_heads(base).astype(BF16)

    jobs = [prepare]
    for target, owner, after in (
        (far, (1 - x) * 2 + 1 - core, send_far),
        (near, other_x, send_near),
        (sister, x * 2 + 1 - core, send_sister),
        (found_ref, v, None),
    ):
        for part in range(share // stage.shape[0]):
            jobs.append(functools.partial(look_up, target, owner, part))
        if after:
            jobs.append(after)
    jobs = jobs[::-1]

    def work(count):
        for _ in range(min(count, len(jobs))):
            jobs.pop()()

    first, second = range(starts[0], starts[1]), range(starts[1], starts[2])
    locals_ = {}

    def each(action, wave, *rest):
        for i in wave:
            action(i, *rest)

    for i in first:
        locals_[i] = begin(i)
    locals_[second[0]] = begin(second[0])
    work(2)
    each(step, first, 1)
    for i in second[1:]:
        locals_[i] = begin(i)
    work(2)
    each(came, first, 0)
    work(2)
    each(step, first, 2)
    work(1)
    each(came, first, 1)
    work(2)
    each(step, second, 1)
    work(2)
    each(step, first, 3)
    each(spread, first)
    work(2)
    each(came, first, 2)
    work(2)
    each(step, second, 2)
    work(1)
    each(came, second, 0)
    work(len(jobs))
    for i in first:
        came(i, 3)
        spread_beside(i)
    each(came, second, 1)
    each(step, second, 3)
    each(spread, second)
    for i in first:
        if units[i][3]:
            x_came(i, "x")
    each(came, second, 2)
    finish_rows()
    for i in first:
        if units[i][3]:
            x_came(i, "yx")
    for i in second:
        came(i, 3)
        spread_beside(i)
    for i in second:
        if units[i][3]:
            x_came(i, "x")
            x_came(i, "yx")
    for copy in sums.values():
        copy.wait_send()

    for i, (source, target, whole, quarter) in enumerate(units):
        b = blocks[i]
        for tag in range(4 if quarter else 2):
            block = whole(y, b)
            remote((i, "core", tag), block, block, twin).wait()
        piece = target(z, y, b)
        remote((i, "y", 0), piece, piece, beside).wait_send()
        if quarter:
            remote((i, "yx", 0), piece, piece, across).wait_send()
        for k in range(1, rows_z):
            for side, sign in sides:
                sent = there(side, k - 1) if k > 1 else True
                pl.when(jnp.logical_and(sent, further(side)))(
                    lambda: remote((i, side, k), piece, piece, above).wait_send()
                )

                @pl.when(there(side, k))
                def _():
                    remote((i, side, k, "y"), piece, piece, beside).wait_send()
                    if quarter:
                        remote((i, side, k, "x"), piece, piece, across).wait_send()
                        remote((i, side, k, "yx"), piece, piece, across).wait_send()


def gather_weights(
    plan, attend_in, attend_out, expand_weights, reduce_weights, wanted, table, row_lengths, gain
):
    shards, rows_y = 8, 2
    rows_z = shards // rows_y
    rows = attend_in.shape[1]
    width = rows * shards
    tall = reduce_weights.shape[1]
    share = wanted.shape[1]
    valid = table.shape[0]

    def full(*tail):
        return jax.ShapeDtypeStruct((rows_z, rows_y, *tail), BF16)

    shapes = (
        [full(rows, attend_in.shape[2])] * 3
        + [full(rows, attend_out.shape[2])] * 3
        + [full(rows, expand_weights.shape[2])] * 2
        + [full(4, tall // 4, width)] * 2
        + [jax.ShapeDtypeStruct((n, width), BF16) for n in [plan.own] * 2 + [plan.heads] * 3]
    )
    copies = 10 * (1 + 4 * (rows_z - 1) + 2) + 4 * (1 + 4 * (rows_z - 1) + 2) + 3
    anywhere, vmem, smem = [
        pl.BlockSpec(memory_space=space) for space in (pl.ANY, pltpu.VMEM, pltpu.SMEM)
    ]
    outs = pl.pallas_call(
        functools.partial(gather_kernel, plan, rows_z, rows_y),
        out_shape=shapes,
        in_specs=[anywhere] * 4 + [smem, anywhere, smem, vmem],
        out_specs=[anywhere] * 10 + [vmem] * 5,
        scratch_shapes=[
            pltpu.VMEM((share, width), BF16),
            pltpu.VMEM((valid, width), BF16),
            pltpu.VMEM((valid + 8, width), F32),
            pltpu.VMEM((share // 3, width), F32),
        ]
        + [pltpu.VMEM((share, width), BF16)] * 6
        + [
            pltpu.SemaphoreType.DMA((copies,)),
            pltpu.SemaphoreType.DMA((copies,)),
            pltpu.SemaphoreType.DMA((14,)),
            pltpu.SemaphoreType.DMA,
        ],
        compiler_params=pltpu.CompilerParams(
            collective_id=0, has_side_effects=True, vmem_limit_bytes=60 * MIB
        ),
        cost_estimate=pl.CostEstimate(flops=0, bytes_accessed=400_000_000, transcendentals=0),
    )(attend_in, attend_out, expand_weights, reduce_weights, wanted, table, row_lengths, gain[None])
    return [o.reshape(-1, o.shape[-1]) for o in outs]


def vocab_exchange_kernel(plan, tile, *refs):
    rows_ref, gain_ref, target_ref, table_ref, ids_ref, lengths_ref, tasks_ref = refs[:7]
    grad_ref, stat_ref, *scratch = refs[7:]
    tail, held, logits_a, logits_b, powers_a, powers_b, scale_a, scale_b = scratch[:8]
    maxima_ref, total_ref, targets_ref, h_ref, columns, parcel, arrived = scratch[8:15]
    stats_out, stats_in, send_sem, recv_sem = scratch[15:]
    rows, width = h_ref.shape
    valid = table_ref.shape[0]
    tiles = (valid + tile - 1) // tile
    padded = tiles * tile
    v = lax.axis_index("vocab")
    x, core = v // 2, lax.rem(v, 2)
    twin, across, diagonal = x * 2 + 1 - core, (1 - x) * 2 + core, (1 - x) * 2 + 1 - core

    barrier = pltpu.get_barrier_semaphore()
    for peer in (twin, across, diagonal):
        pl.semaphore_signal(
            barrier, inc=1, device_id={"vocab": peer}, device_id_type=pl.DeviceIdType.MESH
        )
    pl.semaphore_wait(barrier, 3)

    def remote(source, target, index, peer):
        return pltpu.make_async_remote_copy(
            src_ref=source,
            dst_ref=target,
            send_sem=send_sem.at[index],
            recv_sem=recv_sem.at[index],
            device_id={"vocab": peer},
            device_id_type=pl.DeviceIdType.MESH,
        )

    values = rows_ref[...]
    gain = gain_ref[...]
    inverse = lax.rsqrt(jnp.mean(values * values, -1, keepdims=True) + NORM_EPS)
    h_ref[...] = (values * inverse * gain * width ** (-0.5)).astype(BF16)
    to_twin = remote(h_ref, held.at[0], 0, twin)
    to_across = remote(h_ref, held.at[1], 1, across)
    passed_on = remote(held.at[1], held.at[2], 2, twin)
    results = [
        remote(parcel.at[k], arrived.at[k], 3 + k, peer)
        for k, peer in enumerate((twin, across, diagonal))
    ]
    marks = [
        remote(stats_out.at[k], stats_in.at[k], 6 + k, peer)
        for k, peer in enumerate((twin, across, diagonal))
    ]
    to_twin.start()
    to_across.start()
    held[3] = h_ref[...]

    entry = lax.broadcasted_iota(jnp.int32, (8, rows), 1)
    even = lax.rem(lax.broadcasted_iota(jnp.int32, (8, rows), 0), 2) == 0
    for place in range(plan.group):
        turns = [turn_of(plan, lengths_ref, m, place) for m in range(2)]
        near, far = plan.near[place], plan.far[place]
        picked = jnp.where(
            entry < jnp.where(even, turns[0], turns[1]),
            ids_ref[:, near : near + rows],
            ids_ref[:, far : far + rows],
        )
        columns[place] = jnp.transpose(picked)

    short = padded - valid
    if short:
        tail[: tile - short, :] = table_ref[padded - tile :, :]
        tail[tile - short :, :] = jnp.zeros((short, width), BF16)
    to_twin.wait_recv()

    logits_of, powers_of, scale_of = (logits_a, logits_b), (powers_a, powers_b), (scale_a, scale_b)
    column = lax.broadcasted_iota(jnp.int32, (rows, tile), 1)
    lane = lax.broadcasted_iota(jnp.int32, (rows, LANES), 1)

    def turn(k, _):
        @pl.when(k == 1)
        def _():
            to_across.wait_recv()
            passed_on.start()

        @pl.when(k == 2)
        def _():
            passed_on.wait_recv()

        owner = jnp.where(k == 0, twin, jnp.where(k == 1, across, jnp.where(k == 2, diagonal, v)))

        def part(at):
            if short and at == tiles - 1:
                return tail[...]
            return table_ref[at * tile : (at + 1) * tile, :]

        def scores(at):
            logits_of[at % 2][...] = dot_rows(held[k], part(at))

        def soften(at):
            logits = logits_of[at % 2][...]
            if at == tiles - 1 and padded > valid:
                logits = jnp.where(column < valid - at * tile, logits, MASKED)
            highest = jnp.maximum(maxima_ref[...], jnp.max(logits, -1, keepdims=True))
            powers = jnp.exp(logits - highest)
            scale = jnp.exp(maxima_ref[...] - highest)
            maxima_ref[...] = highest
            total_ref[...] = total_ref[...] * scale + jnp.sum(powers, -1, keepdims=True)
            scale_of[at % 2][...] = scale
            powers_of[at % 2][...] = jnp.where(
                column == targets_ref[...] - at * tile, 0.0, powers
            ).astype(BF16)

        def gather(at):
            term = dot(powers_of[at % 2][...], part(at))
            grad_ref[...] = grad_ref[...] * scale_of[at % 2][...] + term

        column_of = jnp.where(lax.rem(owner, 2) == 0, columns[0], columns[1])
        target = jnp.where(owner < 2, column_of[:, 0:1], column_of[:, 1:2])
        targets_ref[...] = target.astype(jnp.int32) - v * valid
        maxima_ref[...] = jnp.full((rows, 1), MASKED, F32)
        total_ref[...] = jnp.zeros((rows, 1), F32)
        grad_ref[...] = jnp.zeros_like(grad_ref)
        for at in range(tiles + 2):
            if at < tiles:
                scores(at)
            if 0 <= at - 1 < tiles:
                soften(at - 1)
            if at >= 2:
                gather(at - 2)

        @pl.when(k < 3)
        def _():
            parcel[k] = grad_ref[...].astype(BF16)
            side = lax.broadcasted_iota(jnp.int32, (rows, 8), 1)
            pair = jnp.where(side == 0, maxima_ref[...], total_ref[...])
            stats_out[k] = jnp.transpose(pair)

        for index, (mark, result) in enumerate(zip(marks, results)):

            @pl.when(k == index)
            def _():
                mark.start()
                result.start()

        return 0

    lax.fori_loop(0, 4, turn, 0)
    for copy in [*marks, *results]:
        copy.wait_recv()
    pairs = [jnp.transpose(stats_in[k]) for k in range(3)]
    highs = [pair[:, 0:1] for pair in pairs] + [maxima_ref[...]]
    totals = [pair[:, 1:2] for pair in pairs] + [total_ref[...]]
    highest = functools.reduce(jnp.maximum, highs)
    log_total = highest + jnp.log(sum(t * jnp.exp(m - highest) for m, t in zip(highs, totals)))
    summed = grad_ref[...] * jnp.exp(highs[3] - log_total)
    for k in range(3):
        summed = summed + arrived[k].astype(F32) * jnp.exp(highs[k] - log_total)
    target_rows = target_ref[...].astype(F32)
    target_logit = jnp.sum(h_ref[...].astype(F32) * target_rows, -1, keepdims=True)
    coefficient = (jnp.exp(target_logit - log_total) - 1.0).astype(BF16).astype(F32)
    info = row_scalars(plan, lengths_ref, True)
    position = row_positions(info, (rows, 1), 0)
    in_second, in_third = position >= info[0], position >= info[1]
    begin = jnp.where(in_third, info[1], jnp.where(in_second, info[0], 0))
    task = jnp.where(in_third, tasks_ref[x, 2], jnp.where(in_second, tasks_ref[x, 1], tasks_ref[x, 0]))
    counts = (position - begin >= P_SIZE) & (lax.broadcasted_iota(jnp.int32, (rows, 1), 0) < plan.half)
    column_of = jnp.where(core == 0, columns[0], columns[1])
    counted = jnp.where(counts, jnp.where(x == 0, column_of[:, 2:3], column_of[:, 3:4]), 0.0)
    summed = counted * (summed + coefficient * target_rows)
    grad_ref[...] = normed_back(rows_ref[...], gain_ref[...], inverse, summed * width ** (-0.5))
    of_task = jnp.where(lane == task, counted, 0.0)
    losses = jnp.sum(of_task * (log_total - target_logit), 0, keepdims=True)
    counts = jnp.sum(of_task, 0, keepdims=True)
    row = lax.broadcasted_iota(jnp.int32, stat_ref.shape, 0)
    stat_ref[...] = jnp.where(row == 0, losses, jnp.where(row == 1, counts, 0.0))
    for copy in [to_twin, to_across, passed_on, *marks, *results]:
        copy.wait_send()


def vocab_exchange(plan, rows, gain, target_rows, embedding, ids, row_lengths, row_tasks):
    count, width = rows.shape
    valid = embedding.shape[0]
    tile = 2 * VOCAB_BLOCK
    padded = (valid + tile - 1) // tile * tile
    vmem = pl.BlockSpec(memory_space=pltpu.VMEM)
    return pl.pallas_call(
        functools.partial(vocab_exchange_kernel, plan, tile),
        out_shape=[
            jax.ShapeDtypeStruct((count, width), F32),
            jax.ShapeDtypeStruct((8, LANES), F32),
        ],
        in_specs=[vmem] * 5 + [pl.BlockSpec(memory_space=pltpu.SMEM)] * 2,
        out_specs=[vmem] * 2,
        scratch_shapes=[
            pltpu.VMEM((tile, width), BF16),
            pltpu.VMEM((4, count, width), BF16),
            pltpu.VMEM((count, tile), F32),
            pltpu.VMEM((count, tile), F32),
            pltpu.VMEM((count, tile), BF16),
            pltpu.VMEM((count, tile), BF16),
            pltpu.VMEM((count, 1), F32),
            pltpu.VMEM((count, 1), F32),
            pltpu.VMEM((count, 1), F32),
            pltpu.VMEM((count, 1), F32),
            pltpu.VMEM((count, 1), jnp.int32),
            pltpu.VMEM((count, width), BF16),
            pltpu.VMEM((2, count, 8), F32),
            pltpu.VMEM((3, count, width), BF16),
            pltpu.VMEM((3, count, width), BF16),
            pltpu.VMEM((3, 8, count), F32),
            pltpu.VMEM((3, 8, count), F32),
            pltpu.SemaphoreType.DMA((9,)),
            pltpu.SemaphoreType.DMA((9,)),
        ],
        compiler_params=pltpu.CompilerParams(
            collective_id=1, has_side_effects=True, vmem_limit_bytes=44 * MIB
        ),
        cost_estimate=pl.CostEstimate(
            flops=30 * count * padded * width, bytes_accessed=2 * valid * width, transcendentals=0
        ),
    )(rows, gain[None], target_rows, embedding, ids, row_lengths, row_tasks)


def reduce_kernel(rows_dp, task_ref, table_ref, stat_ref, out_ref, stats_out, squares_out, *scratch):
    cast, crossed, swap, swapped, own, outgoing, pieces, result, results = scratch[:9]
    stats, squares, send_sem, recv_sem = scratch[9:]
    features = own.shape[1]
    at, v = lax.axis_index("dp"), lax.axis_index("vocab")
    x, core = v // 2, lax.rem(v, 2)
    twin, across = x * 2 + 1 - core, (1 - x) * 2 + core
    dp_peers = [lax.rem(at + k, rows_dp) for k in range(1, rows_dp)]
    vocab_peers = [lax.rem(v + k, 4) for k in range(1, 4)]

    barrier = pltpu.get_barrier_semaphore()
    for peer in [{"vocab": p} for p in vocab_peers] + [{"dp": p} for p in dp_peers]:
        pl.semaphore_signal(barrier, inc=1, device_id=peer, device_id_type=pl.DeviceIdType.MESH)
    pl.semaphore_wait(barrier, rows_dp + 2)

    def remote(source, target, send, recv, peer):
        return pltpu.make_async_remote_copy(
            src_ref=source,
            dst_ref=target,
            send_sem=send_sem.at[send],
            recv_sem=recv_sem.at[recv],
            device_id=peer,
            device_id_type=pl.DeviceIdType.MESH,
        )

    half = 2 * features
    there = pl.ds(pl.multiple_of((1 - x) * half, half), half)
    here = pl.ds(pl.multiple_of(x * half, half), half)
    stats[0] = stat_ref[...]
    cast[...] = table_ref[there, :].astype(BF16)
    over_x = remote(cast, crossed, 0, 0, {"vocab": across})
    stat_x = remote(stats.at[0], stats.at[1], 1, 1, {"vocab": across})
    over_x.start()
    stat_x.start()
    over_x.wait_recv()
    stat_x.wait_recv()

    stats[2] = stats[0] + stats[1]
    stat_core = remote(stats.at[2], stats.at[3], 2, 2, {"vocab": twin})
    stat_core.start()
    tasks = [[task_ref[m, s] for s in range(task_ref.shape[1])] for m in range(2)]
    other = jnp.where(x == 0, 1, 0)

    def by_task(part, t):
        start = pl.multiple_of(part * features, features)
        mine = table_ref[pl.ds(pl.multiple_of(x * half + part * features, features), features), :]
        theirs = crossed[pl.ds(start, features), :].astype(F32)
        total = jnp.zeros((features, LANES), F32)
        for s in range(task_ref.shape[1]):
            lanes = slice(s * LANES, (s + 1) * LANES)
            mine_task = jnp.where(x == 0, tasks[0][s], tasks[1][s])
            their_task = jnp.where(x == 0, tasks[1][s], tasks[0][s])
            total = total + jnp.where(mine_task == t, mine[:, lanes], 0.0)
            total = total + jnp.where(their_task == t, theirs[:, lanes], 0.0)
        return total

    for t in range(TASKS):
        swap[t] = by_task(1 - core, t).astype(BF16)
    over_core = remote(swap, swapped, 3, 3, {"vocab": twin})
    over_core.start()
    for t in range(TASKS):
        own[t] = by_task(core, t)
    over_core.wait_recv()
    stat_core.wait_recv()
    stats[4 + at] = stats[2] + stats[3]
    for t in range(TASKS):
        own[t] = own[t] + swapped[t].astype(F32)
        outgoing[t] = own[t].astype(BF16)

    base = 4
    spread, tallies = [], []
    for k, peer in enumerate(dp_peers):
        spread.append(
            remote(outgoing.at[peer], pieces.at[at], base + k, base + at, {"dp": peer})
        )
        tallies.append(
            remote(
                stats.at[4 + at],
                stats.at[4 + at],
                base + rows_dp + k,
                base + rows_dp + at,
                {"dp": peer},
            )
        )
    for copy in spread + tallies:
        copy.start()
    total = own[at]
    for peer in dp_peers:
        remote(outgoing.at[peer], pieces.at[peer], base, base + peer, {"dp": peer}).wait_recv()
        total = total + pieces[peer].astype(F32)
    result[...] = total.astype(BF16)
    results[at] = result[...]
    returns = []
    for k, peer in enumerate(dp_peers):
        returns.append(
            remote(
                result,
                results.at[at],
                base + 2 * rows_dp + k,
                base + 2 * rows_dp + at,
                {"dp": peer},
            )
        )
    for copy in returns:
        copy.start()
    for peer in dp_peers:
        remote(
            stats.at[4 + peer], stats.at[4 + peer], base, base + rows_dp + peer, {"dp": peer}
        ).wait_recv()
    tally = functools.reduce(jnp.add, [stats[4 + k] for k in range(rows_dp)])
    stats_out[...] = tally
    for peer in dp_peers:
        remote(result, results.at[peer], base, base + 2 * rows_dp + peer, {"dp": peer}).wait_recv()
    for t in range(TASKS):
        scale = 1.0 / (TASKS * jnp.maximum(tally[1:2, t : t + 1], 1.0))
        scaled = results[t].astype(F32) * scale
        out_ref[t] = scaled
        squares[v, t : t + 1, :] = jnp.sum(scaled * scaled, 0, keepdims=True)
    last = base + 3 * rows_dp
    shares = [
        remote(squares.at[v], squares.at[v], last + k, last + v, {"vocab": peer})
        for k, peer in enumerate(vocab_peers)
    ]
    for copy in shares:
        copy.start()
    for peer in vocab_peers:
        remote(squares.at[peer], squares.at[peer], last, last + peer, {"vocab": peer}).wait_recv()
    squares_out[...] = squares[0] + squares[1] + squares[2] + squares[3]
    for copy in [over_x, stat_x, stat_core, over_core, *spread, *tallies, *returns, *shares]:
        copy.wait_send()


def reduce_over_devices(task_list, table, stats):
    rows_dp = lax.axis_size("dp")
    features = table.shape[0] // 4
    vmem = pl.BlockSpec(memory_space=pltpu.VMEM)
    copies = 4 + 3 * rows_dp + 4
    return pl.pallas_call(
        functools.partial(reduce_kernel, rows_dp),
        out_shape=[
            jax.ShapeDtypeStruct((TASKS, features, LANES), F32),
            jax.ShapeDtypeStruct((8, LANES), F32),
            jax.ShapeDtypeStruct((8, LANES), F32),
        ],
        in_specs=[pl.BlockSpec(memory_space=pltpu.SMEM), vmem, vmem],
        out_specs=[vmem] * 3,
        scratch_shapes=[
            pltpu.VMEM((2 * features, table.shape[1]), BF16),
            pltpu.VMEM((2 * features, table.shape[1]), BF16),
            pltpu.VMEM((TASKS, features, LANES), BF16),
            pltpu.VMEM((TASKS, features, LANES), BF16),
            pltpu.VMEM((TASKS, features, LANES), F32),
            pltpu.VMEM((TASKS, features, LANES), BF16),
            pltpu.VMEM((rows_dp, features, LANES), BF16),
            pltpu.VMEM((features, LANES), BF16),
            pltpu.VMEM((rows_dp, features, LANES), BF16),
            pltpu.VMEM((4 + rows_dp, 8, LANES), F32),
            pltpu.VMEM((4, 8, LANES), F32),
            pltpu.SemaphoreType.DMA((copies,)),
            pltpu.SemaphoreType.DMA((copies,)),
        ],
        compiler_params=pltpu.CompilerParams(
            collective_id=2, has_side_effects=True, vmem_limit_bytes=24 * MIB
        ),
    )(task_list, table, stats)


def on_device(
    tokens,
    targets,
    loss_mask,
    seg_lengths,
    task_ids,
    embedding,
    attend_in,
    attend_out,
    expand_weights,
    reduce_weights,
    norm_gains,
    prompt,
    first_moment,
    row_moment,
    column_moment,
):
    shards = lax.axis_size("vocab")
    micros, span = tokens.shape[0], tokens.shape[-1]
    length = span * shards
    group = shards // micros
    own = length // group
    me = lax.axis_index("vocab")
    micro, place = me // group, me % group
    shard_rows, width = embedding.shape
    share = prompt.shape[-1]

    def around(array, shift):
        pairs = [
            (m * group + r, m * group + (r + shift) % group)
            for m in range(micros)
            for r in range(group)
        ]
        return lax.ppermute(array, "vocab", pairs)

    ids = lax.all_gather(jnp.stack([tokens[:, 0], targets[:, 0], loss_mask[:, 0]]), "vocab")
    ids = jnp.transpose(ids, (1, 2, 0, 3)).reshape(3, micros, length)
    enc_ids = ids[0].reshape(shards, own)

    row_lengths, row_tasks = seg_lengths[:, 0], task_ids[:, 0]
    compact = group == 2 and 2 * span + 2 * P_SIZE <= length - span
    if compact:
        half = (length - SEGS * P_SIZE) // group
        extra = (half + 2 * P_SIZE - own + HALO - 1) // HALO * HALO
        heads = (half + LANES - 1) // LANES * LANES
        near, far = (P_SIZE, half + 2 * P_SIZE), (2 * P_SIZE, half + 3 * P_SIZE)
        plan = Plan(length, group, own, own + extra, heads, half, (0, own - extra), near, far)
    else:
        starts = tuple(p * own for p in range(group))
        plan = Plan(length, group, own, own, own, own, starts, starts, starts)
    held, heads, half, starts = plan.held, plan.heads, plan.half, plan.starts
    turns = [
        row_lengths[:, 0] - P_SIZE if p == 0 else length - row_lengths[:, 2] - plan.near[-1]
        for p in range(group)
    ]
    entries = jnp.arange(heads, dtype=jnp.int32)

    def of_rows(values, m, p):
        near, far = plan.near[p], plan.far[p]
        values = jnp.pad(values, (0, heads + far))
        return jnp.where(
            entries < turns[p][m], values[near : near + heads], values[far : far + heads]
        )

    everyone = [(m, p) for m in range(micros) for p in range(group)]
    dec_ids = jnp.stack(
        [
            jnp.concatenate(
                [
                    jnp.zeros((HALO - 1,), jnp.int32),
                    jnp.pad(ids[1, m], (1, 0))[starts[p] : starts[p] + 1 + held],
                ]
            )
            for m, p in everyone
        ]
    )
    first_row = me * shard_rows

    def here(wanted):
        local = wanted - first_row
        inside = (local >= 0) & (local < shard_rows)
        return local, inside

    prompt_low = jnp.swapaxes(prompt, 1, 2).astype(BF16)
    prompt_low = jnp.pad(prompt_low, ((0, 0), (0, 0), (0, LANES - P_SIZE)))
    prompt_all = lax.all_gather(prompt_low, "vocab", axis=1, tiled=True)
    lengths = lax.dynamic_index_in_dim(row_lengths, micro, 0, False)
    tasks = lax.dynamic_index_in_dim(row_tasks, micro, 0, False)
    weights = (attend_in, attend_out, expand_weights, reduce_weights)
    on_links = lax.axis_size("dp") == 8 and shards == 4 and shard_rows % 32 == 0 and compact
    if on_links:
        local, inside = here(jnp.concatenate([enc_ids, dec_ids], 1))
        wanted = jnp.where(inside, local, shard_rows)
        *flat, enc_rows, keys_low, dec_input, heads_low, target_rows = gather_weights(
            plan, *weights, wanted, embedding, row_lengths, norm_gains[3]
        )
        attend_in, attend_out = flat[:3], flat[3:6]
        expand_weights, reduce_weights = flat[6:8], flat[8:10]
        dec_input = dec_input.astype(F32)
    else:

        def lookup(wanted):
            local, inside = here(wanted.reshape(-1))
            picked = jnp.take(embedding, jnp.clip(local, 0, shard_rows - 1), axis=0)
            picked = jnp.where(inside[:, None], picked, 0)
            return lax.psum_scatter(picked, "vocab", scatter_dimension=0, tiled=True)

        enc_rows, dec_rows = lookup(enc_ids), lookup(dec_ids)
        whole = [lax.all_gather(tensor, "dp", axis=1, tiled=True) for tensor in weights]
        attend_in, attend_out, expand_weights, reduce_weights = whole
        turn = jnp.stack(turns)[place, micro]
        near_row = jnp.asarray(plan.near, jnp.int32)[place]
        far_row = jnp.asarray(plan.far, jnp.int32)[place]
        first_held = jnp.asarray(starts, jnp.int32)[place]
        head_positions = jnp.where(entries < turn, near_row, far_row) + entries
        head_positions = jnp.minimum(head_positions, length - 1)
        _, head_in_segment, head_task = layout(lengths, tasks, head_positions)
        head_mask_row = jnp.stack([of_rows(ids[2, m], m, p) for m, p in everyone])[me]
        counted = (head_mask_row * ((head_in_segment >= P_SIZE) & (entries < half))).astype(F32)

        def head_rows(values):
            values = jnp.pad(values, ((0, heads), (0, 0)))
            shape = (heads, values.shape[1])
            return jnp.where(
                (entries < turn)[:, None],
                lax.dynamic_slice(values, (near_row - first_held, 0), shape),
                lax.dynamic_slice(values, (far_row - first_held, 0), shape),
            )

        held_positions = first_held + jnp.arange(held, dtype=jnp.int32)
        begun = layout(lengths, tasks, held_positions)[1] >= 1
        dec_held = jnp.where(begun[:, None], dec_rows[HALO - 1 : HALO - 1 + held], dec_rows[:1])
        dec_keys = lax.dynamic_slice(dec_held, (place * own - first_held, 0), (own, width))
        keys_low = normed(dec_keys.astype(F32), norm_gains[3])[0].astype(BF16)
        dec_input = head_rows(dec_held).astype(F32)
        heads_low = normed(dec_input, norm_gains[3])[0].astype(BF16)
        target_rows = head_rows(dec_rows[HALO:])

    def key_parts(source, weight):
        pair = dot(source, weight).astype(BF16)
        return [pair] + [around(pair, k) for k in range(1, group)]

    positions = place * own + jnp.arange(own, dtype=jnp.int32)
    segment, in_segment, _ = layout(lengths, tasks, positions)
    is_prompt = in_segment < P_SIZE
    place_of = jnp.where(is_prompt, segment * LANES + in_segment, -1)
    chosen_place = place_of[:, None] == jnp.arange(SEGS * LANES, dtype=jnp.int32)
    chosen_low = chosen_place.astype(BF16)

    if on_links:
        enc_input, enc_queries, enc_pairs, dec_queries, dec_pairs = project(
            plan,
            enc_rows,
            prompt_all,
            keys_low,
            heads_low,
            norm_gains[0],
            row_lengths,
            row_tasks,
            attend_in[0],
            attend_in[1],
        )
    else:
        prompts = jnp.concatenate(
            [lax.dynamic_index_in_dim(prompt_all, tasks[j], 0, False) for j in range(SEGS)], 1
        )
        prompt_rows = dot_rows(chosen_low, prompts)
        enc_input = jnp.where(is_prompt[:, None], prompt_rows, enc_rows.astype(F32))
        normed_low = normed(enc_input, norm_gains[0])[0].astype(BF16)
        enc_pairs = key_parts(normed_low, attend_in[0][:, width:])
        enc_queries = dot(normed_low, attend_in[0][:, :width]).astype(BF16)
        dec_pairs = key_parts(keys_low, attend_in[1][:, width:])
        dec_queries = dot(heads_low, attend_in[1][:, :width]).astype(BF16)
    enc_mid, enc_mixed, enc_logs = attend(
        plan, enc_queries, enc_pairs, enc_input, attend_out[0], row_lengths, False, False
    )
    enc_last, enc_kept = feed(enc_mid, norm_gains[1], expand_weights[0], reduce_weights[0])
    encoded = normed(enc_last, norm_gains[2])[0].astype(BF16)
    cross_pairs = key_parts(encoded, attend_in[2][:, width:])

    dec_first = attend(
        plan, dec_queries, dec_pairs, dec_input, attend_out[1], row_lengths, True, True
    )[0]
    cross_source = normed(dec_first, norm_gains[4])[0].astype(BF16)
    cross_queries = dot(cross_source, attend_in[2][:, :width]).astype(BF16)
    dec_second, cross_mixed, cross_logs = attend(
        plan, cross_queries, cross_pairs, dec_first, attend_out[2], row_lengths, True, False
    )
    dec_last, dec_kept = feed(dec_second, norm_gains[5], expand_weights[1], reduce_weights[1])

    if on_links:
        wide = (plan.far[-1] + heads + LANES - 1) // LANES * LANES
        marks = jnp.pad(
            jnp.concatenate([ids[1], ids[2]]).astype(F32), ((0, 4), (0, wide - length))
        )
        dec_grad, stats = vocab_exchange(
            plan, dec_last, norm_gains[6], target_rows, embedding, marks, row_lengths, row_tasks
        )
    else:
        output_norm, inverse_out = normed(dec_last, norm_gains[6])
        hidden = (output_norm * width ** (-0.5)).astype(BF16)
        all_hidden = lax.all_gather(hidden, "vocab", axis=0, tiled=True)
        head_targets = jnp.concatenate([of_rows(ids[1, m], m, p) for m, p in everyone])
        target_local = head_targets[:, None] - first_row
        part, stats = vocab_pass(all_hidden, target_local, embedding, heads)
        gathered = lax.all_gather(stats[:, :2].T, "vocab")
        maxima = jnp.max(gathered[:, 0], 0)
        log_total = maxima + jnp.log(
            jnp.sum(gathered[:, 1] * jnp.exp(gathered[:, 0] - maxima), 0)
        )
        scaled = part * jnp.exp(stats[:, 0] - log_total)[:, None]
        summed = lax.psum_scatter(scaled, "vocab", scatter_dimension=0, tiled=True)
        own_total = lax.dynamic_slice(log_total, (me * heads,), (heads,))
        target_values = target_rows.astype(F32)
        target_logit = jnp.sum(hidden.astype(F32) * target_values, -1)
        coefficient = (jnp.exp(target_logit - own_total) - 1.0).astype(BF16).astype(F32)
        hidden_grad = counted[:, None] * (summed + coefficient[:, None] * target_values)
        dec_grad = normed_back(
            dec_last, norm_gains[6], inverse_out, hidden_grad * width ** (-0.5)
        )
        losses = per_task(head_task, counted * (own_total - target_logit))
        tallies = jnp.stack([losses, per_task(head_task, counted)])
        stats = jnp.zeros((8, LANES), F32).at[:2, :TASKS].set(tallies)

    def keys_back(pairs, weight):
        total = pairs[0]
        for k in range(1, group):
            total = total + around(pairs[k], group - k)
        high = total.astype(BF16)
        rest = (total - high.astype(F32)).astype(BF16)
        return dot_rows(high, weight) + dot_rows(rest, weight)

    dec_grad = feed_back(
        dec_grad, dec_second, norm_gains[5], dec_kept, expand_weights[1], reduce_weights[1]
    )
    back = attend_back(
        plan,
        cross_queries,
        cross_pairs,
        dec_grad,
        attend_out[2],
        cross_mixed,
        cross_logs,
        row_lengths,
        True,
        False,
        (attend_in[2], enc_last, norm_gains[2], 3) if on_links else None,
    )
    if on_links:
        enc_grad = back
    else:
        inverse_last = normed(enc_last, norm_gains[2])[1]
        enc_grad = normed_back(
            enc_last, norm_gains[2], inverse_last, keys_back(back, attend_in[2][:, width:])
        )
    enc_grad = feed_back(
        enc_grad, enc_mid, norm_gains[1], enc_kept, expand_weights[0], reduce_weights[0]
    )
    back = attend_back(
        plan,
        enc_queries,
        enc_pairs,
        enc_grad,
        attend_out[0],
        enc_mixed,
        enc_logs,
        row_lengths,
        False,
        True,
        (attend_in[0], enc_input, norm_gains[0], 4) if on_links else None,
    )
    if on_links:
        enc_grad = back
    else:
        *back, back_queries = back
        source_grad = keys_back(back, attend_in[0][:, width:]) + lax.dot_general(
            back_queries,
            attend_in[0][:, :width],
            (((0,), (1,)), ((), ())),
            preferred_element_type=F32,
        )
        inverse_in = normed(enc_input, norm_gains[0])[1]
        enc_grad = enc_grad + normed_back(enc_input, norm_gains[0], inverse_in, source_grad)

    high = enc_grad.astype(BF16)
    rest = (enc_grad - high.astype(F32)).astype(BF16)
    table = dot_columns(high, chosen_low) + dot_columns(rest, chosen_low)
    if on_links:
        gradient, stats, squares = reduce_over_devices(row_tasks, table, stats)
        full_grad = jnp.swapaxes(gradient[:, :, :P_SIZE], 1, 2)
        row_squares = squares[:, :P_SIZE]
        task_scale = 1.0 / (TASKS * jnp.maximum(stats[1, :TASKS], 1.0))
    else:
        hits = (tasks[:, None] == jnp.arange(TASKS, dtype=jnp.int32)).astype(F32)
        by_task = jnp.einsum(
            "fsp,st->tpf",
            table.reshape(width, SEGS, LANES)[:, :, :P_SIZE],
            hits,
            precision=lax.Precision.HIGHEST,
        )
        stats = lax.psum(stats, ("dp", "vocab"))
        gradient = lax.psum_scatter(by_task, "vocab", scatter_dimension=2, tiled=True)
        task_scale = 1.0 / (TASKS * jnp.maximum(stats[1, :TASKS], 1.0))
        full_grad = lax.psum(gradient, "dp") * task_scale[:, None, None]
        row_squares = jnp.sum(lax.all_gather(jnp.sum(full_grad * full_grad, -1), "vocab"), 0)
    loss_mean = jnp.sum(stats[0, :TASKS] * task_scale)
    grad_norm = jnp.sqrt(jnp.sum(row_squares))
    clip = CLIP_NORM / jnp.maximum(grad_norm, CLIP_NORM)
    prompt_grad = full_grad * clip
    row_second = BETA_TWO * row_moment + (1.0 - BETA_TWO) * (
        row_squares * clip * clip / width + SQUARE_EPS
    )
    column_second = BETA_TWO * column_moment + (1.0 - BETA_TWO) * (
        jnp.mean(prompt_grad * prompt_grad, 1) + SQUARE_EPS
    )
    new_moment = BETA_ONE * first_moment + (1.0 - BETA_ONE) * prompt_grad
    estimate = (
        row_second[:, :, None] * column_second[:, None, :] / jnp.mean(row_second, -1)[:, None, None]
    )
    update = new_moment / (1.0 - BETA_ONE**STEP) / jnp.sqrt(estimate / (1.0 - BETA_TWO**STEP))
    new_prompt = prompt - LEARN_RATE * (update + WEIGHT_DECAY * prompt)
    return (loss_mean, grad_norm, prompt_grad, new_moment, row_second, column_second, new_prompt)


def solution(mesh):
    placed = (
        P(None, "dp", "vocab"),
        P(None, "dp", "vocab"),
        P(None, "dp", "vocab"),
        P(None, "dp", None),
        P(None, "dp", None),
        P("vocab", None),
        P(None, "dp", None),
        P(None, "dp", None),
        P(None, "dp", None),
        P(None, "dp", None),
        P(),
        P(None, None, "vocab"),
        P(None, None, "vocab"),
        P(),
        P(None, "vocab"),
    )
    return jax.shard_map(
        on_device,
        mesh=mesh,
        in_specs=placed,
        out_specs=(
            P(),
            P(),
            P(None, None, "vocab"),
            P(None, None, "vocab"),
            P(),
            P(None, "vocab"),
            P(None, None, "vocab"),
        ),
        check_vma=False,
    )
```

```python
import collections
import functools

import jax
import jax.numpy as jnp
from jax import lax
from jax.experimental import pallas as pl
from jax.experimental.pallas import tpu as pltpu
from jax.sharding import PartitionSpec as P

DH = 64
P_SIZE = 100
TASKS = 8
STEP = 5
HALO = 16
LANES = 128
SEGS = 3
VOCAB_BLOCK = 1024
HIDDEN_PIECE = 512
MIB = 1024 * 1024

NORM_EPS = 1e-06
CLIP_NORM = 2e-05
BETA_ONE = 0.9
BETA_TWO = 0.999
LEARN_RATE = 1.0
WEIGHT_DECAY = 1e-05
SQUARE_EPS = 1e-30
MASKED = -1e30

F32 = jnp.float32
BF16 = jnp.bfloat16


def dot(left, right):
    return jnp.dot(left, right, preferred_element_type=F32)


def dot_rows(left, right):
    return lax.dot_general(left, right, (((1,), (1,)), ((), ())), preferred_element_type=F32)


def dot_columns(left, right):
    return lax.dot_general(left, right, (((0,), (0,)), ((), ())), preferred_element_type=F32)


def normed(values, gain):
    inverse = lax.rsqrt(jnp.mean(values * values, -1, keepdims=True) + NORM_EPS)
    return (values * inverse * gain, inverse)


def normed_back(values, gain, inverse, gradient):
    unit_rows = values * inverse
    scaled = gradient * gain
    return inverse * (scaled - unit_rows * jnp.mean(scaled * unit_rows, -1, keepdims=True))


def smooth(values):
    return jax.nn.gelu(values, approximate=True)


def layout(lengths, task_list, positions):
    seg_ends = jnp.cumsum(lengths)
    seg_starts = seg_ends - lengths
    segment = jnp.sum((positions[:, None] >= seg_ends[None, :]).astype(jnp.int32), -1)
    member = segment[:, None] == jnp.arange(lengths.shape[0], dtype=jnp.int32)[None, :]
    in_segment = positions - jnp.sum(jnp.where(member, seg_starts[None, :], 0), -1)
    task_of = jnp.sum(jnp.where(member, task_list[None, :], 0), -1)
    return (segment, in_segment, task_of)


def per_task(task_of, amounts):
    hits = task_of[:, None] == jnp.arange(TASKS, dtype=jnp.int32)
    return jnp.sum(jnp.where(hits, amounts[:, None], 0.0), 0)


def pair_lanes(pair, first=0):
    return pl.ds(pl.multiple_of(first + pair * LANES, LANES), LANES)


def head_mask(shape, head, axis=1):
    return (lax.broadcasted_iota(jnp.int32, shape, axis) < DH) == (head == 0)


Plan = collections.namedtuple(
    "Plan", ["length", "group", "own", "held", "heads", "half", "starts", "near", "far"]
)


def chosen(index, values):
    result = values[0]
    for k, value in enumerate(values[1:], 1):
        result = jnp.where(index == k, value, result)
    return result


def turn_of(plan, lengths_ref, m, place):
    last = plan.length - lengths_ref[m, SEGS - 1] - plan.near[-1]
    return jnp.where(place == 0, lengths_ref[m, 0] - P_SIZE, last)


def row_scalars(plan, lengths_ref, decoder):
    v = lax.axis_index("vocab")
    m, place = v // plan.group, lax.rem(v, plan.group)
    first = lengths_ref[m, 0]
    ends = [first, first + lengths_ref[m, 1]]
    if decoder:
        rows = [
            turn_of(plan, lengths_ref, m, place),
            chosen(place, plan.near),
            chosen(place, plan.far),
        ]
    else:
        rows = [0, place * plan.own, place * plan.own]
    starts = [lax.rem(place - k + plan.group, plan.group) * plan.own for k in range(plan.group)]
    return [*ends, *rows, *starts]


def row_positions(info, shape, axis):
    row = lax.broadcasted_iota(jnp.int32, shape, axis)
    return row + jnp.where(row < info[SEGS - 1], info[SEGS], info[SEGS + 1])


def key_positions(info, parts, own, shape, axis):
    row = lax.broadcasted_iota(jnp.int32, shape, axis)
    position = row + info[SEGS + 2]
    for k in range(1, parts):
        position = jnp.where(row < k * own, position, row - k * own + info[SEGS + 2 + k])
    return position


def segment_columns(info, position, is_key):
    segment = sum(jnp.where(position >= info[j], 1, 0) for j in range(SEGS - 1))
    column = lax.rem(lax.broadcasted_iota(jnp.int32, position.shape, 1), DH)
    if is_key:
        return jnp.where((column < SEGS) & (column != segment), MASKED, 0.0).astype(BF16)
    return jnp.where(column == segment, 1.0, 0.0).astype(BF16)


def head_part(values, rest, head):
    return jnp.where(head_mask(values.shape, head), values, rest)


def over_heads(pairs, scores, soften, mix):
    scores(0, 0)
    scores(0, 1)
    soften(0, 0)

    def step(pair, _):
        scores(pair + 1, 0)
        soften(pair, 1)
        mix(pair, 0)
        scores(pair + 1, 1)
        soften(pair + 1, 0)
        mix(pair, 1)
        return 0

    lax.fori_loop(0, pairs - 1, step, 0)
    soften(pairs - 1, 1)
    mix(pairs - 1, 0)
    mix(pairs - 1, 1)


def feed_pieces(rows_ref, gain_ref, one, two, out_ref, before_ref, source, held_of, active_of):
    count = one.shape[1] // HIDDEN_PIECE
    rows = rows_ref[...]
    source[...] = normed(rows, gain_ref[...])[0].astype(BF16)
    out_ref[...] = rows
    for n in range(count + 2):
        if n < count:
            here = slice(n * HIDDEN_PIECE, (n + 1) * HIDDEN_PIECE)
            before = dot(source[...], one[:, here])
            held_of[n % 2][...] = before
            before_ref[:, here] = before
        if 0 < n <= count:
            active_of[(n - 1) % 2][...] = smooth(held_of[(n - 1) % 2][...]).astype(BF16)
        if n >= 2:
            there = slice((n - 2) * HIDDEN_PIECE, (n - 1) * HIDDEN_PIECE)
            out_ref[...] += dot(active_of[n % 2][...], two[there, :])


def attend_kernel(plan, parts, decoder, causal, fed, *refs):
    q_ref, pair_refs = refs[0], refs[1 : 1 + parts]
    residual_ref, weight_ref, lengths_ref = refs[1 + parts : 4 + parts]
    refs = refs[4 + parts :]
    if fed:
        gain_ref, one_hbm, two_hbm, out_ref, mixed_ref, log_ref, last_ref, before_ref = refs[:8]
        *refs, one, two, source, held_a, held_b, active_a, active_b, sems = refs[8:]
        loads = [
            pltpu.make_async_copy(one_hbm, one, sems.at[0]),
            pltpu.make_async_copy(two_hbm, two, sems.at[1]),
        ]
        for load in loads:
            load.start()
    else:
        out_ref, mixed_ref, log_ref, *refs = refs
    info = row_scalars(plan, lengths_ref, decoder)
    bias_ref, q_mark, k_mark, low_ref, scores_a, scores_b, powers_a, powers_b = refs
    width = q_ref.shape[1]
    own = pair_refs[0].shape[0]
    scores_of, powers_of = (scores_a, scores_b), (powers_a, powers_b)
    rows = [slice(k * own, (k + 1) * own) for k in range(parts)]
    q_mark[...] = segment_columns(info, row_positions(info, q_mark.shape, 0), False)
    k_mark[...] = segment_columns(info, key_positions(info, parts, own, k_mark.shape, 0), True)
    if causal:
        shape = bias_ref.shape
        later = row_positions(info, shape, 0) >= key_positions(info, parts, own, shape, 1)
        bias_ref[...] = jnp.where(later, 0.0, MASKED)
    log_ref[...] = jnp.zeros_like(log_ref)
    lane = lax.broadcasted_iota(jnp.int32, log_ref.shape, 1)

    def scores(pair, head):
        query = q_ref[:, pair_lanes(pair)] * jnp.asarray(DH ** (-0.5), BF16)
        query = head_part(query, q_mark[...], head)
        for k in range(parts):
            keys = head_part(pair_refs[k][:, pair_lanes(pair)], k_mark[rows[k], :], head)
            values = dot_rows(query, keys)
            if causal:
                values = values + bias_ref[:, rows[k]]
            scores_of[head][:, rows[k]] = values

    def soften(pair, head):
        values = scores_of[head][...]
        highest = jnp.max(values, -1, keepdims=True)
        powers_of[head][...] = jnp.exp(values - highest).astype(BF16)
        log_ref[...] += jnp.where(lane == 2 * pair + head, highest, 0.0)

    def mix(pair, head):
        value = None
        for k in range(parts):
            values = pair_refs[k][:, pair_lanes(pair, width)]
            values = head_part(values, jnp.ones_like(values), head)
            term = dot(powers_of[head][:, rows[k]], values)
            value = term if value is None else value + term
        total = value[:, LANES - 1 :] if head == 0 else value[:, :1]
        value = value / total
        log_ref[...] += jnp.where(lane == 2 * pair + head, jnp.log(total), 0.0)
        lanes = pair_lanes(pair)
        if head:
            value = jnp.where(head_mask(value.shape, 0), mixed_ref[:, lanes], value)
        mixed_ref[:, lanes] = value
        if head:
            low_ref[:, lanes] = value.astype(BF16)

    over_heads(width // LANES, scores, soften, mix)
    out_ref[...] = residual_ref[...] + dot(low_ref[...], weight_ref[...])
    if fed:
        for load in loads:
            load.wait()
        feed_pieces(
            out_ref, gain_ref, one, two, last_ref, before_ref, source, (held_a, held_b), (active_a, active_b)
        )


def attend(plan, queries, pairs, residual, weight, row_lengths, decoder, causal, feed=None):
    own, width = queries.shape
    parts, length = len(pairs), sum(pair.shape[0] for pair in pairs)
    vmem = pl.BlockSpec(memory_space=pltpu.VMEM)
    operands = [queries, *pairs, residual, weight, row_lengths]
    in_specs = [vmem] * (parts + 3) + [pl.BlockSpec(memory_space=pltpu.SMEM)]
    rows = jax.ShapeDtypeStruct((own, width), F32)
    shapes = [rows, rows, jax.ShapeDtypeStruct((own, LANES), F32)]
    scratch = [
        pltpu.VMEM((own, length) if causal else (8, LANES), F32),
        pltpu.VMEM((own, LANES), BF16),
        pltpu.VMEM((length, LANES), BF16),
        pltpu.VMEM((own, width), BF16),
        pltpu.VMEM((own, length), F32),
        pltpu.VMEM((own, length), F32),
        pltpu.VMEM((own, length), BF16),
        pltpu.VMEM((own, length), BF16),
    ]
    if feed:
        gain, one, two = feed
        operands += [gain[None], one, two]
        in_specs += [vmem] + [pl.BlockSpec(memory_space=pl.ANY)] * 2
        shapes += [rows, jax.ShapeDtypeStruct((own, one.shape[1]), F32)]
        scratch += [pltpu.VMEM(one.shape, BF16), pltpu.VMEM(two.shape, BF16)]
        scratch += [pltpu.VMEM((own, width), BF16)]
        scratch += [pltpu.VMEM((own, HIDDEN_PIECE), F32)] * 2
        scratch += [pltpu.VMEM((own, HIDDEN_PIECE), BF16)] * 2 + [pltpu.SemaphoreType.DMA((2,))]
    return pl.pallas_call(
        functools.partial(attend_kernel, plan, parts, decoder, causal, feed is not None),
        out_shape=shapes,
        in_specs=in_specs,
        out_specs=[vmem] * len(shapes),
        scratch_shapes=scratch,
        compiler_params=pltpu.CompilerParams(vmem_limit_bytes=(26 + own // 32 if feed else 24) * MIB),
        cost_estimate=pl.CostEstimate(
            flops=44 * own * length * width, bytes_accessed=6 * own * width, transcendentals=0
        ),
    )(*operands)


def attend_back_kernel(plan, parts, decoder, want_queries, exchange, *refs):
    q_ref, pair_refs = refs[0], refs[1 : 1 + parts]
    grad_ref, weight_ref, mixed_ref, log_ref, lengths_ref = refs[1 + parts : 6 + parts]
    info = row_scalars(plan, lengths_ref, decoder)
    rest = refs[6 + parts :]
    if exchange:
        in_hbm, rows_hbm, gain_ref, result_ref = rest[:4]
        part_refs, arrived, send_sem, recv_sem = rest[4:6], rest[6], rest[7], rest[8]
        dq_ref, in_ref, rows_ref, late_sems = rest[9:13]
        rest = rest[13:]
        late = [
            pltpu.make_async_copy(in_hbm, in_ref, late_sems.at[0]),
            pltpu.make_async_copy(rows_hbm, rows_ref, late_sems.at[1]),
        ]
        for copy in late:
            copy.start()
        v = lax.axis_index("vocab")
        twin = {"vocab": v // 2 * 2 + 1 - lax.rem(v, 2)}
        barrier = pltpu.get_barrier_semaphore()
        pl.semaphore_signal(barrier, inc=1, device_id=twin, device_id_type=pl.DeviceIdType.MESH)
        pl.semaphore_wait(barrier, 1)
    else:
        part_refs = rest[:parts]
        dq_ref = rest[parts] if want_queries else None
        rest = rest[parts + want_queries :]
    q_mark, k_mark, low_ref, delta_ref, *rest = rest
    scores_of, grads_of, weights_of, steps_of = rest[0:2], rest[2:4], rest[4:6], rest[6:8]
    width = q_ref.shape[1]
    own = pair_refs[0].shape[0]
    pairs = width // LANES
    rows = [slice(k * own, (k + 1) * own) for k in range(parts)]
    scale = jnp.asarray(DH ** (-0.5), BF16)
    q_mark[...] = segment_columns(info, row_positions(info, q_mark.shape, 0), False)
    k_mark[...] = segment_columns(info, key_positions(info, parts, own, k_mark.shape, 0), True)
    low_ref[...] = dot_rows(grad_ref[...].astype(BF16), weight_ref[...]).astype(BF16)
    product = low_ref[...].astype(F32) * mixed_ref[...]
    high = product.astype(BF16)
    shape = (2 * 8, width)
    belongs = lax.broadcasted_iota(jnp.int32, shape, 1) // DH == lax.broadcasted_iota(
        jnp.int32, shape, 0
    )
    belongs = jnp.where(belongs, 1.0, 0.0).astype(BF16)
    delta_ref[...] = dot_rows(belongs, high) + dot_rows(
        belongs, (product - high.astype(F32)).astype(BF16)
    )

    def scores(pair, head):
        query = head_part(q_ref[:, pair_lanes(pair)] * scale, q_mark[...], head)
        grad = low_ref[:, pair_lanes(pair)]
        grad = head_part(grad, jnp.zeros_like(grad), head)
        for k in range(parts):
            keys = head_part(pair_refs[k][:, pair_lanes(pair)], k_mark[rows[k], :], head)
            scores_of[head][rows[k], :] = dot_rows(keys, query)
            grads_of[head][rows[k], :] = dot_rows(pair_refs[k][:, pair_lanes(pair, width)], grad)

    def soften(pair, head):
        at = pl.ds(2 * pair + head, 1)
        weights = jnp.exp(scores_of[head][...] - log_ref[at, :])
        weights_of[head][...] = weights.astype(BF16)
        steps_of[head][...] = (weights * (grads_of[head][...] - delta_ref[at, :])).astype(BF16)

    def away(pair, which):
        lanes = pair_lanes(pair, which * width)
        return pltpu.make_async_remote_copy(
            src_ref=part_refs[1].at[:, lanes],
            dst_ref=arrived.at[:, lanes],
            send_sem=send_sem.at[pair, which],
            recv_sem=recv_sem.at[pair, which],
            device_id=twin,
            device_id_type=pl.DeviceIdType.MESH,
        )

    def mix(pair, head):
        keys, values = pair_lanes(pair), pair_lanes(pair, width)
        query, grad = q_ref[:, keys] * scale, low_ref[:, keys]
        query = head_part(query, jnp.zeros_like(query), head)
        grad = head_part(grad, jnp.zeros_like(grad), head)
        dq = None
        for k in reversed(range(parts)):
            step = steps_of[head][rows[k], :]
            dk = dot(step, query)
            dv = dot(weights_of[head][rows[k], :], grad)
            part_refs[k][:, keys] = dk if head == 0 else part_refs[k][:, keys] + dk
            part_refs[k][:, values] = dv if head == 0 else part_refs[k][:, values] + dv
            if want_queries:
                term = dot_columns(pair_refs[k][:, keys], step)
                dq = term if dq is None else dq + term
        if want_queries:
            here = pl.ds(pl.multiple_of(pair * LANES, LANES), LANES)
            dq = dq * DH ** (-0.5)
            if head:
                dq = jnp.where(head_mask(dq.shape, 0, 0), dq_ref[here, :].astype(F32), dq)
            dq_ref[here, :] = dq.astype(dq_ref.dtype)
        if exchange and head:
            away(pair, 0).start()
            away(pair, 1).start()

    over_heads(pairs, scores, soften, mix)
    if not exchange:
        return
    total = None
    for copy in late:
        copy.wait()
    if want_queries:
        total = dot_rows(jnp.transpose(dq_ref[...]).astype(BF16), in_ref[:, :width])
    for pair in range(pairs):
        away(pair, 0).wait_recv()
        away(pair, 1).wait_recv()
    both = part_refs[0][...] + arrived[...]
    high = both.astype(BF16)
    low = (both - high.astype(F32)).astype(BF16)
    back = dot_rows(high, in_ref[:, width:]) + dot_rows(low, in_ref[:, width:])
    total = back if total is None else total + back
    values, gain = rows_ref[...], gain_ref[...]
    inverse = lax.rsqrt(jnp.mean(values * values, -1, keepdims=True) + NORM_EPS)
    total = normed_back(values, gain, inverse, total)
    result_ref[...] = grad_ref[...] + total if want_queries else total
    for pair in range(pairs):
        away(pair, 0).wait_send()
        away(pair, 1).wait_send()


def attend_back(
    plan, queries, pairs, gradient, weight, mixed, logs, row_lengths, decoder, want_queries, through
):
    heads, width = queries.shape
    own = pairs[0].shape[0]
    parts, length = len(pairs), sum(pair.shape[0] for pair in pairs)
    vmem = pl.BlockSpec(memory_space=pltpu.VMEM)
    operands = [queries, *pairs, gradient, weight, mixed, logs.T[:16], row_lengths]
    in_specs = [vmem] * (parts + 5) + [pl.BlockSpec(memory_space=pltpu.SMEM)]
    scratch = [
        pltpu.VMEM((heads, LANES), BF16),
        pltpu.VMEM((length, LANES), BF16),
        pltpu.VMEM((heads, width), BF16),
        pltpu.VMEM((16, heads), F32),
    ]
    scratch += [pltpu.VMEM((length, heads), F32)] * 4 + [pltpu.VMEM((length, heads), BF16)] * 4
    if through:
        attend_in, rows, gain, collective_id = through
        operands += [attend_in, rows, gain[None]]
        in_specs += [pl.BlockSpec(memory_space=pl.ANY)] * 2 + [vmem]
        shapes = jax.ShapeDtypeStruct(rows.shape, F32)
        out_specs = vmem
        each = pltpu.SemaphoreType.DMA((width // LANES, 2))
        scratch = (
            [pltpu.VMEM((own, 2 * width), F32)] * 3
            + [each, each, pltpu.VMEM((width, heads) if want_queries else (8, LANES), F32)]
            + [pltpu.VMEM(attend_in.shape, BF16), pltpu.VMEM(rows.shape, F32)]
            + [pltpu.SemaphoreType.DMA((2,))]
            + scratch
        )
        params = pltpu.CompilerParams(
            collective_id=collective_id, has_side_effects=True, vmem_limit_bytes=46 * MIB
        )
    else:
        shapes = [jax.ShapeDtypeStruct(pair.shape, F32) for pair in pairs]
        if want_queries:
            shapes.append(jax.ShapeDtypeStruct((width, heads), BF16))
        out_specs = [vmem] * len(shapes)
        params = pltpu.CompilerParams(vmem_limit_bytes=34 * MIB)
    return pl.pallas_call(
        functools.partial(
            attend_back_kernel, plan, parts, decoder, want_queries, through is not None
        ),
        out_shape=shapes,
        in_specs=in_specs,
        out_specs=out_specs,
        scratch_shapes=scratch,
        compiler_params=params,
        cost_estimate=pl.CostEstimate(
            flops=80 * heads * length * width, bytes_accessed=20 * own * width, transcendentals=0
        ),
    )(*operands)


def smooth_slope(u):
    rate = (2.0 / jnp.pi) ** 0.5
    bend = jnp.tanh(rate * (u + 0.044715 * (u * u * u)))
    inner = rate * (1.0 + 3.0 * 0.044715 * (u * u))
    return 0.5 * (1.0 + bend) + 0.5 * u * (1.0 - bend * bend) * inner


def feed_back_kernel(grad_ref, rows_ref, gain_ref, before_ref, one_ref, two_ref, out_ref, low, *scratch):
    active_of, step_of = scratch[0:2], scratch[2:4]
    count = one_ref.shape[1] // HIDDEN_PIECE
    low[...] = grad_ref[...].astype(BF16)
    out_ref[...] = jnp.zeros_like(out_ref)
    for n in range(count + 2):
        if n < count:
            here = slice(n * HIDDEN_PIECE, (n + 1) * HIDDEN_PIECE)
            active_of[n % 2][...] = dot_rows(low[...], two_ref[here, :])
        if 0 < n <= count:
            here = slice((n - 1) * HIDDEN_PIECE, n * HIDDEN_PIECE)
            step_of[(n - 1) % 2][...] = (
                active_of[(n - 1) % 2][...] * smooth_slope(before_ref[:, here])
            ).astype(BF16)
        if n >= 2:
            here = slice((n - 2) * HIDDEN_PIECE, (n - 1) * HIDDEN_PIECE)
            out_ref[...] += dot_rows(step_of[n % 2][...], one_ref[:, here])
    rows = rows_ref[...]
    inverse = lax.rsqrt(jnp.mean(rows * rows, -1, keepdims=True) + NORM_EPS)
    out_ref[...] = grad_ref[...] + normed_back(rows, gain_ref[...], inverse, out_ref[...])


def feed_back(gradient, rows, gain, before, one, two):
    own, width = rows.shape
    hidden = one.shape[1]
    vmem = pl.BlockSpec(memory_space=pltpu.VMEM)
    return pl.pallas_call(
        feed_back_kernel,
        out_shape=jax.ShapeDtypeStruct((own, width), F32),
        in_specs=[vmem] * 6,
        out_specs=vmem,
        scratch_shapes=[pltpu.VMEM((own, width), BF16)]
        + [pltpu.VMEM((own, HIDDEN_PIECE), F32)] * 2
        + [pltpu.VMEM((own, HIDDEN_PIECE), BF16)] * 2,
        compiler_params=pltpu.CompilerParams(vmem_limit_bytes=30 * MIB),
        cost_estimate=pl.CostEstimate(
            flops=4 * own * width * hidden, bytes_accessed=4 * width * hidden, transcendentals=0
        ),
    )(gradient, rows, gain[None], before, one, two)


def prompted(plan, rows_ref, prompt_ref, lengths_ref, tasks_ref):
    info = row_scalars(plan, lengths_ref, False)
    m = lax.axis_index("vocab") // plan.group
    shape = (plan.own, LANES)
    position = row_positions(info, shape, 0)
    lane = lax.broadcasted_iota(jnp.int32, shape, 1)
    begin = jnp.where(position >= info[1], info[1], jnp.where(position >= info[0], info[0], 0))
    place = position - begin
    total = None
    for j, start in enumerate([0, info[0], info[1]]):
        hit = (begin == start) & (place == lane) & (place < P_SIZE)
        term = dot_rows(jnp.where(hit, 1.0, 0.0).astype(BF16), prompt_ref[tasks_ref[m, j]])
        total = term if total is None else total + term
    return jnp.where(place[:, 0:1] < P_SIZE, total, rows_ref[...].astype(F32))


def project_kernel(plan, *refs):
    rows_ref, prompt_ref, keys_ref, heads_ref, gain_ref, lengths_ref, tasks_ref = refs[:7]
    first_hbm, second_hbm, out_ref, enc_q, enc_own, enc_other, dec_q, dec_own, dec_other = refs[7:16]
    first, second, sems, send_sem, recv_sem = refs[16:]
    width = rows_ref.shape[1]
    v = lax.axis_index("vocab")
    twin = {"vocab": v // 2 * 2 + 1 - lax.rem(v, 2)}
    barrier = pltpu.get_barrier_semaphore()
    pl.semaphore_signal(barrier, inc=1, device_id=twin, device_id_type=pl.DeviceIdType.MESH)
    pl.semaphore_wait(barrier, 1)
    loads = [
        pltpu.make_async_copy(first_hbm, first, sems.at[0]),
        pltpu.make_async_copy(second_hbm, second, sems.at[1]),
    ]
    for load in loads:
        load.start()

    def share(source, target, index):
        return pltpu.make_async_remote_copy(
            src_ref=source,
            dst_ref=target,
            send_sem=send_sem.at[index],
            recv_sem=recv_sem.at[index],
            device_id=twin,
            device_id_type=pl.DeviceIdType.MESH,
        )

    shares = [share(enc_own, enc_other, 0), share(dec_own, dec_other, 1)]
    rows = prompted(plan, rows_ref, prompt_ref, lengths_ref, tasks_ref)
    out_ref[...] = rows
    low = normed(rows, gain_ref[...])[0].astype(BF16)
    loads[0].wait()
    enc_own[...] = dot(low, first[:, width:]).astype(BF16)
    shares[0].start()
    enc_q[...] = dot(low, first[:, :width]).astype(BF16)
    loads[1].wait()
    dec_own[...] = dot(keys_ref[...], second[:, width:]).astype(BF16)
    shares[1].start()
    dec_q[...] = dot(heads_ref[...], second[:, :width]).astype(BF16)
    for copy in shares:
        copy.wait()


def project(plan, rows, prompts, keys, heads, gain, row_lengths, row_tasks, first, second):
    width = rows.shape[1]
    vmem, smem = pl.BlockSpec(memory_space=pltpu.VMEM), pl.BlockSpec(memory_space=pltpu.SMEM)
    anywhere = pl.BlockSpec(memory_space=pl.ANY)
    pair = jax.ShapeDtypeStruct((plan.own, 2 * width), BF16)
    outs = pl.pallas_call(
        functools.partial(project_kernel, plan),
        out_shape=[
            jax.ShapeDtypeStruct(rows.shape, F32),
            jax.ShapeDtypeStruct(rows.shape, BF16),
            pair,
            pair,
            jax.ShapeDtypeStruct(heads.shape, BF16),
            pair,
            pair,
        ],
        in_specs=[vmem] * 5 + [smem] * 2 + [anywhere] * 2,
        out_specs=[vmem] * 7,
        scratch_shapes=[pltpu.VMEM(first.shape, BF16)] * 2 + [pltpu.SemaphoreType.DMA((2,))] * 3,
        compiler_params=pltpu.CompilerParams(
            collective_id=5, has_side_effects=True, vmem_limit_bytes=40 * MIB
        ),
        cost_estimate=pl.CostEstimate(
            flops=10 * rows.size * width, bytes_accessed=4 * first.size, transcendentals=0
        ),
    )(rows, prompts, keys, heads, gain[None], row_lengths, row_tasks, first, second)
    return outs[0], outs[1], outs[2:4], outs[4], outs[5:7]


def vocab_kernel(tile, valid, h_ref, target_ref, table_hbm, grad_ref, stat_ref, table, sem):
    padded = table.shape[0]

    @pl.when(pl.program_id(0) == 0)
    def _():
        copy = pltpu.make_async_copy(table_hbm, table.at[pl.ds(0, valid), :], sem)
        copy.start()
        if padded > valid:
            table[valid:, :] = jnp.zeros((padded - valid, table.shape[1]), BF16)
        copy.wait()

    rows = h_ref.shape[0]
    hidden = h_ref[...]
    column = lax.broadcasted_iota(jnp.int32, (rows, tile), 1)
    target = target_ref[...]

    def block(at, carry, last):
        maxima, total = carry
        part = table[pl.ds(pl.multiple_of(at * tile, tile), tile), :]
        logits = dot_rows(hidden, part)
        if last and padded > valid:
            logits = jnp.where(column < valid - (padded - tile), logits, MASKED)
        highest = jnp.maximum(maxima, jnp.max(logits, -1, keepdims=True))
        powers = jnp.exp(logits - highest)
        scale = jnp.exp(maxima - highest)
        total = total * scale + jnp.sum(powers, -1, keepdims=True)
        powers = jnp.where(column == target - at * tile, 0.0, powers).astype(BF16)
        grad_ref[...] = grad_ref[...] * scale + dot(powers, part)
        return (highest, total)

    grad_ref[...] = jnp.zeros_like(grad_ref)
    blocks = padded // tile
    carry = (jnp.full((rows, 1), MASKED, F32), jnp.zeros((rows, 1), F32))
    carry = lax.fori_loop(0, blocks - 1, lambda at, c: block(at, c, False), carry)
    maxima, total = block(blocks - 1, carry, True)
    lane = lax.broadcasted_iota(jnp.int32, stat_ref.shape, 1)
    stat_ref[...] = jnp.where(lane == 0, maxima, total)


def vocab_pass(hidden, target_local, embedding, rows):
    count, width = hidden.shape
    valid = embedding.shape[0]
    tile = VOCAB_BLOCK
    padded = (valid + tile - 1) // tile * tile
    return pl.pallas_call(
        functools.partial(vocab_kernel, tile, valid),
        grid=(count // rows,),
        out_shape=[
            jax.ShapeDtypeStruct((count, width), F32),
            jax.ShapeDtypeStruct((count, LANES), F32),
        ],
        in_specs=[
            pl.BlockSpec((rows, width), lambda i: (i, 0)),
            pl.BlockSpec((rows, 1), lambda i: (i, 0)),
            pl.BlockSpec(memory_space=pl.ANY),
        ],
        out_specs=[
            pl.BlockSpec((rows, width), lambda i: (i, 0)),
            pl.BlockSpec((rows, LANES), lambda i: (i, 0)),
        ],
        scratch_shapes=[pltpu.VMEM((padded, width), BF16), pltpu.SemaphoreType.DMA],
        compiler_params=pltpu.CompilerParams(vmem_limit_bytes=56 * MIB),
        cost_estimate=pl.CostEstimate(
            flops=4 * count * padded * width, bytes_accessed=2 * valid * width, transcendentals=0
        ),
    )(hidden, target_local, embedding)


def gather_kernel(plan, rows_z, rows_y, *refs):
    in_ref, out_ref, expand_ref, reduce_ref, wanted_ref, table_hbm, lengths_ref, gain_ref = refs[:8]
    in_full, out_full, expand_full, reduce_full = refs[8:11], refs[11:14], refs[14:16], refs[16:18]
    enc_rows, dec_keys, dec_rows, dec_heads, target_rows = refs[18:23]
    found_ref, table_low, table, stage, far, near, sister, from_core, from_x, from_sister = refs[23:33]
    send_sem, recv_sem, local_sem, table_sem = refs[33:]
    at, v = lax.axis_index("dp"), lax.axis_index("vocab")
    z, y, x, core = at // rows_y, lax.rem(at, rows_y), v // 2, lax.rem(v, 2)
    top = rows_z - 1
    above = {"dp": jnp.minimum(z + 1, top) * rows_y + y, "vocab": v}
    below = {"dp": jnp.maximum(z - 1, 0) * rows_y + y, "vocab": v}
    beside = {"dp": z * rows_y + (1 - y), "vocab": v}
    other_x = (1 - x) * 2 + core
    across = {"dp": at, "vocab": other_x}
    twin = {"dp": at, "vocab": x * 2 + (1 - core)}

    barrier = pltpu.get_barrier_semaphore()

    def greet(peer):
        pl.semaphore_signal(barrier, inc=1, device_id=peer, device_id_type=pl.DeviceIdType.MESH)

    pl.when(z < top)(lambda: greet(above))
    pl.when(z > 0)(lambda: greet(below))
    greet(beside)
    greet(across)
    greet(twin)
    inner = jnp.logical_and(z > 0, z < top)
    pl.when(inner)(lambda: pl.semaphore_wait(barrier, 5))
    pl.when(jnp.logical_not(inner))(lambda: pl.semaphore_wait(barrier, 4))

    names, tallies = {}, [0, 0]

    def remote(name, source, target, peer):
        if name not in names:
            names[name] = tallies[0]
            tallies[0] += 1
        return pltpu.make_async_remote_copy(
            src_ref=source,
            dst_ref=target,
            send_sem=send_sem.at[names[name]],
            recv_sem=recv_sem.at[names[name]],
            device_id=peer,
            device_id_type=pl.DeviceIdType.MESH,
        )

    def local(source, target):
        copy = pltpu.make_async_copy(source, target, local_sem.at[tallies[1]])
        tallies[1] += 1
        copy.start()
        return copy

    def columns(ref, full, index, blocks):
        wide = ref.shape[2] // blocks
        here = lambda b: pl.ds(pl.multiple_of(b * wide, wide), wide)
        return (
            lambda b: ref.at[index, :, here(b)],
            lambda zs, ys, b: full.at[zs, ys, :, here(b)],
            lambda ys, b: full.at[:, ys, :, here(b)],
            blocks == 4,
        )

    def row_blocks(ref, full, index):
        count = ref.shape[1] // 4
        return (
            lambda b: ref.at[index, pl.ds(pl.multiple_of(b * count, count), count), :],
            lambda zs, ys, b: full.at[zs, ys, b],
            lambda ys, b: full.at[:, ys, b],
            True,
        )

    def attention(j):
        return [columns(in_ref, in_full[j], j, 2), columns(out_ref, out_full[j], j, 2)]

    def feed(j):
        return [columns(expand_ref, expand_full[j], j, 4), row_blocks(reduce_ref, reduce_full[j], j)]

    waves = [feed(0) + attention(0), feed(1) + attention(1) + attention(2)]
    units = [u for wave in waves for u in wave]
    starts = [0, len(waves[0]), len(units)]
    blocks = [v if u[3] else core for u in units]
    sides = (("up", -1), ("down", 1))

    def there(side, k):
        return z - k >= 0 if side == "up" else z + k <= top

    def further(side):
        return z < top if side == "up" else z > 0

    def begin(i):
        source, target, _, quarter = units[i]
        b = blocks[i]
        piece = target(z, y, b)
        pl.when(z < top)(lambda: remote((i, "up", 1), source(b), piece, above).start())
        pl.when(z > 0)(lambda: remote((i, "down", 1), source(b), piece, below).start())
        remote((i, "y", 0), source(b), piece, beside).start()
        copies = [local(source(b), piece)]
        if quarter:
            copies.append(local(source(other_x), target(z, y, other_x)))
        return copies

    def step(i, k):
        _, target, _, quarter = units[i]
        for side, sign in sides:

            @pl.when(there(side, k))
            def _():
                piece = target(z + sign * k, y, blocks[i])
                remote((i, side, k), piece, piece, above).wait_recv()
                if k < top:

                    @pl.when(further(side))
                    def _():
                        peer = above if side == "up" else below
                        remote((i, side, k + 1), piece, piece, peer).start()

                remote((i, side, k, "y"), piece, piece, beside).start()
                if quarter:
                    remote((i, side, k, "x"), piece, piece, across).start()

    def came(i, k):
        _, target, _, quarter = units[i]
        if k == 0:
            piece = target(z, 1 - y, blocks[i])
            remote((i, "y", 0), piece, piece, beside).wait_recv()
            if quarter:
                remote((i, "yx", 0), piece, piece, across).start()
            return
        for side, sign in sides:

            @pl.when(there(side, k))
            def _():
                piece = target(z + sign * k, 1 - y, blocks[i])
                remote((i, side, k, "y"), piece, piece, beside).wait_recv()
                if quarter:
                    remote((i, side, k, "yx"), piece, piece, across).start()

    def to_twin(i, column, b, tag):
        block = units[i][2](column, b)
        remote((i, "core", tag), block, block, twin).start()

    def spread(i):
        for copy in locals_[i]:
            copy.wait()
        to_twin(i, y, blocks[i], 0)

    def spread_beside(i):
        to_twin(i, 1 - y, blocks[i], 1)

    def x_came(i, tag):
        _, target, _, _ = units[i]
        if tag == "yx":
            piece = target(z, 1 - y, other_x)
            remote((i, "yx", 0), piece, piece, across).wait_recv()
        for k in range(1, rows_z):
            for side, sign in sides:

                @pl.when(there(side, k))
                def _():
                    piece = target(z + sign * k, y if tag == "x" else 1 - y, other_x)
                    remote((i, side, k, tag), piece, piece, across).wait_recv()

        to_twin(i, y if tag == "x" else 1 - y, other_x, 2 if tag == "x" else 3)

    valid, width = table_low.shape
    share = far.shape[0]
    table_copy = pltpu.make_async_copy(table_hbm, table_low, table_sem)
    table_copy.start()

    def widen(at, _):
        here = pl.ds(pl.multiple_of(at * 32, 32), 32)
        table[here, :] = table_low[here, :].astype(F32)
        return 0

    def prepare():
        table_copy.wait()
        table[valid:, :] = jnp.zeros((table.shape[0] - valid, width), F32)
        lax.fori_loop(0, valid // 32, widen, 0)

    def look_up(target, owner, part):
        count = stage.shape[0]

        def rows(at, _):
            for step in range(8):
                i = at * 8 + step
                row = wanted_ref[owner, part * count + i]
                stage[pl.ds(i, 1), :] = table[pl.ds(row, 1), :]
            return 0

        lax.fori_loop(0, count // 8, rows, 0)
        target[part * count : (part + 1) * count, :] = stage[...].astype(BF16)

    sums = {
        "far": remote("far", far, from_core, twin),
        "near": remote("near", near, from_x, across),
        "sister": remote("sister", sister, from_sister, twin),
    }

    def send_far():
        sums["far"].start()

    def send_near():
        sums["far"].wait_recv()
        near[...] = (near[...].astype(F32) + from_core[...].astype(F32)).astype(BF16)
        sums["near"].start()

    def send_sister():
        sums["sister"].start()

    def finish_rows():
        sums["sister"].wait_recv()
        sums["near"].wait_recv()
        total = found_ref[...].astype(F32) + from_sister[...].astype(F32)
        table[:share, :] = total + from_x[...].astype(F32)
        enc_rows[...] = table[: plan.own, :].astype(BF16)
        ends = [lengths_ref[x, 0], lengths_ref[x, 0] + lengths_ref[x, 1]]
        position = lax.broadcasted_iota(jnp.int32, (plan.held, 1), 0) + chosen(core, plan.starts)
        first_of = (position == 0) | (position == ends[0]) | (position == ends[1])
        base, held = plan.own + HALO, 2 * plan.own + plan.held
        table[held : held + plan.held, :] = jnp.where(
            first_of,
            table[plan.own : plan.own + 1, :],
            table[base - 1 : base - 1 + plan.held, :],
        )
        shift = held + core * (plan.own - plan.starts[1])
        keys = table[pl.ds(pl.multiple_of(shift, HALO), plan.own), :]
        gain = gain_ref[...]
        dec_keys[...] = normed(keys, gain)[0].astype(BF16)
        before_turn = lax.broadcasted_iota(jnp.int32, (plan.heads, 1), 0) < turn_of(
            plan, lengths_ref, x, core
        )

        def own_heads(first):
            def rows(offsets):
                first_place, second_place = [
                    table[first + o - s : first + o - s + plan.heads, :]
                    for o, s in zip(offsets, plan.starts)
                ]
                return jnp.where(core == 0, first_place, second_place)

            return jnp.where(before_turn, rows(plan.near), rows(plan.far))

        values = own_heads(held)
        dec_rows[...] = values
        dec_heads[...] = normed(values, gain)[0].astype(BF16)
        target_rows[...] = own_heads(base).astype(BF16)

    jobs = [prepare]
    for target, owner, after in (
        (far, (1 - x) * 2 + 1 - core, send_far),
        (near, other_x, send_near),
        (sister, x * 2 + 1 - core, send_sister),
        (found_ref, v, None),
    ):
        for part in range(share // stage.shape[0]):
            jobs.append(functools.partial(look_up, target, owner, part))
        if after:
            jobs.append(after)
    jobs = jobs[::-1]

    def work(count):
        for _ in range(min(count, len(jobs))):
            jobs.pop()()

    first, second = range(starts[0], starts[1]), range(starts[1], starts[2])
    locals_ = {}

    def each(action, wave, *rest):
        for i in wave:
            action(i, *rest)

    for i in first:
        locals_[i] = begin(i)
    locals_[second[0]] = begin(second[0])
    work(2)
    each(step, first, 1)
    for i in second[1:]:
        locals_[i] = begin(i)
    work(2)
    each(came, first, 0)
    work(2)
    each(step, first, 2)
    work(1)
    each(came, first, 1)
    work(2)
    each(step, second, 1)
    work(2)
    each(step, first, 3)
    each(spread, first)
    work(2)
    each(came, first, 2)
    work(2)
    each(step, second, 2)
    work(1)
    each(came, second, 0)
    work(len(jobs))
    for i in first:
        came(i, 3)
        spread_beside(i)
    each(came, second, 1)
    each(step, second, 3)
    each(spread, second)
    for i in first:
        if units[i][3]:
            x_came(i, "x")
    each(came, second, 2)
    finish_rows()
    for i in first:
        if units[i][3]:
            x_came(i, "yx")
    for i in second:
        came(i, 3)
        spread_beside(i)
    for i in second:
        if units[i][3]:
            x_came(i, "x")
            x_came(i, "yx")
    for copy in sums.values():
        copy.wait_send()

    for i, (source, target, whole, quarter) in enumerate(units):
        b = blocks[i]
        for tag in range(4 if quarter else 2):
            block = whole(y, b)
            remote((i, "core", tag), block, block, twin).wait()
        piece = target(z, y, b)
        remote((i, "y", 0), piece, piece, beside).wait_send()
        if quarter:
            remote((i, "yx", 0), piece, piece, across).wait_send()
        for k in range(1, rows_z):
            for side, sign in sides:
                sent = there(side, k - 1) if k > 1 else True
                pl.when(jnp.logical_and(sent, further(side)))(
                    lambda: remote((i, side, k), piece, piece, above).wait_send()
                )

                @pl.when(there(side, k))
                def _():
                    remote((i, side, k, "y"), piece, piece, beside).wait_send()
                    if quarter:
                        remote((i, side, k, "x"), piece, piece, across).wait_send()
                        remote((i, side, k, "yx"), piece, piece, across).wait_send()


def gather_weights(
    plan, attend_in, attend_out, expand_weights, reduce_weights, wanted, table, row_lengths, gain
):
    shards, rows_y = 8, 2
    rows_z = shards // rows_y
    rows = attend_in.shape[1]
    width = rows * shards
    tall = reduce_weights.shape[1]
    share = wanted.shape[1]
    valid = table.shape[0]

    def full(*tail):
        return jax.ShapeDtypeStruct((rows_z, rows_y, *tail), BF16)

    shapes = (
        [full(rows, attend_in.shape[2])] * 3
        + [full(rows, attend_out.shape[2])] * 3
        + [full(rows, expand_weights.shape[2])] * 2
        + [full(4, tall // 4, width)] * 2
        + [jax.ShapeDtypeStruct((plan.own, width), BF16)] * 2
        + [jax.ShapeDtypeStruct((plan.heads, width), kind) for kind in (F32, BF16, BF16)]
    )
    copies = 10 * (1 + 4 * (rows_z - 1) + 2) + 4 * (1 + 4 * (rows_z - 1) + 2) + 3
    anywhere, vmem, smem = [
        pl.BlockSpec(memory_space=space) for space in (pl.ANY, pltpu.VMEM, pltpu.SMEM)
    ]
    outs = pl.pallas_call(
        functools.partial(gather_kernel, plan, rows_z, rows_y),
        out_shape=shapes,
        in_specs=[anywhere] * 4 + [smem, anywhere, smem, vmem],
        out_specs=[anywhere] * 10 + [vmem] * 5,
        scratch_shapes=[
            pltpu.VMEM((share, width), BF16),
            pltpu.VMEM((valid, width), BF16),
            pltpu.VMEM((valid + 8, width), F32),
            pltpu.VMEM((share // 3, width), F32),
        ]
        + [pltpu.VMEM((share, width), BF16)] * 6
        + [
            pltpu.SemaphoreType.DMA((copies,)),
            pltpu.SemaphoreType.DMA((copies,)),
            pltpu.SemaphoreType.DMA((14,)),
            pltpu.SemaphoreType.DMA,
        ],
        compiler_params=pltpu.CompilerParams(
            collective_id=0, has_side_effects=True, vmem_limit_bytes=60 * MIB
        ),
        cost_estimate=pl.CostEstimate(flops=0, bytes_accessed=400_000_000, transcendentals=0),
    )(attend_in, attend_out, expand_weights, reduce_weights, wanted, table, row_lengths, gain[None])
    return [o.reshape(-1, o.shape[-1]) for o in outs]


def vocab_exchange_kernel(plan, tile, *refs):
    rows_ref, gain_ref, target_ref, table_ref, ids_ref, lengths_ref, tasks_ref = refs[:7]
    grad_ref, stat_ref, *scratch = refs[7:]
    tail, held, logits_a, logits_b, powers_a, powers_b, scale_a, scale_b = scratch[:8]
    maxima_ref, total_ref, targets_ref, h_ref, columns, parcel, arrived = scratch[8:15]
    stats_out, stats_in, send_sem, recv_sem = scratch[15:]
    rows, width = h_ref.shape
    valid = table_ref.shape[0]
    tiles = (valid + tile - 1) // tile
    padded = tiles * tile
    v = lax.axis_index("vocab")
    x, core = v // 2, lax.rem(v, 2)
    twin, across, diagonal = x * 2 + 1 - core, (1 - x) * 2 + core, (1 - x) * 2 + 1 - core

    barrier = pltpu.get_barrier_semaphore()
    for peer in (twin, across, diagonal):
        pl.semaphore_signal(
            barrier, inc=1, device_id={"vocab": peer}, device_id_type=pl.DeviceIdType.MESH
        )
    pl.semaphore_wait(barrier, 3)

    def remote(source, target, index, peer):
        return pltpu.make_async_remote_copy(
            src_ref=source,
            dst_ref=target,
            send_sem=send_sem.at[index],
            recv_sem=recv_sem.at[index],
            device_id={"vocab": peer},
            device_id_type=pl.DeviceIdType.MESH,
        )

    values = rows_ref[...]
    gain = gain_ref[...]
    inverse = lax.rsqrt(jnp.mean(values * values, -1, keepdims=True) + NORM_EPS)
    h_ref[...] = (values * inverse * gain * width ** (-0.5)).astype(BF16)
    to_twin = remote(h_ref, held.at[0], 0, twin)
    to_across = remote(h_ref, held.at[1], 1, across)
    passed_on = remote(held.at[1], held.at[2], 2, twin)
    results = [
        remote(parcel.at[k], arrived.at[k], 3 + k, peer)
        for k, peer in enumerate((twin, across, diagonal))
    ]
    marks = [
        remote(stats_out.at[k], stats_in.at[k], 6 + k, peer)
        for k, peer in enumerate((twin, across, diagonal))
    ]
    to_twin.start()
    to_across.start()
    held[3] = h_ref[...]

    entry = lax.broadcasted_iota(jnp.int32, (8, rows), 1)
    even = lax.rem(lax.broadcasted_iota(jnp.int32, (8, rows), 0), 2) == 0
    for place in range(plan.group):
        turns = [turn_of(plan, lengths_ref, m, place) for m in range(2)]
        near, far = plan.near[place], plan.far[place]
        picked = jnp.where(
            entry < jnp.where(even, turns[0], turns[1]),
            ids_ref[:, near : near + rows],
            ids_ref[:, far : far + rows],
        )
        columns[place] = jnp.transpose(picked)

    short = padded - valid
    if short:
        tail[: tile - short, :] = table_ref[padded - tile :, :]
        tail[tile - short :, :] = jnp.zeros((short, width), BF16)
    to_twin.wait_recv()

    logits_of, powers_of, scale_of = (logits_a, logits_b), (powers_a, powers_b), (scale_a, scale_b)
    column = lax.broadcasted_iota(jnp.int32, (rows, tile), 1)
    lane = lax.broadcasted_iota(jnp.int32, (rows, LANES), 1)

    def turn(k, _):
        @pl.when(k == 1)
        def _():
            to_across.wait_recv()
            passed_on.start()

        @pl.when(k == 2)
        def _():
            passed_on.wait_recv()

        owner = jnp.where(k == 0, twin, jnp.where(k == 1, across, jnp.where(k == 2, diagonal, v)))

        def part(at):
            if short and at == tiles - 1:
                return tail[...]
            return table_ref[at * tile : (at + 1) * tile, :]

        def scores(at):
            logits_of[at % 2][...] = dot_rows(held[k], part(at))

        def soften(at):
            logits = logits_of[at % 2][...]
            if at == tiles - 1 and padded > valid:
                logits = jnp.where(column < valid - at * tile, logits, MASKED)
            highest = jnp.maximum(maxima_ref[...], jnp.max(logits, -1, keepdims=True))
            powers = jnp.exp(logits - highest)
            scale = jnp.exp(maxima_ref[...] - highest)
            maxima_ref[...] = highest
            total_ref[...] = total_ref[...] * scale + jnp.sum(powers, -1, keepdims=True)
            scale_of[at % 2][...] = scale
            powers_of[at % 2][...] = jnp.where(
                column == targets_ref[...] - at * tile, 0.0, powers
            ).astype(BF16)

        def gather(at):
            term = dot(powers_of[at % 2][...], part(at))
            grad_ref[...] = grad_ref[...] * scale_of[at % 2][...] + term

        column_of = jnp.where(lax.rem(owner, 2) == 0, columns[0], columns[1])
        target = jnp.where(owner < 2, column_of[:, 0:1], column_of[:, 1:2])
        targets_ref[...] = target.astype(jnp.int32) - v * valid
        maxima_ref[...] = jnp.full((rows, 1), MASKED, F32)
        total_ref[...] = jnp.zeros((rows, 1), F32)
        grad_ref[...] = jnp.zeros_like(grad_ref)
        for at in range(tiles + 2):
            if at < tiles:
                scores(at)
            if 0 <= at - 1 < tiles:
                soften(at - 1)
            if at >= 2:
                gather(at - 2)

        @pl.when(k < 3)
        def _():
            parcel[k] = grad_ref[...].astype(BF16)
            side = lax.broadcasted_iota(jnp.int32, (rows, 8), 1)
            pair = jnp.where(side == 0, maxima_ref[...], total_ref[...])
            stats_out[k] = jnp.transpose(pair)

        for index, (mark, result) in enumerate(zip(marks, results)):

            @pl.when(k == index)
            def _():
                mark.start()
                result.start()

        return 0

    lax.fori_loop(0, 4, turn, 0)
    for copy in [*marks, *results]:
        copy.wait_recv()
    pairs = [jnp.transpose(stats_in[k]) for k in range(3)]
    highs = [pair[:, 0:1] for pair in pairs] + [maxima_ref[...]]
    totals = [pair[:, 1:2] for pair in pairs] + [total_ref[...]]
    highest = functools.reduce(jnp.maximum, highs)
    log_total = highest + jnp.log(sum(t * jnp.exp(m - highest) for m, t in zip(highs, totals)))
    summed = grad_ref[...] * jnp.exp(highs[3] - log_total)
    for k in range(3):
        summed = summed + arrived[k].astype(F32) * jnp.exp(highs[k] - log_total)
    target_rows = target_ref[...].astype(F32)
    target_logit = jnp.sum(h_ref[...].astype(F32) * target_rows, -1, keepdims=True)
    coefficient = (jnp.exp(target_logit - log_total) - 1.0).astype(BF16).astype(F32)
    info = row_scalars(plan, lengths_ref, True)
    position = row_positions(info, (rows, 1), 0)
    in_second, in_third = position >= info[0], position >= info[1]
    begin = jnp.where(in_third, info[1], jnp.where(in_second, info[0], 0))
    task = jnp.where(in_third, tasks_ref[x, 2], jnp.where(in_second, tasks_ref[x, 1], tasks_ref[x, 0]))
    counts = (position - begin >= P_SIZE) & (lax.broadcasted_iota(jnp.int32, (rows, 1), 0) < plan.half)
    column_of = jnp.where(core == 0, columns[0], columns[1])
    counted = jnp.where(counts, jnp.where(x == 0, column_of[:, 2:3], column_of[:, 3:4]), 0.0)
    summed = counted * (summed + coefficient * target_rows)
    grad_ref[...] = normed_back(rows_ref[...], gain_ref[...], inverse, summed * width ** (-0.5))
    of_task = jnp.where(lane == task, counted, 0.0)
    losses = jnp.sum(of_task * (log_total - target_logit), 0, keepdims=True)
    counts = jnp.sum(of_task, 0, keepdims=True)
    row = lax.broadcasted_iota(jnp.int32, stat_ref.shape, 0)
    stat_ref[...] = jnp.where(row == 0, losses, jnp.where(row == 1, counts, 0.0))
    for copy in [to_twin, to_across, passed_on, *marks, *results]:
        copy.wait_send()


def vocab_exchange(plan, rows, gain, target_rows, embedding, ids, row_lengths, row_tasks):
    count, width = rows.shape
    valid = embedding.shape[0]
    tile = 2 * VOCAB_BLOCK
    padded = (valid + tile - 1) // tile * tile
    vmem = pl.BlockSpec(memory_space=pltpu.VMEM)
    return pl.pallas_call(
        functools.partial(vocab_exchange_kernel, plan, tile),
        out_shape=[
            jax.ShapeDtypeStruct((count, width), F32),
            jax.ShapeDtypeStruct((8, LANES), F32),
        ],
        in_specs=[vmem] * 5 + [pl.BlockSpec(memory_space=pltpu.SMEM)] * 2,
        out_specs=[vmem] * 2,
        scratch_shapes=[
            pltpu.VMEM((tile, width), BF16),
            pltpu.VMEM((4, count, width), BF16),
            pltpu.VMEM((count, tile), F32),
            pltpu.VMEM((count, tile), F32),
            pltpu.VMEM((count, tile), BF16),
            pltpu.VMEM((count, tile), BF16),
            pltpu.VMEM((count, 1), F32),
            pltpu.VMEM((count, 1), F32),
            pltpu.VMEM((count, 1), F32),
            pltpu.VMEM((count, 1), F32),
            pltpu.VMEM((count, 1), jnp.int32),
            pltpu.VMEM((count, width), BF16),
            pltpu.VMEM((2, count, 8), F32),
            pltpu.VMEM((3, count, width), BF16),
            pltpu.VMEM((3, count, width), BF16),
            pltpu.VMEM((3, 8, count), F32),
            pltpu.VMEM((3, 8, count), F32),
            pltpu.SemaphoreType.DMA((9,)),
            pltpu.SemaphoreType.DMA((9,)),
        ],
        compiler_params=pltpu.CompilerParams(
            collective_id=1, has_side_effects=True, vmem_limit_bytes=44 * MIB
        ),
        cost_estimate=pl.CostEstimate(
            flops=30 * count * padded * width, bytes_accessed=2 * valid * width, transcendentals=0
        ),
    )(rows, gain[None], target_rows, embedding, ids, row_lengths, row_tasks)


def reduce_kernel(rows_dp, task_ref, table_ref, stat_ref, out_ref, stats_out, squares_out, *scratch):
    cast, crossed, swap, swapped, own, outgoing, pieces, result, results = scratch[:9]
    stats, squares, send_sem, recv_sem = scratch[9:]
    features = own.shape[1]
    at, v = lax.axis_index("dp"), lax.axis_index("vocab")
    x, core = v // 2, lax.rem(v, 2)
    twin, across = x * 2 + 1 - core, (1 - x) * 2 + core
    dp_peers = [lax.rem(at + k, rows_dp) for k in range(1, rows_dp)]
    vocab_peers = [lax.rem(v + k, 4) for k in range(1, 4)]

    barrier = pltpu.get_barrier_semaphore()
    for peer in [{"vocab": p} for p in vocab_peers] + [{"dp": p} for p in dp_peers]:
        pl.semaphore_signal(barrier, inc=1, device_id=peer, device_id_type=pl.DeviceIdType.MESH)
    pl.semaphore_wait(barrier, rows_dp + 2)

    def remote(source, target, send, recv, peer):
        return pltpu.make_async_remote_copy(
            src_ref=source,
            dst_ref=target,
            send_sem=send_sem.at[send],
            recv_sem=recv_sem.at[recv],
            device_id=peer,
            device_id_type=pl.DeviceIdType.MESH,
        )

    half = 2 * features
    there = pl.ds(pl.multiple_of((1 - x) * half, half), half)
    here = pl.ds(pl.multiple_of(x * half, half), half)
    stats[0] = stat_ref[...]
    cast[...] = table_ref[there, :].astype(BF16)
    over_x = remote(cast, crossed, 0, 0, {"vocab": across})
    stat_x = remote(stats.at[0], stats.at[1], 1, 1, {"vocab": across})
    over_x.start()
    stat_x.start()
    over_x.wait_recv()
    stat_x.wait_recv()

    stats[2] = stats[0] + stats[1]
    stat_core = remote(stats.at[2], stats.at[3], 2, 2, {"vocab": twin})
    stat_core.start()
    tasks = [[task_ref[m, s] for s in range(task_ref.shape[1])] for m in range(2)]
    other = jnp.where(x == 0, 1, 0)

    def by_task(part, t):
        start = pl.multiple_of(part * features, features)
        mine = table_ref[pl.ds(pl.multiple_of(x * half + part * features, features), features), :]
        theirs = crossed[pl.ds(start, features), :].astype(F32)
        total = jnp.zeros((features, LANES), F32)
        for s in range(task_ref.shape[1]):
            lanes = slice(s * LANES, (s + 1) * LANES)
            mine_task = jnp.where(x == 0, tasks[0][s], tasks[1][s])
            their_task = jnp.where(x == 0, tasks[1][s], tasks[0][s])
            total = total + jnp.where(mine_task == t, mine[:, lanes], 0.0)
            total = total + jnp.where(their_task == t, theirs[:, lanes], 0.0)
        return total

    for t in range(TASKS):
        swap[t] = by_task(1 - core, t).astype(BF16)
    over_core = remote(swap, swapped, 3, 3, {"vocab": twin})
    over_core.start()
    for t in range(TASKS):
        own[t] = by_task(core, t)
    over_core.wait_recv()
    stat_core.wait_recv()
    stats[4 + at] = stats[2] + stats[3]
    for t in range(TASKS):
        own[t] = own[t] + swapped[t].astype(F32)
        outgoing[t] = own[t].astype(BF16)

    base = 4
    spread, tallies = [], []
    for k, peer in enumerate(dp_peers):
        spread.append(
            remote(outgoing.at[peer], pieces.at[at], base + k, base + at, {"dp": peer})
        )
        tallies.append(
            remote(
                stats.at[4 + at],
                stats.at[4 + at],
                base + rows_dp + k,
                base + rows_dp + at,
                {"dp": peer},
            )
        )
    for copy in spread + tallies:
        copy.start()
    total = own[at]
    for peer in dp_peers:
        remote(outgoing.at[peer], pieces.at[peer], base, base + peer, {"dp": peer}).wait_recv()
        total = total + pieces[peer].astype(F32)
    result[...] = total.astype(BF16)
    results[at] = result[...]
    returns = []
    for k, peer in enumerate(dp_peers):
        returns.append(
            remote(
                result,
                results.at[at],
                base + 2 * rows_dp + k,
                base + 2 * rows_dp + at,
                {"dp": peer},
            )
        )
    for copy in returns:
        copy.start()
    for peer in dp_peers:
        remote(
            stats.at[4 + peer], stats.at[4 + peer], base, base + rows_dp + peer, {"dp": peer}
        ).wait_recv()
    tally = functools.reduce(jnp.add, [stats[4 + k] for k in range(rows_dp)])
    stats_out[...] = tally
    for peer in dp_peers:
        remote(result, results.at[peer], base, base + 2 * rows_dp + peer, {"dp": peer}).wait_recv()
    for t in range(TASKS):
        scale = 1.0 / (TASKS * jnp.maximum(tally[1:2, t : t + 1], 1.0))
        scaled = results[t].astype(F32) * scale
        out_ref[t] = scaled
        squares[v, t : t + 1, :] = jnp.sum(scaled * scaled, 0, keepdims=True)
    last = base + 3 * rows_dp
    shares = [
        remote(squares.at[v], squares.at[v], last + k, last + v, {"vocab": peer})
        for k, peer in enumerate(vocab_peers)
    ]
    for copy in shares:
        copy.start()
    for peer in vocab_peers:
        remote(squares.at[peer], squares.at[peer], last, last + peer, {"vocab": peer}).wait_recv()
    squares_out[...] = squares[0] + squares[1] + squares[2] + squares[3]
    for copy in [over_x, stat_x, stat_core, over_core, *spread, *tallies, *returns, *shares]:
        copy.wait_send()


def reduce_over_devices(task_list, table, stats):
    rows_dp = lax.axis_size("dp")
    features = table.shape[0] // 4
    vmem = pl.BlockSpec(memory_space=pltpu.VMEM)
    copies = 4 + 3 * rows_dp + 4
    return pl.pallas_call(
        functools.partial(reduce_kernel, rows_dp),
        out_shape=[
            jax.ShapeDtypeStruct((TASKS, features, LANES), F32),
            jax.ShapeDtypeStruct((8, LANES), F32),
            jax.ShapeDtypeStruct((8, LANES), F32),
        ],
        in_specs=[pl.BlockSpec(memory_space=pltpu.SMEM), vmem, vmem],
        out_specs=[vmem] * 3,
        scratch_shapes=[
            pltpu.VMEM((2 * features, table.shape[1]), BF16),
            pltpu.VMEM((2 * features, table.shape[1]), BF16),
            pltpu.VMEM((TASKS, features, LANES), BF16),
            pltpu.VMEM((TASKS, features, LANES), BF16),
            pltpu.VMEM((TASKS, features, LANES), F32),
            pltpu.VMEM((TASKS, features, LANES), BF16),
            pltpu.VMEM((rows_dp, features, LANES), BF16),
            pltpu.VMEM((features, LANES), BF16),
            pltpu.VMEM((rows_dp, features, LANES), BF16),
            pltpu.VMEM((4 + rows_dp, 8, LANES), F32),
            pltpu.VMEM((4, 8, LANES), F32),
            pltpu.SemaphoreType.DMA((copies,)),
            pltpu.SemaphoreType.DMA((copies,)),
        ],
        compiler_params=pltpu.CompilerParams(
            collective_id=2, has_side_effects=True, vmem_limit_bytes=24 * MIB
        ),
    )(task_list, table, stats)


def on_device(
    tokens,
    targets,
    loss_mask,
    seg_lengths,
    task_ids,
    embedding,
    attend_in,
    attend_out,
    expand_weights,
    reduce_weights,
    norm_gains,
    prompt,
    first_moment,
    row_moment,
    column_moment,
):
    shards = lax.axis_size("vocab")
    micros, span = tokens.shape[0], tokens.shape[-1]
    length = span * shards
    group = shards // micros
    own = length // group
    me = lax.axis_index("vocab")
    micro, place = me // group, me % group
    shard_rows, width = embedding.shape
    share = prompt.shape[-1]

    def around(array, shift):
        pairs = [
            (m * group + r, m * group + (r + shift) % group)
            for m in range(micros)
            for r in range(group)
        ]
        return lax.ppermute(array, "vocab", pairs)

    ids = lax.all_gather(jnp.stack([tokens[:, 0], targets[:, 0], loss_mask[:, 0]]), "vocab")
    ids = jnp.transpose(ids, (1, 2, 0, 3)).reshape(3, micros, length)
    enc_ids = ids[0].reshape(shards, own)

    row_lengths, row_tasks = seg_lengths[:, 0], task_ids[:, 0]
    compact = group == 2 and 2 * span + 2 * P_SIZE <= length - span
    if compact:
        half = (length - SEGS * P_SIZE) // group
        extra = (half + 2 * P_SIZE - own + HALO - 1) // HALO * HALO
        heads = (half + LANES - 1) // LANES * LANES
        near, far = (P_SIZE, half + 2 * P_SIZE), (2 * P_SIZE, half + 3 * P_SIZE)
        plan = Plan(length, group, own, own + extra, heads, half, (0, own - extra), near, far)
    else:
        starts = tuple(p * own for p in range(group))
        plan = Plan(length, group, own, own, own, own, starts, starts, starts)
    held, heads, half, starts = plan.held, plan.heads, plan.half, plan.starts
    turns = [
        row_lengths[:, 0] - P_SIZE if p == 0 else length - row_lengths[:, 2] - plan.near[-1]
        for p in range(group)
    ]
    entries = jnp.arange(heads, dtype=jnp.int32)

    def of_rows(values, m, p):
        near, far = plan.near[p], plan.far[p]
        values = jnp.pad(values, (0, heads + far))
        return jnp.where(
            entries < turns[p][m], values[near : near + heads], values[far : far + heads]
        )

    everyone = [(m, p) for m in range(micros) for p in range(group)]
    dec_ids = jnp.stack(
        [
            jnp.concatenate(
                [
                    jnp.zeros((HALO - 1,), jnp.int32),
                    jnp.pad(ids[1, m], (1, 0))[starts[p] : starts[p] + 1 + held],
                ]
            )
            for m, p in everyone
        ]
    )
    first_row = me * shard_rows

    def here(wanted):
        local = wanted - first_row
        inside = (local >= 0) & (local < shard_rows)
        return local, inside

    prompt_low = jnp.swapaxes(prompt, 1, 2).astype(BF16)
    prompt_low = jnp.pad(prompt_low, ((0, 0), (0, 0), (0, LANES - P_SIZE)))
    prompt_all = lax.all_gather(prompt_low, "vocab", axis=1, tiled=True)
    lengths = lax.dynamic_index_in_dim(row_lengths, micro, 0, False)
    tasks = lax.dynamic_index_in_dim(row_tasks, micro, 0, False)
    weights = (attend_in, attend_out, expand_weights, reduce_weights)
    on_links = lax.axis_size("dp") == 8 and shards == 4 and shard_rows % 32 == 0 and compact
    if on_links:
        local, inside = here(jnp.concatenate([enc_ids, dec_ids], 1))
        wanted = jnp.where(inside, local, shard_rows)
        *flat, enc_rows, keys_low, dec_input, heads_low, target_rows = gather_weights(
            plan, *weights, wanted, embedding, row_lengths, norm_gains[3]
        )
        attend_in, attend_out = flat[:3], flat[3:6]
        expand_weights, reduce_weights = flat[6:8], flat[8:10]
    else:

        def lookup(wanted):
            local, inside = here(wanted.reshape(-1))
            picked = jnp.take(embedding, jnp.clip(local, 0, shard_rows - 1), axis=0)
            picked = jnp.where(inside[:, None], picked, 0)
            return lax.psum_scatter(picked, "vocab", scatter_dimension=0, tiled=True)

        enc_rows, dec_rows = lookup(enc_ids), lookup(dec_ids)
        whole = [lax.all_gather(tensor, "dp", axis=1, tiled=True) for tensor in weights]
        attend_in, attend_out, expand_weights, reduce_weights = whole
        turn = jnp.stack(turns)[place, micro]
        near_row = jnp.asarray(plan.near, jnp.int32)[place]
        far_row = jnp.asarray(plan.far, jnp.int32)[place]
        first_held = jnp.asarray(starts, jnp.int32)[place]
        head_positions = jnp.where(entries < turn, near_row, far_row) + entries
        head_positions = jnp.minimum(head_positions, length - 1)
        _, head_in_segment, head_task = layout(lengths, tasks, head_positions)
        head_mask_row = jnp.stack([of_rows(ids[2, m], m, p) for m, p in everyone])[me]
        counted = (head_mask_row * ((head_in_segment >= P_SIZE) & (entries < half))).astype(F32)

        def head_rows(values):
            values = jnp.pad(values, ((0, heads), (0, 0)))
            shape = (heads, values.shape[1])
            return jnp.where(
                (entries < turn)[:, None],
                lax.dynamic_slice(values, (near_row - first_held, 0), shape),
                lax.dynamic_slice(values, (far_row - first_held, 0), shape),
            )

        held_positions = first_held + jnp.arange(held, dtype=jnp.int32)
        begun = layout(lengths, tasks, held_positions)[1] >= 1
        dec_held = jnp.where(begun[:, None], dec_rows[HALO - 1 : HALO - 1 + held], dec_rows[:1])
        dec_keys = lax.dynamic_slice(dec_held, (place * own - first_held, 0), (own, width))
        keys_low = normed(dec_keys.astype(F32), norm_gains[3])[0].astype(BF16)
        dec_input = head_rows(dec_held).astype(F32)
        heads_low = normed(dec_input, norm_gains[3])[0].astype(BF16)
        target_rows = head_rows(dec_rows[HALO:])

    def key_parts(source, weight):
        pair = dot(source, weight).astype(BF16)
        return [pair] + [around(pair, k) for k in range(1, group)]

    positions = place * own + jnp.arange(own, dtype=jnp.int32)
    segment, in_segment, _ = layout(lengths, tasks, positions)
    is_prompt = in_segment < P_SIZE
    place_of = jnp.where(is_prompt, segment * LANES + in_segment, -1)
    chosen_place = place_of[:, None] == jnp.arange(SEGS * LANES, dtype=jnp.int32)
    chosen_low = chosen_place.astype(BF16)

    if on_links:
        enc_input, enc_queries, enc_pairs, dec_queries, dec_pairs = project(
            plan,
            enc_rows,
            prompt_all,
            keys_low,
            heads_low,
            norm_gains[0],
            row_lengths,
            row_tasks,
            attend_in[0],
            attend_in[1],
        )
    else:
        prompts = jnp.concatenate(
            [lax.dynamic_index_in_dim(prompt_all, tasks[j], 0, False) for j in range(SEGS)], 1
        )
        prompt_rows = dot_rows(chosen_low, prompts)
        enc_input = jnp.where(is_prompt[:, None], prompt_rows, enc_rows.astype(F32))
        normed_low = normed(enc_input, norm_gains[0])[0].astype(BF16)
        enc_pairs = key_parts(normed_low, attend_in[0][:, width:])
        enc_queries = dot(normed_low, attend_in[0][:, :width]).astype(BF16)
        dec_pairs = key_parts(keys_low, attend_in[1][:, width:])
        dec_queries = dot(heads_low, attend_in[1][:, :width]).astype(BF16)
    enc_mid, enc_mixed, enc_logs, enc_last, enc_kept = attend(
        plan,
        enc_queries,
        enc_pairs,
        enc_input,
        attend_out[0],
        row_lengths,
        False,
        False,
        (norm_gains[1], expand_weights[0], reduce_weights[0]),
    )
    encoded = normed(enc_last, norm_gains[2])[0].astype(BF16)
    cross_pairs = key_parts(encoded, attend_in[2][:, width:])

    dec_first = attend(
        plan, dec_queries, dec_pairs, dec_input, attend_out[1], row_lengths, True, True
    )[0]
    cross_source = normed(dec_first, norm_gains[4])[0].astype(BF16)
    cross_queries = dot(cross_source, attend_in[2][:, :width]).astype(BF16)
    dec_second, cross_mixed, cross_logs, dec_last, dec_kept = attend(
        plan,
        cross_queries,
        cross_pairs,
        dec_first,
        attend_out[2],
        row_lengths,
        True,
        False,
        (norm_gains[5], expand_weights[1], reduce_weights[1]),
    )

    if on_links:
        wide = (plan.far[-1] + heads + LANES - 1) // LANES * LANES
        marks = jnp.pad(
            jnp.concatenate([ids[1], ids[2]]).astype(F32), ((0, 4), (0, wide - length))
        )
        dec_grad, stats = vocab_exchange(
            plan, dec_last, norm_gains[6], target_rows, embedding, marks, row_lengths, row_tasks
        )
    else:
        output_norm, inverse_out = normed(dec_last, norm_gains[6])
        hidden = (output_norm * width ** (-0.5)).astype(BF16)
        all_hidden = lax.all_gather(hidden, "vocab", axis=0, tiled=True)
        head_targets = jnp.concatenate([of_rows(ids[1, m], m, p) for m, p in everyone])
        target_local = head_targets[:, None] - first_row
        part, stats = vocab_pass(all_hidden, target_local, embedding, heads)
        gathered = lax.all_gather(stats[:, :2].T, "vocab")
        maxima = jnp.max(gathered[:, 0], 0)
        log_total = maxima + jnp.log(
            jnp.sum(gathered[:, 1] * jnp.exp(gathered[:, 0] - maxima), 0)
        )
        scaled = part * jnp.exp(stats[:, 0] - log_total)[:, None]
        summed = lax.psum_scatter(scaled, "vocab", scatter_dimension=0, tiled=True)
        own_total = lax.dynamic_slice(log_total, (me * heads,), (heads,))
        target_values = target_rows.astype(F32)
        target_logit = jnp.sum(hidden.astype(F32) * target_values, -1)
        coefficient = (jnp.exp(target_logit - own_total) - 1.0).astype(BF16).astype(F32)
        hidden_grad = counted[:, None] * (summed + coefficient[:, None] * target_values)
        dec_grad = normed_back(
            dec_last, norm_gains[6], inverse_out, hidden_grad * width ** (-0.5)
        )
        losses = per_task(head_task, counted * (own_total - target_logit))
        tallies = jnp.stack([losses, per_task(head_task, counted)])
        stats = jnp.zeros((8, LANES), F32).at[:2, :TASKS].set(tallies)

    def keys_back(pairs, weight):
        total = pairs[0]
        for k in range(1, group):
            total = total + around(pairs[k], group - k)
        high = total.astype(BF16)
        rest = (total - high.astype(F32)).astype(BF16)
        return dot_rows(high, weight) + dot_rows(rest, weight)

    dec_grad = feed_back(
        dec_grad, dec_second, norm_gains[5], dec_kept, expand_weights[1], reduce_weights[1]
    )
    back = attend_back(
        plan,
        cross_queries,
        cross_pairs,
        dec_grad,
        attend_out[2],
        cross_mixed,
        cross_logs,
        row_lengths,
        True,
        False,
        (attend_in[2], enc_last, norm_gains[2], 3) if on_links else None,
    )
    if on_links:
        enc_grad = back
    else:
        inverse_last = normed(enc_last, norm_gains[2])[1]
        enc_grad = normed_back(
            enc_last, norm_gains[2], inverse_last, keys_back(back, attend_in[2][:, width:])
        )
    enc_grad = feed_back(
        enc_grad, enc_mid, norm_gains[1], enc_kept, expand_weights[0], reduce_weights[0]
    )
    back = attend_back(
        plan,
        enc_queries,
        enc_pairs,
        enc_grad,
        attend_out[0],
        enc_mixed,
        enc_logs,
        row_lengths,
        False,
        True,
        (attend_in[0], enc_input, norm_gains[0], 4) if on_links else None,
    )
    if on_links:
        enc_grad = back
    else:
        *back, back_queries = back
        source_grad = keys_back(back, attend_in[0][:, width:]) + lax.dot_general(
            back_queries,
            attend_in[0][:, :width],
            (((0,), (1,)), ((), ())),
            preferred_element_type=F32,
        )
        inverse_in = normed(enc_input, norm_gains[0])[1]
        enc_grad = enc_grad + normed_back(enc_input, norm_gains[0], inverse_in, source_grad)

    high = enc_grad.astype(BF16)
    rest = (enc_grad - high.astype(F32)).astype(BF16)
    table = dot_columns(high, chosen_low) + dot_columns(rest, chosen_low)
    if on_links:
        gradient, stats, squares = reduce_over_devices(row_tasks, table, stats)
        full_grad = jnp.swapaxes(gradient[:, :, :P_SIZE], 1, 2)
        row_squares = squares[:, :P_SIZE]
        task_scale = 1.0 / (TASKS * jnp.maximum(stats[1, :TASKS], 1.0))
    else:
        hits = (tasks[:, None] == jnp.arange(TASKS, dtype=jnp.int32)).astype(F32)
        by_task = jnp.einsum(
            "fsp,st->tpf",
            table.reshape(width, SEGS, LANES)[:, :, :P_SIZE],
            hits,
            precision=lax.Precision.HIGHEST,
        )
        stats = lax.psum(stats, ("dp", "vocab"))
        gradient = lax.psum_scatter(by_task, "vocab", scatter_dimension=2, tiled=True)
        task_scale = 1.0 / (TASKS * jnp.maximum(stats[1, :TASKS], 1.0))
        full_grad = lax.psum(gradient, "dp") * task_scale[:, None, None]
        row_squares = jnp.sum(lax.all_gather(jnp.sum(full_grad * full_grad, -1), "vocab"), 0)
    loss_mean = jnp.sum(stats[0, :TASKS] * task_scale)
    grad_norm = jnp.sqrt(jnp.sum(row_squares))
    clip = CLIP_NORM / jnp.maximum(grad_norm, CLIP_NORM)
    prompt_grad = full_grad * clip
    row_second = BETA_TWO * row_moment + (1.0 - BETA_TWO) * (
        row_squares * clip * clip / width + SQUARE_EPS
    )
    column_second = BETA_TWO * column_moment + (1.0 - BETA_TWO) * (
        jnp.mean(prompt_grad * prompt_grad, 1) + SQUARE_EPS
    )
    new_moment = BETA_ONE * first_moment + (1.0 - BETA_ONE) * prompt_grad
    estimate = (
        row_second[:, :, None] * column_second[:, None, :] / jnp.mean(row_second, -1)[:, None, None]
    )
    update = new_moment / (1.0 - BETA_ONE**STEP) / jnp.sqrt(estimate / (1.0 - BETA_TWO**STEP))
    new_prompt = prompt - LEARN_RATE * (update + WEIGHT_DECAY * prompt)
    return (loss_mean, grad_norm, prompt_grad, new_moment, row_second, column_second, new_prompt)


def solution(mesh):
    placed = (
        P(None, "dp", "vocab"),
        P(None, "dp", "vocab"),
        P(None, "dp", "vocab"),
        P(None, "dp", None),
        P(None, "dp", None),
        P("vocab", None),
        P(None, "dp", None),
        P(None, "dp", None),
        P(None, "dp", None),
        P(None, "dp", None),
        P(),
        P(None, None, "vocab"),
        P(None, None, "vocab"),
        P(),
        P(None, "vocab"),
    )
    return jax.shard_map(
        on_device,
        mesh=mesh,
        in_specs=placed,
        out_specs=(
            P(),
            P(),
            P(None, None, "vocab"),
            P(None, None, "vocab"),
            P(),
            P(None, "vocab"),
            P(None, None, "vocab"),
        ),
        check_vma=False,
    )
```

```python
import collections
import functools

import jax
import jax.numpy as jnp
from jax import lax
from jax.experimental import pallas as pl
from jax.experimental.pallas import tpu as pltpu
from jax.sharding import PartitionSpec as P

DH = 64
P_SIZE = 100
TASKS = 8
STEP = 5
HALO = 16
LANES = 128
SEGS = 3
VOCAB_BLOCK = 1024
HIDDEN_PIECE = 512
MIB = 1024 * 1024

NORM_EPS = 1e-06
CLIP_NORM = 2e-05
BETA_ONE = 0.9
BETA_TWO = 0.999
LEARN_RATE = 1.0
WEIGHT_DECAY = 1e-05
SQUARE_EPS = 1e-30
MASKED = -1e30

F32 = jnp.float32
BF16 = jnp.bfloat16


def dot(left, right):
    return jnp.dot(left, right, preferred_element_type=F32)


def dot_rows(left, right):
    return lax.dot_general(left, right, (((1,), (1,)), ((), ())), preferred_element_type=F32)


def dot_columns(left, right):
    return lax.dot_general(left, right, (((0,), (0,)), ((), ())), preferred_element_type=F32)


def normed(values, gain):
    inverse = lax.rsqrt(jnp.mean(values * values, -1, keepdims=True) + NORM_EPS)
    return (values * inverse * gain, inverse)


def normed_back(values, gain, inverse, gradient):
    unit_rows = values * inverse
    scaled = gradient * gain
    return inverse * (scaled - unit_rows * jnp.mean(scaled * unit_rows, -1, keepdims=True))


def smooth(values):
    return jax.nn.gelu(values, approximate=True)


def layout(lengths, task_list, positions):
    seg_ends = jnp.cumsum(lengths)
    seg_starts = seg_ends - lengths
    segment = jnp.sum((positions[:, None] >= seg_ends[None, :]).astype(jnp.int32), -1)
    member = segment[:, None] == jnp.arange(lengths.shape[0], dtype=jnp.int32)[None, :]
    in_segment = positions - jnp.sum(jnp.where(member, seg_starts[None, :], 0), -1)
    task_of = jnp.sum(jnp.where(member, task_list[None, :], 0), -1)
    return (segment, in_segment, task_of)


def per_task(task_of, amounts):
    hits = task_of[:, None] == jnp.arange(TASKS, dtype=jnp.int32)
    return jnp.sum(jnp.where(hits, amounts[:, None], 0.0), 0)


def pair_lanes(pair, first=0):
    return pl.ds(pl.multiple_of(first + pair * LANES, LANES), LANES)


def head_mask(shape, head, axis=1):
    return (lax.broadcasted_iota(jnp.int32, shape, axis) < DH) == (head == 0)


Plan = collections.namedtuple(
    "Plan", ["length", "group", "own", "held", "heads", "half", "starts", "near", "far"]
)


def chosen(index, values):
    result = values[0]
    for k, value in enumerate(values[1:], 1):
        result = jnp.where(index == k, value, result)
    return result


def turn_of(plan, lengths_ref, m, place):
    last = plan.length - lengths_ref[m, SEGS - 1] - plan.near[-1]
    return jnp.where(place == 0, lengths_ref[m, 0] - P_SIZE, last)


def row_scalars(plan, lengths_ref, decoder):
    v = lax.axis_index("vocab")
    m, place = v // plan.group, lax.rem(v, plan.group)
    first = lengths_ref[m, 0]
    ends = [first, first + lengths_ref[m, 1]]
    if decoder:
        rows = [
            turn_of(plan, lengths_ref, m, place),
            chosen(place, plan.near),
            chosen(place, plan.far),
        ]
    else:
        rows = [0, place * plan.own, place * plan.own]
    starts = [lax.rem(place - k + plan.group, plan.group) * plan.own for k in range(plan.group)]
    return [*ends, *rows, *starts]


def row_positions(info, shape, axis):
    row = lax.broadcasted_iota(jnp.int32, shape, axis)
    return row + jnp.where(row < info[SEGS - 1], info[SEGS], info[SEGS + 1])


def key_positions(info, parts, own, shape, axis):
    row = lax.broadcasted_iota(jnp.int32, shape, axis)
    position = row + info[SEGS + 2]
    for k in range(1, parts):
        position = jnp.where(row < k * own, position, row - k * own + info[SEGS + 2 + k])
    return position


def segment_columns(info, position, is_key):
    segment = sum(jnp.where(position >= info[j], 1, 0) for j in range(SEGS - 1))
    column = lax.rem(lax.broadcasted_iota(jnp.int32, position.shape, 1), DH)
    if is_key:
        return jnp.where((column < SEGS) & (column != segment), MASKED, 0.0).astype(BF16)
    return jnp.where(column == segment, 1.0, 0.0).astype(BF16)


def head_part(values, rest, head):
    return jnp.where(head_mask(values.shape, head), values, rest)


def over_heads(pairs, scores, soften, mix):
    scores(0, 0)
    scores(0, 1)
    soften(0, 0)

    def step(pair, _):
        scores(pair + 1, 0)
        soften(pair, 1)
        mix(pair, 0)
        scores(pair + 1, 1)
        soften(pair + 1, 0)
        mix(pair, 1)
        return 0

    lax.fori_loop(0, pairs - 1, step, 0)
    soften(pairs - 1, 1)
    mix(pairs - 1, 0)
    mix(pairs - 1, 1)


def feed_pieces(rows_ref, gain_ref, one, two, out_ref, before_ref, source, held_of, active_of):
    count = one.shape[1] // HIDDEN_PIECE
    rows = rows_ref[...]
    source[...] = normed(rows, gain_ref[...])[0].astype(BF16)
    out_ref[...] = rows
    for n in range(count + 2):
        if n < count:
            here = slice(n * HIDDEN_PIECE, (n + 1) * HIDDEN_PIECE)
            before = dot(source[...], one[:, here])
            held_of[n % 2][...] = before
            before_ref[:, here] = before
        if 0 < n <= count:
            active_of[(n - 1) % 2][...] = smooth(held_of[(n - 1) % 2][...]).astype(BF16)
        if n >= 2:
            there = slice((n - 2) * HIDDEN_PIECE, (n - 1) * HIDDEN_PIECE)
            out_ref[...] += dot(active_of[n % 2][...], two[there, :])


def attend_kernel(plan, parts, decoder, causal, fed, *refs):
    q_ref, pair_refs = refs[0], refs[1 : 1 + parts]
    residual_ref, weight_ref, lengths_ref = refs[1 + parts : 4 + parts]
    refs = refs[4 + parts :]
    if fed:
        gain_ref, one_hbm, two_hbm, out_ref, mixed_ref, log_ref, last_ref, before_ref = refs[:8]
        *refs, one, two, source, held_a, held_b, active_a, active_b, sems = refs[8:]
        loads = [
            pltpu.make_async_copy(one_hbm, one, sems.at[0]),
            pltpu.make_async_copy(two_hbm, two, sems.at[1]),
        ]
        for load in loads:
            load.start()
    else:
        out_ref, mixed_ref, log_ref, *refs = refs
    info = row_scalars(plan, lengths_ref, decoder)
    bias_ref, q_mark, k_mark, low_ref, scores_a, scores_b, powers_a, powers_b = refs
    width = q_ref.shape[1]
    own = pair_refs[0].shape[0]
    scores_of, powers_of = (scores_a, scores_b), (powers_a, powers_b)
    rows = [slice(k * own, (k + 1) * own) for k in range(parts)]
    q_mark[...] = segment_columns(info, row_positions(info, q_mark.shape, 0), False)
    k_mark[...] = segment_columns(info, key_positions(info, parts, own, k_mark.shape, 0), True)
    if causal:
        shape = bias_ref.shape
        later = row_positions(info, shape, 0) >= key_positions(info, parts, own, shape, 1)
        bias_ref[...] = jnp.where(later, 0.0, MASKED)
    log_ref[...] = jnp.zeros_like(log_ref)
    lane = lax.broadcasted_iota(jnp.int32, log_ref.shape, 1)

    def scores(pair, head):
        query = q_ref[:, pair_lanes(pair)] * jnp.asarray(DH ** (-0.5), BF16)
        query = head_part(query, q_mark[...], head)
        for k in range(parts):
            keys = head_part(pair_refs[k][:, pair_lanes(pair)], k_mark[rows[k], :], head)
            values = dot_rows(query, keys)
            if causal:
                values = values + bias_ref[:, rows[k]]
            scores_of[head][:, rows[k]] = values

    def soften(pair, head):
        values = scores_of[head][...]
        highest = jnp.max(values, -1, keepdims=True)
        powers_of[head][...] = jnp.exp(values - highest).astype(BF16)
        log_ref[...] += jnp.where(lane == 2 * pair + head, highest, 0.0)

    def mix(pair, head):
        value = None
        for k in range(parts):
            values = pair_refs[k][:, pair_lanes(pair, width)]
            values = head_part(values, jnp.ones_like(values), head)
            term = dot(powers_of[head][:, rows[k]], values)
            value = term if value is None else value + term
        total = value[:, LANES - 1 :] if head == 0 else value[:, :1]
        value = value / total
        log_ref[...] += jnp.where(lane == 2 * pair + head, jnp.log(total), 0.0)
        lanes = pair_lanes(pair)
        if head:
            value = jnp.where(head_mask(value.shape, 0), mixed_ref[:, lanes], value)
        mixed_ref[:, lanes] = value
        if head:
            low_ref[:, lanes] = value.astype(BF16)

    over_heads(width // LANES, scores, soften, mix)
    out_ref[...] = residual_ref[...] + dot(low_ref[...], weight_ref[...])
    if fed:
        for load in loads:
            load.wait()
        feed_pieces(
            out_ref, gain_ref, one, two, last_ref, before_ref, source, (held_a, held_b), (active_a, active_b)
        )


def attend(plan, queries, pairs, residual, weight, row_lengths, decoder, causal, feed=None):
    own, width = queries.shape
    parts, length = len(pairs), sum(pair.shape[0] for pair in pairs)
    vmem = pl.BlockSpec(memory_space=pltpu.VMEM)
    operands = [queries, *pairs, residual, weight, row_lengths]
    in_specs = [vmem] * (parts + 3) + [pl.BlockSpec(memory_space=pltpu.SMEM)]
    rows = jax.ShapeDtypeStruct((own, width), F32)
    shapes = [rows, rows, jax.ShapeDtypeStruct((own, LANES), F32)]
    scratch = [
        pltpu.VMEM((own, length) if causal else (8, LANES), F32),
        pltpu.VMEM((own, LANES), BF16),
        pltpu.VMEM((length, LANES), BF16),
        pltpu.VMEM((own, width), BF16),
        pltpu.VMEM((own, length), F32),
        pltpu.VMEM((own, length), F32),
        pltpu.VMEM((own, length), BF16),
        pltpu.VMEM((own, length), BF16),
    ]
    if feed:
        gain, one, two = feed
        operands += [gain[None], one, two]
        in_specs += [vmem] + [pl.BlockSpec(memory_space=pl.ANY)] * 2
        shapes += [rows, jax.ShapeDtypeStruct((own, one.shape[1]), F32)]
        scratch += [pltpu.VMEM(one.shape, BF16), pltpu.VMEM(two.shape, BF16)]
        scratch += [pltpu.VMEM((own, width), BF16)]
        scratch += [pltpu.VMEM((own, HIDDEN_PIECE), F32)] * 2
        scratch += [pltpu.VMEM((own, HIDDEN_PIECE), BF16)] * 2 + [pltpu.SemaphoreType.DMA((2,))]
    return pl.pallas_call(
        functools.partial(attend_kernel, plan, parts, decoder, causal, feed is not None),
        out_shape=shapes,
        in_specs=in_specs,
        out_specs=[vmem] * len(shapes),
        scratch_shapes=scratch,
        compiler_params=pltpu.CompilerParams(vmem_limit_bytes=(26 + own // 32 if feed else 24) * MIB),
        cost_estimate=pl.CostEstimate(
            flops=44 * own * length * width, bytes_accessed=6 * own * width, transcendentals=0
        ),
    )(*operands)


def attend_back_kernel(plan, parts, decoder, want_queries, exchange, *refs):
    q_ref, pair_refs = refs[0], refs[1 : 1 + parts]
    grad_ref, weight_ref, mixed_ref, log_ref, lengths_ref = refs[1 + parts : 6 + parts]
    info = row_scalars(plan, lengths_ref, decoder)
    rest = refs[6 + parts :]
    if exchange:
        in_hbm, rows_hbm, gain_ref, result_ref = rest[:4]
        part_refs, arrived, send_sem, recv_sem = rest[4:6], rest[6], rest[7], rest[8]
        dq_ref, in_ref, rows_ref, late_sems = rest[9:13]
        rest = rest[13:]
        late = [
            pltpu.make_async_copy(in_hbm, in_ref, late_sems.at[0]),
            pltpu.make_async_copy(rows_hbm, rows_ref, late_sems.at[1]),
        ]
        for copy in late:
            copy.start()
        v = lax.axis_index("vocab")
        twin = {"vocab": v // 2 * 2 + 1 - lax.rem(v, 2)}
        barrier = pltpu.get_barrier_semaphore()
        pl.semaphore_signal(barrier, inc=1, device_id=twin, device_id_type=pl.DeviceIdType.MESH)
        pl.semaphore_wait(barrier, 1)
    else:
        part_refs = rest[:parts]
        dq_ref = rest[parts] if want_queries else None
        rest = rest[parts + want_queries :]
    q_mark, k_mark, low_ref, delta_ref, *rest = rest
    scores_of, grads_of, weights_of, steps_of = rest[0:2], rest[2:4], rest[4:6], rest[6:8]
    width = q_ref.shape[1]
    own = pair_refs[0].shape[0]
    pairs = width // LANES
    rows = [slice(k * own, (k + 1) * own) for k in range(parts)]
    scale = jnp.asarray(DH ** (-0.5), BF16)
    q_mark[...] = segment_columns(info, row_positions(info, q_mark.shape, 0), False)
    k_mark[...] = segment_columns(info, key_positions(info, parts, own, k_mark.shape, 0), True)
    low_ref[...] = dot_rows(grad_ref[...].astype(BF16), weight_ref[...]).astype(BF16)
    product = low_ref[...].astype(F32) * mixed_ref[...]
    high = product.astype(BF16)
    shape = (2 * 8, width)
    belongs = lax.broadcasted_iota(jnp.int32, shape, 1) // DH == lax.broadcasted_iota(
        jnp.int32, shape, 0
    )
    belongs = jnp.where(belongs, 1.0, 0.0).astype(BF16)
    delta_ref[...] = dot_rows(belongs, high) + dot_rows(
        belongs, (product - high.astype(F32)).astype(BF16)
    )

    def scores(pair, head):
        query = head_part(q_ref[:, pair_lanes(pair)] * scale, q_mark[...], head)
        grad = low_ref[:, pair_lanes(pair)]
        grad = head_part(grad, jnp.zeros_like(grad), head)
        for k in range(parts):
            keys = head_part(pair_refs[k][:, pair_lanes(pair)], k_mark[rows[k], :], head)
            scores_of[head][rows[k], :] = dot_rows(keys, query)
            grads_of[head][rows[k], :] = dot_rows(pair_refs[k][:, pair_lanes(pair, width)], grad)

    def soften(pair, head):
        at = pl.ds(2 * pair + head, 1)
        weights = jnp.exp(scores_of[head][...] - log_ref[at, :])
        weights_of[head][...] = weights.astype(BF16)
        steps_of[head][...] = (weights * (grads_of[head][...] - delta_ref[at, :])).astype(BF16)

    def away(pair, which):
        lanes = pair_lanes(pair, which * width)
        return pltpu.make_async_remote_copy(
            src_ref=part_refs[1].at[:, lanes],
            dst_ref=arrived.at[:, lanes],
            send_sem=send_sem.at[pair, which],
            recv_sem=recv_sem.at[pair, which],
            device_id=twin,
            device_id_type=pl.DeviceIdType.MESH,
        )

    def mix(pair, head):
        keys, values = pair_lanes(pair), pair_lanes(pair, width)
        query, grad = q_ref[:, keys] * scale, low_ref[:, keys]
        query = head_part(query, jnp.zeros_like(query), head)
        grad = head_part(grad, jnp.zeros_like(grad), head)
        dq = None
        for k in reversed(range(parts)):
            step = steps_of[head][rows[k], :]
            dk = dot(step, query)
            dv = dot(weights_of[head][rows[k], :], grad)
            part_refs[k][:, keys] = dk if head == 0 else part_refs[k][:, keys] + dk
            part_refs[k][:, values] = dv if head == 0 else part_refs[k][:, values] + dv
            if want_queries:
                term = dot_columns(pair_refs[k][:, keys], step)
                dq = term if dq is None else dq + term
        if want_queries:
            here = pl.ds(pl.multiple_of(pair * LANES, LANES), LANES)
            dq = dq * DH ** (-0.5)
            if head:
                dq = jnp.where(head_mask(dq.shape, 0, 0), dq_ref[here, :].astype(F32), dq)
            dq_ref[here, :] = dq.astype(dq_ref.dtype)
        if exchange and head:
            away(pair, 0).start()
            away(pair, 1).start()

    over_heads(pairs, scores, soften, mix)
    if not exchange:
        return
    total = None
    for copy in late:
        copy.wait()
    if want_queries:
        total = dot_rows(jnp.transpose(dq_ref[...]).astype(BF16), in_ref[:, :width])
    for pair in range(pairs):
        away(pair, 0).wait_recv()
        away(pair, 1).wait_recv()
    both = part_refs[0][...] + arrived[...]
    high = both.astype(BF16)
    low = (both - high.astype(F32)).astype(BF16)
    back = dot_rows(high, in_ref[:, width:]) + dot_rows(low, in_ref[:, width:])
    total = back if total is None else total + back
    values, gain = rows_ref[...], gain_ref[...]
    inverse = lax.rsqrt(jnp.mean(values * values, -1, keepdims=True) + NORM_EPS)
    total = normed_back(values, gain, inverse, total)
    result_ref[...] = grad_ref[...] + total if want_queries else total
    for pair in range(pairs):
        away(pair, 0).wait_send()
        away(pair, 1).wait_send()


def attend_back(
    plan, queries, pairs, gradient, weight, mixed, logs, row_lengths, decoder, want_queries, through
):
    heads, width = queries.shape
    own = pairs[0].shape[0]
    parts, length = len(pairs), sum(pair.shape[0] for pair in pairs)
    vmem = pl.BlockSpec(memory_space=pltpu.VMEM)
    operands = [queries, *pairs, gradient, weight, mixed, logs.T[:16], row_lengths]
    in_specs = [vmem] * (parts + 5) + [pl.BlockSpec(memory_space=pltpu.SMEM)]
    scratch = [
        pltpu.VMEM((heads, LANES), BF16),
        pltpu.VMEM((length, LANES), BF16),
        pltpu.VMEM((heads, width), BF16),
        pltpu.VMEM((16, heads), F32),
    ]
    scratch += [pltpu.VMEM((length, heads), F32)] * 4 + [pltpu.VMEM((length, heads), BF16)] * 4
    if through:
        attend_in, rows, gain, collective_id = through
        operands += [attend_in, rows, gain[None]]
        in_specs += [pl.BlockSpec(memory_space=pl.ANY)] * 2 + [vmem]
        shapes = jax.ShapeDtypeStruct(rows.shape, F32)
        out_specs = vmem
        each = pltpu.SemaphoreType.DMA((width // LANES, 2))
        scratch = (
            [pltpu.VMEM((own, 2 * width), F32)] * 3
            + [each, each, pltpu.VMEM((width, heads) if want_queries else (8, LANES), F32)]
            + [pltpu.VMEM(attend_in.shape, BF16), pltpu.VMEM(rows.shape, F32)]
            + [pltpu.SemaphoreType.DMA((2,))]
            + scratch
        )
        params = pltpu.CompilerParams(
            collective_id=collective_id,
            has_side_effects=True,
            vmem_limit_bytes=(30 + heads // 32) * MIB,
        )
    else:
        shapes = [jax.ShapeDtypeStruct(pair.shape, F32) for pair in pairs]
        if want_queries:
            shapes.append(jax.ShapeDtypeStruct((width, heads), BF16))
        out_specs = [vmem] * len(shapes)
        params = pltpu.CompilerParams(vmem_limit_bytes=34 * MIB)
    return pl.pallas_call(
        functools.partial(
            attend_back_kernel, plan, parts, decoder, want_queries, through is not None
        ),
        out_shape=shapes,
        in_specs=in_specs,
        out_specs=out_specs,
        scratch_shapes=scratch,
        compiler_params=params,
        cost_estimate=pl.CostEstimate(
            flops=80 * heads * length * width, bytes_accessed=20 * own * width, transcendentals=0
        ),
    )(*operands)


def smooth_slope(u):
    rate = (2.0 / jnp.pi) ** 0.5
    bend = jnp.tanh(rate * (u + 0.044715 * (u * u * u)))
    inner = rate * (1.0 + 3.0 * 0.044715 * (u * u))
    return 0.5 * (1.0 + bend) + 0.5 * u * (1.0 - bend * bend) * inner


def feed_back_kernel(grad_ref, rows_ref, gain_ref, before_ref, one_ref, two_ref, out_ref, low, *scratch):
    active_of, step_of = scratch[0:2], scratch[2:4]
    count = one_ref.shape[1] // HIDDEN_PIECE
    low[...] = grad_ref[...].astype(BF16)
    out_ref[...] = jnp.zeros_like(out_ref)
    for n in range(count + 2):
        if n < count:
            here = slice(n * HIDDEN_PIECE, (n + 1) * HIDDEN_PIECE)
            active_of[n % 2][...] = dot_rows(low[...], two_ref[here, :])
        if 0 < n <= count:
            here = slice((n - 1) * HIDDEN_PIECE, n * HIDDEN_PIECE)
            step_of[(n - 1) % 2][...] = (
                active_of[(n - 1) % 2][...] * smooth_slope(before_ref[:, here])
            ).astype(BF16)
        if n >= 2:
            here = slice((n - 2) * HIDDEN_PIECE, (n - 1) * HIDDEN_PIECE)
            out_ref[...] += dot_rows(step_of[n % 2][...], one_ref[:, here])
    rows = rows_ref[...]
    inverse = lax.rsqrt(jnp.mean(rows * rows, -1, keepdims=True) + NORM_EPS)
    out_ref[...] = grad_ref[...] + normed_back(rows, gain_ref[...], inverse, out_ref[...])


def feed_back(gradient, rows, gain, before, one, two):
    own, width = rows.shape
    hidden = one.shape[1]
    vmem = pl.BlockSpec(memory_space=pltpu.VMEM)
    return pl.pallas_call(
        feed_back_kernel,
        out_shape=jax.ShapeDtypeStruct((own, width), F32),
        in_specs=[vmem] * 6,
        out_specs=vmem,
        scratch_shapes=[pltpu.VMEM((own, width), BF16)]
        + [pltpu.VMEM((own, HIDDEN_PIECE), F32)] * 2
        + [pltpu.VMEM((own, HIDDEN_PIECE), BF16)] * 2,
        compiler_params=pltpu.CompilerParams(vmem_limit_bytes=30 * MIB),
        cost_estimate=pl.CostEstimate(
            flops=4 * own * width * hidden, bytes_accessed=4 * width * hidden, transcendentals=0
        ),
    )(gradient, rows, gain[None], before, one, two)


def prompted(plan, rows_ref, prompt_ref, lengths_ref, tasks_ref):
    info = row_scalars(plan, lengths_ref, False)
    m = lax.axis_index("vocab") // plan.group
    shape = (plan.own, LANES)
    position = row_positions(info, shape, 0)
    lane = lax.broadcasted_iota(jnp.int32, shape, 1)
    begin = jnp.where(position >= info[1], info[1], jnp.where(position >= info[0], info[0], 0))
    place = position - begin
    total = None
    for j, start in enumerate([0, info[0], info[1]]):
        hit = (begin == start) & (place == lane) & (place < P_SIZE)
        term = dot_rows(jnp.where(hit, 1.0, 0.0).astype(BF16), prompt_ref[tasks_ref[m, j]])
        total = term if total is None else total + term
    return jnp.where(place[:, 0:1] < P_SIZE, total, rows_ref[...].astype(F32))


def project_kernel(plan, *refs):
    rows_ref, prompt_ref, keys_ref, heads_ref, gain_ref, lengths_ref, tasks_ref = refs[:7]
    first_hbm, second_hbm, out_ref, enc_q, enc_own, enc_other, dec_q, dec_own, dec_other = refs[7:16]
    first, second, sems, send_sem, recv_sem = refs[16:]
    width = rows_ref.shape[1]
    v = lax.axis_index("vocab")
    twin = {"vocab": v // 2 * 2 + 1 - lax.rem(v, 2)}
    barrier = pltpu.get_barrier_semaphore()
    pl.semaphore_signal(barrier, inc=1, device_id=twin, device_id_type=pl.DeviceIdType.MESH)
    pl.semaphore_wait(barrier, 1)
    loads = [
        pltpu.make_async_copy(first_hbm, first, sems.at[0]),
        pltpu.make_async_copy(second_hbm, second, sems.at[1]),
    ]
    for load in loads:
        load.start()

    def share(source, target, index):
        return pltpu.make_async_remote_copy(
            src_ref=source,
            dst_ref=target,
            send_sem=send_sem.at[index],
            recv_sem=recv_sem.at[index],
            device_id=twin,
            device_id_type=pl.DeviceIdType.MESH,
        )

    shares = [share(enc_own, enc_other, 0), share(dec_own, dec_other, 1)]
    rows = prompted(plan, rows_ref, prompt_ref, lengths_ref, tasks_ref)
    out_ref[...] = rows
    low = normed(rows, gain_ref[...])[0].astype(BF16)
    loads[0].wait()
    enc_own[...] = dot(low, first[:, width:]).astype(BF16)
    shares[0].start()
    enc_q[...] = dot(low, first[:, :width]).astype(BF16)
    loads[1].wait()
    dec_own[...] = dot(keys_ref[...], second[:, width:]).astype(BF16)
    shares[1].start()
    dec_q[...] = dot(heads_ref[...], second[:, :width]).astype(BF16)
    for copy in shares:
        copy.wait()


def project(plan, rows, prompts, keys, heads, gain, row_lengths, row_tasks, first, second):
    width = rows.shape[1]
    vmem, smem = pl.BlockSpec(memory_space=pltpu.VMEM), pl.BlockSpec(memory_space=pltpu.SMEM)
    anywhere = pl.BlockSpec(memory_space=pl.ANY)
    pair = jax.ShapeDtypeStruct((plan.own, 2 * width), BF16)
    outs = pl.pallas_call(
        functools.partial(project_kernel, plan),
        out_shape=[
            jax.ShapeDtypeStruct(rows.shape, F32),
            jax.ShapeDtypeStruct(rows.shape, BF16),
            pair,
            pair,
            jax.ShapeDtypeStruct(heads.shape, BF16),
            pair,
            pair,
        ],
        in_specs=[vmem] * 5 + [smem] * 2 + [anywhere] * 2,
        out_specs=[vmem] * 7,
        scratch_shapes=[pltpu.VMEM(first.shape, BF16)] * 2 + [pltpu.SemaphoreType.DMA((2,))] * 3,
        compiler_params=pltpu.CompilerParams(
            collective_id=5, has_side_effects=True, vmem_limit_bytes=40 * MIB
        ),
        cost_estimate=pl.CostEstimate(
            flops=10 * rows.size * width, bytes_accessed=4 * first.size, transcendentals=0
        ),
    )(rows, prompts, keys, heads, gain[None], row_lengths, row_tasks, first, second)
    return outs[0], outs[1], outs[2:4], outs[4], outs[5:7]


def vocab_kernel(tile, valid, h_ref, target_ref, table_hbm, grad_ref, stat_ref, table, sem):
    padded = table.shape[0]

    @pl.when(pl.program_id(0) == 0)
    def _():
        copy = pltpu.make_async_copy(table_hbm, table.at[pl.ds(0, valid), :], sem)
        copy.start()
        if padded > valid:
            table[valid:, :] = jnp.zeros((padded - valid, table.shape[1]), BF16)
        copy.wait()

    rows = h_ref.shape[0]
    hidden = h_ref[...]
    column = lax.broadcasted_iota(jnp.int32, (rows, tile), 1)
    target = target_ref[...]

    def block(at, carry, last):
        maxima, total = carry
        part = table[pl.ds(pl.multiple_of(at * tile, tile), tile), :]
        logits = dot_rows(hidden, part)
        if last and padded > valid:
            logits = jnp.where(column < valid - (padded - tile), logits, MASKED)
        highest = jnp.maximum(maxima, jnp.max(logits, -1, keepdims=True))
        powers = jnp.exp(logits - highest)
        scale = jnp.exp(maxima - highest)
        total = total * scale + jnp.sum(powers, -1, keepdims=True)
        powers = jnp.where(column == target - at * tile, 0.0, powers).astype(BF16)
        grad_ref[...] = grad_ref[...] * scale + dot(powers, part)
        return (highest, total)

    grad_ref[...] = jnp.zeros_like(grad_ref)
    blocks = padded // tile
    carry = (jnp.full((rows, 1), MASKED, F32), jnp.zeros((rows, 1), F32))
    carry = lax.fori_loop(0, blocks - 1, lambda at, c: block(at, c, False), carry)
    maxima, total = block(blocks - 1, carry, True)
    lane = lax.broadcasted_iota(jnp.int32, stat_ref.shape, 1)
    stat_ref[...] = jnp.where(lane == 0, maxima, total)


def vocab_pass(hidden, target_local, embedding, rows):
    count, width = hidden.shape
    valid = embedding.shape[0]
    tile = VOCAB_BLOCK
    padded = (valid + tile - 1) // tile * tile
    return pl.pallas_call(
        functools.partial(vocab_kernel, tile, valid),
        grid=(count // rows,),
        out_shape=[
            jax.ShapeDtypeStruct((count, width), F32),
            jax.ShapeDtypeStruct((count, LANES), F32),
        ],
        in_specs=[
            pl.BlockSpec((rows, width), lambda i: (i, 0)),
            pl.BlockSpec((rows, 1), lambda i: (i, 0)),
            pl.BlockSpec(memory_space=pl.ANY),
        ],
        out_specs=[
            pl.BlockSpec((rows, width), lambda i: (i, 0)),
            pl.BlockSpec((rows, LANES), lambda i: (i, 0)),
        ],
        scratch_shapes=[pltpu.VMEM((padded, width), BF16), pltpu.SemaphoreType.DMA],
        compiler_params=pltpu.CompilerParams(vmem_limit_bytes=56 * MIB),
        cost_estimate=pl.CostEstimate(
            flops=4 * count * padded * width, bytes_accessed=2 * valid * width, transcendentals=0
        ),
    )(hidden, target_local, embedding)


def gather_kernel(plan, rows_z, rows_y, *refs):
    in_ref, out_ref, expand_ref, reduce_ref, wanted_ref, table_hbm, lengths_ref, gain_ref = refs[:8]
    in_full, out_full, expand_full, reduce_full = refs[8:11], refs[11:14], refs[14:16], refs[16:18]
    enc_rows, dec_keys, dec_rows, dec_heads, target_rows = refs[18:23]
    found_ref, table_low, table, stage, far, near, sister, from_core, from_x, from_sister = refs[23:33]
    send_sem, recv_sem, local_sem, table_sem = refs[33:]
    at, v = lax.axis_index("dp"), lax.axis_index("vocab")
    z, y, x, core = at // rows_y, lax.rem(at, rows_y), v // 2, lax.rem(v, 2)
    top = rows_z - 1
    above = {"dp": jnp.minimum(z + 1, top) * rows_y + y, "vocab": v}
    below = {"dp": jnp.maximum(z - 1, 0) * rows_y + y, "vocab": v}
    beside = {"dp": z * rows_y + (1 - y), "vocab": v}
    other_x = (1 - x) * 2 + core
    across = {"dp": at, "vocab": other_x}
    twin = {"dp": at, "vocab": x * 2 + (1 - core)}

    barrier = pltpu.get_barrier_semaphore()

    def greet(peer):
        pl.semaphore_signal(barrier, inc=1, device_id=peer, device_id_type=pl.DeviceIdType.MESH)

    pl.when(z < top)(lambda: greet(above))
    pl.when(z > 0)(lambda: greet(below))
    greet(beside)
    greet(across)
    greet(twin)
    inner = jnp.logical_and(z > 0, z < top)
    pl.when(inner)(lambda: pl.semaphore_wait(barrier, 5))
    pl.when(jnp.logical_not(inner))(lambda: pl.semaphore_wait(barrier, 4))

    names, tallies = {}, [0, 0]

    def remote(name, source, target, peer):
        if name not in names:
            names[name] = tallies[0]
            tallies[0] += 1
        return pltpu.make_async_remote_copy(
            src_ref=source,
            dst_ref=target,
            send_sem=send_sem.at[names[name]],
            recv_sem=recv_sem.at[names[name]],
            device_id=peer,
            device_id_type=pl.DeviceIdType.MESH,
        )

    def local(source, target):
        copy = pltpu.make_async_copy(source, target, local_sem.at[tallies[1]])
        tallies[1] += 1
        copy.start()
        return copy

    def columns(ref, full, index, blocks):
        wide = ref.shape[2] // blocks
        here = lambda b: pl.ds(pl.multiple_of(b * wide, wide), wide)
        return (
            lambda b: ref.at[index, :, here(b)],
            lambda zs, ys, b: full.at[zs, ys, :, here(b)],
            lambda ys, b: full.at[:, ys, :, here(b)],
            blocks == 4,
        )

    def row_blocks(ref, full, index):
        count = ref.shape[1] // 4
        return (
            lambda b: ref.at[index, pl.ds(pl.multiple_of(b * count, count), count), :],
            lambda zs, ys, b: full.at[zs, ys, b],
            lambda ys, b: full.at[:, ys, b],
            True,
        )

    def attention(j):
        return [columns(in_ref, in_full[j], j, 2), columns(out_ref, out_full[j], j, 2)]

    def feed(j):
        return [columns(expand_ref, expand_full[j], j, 4), row_blocks(reduce_ref, reduce_full[j], j)]

    waves = [feed(0) + attention(0), feed(1) + attention(1) + attention(2)]
    units = [u for wave in waves for u in wave]
    starts = [0, len(waves[0]), len(units)]
    blocks = [v if u[3] else core for u in units]
    sides = (("up", -1), ("down", 1))

    def there(side, k):
        return z - k >= 0 if side == "up" else z + k <= top

    def further(side):
        return z < top if side == "up" else z > 0

    def begin(i):
        source, target, _, quarter = units[i]
        b = blocks[i]
        piece = target(z, y, b)
        pl.when(z < top)(lambda: remote((i, "up", 1), source(b), piece, above).start())
        pl.when(z > 0)(lambda: remote((i, "down", 1), source(b), piece, below).start())
        remote((i, "y", 0), source(b), piece, beside).start()
        copies = [local(source(b), piece)]
        if quarter:
            copies.append(local(source(other_x), target(z, y, other_x)))
        return copies

    def step(i, k):
        _, target, _, quarter = units[i]
        for side, sign in sides:

            @pl.when(there(side, k))
            def _():
                piece = target(z + sign * k, y, blocks[i])
                remote((i, side, k), piece, piece, above).wait_recv()
                if k < top:

                    @pl.when(further(side))
                    def _():
                        peer = above if side == "up" else below
                        remote((i, side, k + 1), piece, piece, peer).start()

                remote((i, side, k, "y"), piece, piece, beside).start()
                if quarter:
                    remote((i, side, k, "x"), piece, piece, across).start()

    def came(i, k):
        _, target, _, quarter = units[i]
        if k == 0:
            piece = target(z, 1 - y, blocks[i])
            remote((i, "y", 0), piece, piece, beside).wait_recv()
            if quarter:
                remote((i, "yx", 0), piece, piece, across).start()
            return
        for side, sign in sides:

            @pl.when(there(side, k))
            def _():
                piece = target(z + sign * k, 1 - y, blocks[i])
                remote((i, side, k, "y"), piece, piece, beside).wait_recv()
                if quarter:
                    remote((i, side, k, "yx"), piece, piece, across).start()

    def to_twin(i, column, b, tag):
        block = units[i][2](column, b)
        remote((i, "core", tag), block, block, twin).start()

    def spread(i):
        for copy in locals_[i]:
            copy.wait()
        to_twin(i, y, blocks[i], 0)

    def spread_beside(i):
        to_twin(i, 1 - y, blocks[i], 1)

    def x_came(i, tag):
        _, target, _, _ = units[i]
        if tag == "yx":
            piece = target(z, 1 - y, other_x)
            remote((i, "yx", 0), piece, piece, across).wait_recv()
        for k in range(1, rows_z):
            for side, sign in sides:

                @pl.when(there(side, k))
                def _():
                    piece = target(z + sign * k, y if tag == "x" else 1 - y, other_x)
                    remote((i, side, k, tag), piece, piece, across).wait_recv()

        to_twin(i, y if tag == "x" else 1 - y, other_x, 2 if tag == "x" else 3)

    valid, width = table_low.shape
    share = far.shape[0]
    table_copy = pltpu.make_async_copy(table_hbm, table_low, table_sem)
    table_copy.start()

    def widen(at, _):
        here = pl.ds(pl.multiple_of(at * 32, 32), 32)
        table[here, :] = table_low[here, :].astype(F32)
        return 0

    def prepare():
        table_copy.wait()
        table[valid:, :] = jnp.zeros((table.shape[0] - valid, width), F32)
        lax.fori_loop(0, valid // 32, widen, 0)

    def look_up(target, owner, part):
        count = stage.shape[0]

        def rows(at, _):
            for step in range(8):
                i = at * 8 + step
                row = wanted_ref[owner, part * count + i]
                stage[pl.ds(i, 1), :] = table[pl.ds(row, 1), :]
            return 0

        lax.fori_loop(0, count // 8, rows, 0)
        target[part * count : (part + 1) * count, :] = stage[...].astype(BF16)

    sums = {
        "far": remote("far", far, from_core, twin),
        "near": remote("near", near, from_x, across),
        "sister": remote("sister", sister, from_sister, twin),
    }

    def send_far():
        sums["far"].start()

    def send_near():
        sums["far"].wait_recv()
        near[...] = (near[...].astype(F32) + from_core[...].astype(F32)).astype(BF16)
        sums["near"].start()

    def send_sister():
        sums["sister"].start()

    def finish_rows():
        sums["sister"].wait_recv()
        sums["near"].wait_recv()
        total = found_ref[...].astype(F32) + from_sister[...].astype(F32)
        table[:share, :] = total + from_x[...].astype(F32)
        enc_rows[...] = table[: plan.own, :].astype(BF16)
        ends = [lengths_ref[x, 0], lengths_ref[x, 0] + lengths_ref[x, 1]]
        position = lax.broadcasted_iota(jnp.int32, (plan.held, 1), 0) + chosen(core, plan.starts)
        first_of = (position == 0) | (position == ends[0]) | (position == ends[1])
        base, held = plan.own + HALO, 2 * plan.own + plan.held
        table[held : held + plan.held, :] = jnp.where(
            first_of,
            table[plan.own : plan.own + 1, :],
            table[base - 1 : base - 1 + plan.held, :],
        )
        shift = held + core * (plan.own - plan.starts[1])
        keys = table[pl.ds(pl.multiple_of(shift, HALO), plan.own), :]
        gain = gain_ref[...]
        dec_keys[...] = normed(keys, gain)[0].astype(BF16)
        before_turn = lax.broadcasted_iota(jnp.int32, (plan.heads, 1), 0) < turn_of(
            plan, lengths_ref, x, core
        )

        def own_heads(first):
            def rows(offsets):
                first_place, second_place = [
                    table[first + o - s : first + o - s + plan.heads, :]
                    for o, s in zip(offsets, plan.starts)
                ]
                return jnp.where(core == 0, first_place, second_place)

            return jnp.where(before_turn, rows(plan.near), rows(plan.far))

        values = own_heads(held)
        dec_rows[...] = values
        dec_heads[...] = normed(values, gain)[0].astype(BF16)
        target_rows[...] = own_heads(base).astype(BF16)

    jobs = [prepare]
    for target, owner, after in (
        (far, (1 - x) * 2 + 1 - core, send_far),
        (near, other_x, send_near),
        (sister, x * 2 + 1 - core, send_sister),
        (found_ref, v, None),
    ):
        for part in range(share // stage.shape[0]):
            jobs.append(functools.partial(look_up, target, owner, part))
        if after:
            jobs.append(after)
    jobs = jobs[::-1]

    def work(count):
        for _ in range(min(count, len(jobs))):
            jobs.pop()()

    first, second = range(starts[0], starts[1]), range(starts[1], starts[2])
    locals_ = {}

    def each(action, wave, *rest):
        for i in wave:
            action(i, *rest)

    for i in first:
        locals_[i] = begin(i)
    locals_[second[0]] = begin(second[0])
    work(2)
    each(step, first, 1)
    for i in second[1:]:
        locals_[i] = begin(i)
    work(2)
    each(came, first, 0)
    work(2)
    each(step, first, 2)
    work(1)
    each(came, first, 1)
    work(2)
    each(step, second, 1)
    work(2)
    each(step, first, 3)
    each(spread, first)
    work(2)
    each(came, first, 2)
    work(2)
    each(step, second, 2)
    work(1)
    each(came, second, 0)
    work(len(jobs))
    for i in first:
        came(i, 3)
        spread_beside(i)
    each(came, second, 1)
    each(step, second, 3)
    each(spread, second)
    for i in first:
        if units[i][3]:
            x_came(i, "x")
    each(came, second, 2)
    finish_rows()
    for i in first:
        if units[i][3]:
            x_came(i, "yx")
    for i in second:
        came(i, 3)
        spread_beside(i)
    for i in second:
        if units[i][3]:
            x_came(i, "x")
            x_came(i, "yx")
    for copy in sums.values():
        copy.wait_send()

    for i, (source, target, whole, quarter) in enumerate(units):
        b = blocks[i]
        for tag in range(4 if quarter else 2):
            block = whole(y, b)
            remote((i, "core", tag), block, block, twin).wait()
        piece = target(z, y, b)
        remote((i, "y", 0), piece, piece, beside).wait_send()
        if quarter:
            remote((i, "yx", 0), piece, piece, across).wait_send()
        for k in range(1, rows_z):
            for side, sign in sides:
                sent = there(side, k - 1) if k > 1 else True
                pl.when(jnp.logical_and(sent, further(side)))(
                    lambda: remote((i, side, k), piece, piece, above).wait_send()
                )

                @pl.when(there(side, k))
                def _():
                    remote((i, side, k, "y"), piece, piece, beside).wait_send()
                    if quarter:
                        remote((i, side, k, "x"), piece, piece, across).wait_send()
                        remote((i, side, k, "yx"), piece, piece, across).wait_send()


def gather_weights(
    plan, attend_in, attend_out, expand_weights, reduce_weights, wanted, table, row_lengths, gain
):
    shards, rows_y = 8, 2
    rows_z = shards // rows_y
    rows = attend_in.shape[1]
    width = rows * shards
    tall = reduce_weights.shape[1]
    share = wanted.shape[1]
    valid = table.shape[0]

    def full(*tail):
        return jax.ShapeDtypeStruct((rows_z, rows_y, *tail), BF16)

    shapes = (
        [full(rows, attend_in.shape[2])] * 3
        + [full(rows, attend_out.shape[2])] * 3
        + [full(rows, expand_weights.shape[2])] * 2
        + [full(4, tall // 4, width)] * 2
        + [jax.ShapeDtypeStruct((plan.own, width), BF16)] * 2
        + [jax.ShapeDtypeStruct((plan.heads, width), kind) for kind in (F32, BF16, BF16)]
    )
    copies = 10 * (1 + 4 * (rows_z - 1) + 2) + 4 * (1 + 4 * (rows_z - 1) + 2) + 3
    anywhere, vmem, smem = [
        pl.BlockSpec(memory_space=space) for space in (pl.ANY, pltpu.VMEM, pltpu.SMEM)
    ]
    outs = pl.pallas_call(
        functools.partial(gather_kernel, plan, rows_z, rows_y),
        out_shape=shapes,
        in_specs=[anywhere] * 4 + [smem, anywhere, smem, vmem],
        out_specs=[anywhere] * 10 + [vmem] * 5,
        scratch_shapes=[
            pltpu.VMEM((share, width), BF16),
            pltpu.VMEM((valid, width), BF16),
            pltpu.VMEM((valid + 8, width), F32),
            pltpu.VMEM((share // 3, width), F32),
        ]
        + [pltpu.VMEM((share, width), BF16)] * 6
        + [
            pltpu.SemaphoreType.DMA((copies,)),
            pltpu.SemaphoreType.DMA((copies,)),
            pltpu.SemaphoreType.DMA((14,)),
            pltpu.SemaphoreType.DMA,
        ],
        compiler_params=pltpu.CompilerParams(
            collective_id=0, has_side_effects=True, vmem_limit_bytes=60 * MIB
        ),
        cost_estimate=pl.CostEstimate(flops=0, bytes_accessed=400_000_000, transcendentals=0),
    )(attend_in, attend_out, expand_weights, reduce_weights, wanted, table, row_lengths, gain[None])
    return [o.reshape(-1, o.shape[-1]) for o in outs]


def vocab_exchange_kernel(plan, tile, *refs):
    rows_ref, gain_ref, target_ref, table_ref, ids_ref, lengths_ref, tasks_ref = refs[:7]
    grad_ref, stat_ref, *scratch = refs[7:]
    tail, held, logits_a, logits_b, powers_a, powers_b, scale_a, scale_b = scratch[:8]
    maxima_ref, total_ref, targets_ref, h_ref, columns, parcel, arrived = scratch[8:15]
    stats_out, stats_in, send_sem, recv_sem = scratch[15:]
    rows, width = h_ref.shape
    valid = table_ref.shape[0]
    tiles = (valid + tile - 1) // tile
    padded = tiles * tile
    v = lax.axis_index("vocab")
    x, core = v // 2, lax.rem(v, 2)
    twin, across, diagonal = x * 2 + 1 - core, (1 - x) * 2 + core, (1 - x) * 2 + 1 - core

    barrier = pltpu.get_barrier_semaphore()
    for peer in (twin, across, diagonal):
        pl.semaphore_signal(
            barrier, inc=1, device_id={"vocab": peer}, device_id_type=pl.DeviceIdType.MESH
        )
    pl.semaphore_wait(barrier, 3)

    def remote(source, target, index, peer):
        return pltpu.make_async_remote_copy(
            src_ref=source,
            dst_ref=target,
            send_sem=send_sem.at[index],
            recv_sem=recv_sem.at[index],
            device_id={"vocab": peer},
            device_id_type=pl.DeviceIdType.MESH,
        )

    values = rows_ref[...]
    gain = gain_ref[...]
    inverse = lax.rsqrt(jnp.mean(values * values, -1, keepdims=True) + NORM_EPS)
    h_ref[...] = (values * inverse * gain * width ** (-0.5)).astype(BF16)
    to_twin = remote(h_ref, held.at[0], 0, twin)
    to_across = remote(h_ref, held.at[1], 1, across)
    passed_on = remote(held.at[1], held.at[2], 2, twin)
    results = [
        remote(parcel.at[k], arrived.at[k], 3 + k, peer)
        for k, peer in enumerate((twin, across, diagonal))
    ]
    marks = [
        remote(stats_out.at[k], stats_in.at[k], 6 + k, peer)
        for k, peer in enumerate((twin, across, diagonal))
    ]
    to_twin.start()
    to_across.start()
    held[3] = h_ref[...]

    entry = lax.broadcasted_iota(jnp.int32, (8, rows), 1)
    even = lax.rem(lax.broadcasted_iota(jnp.int32, (8, rows), 0), 2) == 0
    for place in range(plan.group):
        turns = [turn_of(plan, lengths_ref, m, place) for m in range(2)]
        near, far = plan.near[place], plan.far[place]
        picked = jnp.where(
            entry < jnp.where(even, turns[0], turns[1]),
            ids_ref[:, near : near + rows],
            ids_ref[:, far : far + rows],
        )
        columns[place] = jnp.transpose(picked)

    short = padded - valid
    if short:
        tail[: tile - short, :] = table_ref[padded - tile :, :]
        tail[tile - short :, :] = jnp.zeros((short, width), BF16)
    to_twin.wait_recv()

    logits_of, powers_of, scale_of = (logits_a, logits_b), (powers_a, powers_b), (scale_a, scale_b)
    column = lax.broadcasted_iota(jnp.int32, (rows, tile), 1)
    lane = lax.broadcasted_iota(jnp.int32, (rows, LANES), 1)

    def turn(k, _):
        @pl.when(k == 1)
        def _():
            to_across.wait_recv()
            passed_on.start()

        @pl.when(k == 2)
        def _():
            passed_on.wait_recv()

        owner = jnp.where(k == 0, twin, jnp.where(k == 1, across, jnp.where(k == 2, diagonal, v)))

        def part(at):
            if short and at == tiles - 1:
                return tail[...]
            return table_ref[at * tile : (at + 1) * tile, :]

        def scores(at):
            logits_of[at % 2][...] = dot_rows(held[k], part(at))

        def soften(at):
            logits = logits_of[at % 2][...]
            if at == tiles - 1 and padded > valid:
                logits = jnp.where(column < valid - at * tile, logits, MASKED)
            highest = jnp.maximum(maxima_ref[...], jnp.max(logits, -1, keepdims=True))
            powers = jnp.exp(logits - highest)
            scale = jnp.exp(maxima_ref[...] - highest)
            maxima_ref[...] = highest
            total_ref[...] = total_ref[...] * scale + jnp.sum(powers, -1, keepdims=True)
            scale_of[at % 2][...] = scale
            powers_of[at % 2][...] = jnp.where(
                column == targets_ref[...] - at * tile, 0.0, powers
            ).astype(BF16)

        def gather(at):
            term = dot(powers_of[at % 2][...], part(at))
            grad_ref[...] = grad_ref[...] * scale_of[at % 2][...] + term

        column_of = jnp.where(lax.rem(owner, 2) == 0, columns[0], columns[1])
        target = jnp.where(owner < 2, column_of[:, 0:1], column_of[:, 1:2])
        targets_ref[...] = target.astype(jnp.int32) - v * valid
        maxima_ref[...] = jnp.full((rows, 1), MASKED, F32)
        total_ref[...] = jnp.zeros((rows, 1), F32)
        grad_ref[...] = jnp.zeros_like(grad_ref)
        for at in range(tiles + 2):
            if at < tiles:
                scores(at)
            if 0 <= at - 1 < tiles:
                soften(at - 1)
            if at >= 2:
                gather(at - 2)

        @pl.when(k < 3)
        def _():
            parcel[k] = grad_ref[...].astype(BF16)
            side = lax.broadcasted_iota(jnp.int32, (rows, 8), 1)
            pair = jnp.where(side == 0, maxima_ref[...], total_ref[...])
            stats_out[k] = jnp.transpose(pair)

        for index, (mark, result) in enumerate(zip(marks, results)):

            @pl.when(k == index)
            def _():
                mark.start()
                result.start()

        return 0

    lax.fori_loop(0, 4, turn, 0)
    for copy in [*marks, *results]:
        copy.wait_recv()
    pairs = [jnp.transpose(stats_in[k]) for k in range(3)]
    highs = [pair[:, 0:1] for pair in pairs] + [maxima_ref[...]]
    totals = [pair[:, 1:2] for pair in pairs] + [total_ref[...]]
    highest = functools.reduce(jnp.maximum, highs)
    log_total = highest + jnp.log(sum(t * jnp.exp(m - highest) for m, t in zip(highs, totals)))
    summed = grad_ref[...] * jnp.exp(highs[3] - log_total)
    for k in range(3):
        summed = summed + arrived[k].astype(F32) * jnp.exp(highs[k] - log_total)
    target_rows = target_ref[...].astype(F32)
    target_logit = jnp.sum(h_ref[...].astype(F32) * target_rows, -1, keepdims=True)
    coefficient = (jnp.exp(target_logit - log_total) - 1.0).astype(BF16).astype(F32)
    info = row_scalars(plan, lengths_ref, True)
    position = row_positions(info, (rows, 1), 0)
    in_second, in_third = position >= info[0], position >= info[1]
    begin = jnp.where(in_third, info[1], jnp.where(in_second, info[0], 0))
    task = jnp.where(in_third, tasks_ref[x, 2], jnp.where(in_second, tasks_ref[x, 1], tasks_ref[x, 0]))
    counts = (position - begin >= P_SIZE) & (lax.broadcasted_iota(jnp.int32, (rows, 1), 0) < plan.half)
    column_of = jnp.where(core == 0, columns[0], columns[1])
    counted = jnp.where(counts, jnp.where(x == 0, column_of[:, 2:3], column_of[:, 3:4]), 0.0)
    summed = counted * (summed + coefficient * target_rows)
    grad_ref[...] = normed_back(rows_ref[...], gain_ref[...], inverse, summed * width ** (-0.5))
    of_task = jnp.where(lane == task, counted, 0.0)
    losses = jnp.sum(of_task * (log_total - target_logit), 0, keepdims=True)
    counts = jnp.sum(of_task, 0, keepdims=True)
    row = lax.broadcasted_iota(jnp.int32, stat_ref.shape, 0)
    stat_ref[...] = jnp.where(row == 0, losses, jnp.where(row == 1, counts, 0.0))
    for copy in [to_twin, to_across, passed_on, *marks, *results]:
        copy.wait_send()


def vocab_exchange(plan, rows, gain, target_rows, embedding, ids, row_lengths, row_tasks):
    count, width = rows.shape
    valid = embedding.shape[0]
    tile = 2 * VOCAB_BLOCK
    padded = (valid + tile - 1) // tile * tile
    vmem = pl.BlockSpec(memory_space=pltpu.VMEM)
    return pl.pallas_call(
        functools.partial(vocab_exchange_kernel, plan, tile),
        out_shape=[
            jax.ShapeDtypeStruct((count, width), F32),
            jax.ShapeDtypeStruct((8, LANES), F32),
        ],
        in_specs=[vmem] * 5 + [pl.BlockSpec(memory_space=pltpu.SMEM)] * 2,
        out_specs=[vmem] * 2,
        scratch_shapes=[
            pltpu.VMEM((tile, width), BF16),
            pltpu.VMEM((4, count, width), BF16),
            pltpu.VMEM((count, tile), F32),
            pltpu.VMEM((count, tile), F32),
            pltpu.VMEM((count, tile), BF16),
            pltpu.VMEM((count, tile), BF16),
            pltpu.VMEM((count, 1), F32),
            pltpu.VMEM((count, 1), F32),
            pltpu.VMEM((count, 1), F32),
            pltpu.VMEM((count, 1), F32),
            pltpu.VMEM((count, 1), jnp.int32),
            pltpu.VMEM((count, width), BF16),
            pltpu.VMEM((2, count, 8), F32),
            pltpu.VMEM((3, count, width), BF16),
            pltpu.VMEM((3, count, width), BF16),
            pltpu.VMEM((3, 8, count), F32),
            pltpu.VMEM((3, 8, count), F32),
            pltpu.SemaphoreType.DMA((9,)),
            pltpu.SemaphoreType.DMA((9,)),
        ],
        compiler_params=pltpu.CompilerParams(
            collective_id=1, has_side_effects=True, vmem_limit_bytes=44 * MIB
        ),
        cost_estimate=pl.CostEstimate(
            flops=30 * count * padded * width, bytes_accessed=2 * valid * width, transcendentals=0
        ),
    )(rows, gain[None], target_rows, embedding, ids, row_lengths, row_tasks)


def reduce_kernel(rows_dp, task_ref, table_ref, stat_ref, out_ref, stats_out, squares_out, *scratch):
    cast, crossed, swap, swapped, own, others, outgoing, pieces, result, results = scratch[:10]
    stats, squares, send_sem, recv_sem = scratch[10:]
    features = own.shape[1]
    at, v = lax.axis_index("dp"), lax.axis_index("vocab")
    x, core = v // 2, lax.rem(v, 2)
    twin, across = x * 2 + 1 - core, (1 - x) * 2 + core
    dp_peers = [lax.rem(at + k, rows_dp) for k in range(1, rows_dp)]
    vocab_peers = [lax.rem(v + k, 4) for k in range(1, 4)]

    barrier = pltpu.get_barrier_semaphore()
    for peer in [{"vocab": p} for p in vocab_peers] + [{"dp": p} for p in dp_peers]:
        pl.semaphore_signal(barrier, inc=1, device_id=peer, device_id_type=pl.DeviceIdType.MESH)
    pl.semaphore_wait(barrier, rows_dp + 2)

    def remote(source, target, send, recv, peer):
        return pltpu.make_async_remote_copy(
            src_ref=source,
            dst_ref=target,
            send_sem=send_sem.at[send],
            recv_sem=recv_sem.at[recv],
            device_id=peer,
            device_id_type=pl.DeviceIdType.MESH,
        )

    half = 2 * features
    there = pl.ds(pl.multiple_of((1 - x) * half, half), half)
    here = pl.ds(pl.multiple_of(x * half, half), half)
    stats[0] = stat_ref[...]
    cast[...] = table_ref[there, :].astype(BF16)
    over_x = remote(cast, crossed, 0, 0, {"vocab": across})
    stat_x = remote(stats.at[0], stats.at[1], 1, 1, {"vocab": across})
    over_x.start()
    stat_x.start()
    tasks = [[task_ref[m, s] for s in range(task_ref.shape[1])] for m in range(2)]

    def by_task(part, t, came):
        total = jnp.zeros((features, LANES), F32)
        if came:
            start = pl.multiple_of(part * features, features)
            rows = crossed[pl.ds(start, features), :].astype(F32)
            order = tasks[::-1]
        else:
            start = pl.multiple_of(x * half + part * features, features)
            rows = table_ref[pl.ds(start, features), :]
            order = tasks
        for s in range(task_ref.shape[1]):
            task = jnp.where(x == 0, order[0][s], order[1][s])
            total = total + jnp.where(task == t, rows[:, s * LANES : (s + 1) * LANES], 0.0)
        return total

    for t in range(TASKS):
        others[t] = by_task(1 - core, t, False)
        own[t] = by_task(core, t, False)
    stat_x.wait_recv()
    stats[2] = stats[0] + stats[1]
    stat_core = remote(stats.at[2], stats.at[3], 2, 2, {"vocab": twin})
    stat_core.start()
    over_x.wait_recv()
    for t in range(TASKS):
        swap[t] = (others[t] + by_task(1 - core, t, True)).astype(BF16)
    over_core = remote(swap, swapped, 3, 3, {"vocab": twin})
    over_core.start()
    for t in range(TASKS):
        own[t] = own[t] + by_task(core, t, True)
    over_core.wait_recv()
    stat_core.wait_recv()
    stats[4 + at] = stats[2] + stats[3]
    for t in range(TASKS):
        own[t] = own[t] + swapped[t].astype(F32)
        outgoing[t] = own[t].astype(BF16)

    base = 4
    spread, tallies = [], []
    for k, peer in enumerate(dp_peers):
        spread.append(
            remote(outgoing.at[peer], pieces.at[at], base + k, base + at, {"dp": peer})
        )
        tallies.append(
            remote(
                stats.at[4 + at],
                stats.at[4 + at],
                base + rows_dp + k,
                base + rows_dp + at,
                {"dp": peer},
            )
        )
    for copy in spread + tallies:
        copy.start()
    total = own[at]
    for peer in dp_peers:
        remote(outgoing.at[peer], pieces.at[peer], base, base + peer, {"dp": peer}).wait_recv()
        total = total + pieces[peer].astype(F32)
    result[...] = total.astype(BF16)
    results[at] = result[...]
    returns = []
    for k, peer in enumerate(dp_peers):
        returns.append(
            remote(
                result,
                results.at[at],
                base + 2 * rows_dp + k,
                base + 2 * rows_dp + at,
                {"dp": peer},
            )
        )
    for copy in returns:
        copy.start()
    for peer in dp_peers:
        remote(
            stats.at[4 + peer], stats.at[4 + peer], base, base + rows_dp + peer, {"dp": peer}
        ).wait_recv()
    tally = functools.reduce(jnp.add, [stats[4 + k] for k in range(rows_dp)])
    stats_out[...] = tally
    for peer in dp_peers:
        remote(result, results.at[peer], base, base + 2 * rows_dp + peer, {"dp": peer}).wait_recv()
    for t in range(TASKS):
        scale = 1.0 / (TASKS * jnp.maximum(tally[1:2, t : t + 1], 1.0))
        scaled = results[t].astype(F32) * scale
        out_ref[t] = scaled
        squares[v, t : t + 1, :] = jnp.sum(scaled * scaled, 0, keepdims=True)
    last = base + 3 * rows_dp
    shares = [
        remote(squares.at[v], squares.at[v], last + k, last + v, {"vocab": peer})
        for k, peer in enumerate(vocab_peers)
    ]
    for copy in shares:
        copy.start()
    for peer in vocab_peers:
        remote(squares.at[peer], squares.at[peer], last, last + peer, {"vocab": peer}).wait_recv()
    squares_out[...] = squares[0] + squares[1] + squares[2] + squares[3]
    for copy in [over_x, stat_x, stat_core, over_core, *spread, *tallies, *returns, *shares]:
        copy.wait_send()


def reduce_over_devices(task_list, table, stats):
    rows_dp = lax.axis_size("dp")
    features = table.shape[0] // 4
    vmem = pl.BlockSpec(memory_space=pltpu.VMEM)
    copies = 4 + 3 * rows_dp + 4
    return pl.pallas_call(
        functools.partial(reduce_kernel, rows_dp),
        out_shape=[
            jax.ShapeDtypeStruct((TASKS, features, LANES), F32),
            jax.ShapeDtypeStruct((8, LANES), F32),
            jax.ShapeDtypeStruct((8, LANES), F32),
        ],
        in_specs=[pl.BlockSpec(memory_space=pltpu.SMEM), vmem, vmem],
        out_specs=[vmem] * 3,
        scratch_shapes=[
            pltpu.VMEM((2 * features, table.shape[1]), BF16),
            pltpu.VMEM((2 * features, table.shape[1]), BF16),
            pltpu.VMEM((TASKS, features, LANES), BF16),
            pltpu.VMEM((TASKS, features, LANES), BF16),
            pltpu.VMEM((TASKS, features, LANES), F32),
            pltpu.VMEM((TASKS, features, LANES), F32),
            pltpu.VMEM((TASKS, features, LANES), BF16),
            pltpu.VMEM((rows_dp, features, LANES), BF16),
            pltpu.VMEM((features, LANES), BF16),
            pltpu.VMEM((rows_dp, features, LANES), BF16),
            pltpu.VMEM((4 + rows_dp, 8, LANES), F32),
            pltpu.VMEM((4, 8, LANES), F32),
            pltpu.SemaphoreType.DMA((copies,)),
            pltpu.SemaphoreType.DMA((copies,)),
        ],
        compiler_params=pltpu.CompilerParams(
            collective_id=2, has_side_effects=True, vmem_limit_bytes=24 * MIB
        ),
    )(task_list, table, stats)


def on_device(
    tokens,
    targets,
    loss_mask,
    seg_lengths,
    task_ids,
    embedding,
    attend_in,
    attend_out,
    expand_weights,
    reduce_weights,
    norm_gains,
    prompt,
    first_moment,
    row_moment,
    column_moment,
):
    shards = lax.axis_size("vocab")
    micros, span = tokens.shape[0], tokens.shape[-1]
    length = span * shards
    group = shards // micros
    own = length // group
    me = lax.axis_index("vocab")
    micro, place = me // group, me % group
    shard_rows, width = embedding.shape
    share = prompt.shape[-1]

    def around(array, shift):
        pairs = [
            (m * group + r, m * group + (r + shift) % group)
            for m in range(micros)
            for r in range(group)
        ]
        return lax.ppermute(array, "vocab", pairs)

    ids = lax.all_gather(jnp.stack([tokens[:, 0], targets[:, 0], loss_mask[:, 0]]), "vocab")
    ids = jnp.transpose(ids, (1, 2, 0, 3)).reshape(3, micros, length)
    enc_ids = ids[0].reshape(shards, own)

    row_lengths, row_tasks = seg_lengths[:, 0], task_ids[:, 0]
    compact = group == 2 and 2 * span + 2 * P_SIZE <= length - span
    if compact:
        half = (length - SEGS * P_SIZE) // group
        extra = (half + 2 * P_SIZE - own + HALO - 1) // HALO * HALO
        heads = (half + LANES - 1) // LANES * LANES
        near, far = (P_SIZE, half + 2 * P_SIZE), (2 * P_SIZE, half + 3 * P_SIZE)
        plan = Plan(length, group, own, own + extra, heads, half, (0, own - extra), near, far)
    else:
        starts = tuple(p * own for p in range(group))
        plan = Plan(length, group, own, own, own, own, starts, starts, starts)
    held, heads, half, starts = plan.held, plan.heads, plan.half, plan.starts
    turns = [
        row_lengths[:, 0] - P_SIZE if p == 0 else length - row_lengths[:, 2] - plan.near[-1]
        for p in range(group)
    ]
    entries = jnp.arange(heads, dtype=jnp.int32)

    def of_rows(values, m, p):
        near, far = plan.near[p], plan.far[p]
        values = jnp.pad(values, (0, heads + far))
        return jnp.where(
            entries < turns[p][m], values[near : near + heads], values[far : far + heads]
        )

    everyone = [(m, p) for m in range(micros) for p in range(group)]
    dec_ids = jnp.stack(
        [
            jnp.concatenate(
                [
                    jnp.zeros((HALO - 1,), jnp.int32),
                    jnp.pad(ids[1, m], (1, 0))[starts[p] : starts[p] + 1 + held],
                ]
            )
            for m, p in everyone
        ]
    )
    first_row = me * shard_rows

    def here(wanted):
        local = wanted - first_row
        inside = (local >= 0) & (local < shard_rows)
        return local, inside

    prompt_low = jnp.swapaxes(prompt, 1, 2).astype(BF16)
    prompt_low = jnp.pad(prompt_low, ((0, 0), (0, 0), (0, LANES - P_SIZE)))
    prompt_all = lax.all_gather(prompt_low, "vocab", axis=1, tiled=True)
    lengths = lax.dynamic_index_in_dim(row_lengths, micro, 0, False)
    tasks = lax.dynamic_index_in_dim(row_tasks, micro, 0, False)
    weights = (attend_in, attend_out, expand_weights, reduce_weights)
    on_links = lax.axis_size("dp") == 8 and shards == 4 and shard_rows % 32 == 0 and compact
    if on_links:
        local, inside = here(jnp.concatenate([enc_ids, dec_ids], 1))
        wanted = jnp.where(inside, local, shard_rows)
        *flat, enc_rows, keys_low, dec_input, heads_low, target_rows = gather_weights(
            plan, *weights, wanted, embedding, row_lengths, norm_gains[3]
        )
        attend_in, attend_out = flat[:3], flat[3:6]
        expand_weights, reduce_weights = flat[6:8], flat[8:10]
    else:

        def lookup(wanted):
            local, inside = here(wanted.reshape(-1))
            picked = jnp.take(embedding, jnp.clip(local, 0, shard_rows - 1), axis=0)
            picked = jnp.where(inside[:, None], picked, 0)
            return lax.psum_scatter(picked, "vocab", scatter_dimension=0, tiled=True)

        enc_rows, dec_rows = lookup(enc_ids), lookup(dec_ids)
        whole = [lax.all_gather(tensor, "dp", axis=1, tiled=True) for tensor in weights]
        attend_in, attend_out, expand_weights, reduce_weights = whole
        turn = jnp.stack(turns)[place, micro]
        near_row = jnp.asarray(plan.near, jnp.int32)[place]
        far_row = jnp.asarray(plan.far, jnp.int32)[place]
        first_held = jnp.asarray(starts, jnp.int32)[place]
        head_positions = jnp.where(entries < turn, near_row, far_row) + entries
        head_positions = jnp.minimum(head_positions, length - 1)
        _, head_in_segment, head_task = layout(lengths, tasks, head_positions)
        head_mask_row = jnp.stack([of_rows(ids[2, m], m, p) for m, p in everyone])[me]
        counted = (head_mask_row * ((head_in_segment >= P_SIZE) & (entries < half))).astype(F32)

        def head_rows(values):
            values = jnp.pad(values, ((0, heads), (0, 0)))
            shape = (heads, values.shape[1])
            return jnp.where(
                (entries < turn)[:, None],
                lax.dynamic_slice(values, (near_row - first_held, 0), shape),
                lax.dynamic_slice(values, (far_row - first_held, 0), shape),
            )

        held_positions = first_held + jnp.arange(held, dtype=jnp.int32)
        begun = layout(lengths, tasks, held_positions)[1] >= 1
        dec_held = jnp.where(begun[:, None], dec_rows[HALO - 1 : HALO - 1 + held], dec_rows[:1])
        dec_keys = lax.dynamic_slice(dec_held, (place * own - first_held, 0), (own, width))
        keys_low = normed(dec_keys.astype(F32), norm_gains[3])[0].astype(BF16)
        dec_input = head_rows(dec_held).astype(F32)
        heads_low = normed(dec_input, norm_gains[3])[0].astype(BF16)
        target_rows = head_rows(dec_rows[HALO:])

    def key_parts(source, weight):
        pair = dot(source, weight).astype(BF16)
        return [pair] + [around(pair, k) for k in range(1, group)]

    positions = place * own + jnp.arange(own, dtype=jnp.int32)
    segment, in_segment, _ = layout(lengths, tasks, positions)
    is_prompt = in_segment < P_SIZE
    place_of = jnp.where(is_prompt, segment * LANES + in_segment, -1)
    chosen_place = place_of[:, None] == jnp.arange(SEGS * LANES, dtype=jnp.int32)
    chosen_low = chosen_place.astype(BF16)

    if on_links:
        enc_input, enc_queries, enc_pairs, dec_queries, dec_pairs = project(
            plan,
            enc_rows,
            prompt_all,
            keys_low,
            heads_low,
            norm_gains[0],
            row_lengths,
            row_tasks,
            attend_in[0],
            attend_in[1],
        )
    else:
        prompts = jnp.concatenate(
            [lax.dynamic_index_in_dim(prompt_all, tasks[j], 0, False) for j in range(SEGS)], 1
        )
        prompt_rows = dot_rows(chosen_low, prompts)
        enc_input = jnp.where(is_prompt[:, None], prompt_rows, enc_rows.astype(F32))
        normed_low = normed(enc_input, norm_gains[0])[0].astype(BF16)
        enc_pairs = key_parts(normed_low, attend_in[0][:, width:])
        enc_queries = dot(normed_low, attend_in[0][:, :width]).astype(BF16)
        dec_pairs = key_parts(keys_low, attend_in[1][:, width:])
        dec_queries = dot(heads_low, attend_in[1][:, :width]).astype(BF16)
    enc_mid, enc_mixed, enc_logs, enc_last, enc_kept = attend(
        plan,
        enc_queries,
        enc_pairs,
        enc_input,
        attend_out[0],
        row_lengths,
        False,
        False,
        (norm_gains[1], expand_weights[0], reduce_weights[0]),
    )
    encoded = normed(enc_last, norm_gains[2])[0].astype(BF16)
    cross_pairs = key_parts(encoded, attend_in[2][:, width:])

    dec_first = attend(
        plan, dec_queries, dec_pairs, dec_input, attend_out[1], row_lengths, True, True
    )[0]
    cross_source = normed(dec_first, norm_gains[4])[0].astype(BF16)
    cross_queries = dot(cross_source, attend_in[2][:, :width]).astype(BF16)
    dec_second, cross_mixed, cross_logs, dec_last, dec_kept = attend(
        plan,
        cross_queries,
        cross_pairs,
        dec_first,
        attend_out[2],
        row_lengths,
        True,
        False,
        (norm_gains[5], expand_weights[1], reduce_weights[1]),
    )

    if on_links:
        wide = (plan.far[-1] + heads + LANES - 1) // LANES * LANES
        marks = jnp.pad(
            jnp.concatenate([ids[1], ids[2]]).astype(F32), ((0, 4), (0, wide - length))
        )
        dec_grad, stats = vocab_exchange(
            plan, dec_last, norm_gains[6], target_rows, embedding, marks, row_lengths, row_tasks
        )
    else:
        output_norm, inverse_out = normed(dec_last, norm_gains[6])
        hidden = (output_norm * width ** (-0.5)).astype(BF16)
        all_hidden = lax.all_gather(hidden, "vocab", axis=0, tiled=True)
        head_targets = jnp.concatenate([of_rows(ids[1, m], m, p) for m, p in everyone])
        target_local = head_targets[:, None] - first_row
        part, stats = vocab_pass(all_hidden, target_local, embedding, heads)
        gathered = lax.all_gather(stats[:, :2].T, "vocab")
        maxima = jnp.max(gathered[:, 0], 0)
        log_total = maxima + jnp.log(
            jnp.sum(gathered[:, 1] * jnp.exp(gathered[:, 0] - maxima), 0)
        )
        scaled = part * jnp.exp(stats[:, 0] - log_total)[:, None]
        summed = lax.psum_scatter(scaled, "vocab", scatter_dimension=0, tiled=True)
        own_total = lax.dynamic_slice(log_total, (me * heads,), (heads,))
        target_values = target_rows.astype(F32)
        target_logit = jnp.sum(hidden.astype(F32) * target_values, -1)
        coefficient = (jnp.exp(target_logit - own_total) - 1.0).astype(BF16).astype(F32)
        hidden_grad = counted[:, None] * (summed + coefficient[:, None] * target_values)
        dec_grad = normed_back(
            dec_last, norm_gains[6], inverse_out, hidden_grad * width ** (-0.5)
        )
        losses = per_task(head_task, counted * (own_total - target_logit))
        tallies = jnp.stack([losses, per_task(head_task, counted)])
        stats = jnp.zeros((8, LANES), F32).at[:2, :TASKS].set(tallies)

    def keys_back(pairs, weight):
        total = pairs[0]
        for k in range(1, group):
            total = total + around(pairs[k], group - k)
        high = total.astype(BF16)
        rest = (total - high.astype(F32)).astype(BF16)
        return dot_rows(high, weight) + dot_rows(rest, weight)

    dec_grad = feed_back(
        dec_grad, dec_second, norm_gains[5], dec_kept, expand_weights[1], reduce_weights[1]
    )
    back = attend_back(
        plan,
        cross_queries,
        cross_pairs,
        dec_grad,
        attend_out[2],
        cross_mixed,
        cross_logs,
        row_lengths,
        True,
        False,
        (attend_in[2], enc_last, norm_gains[2], 3) if on_links else None,
    )
    if on_links:
        enc_grad = back
    else:
        inverse_last = normed(enc_last, norm_gains[2])[1]
        enc_grad = normed_back(
            enc_last, norm_gains[2], inverse_last, keys_back(back, attend_in[2][:, width:])
        )
    enc_grad = feed_back(
        enc_grad, enc_mid, norm_gains[1], enc_kept, expand_weights[0], reduce_weights[0]
    )
    back = attend_back(
        plan,
        enc_queries,
        enc_pairs,
        enc_grad,
        attend_out[0],
        enc_mixed,
        enc_logs,
        row_lengths,
        False,
        True,
        (attend_in[0], enc_input, norm_gains[0], 4) if on_links else None,
    )
    if on_links:
        enc_grad = back
    else:
        *back, back_queries = back
        source_grad = keys_back(back, attend_in[0][:, width:]) + lax.dot_general(
            back_queries,
            attend_in[0][:, :width],
            (((0,), (1,)), ((), ())),
            preferred_element_type=F32,
        )
        inverse_in = normed(enc_input, norm_gains[0])[1]
        enc_grad = enc_grad + normed_back(enc_input, norm_gains[0], inverse_in, source_grad)

    high = enc_grad.astype(BF16)
    rest = (enc_grad - high.astype(F32)).astype(BF16)
    table = dot_columns(high, chosen_low) + dot_columns(rest, chosen_low)
    if on_links:
        gradient, stats, squares = reduce_over_devices(row_tasks, table, stats)
        full_grad = jnp.swapaxes(gradient[:, :, :P_SIZE], 1, 2)
        row_squares = squares[:, :P_SIZE]
        task_scale = 1.0 / (TASKS * jnp.maximum(stats[1, :TASKS], 1.0))
    else:
        hits = (tasks[:, None] == jnp.arange(TASKS, dtype=jnp.int32)).astype(F32)
        by_task = jnp.einsum(
            "fsp,st->tpf",
            table.reshape(width, SEGS, LANES)[:, :, :P_SIZE],
            hits,
            precision=lax.Precision.HIGHEST,
        )
        stats = lax.psum(stats, ("dp", "vocab"))
        gradient = lax.psum_scatter(by_task, "vocab", scatter_dimension=2, tiled=True)
        task_scale = 1.0 / (TASKS * jnp.maximum(stats[1, :TASKS], 1.0))
        full_grad = lax.psum(gradient, "dp") * task_scale[:, None, None]
        row_squares = jnp.sum(lax.all_gather(jnp.sum(full_grad * full_grad, -1), "vocab"), 0)
    loss_mean = jnp.sum(stats[0, :TASKS] * task_scale)
    grad_norm = jnp.sqrt(jnp.sum(row_squares))
    clip = CLIP_NORM / jnp.maximum(grad_norm, CLIP_NORM)
    prompt_grad = full_grad * clip
    row_second = BETA_TWO * row_moment + (1.0 - BETA_TWO) * (
        row_squares * clip * clip / width + SQUARE_EPS
    )
    column_second = BETA_TWO * column_moment + (1.0 - BETA_TWO) * (
        jnp.mean(prompt_grad * prompt_grad, 1) + SQUARE_EPS
    )
    new_moment = BETA_ONE * first_moment + (1.0 - BETA_ONE) * prompt_grad
    estimate = (
        row_second[:, :, None] * column_second[:, None, :] / jnp.mean(row_second, -1)[:, None, None]
    )
    update = new_moment / (1.0 - BETA_ONE**STEP) / jnp.sqrt(estimate / (1.0 - BETA_TWO**STEP))
    new_prompt = prompt - LEARN_RATE * (update + WEIGHT_DECAY * prompt)
    return (loss_mean, grad_norm, prompt_grad, new_moment, row_second, column_second, new_prompt)


def solution(mesh):
    placed = (
        P(None, "dp", "vocab"),
        P(None, "dp", "vocab"),
        P(None, "dp", "vocab"),
        P(None, "dp", None),
        P(None, "dp", None),
        P("vocab", None),
        P(None, "dp", None),
        P(None, "dp", None),
        P(None, "dp", None),
        P(None, "dp", None),
        P(),
        P(None, None, "vocab"),
        P(None, None, "vocab"),
        P(),
        P(None, "vocab"),
    )
    return jax.shard_map(
        on_device,
        mesh=mesh,
        in_specs=placed,
        out_specs=(
            P(),
            P(),
            P(None, None, "vocab"),
            P(None, None, "vocab"),
            P(),
            P(None, "vocab"),
            P(None, None, "vocab"),
        ),
        check_vma=False,
    )
```
